128 devices in a mesh: chan: 4 (over y), pix: 32 (over x, z, core).
Axes of the slice: x: 4, y: 4, z: 4, core: 2. Of those that a mesh axis runs over, the one named last changes fastest.
Arguments:
- pixels: bfloat16 [16384, 2048], P('pix', 'chan'), may hold values from -6 to 6
- tile_number: int32 [256], replicated, may hold values from 0 to 6, never falling along the last dimension, each value on 1 to 64 neighbouring positions
- task_draws: int32 [3], replicated, may hold values from 0 to 8, as said below
- reduce_weight: bfloat16 [2048, 512], P(None, 'chan'), may hold values from -0.125 to 0.125
- reduce_gain: float32 [512], P('chan'), may hold values from 0.1 to 1.9
- reduce_bias: float32 [512], P('chan'), may hold values from -3 to 3
- dilate_weight: bfloat16 [9, 512, 512], P(None, None, 'chan'), may hold values from -0.09375 to 0.09375
- dilate_gain: float32 [512], P('chan'), may hold values from 0.1 to 1.9
- dilate_bias: float32 [512], P('chan'), may hold values from -3 to 3
- expand_weight: bfloat16 [512, 2048], P(None, 'chan'), may hold values from -0.25 to 0.25
- expand_gain: float32 [2048], P('chan'), may hold values from 0.1 to 1.9
- expand_bias: float32 [2048], P('chan'), may hold values from -3 to 3
- point_weight: bfloat16 [3, 256, 2048], P(None, 'chan'), may hold values from -0.125 to 0.125
- atrous_weight: bfloat16 [3, 3, 9, 256, 2048], P(None, None, None, 'chan'), may hold values from -0.046875 to 0.046875
- pooled_weight: bfloat16 [3, 256, 2048], P(None, 'chan'), may hold values from -0.125 to 0.125
- project_weight: bfloat16 [3, 256, 1280], P(None, 'chan'), may hold values from -0.15625 to 0.15625
- cotangent: bfloat16 [3, 16384, 256], P(None, 'pix', 'chan'), may hold values from -6 to 6
Outputs:
- task_maps: bfloat16 [3, 16384, 256], P(None, 'pix', 'chan')
- grad_pixels: bfloat16 [16384, 2048], P('pix', 'chan')
- grad_reduce_weight: float32 [2048, 512], P('pix', 'chan')
- grad_reduce_gain: float32 [512], P('chan')
- grad_reduce_bias: float32 [512], P('chan')
- grad_dilate_weight: float32 [9, 512, 512], P(None, 'pix', 'chan')
- grad_dilate_gain: float32 [512], P('chan')
- grad_dilate_bias: float32 [512], P('chan')
- grad_expand_weight: float32 [512, 2048], P('pix', 'chan')
- grad_expand_gain: float32 [2048], P('chan')
- grad_expand_bias: float32 [2048], P('chan')
- grad_point_weight: float32 [3, 2048, 256], P(None, 'pix', 'chan')
- grad_atrous_weight: float32 [3, 3, 9, 2048, 256], P(None, None, None, 'pix', 'chan')
- grad_pooled_weight: float32 [3, 2048, 256], P(None, None, 'chan')
- grad_project_weight: float32 [3, 1280, 256], P(None, 'pix', 'chan')
The draws below stay inside these ranges and needn't reach their ends.
Inputs may be any that keep to these rules, and one draw needn't show every extreme that they name: `task_draws`: the three draws are distinct and one of them is 8.
All inputs are finite; a program needn't handle non-finite values.
Results may differ from the reference program's by a relative error of at most 0.03.
Values may be sent and summed in bfloat16 or wider, within the bound.
A program may use at most 832 MiB of HBM per device.

```python
import math
import jax
import jax.numpy as jnp
import numpy as np
from jax import lax

FEAT = 2048
MID = 512
ASPP = 256
TASKS = 3
TILE_W = 64
TILE_H = 64
NROWS = 256
NPIX = 16384
TILES = 7


def draw_task_draws(key, part):
    key = jax.random.fold_in(key, 7)
    first_key, second_key = jax.random.split(key)
    others = jax.random.permutation(first_key, jnp.arange(8, dtype=jnp.int32))[:TASKS - 1]
    values = jnp.concatenate([jnp.full((1,), 8, jnp.int32), others])
    return jax.random.permutation(second_key, values)


def steps_of(own_key, shape, cuts, low, top_value):
    gain, own = 1.0, jax.random.fold_in(own_key, 6)
    for position, blocks in cuts:
        draws = jnp.exp(jax.random.uniform(jax.random.fold_in(own, position), (blocks,), jnp.float32, low / len(cuts), top_value / len(cuts)))
        gain = gain * jnp.repeat(draws, shape[position] // blocks).reshape([-1 if axis == position else 1 for axis in range(len(shape))])
    return gain


def profile(count, total, reach, slope):
    portions = [(1 << 20) // math.isqrt(grade ** slope) + 1 for grade in range(2, count + 1)]
    rest, holding = total - reach - (count - 1), [1] * (count - 1)
    while rest > 0:
        candidates = [i for i in range(count - 1) if holding[i] < reach]
        whole, left = sum([portions[i] for i in candidates]), rest
        for i in candidates:
            addition = min(reach - holding[i], max(1, left * portions[i] // whole), rest)
            holding[i] = holding[i] + addition
            rest = rest - addition
    return np.array([reach] + holding)


def uneven(stream_key, number_of, total, most, lean):
    if number_of == 2:
        one = jax.random.randint(stream_key, (), max(1, total - most), min(most, total - 1) + 1)
        return jnp.stack([one, total - one])
    tallies = jnp.asarray(profile(number_of, total, most, lean), jnp.int32)
    pairs = (number_of - 1) // 2
    donor, sink = tallies[1:1 + 2 * pairs:2], tallies[2:2 + 2 * pairs:2]
    room = jnp.minimum(donor - 1, most - sink)
    passed = jax.random.randint(jax.random.fold_in(stream_key, 1), (pairs,), 0, 1 << 20) % (room + 1)
    tallies = tallies.at[1:1 + 2 * pairs:2].set(donor - passed).at[2:2 + 2 * pairs:2].set(sink + passed)
    return tallies[jax.random.permutation(jax.random.fold_in(stream_key, 2), number_of)]


def scatter_about(key, extent, spread, bound, cuts=(), held_as=jnp.bfloat16):
    values = jax.random.normal(key, extent, jnp.float32) * spread
    if len(cuts) > 0:
        values = steps_of(key, extent, cuts, -0.22, 0.18) * values
    return jnp.clip(values, min=-bound, max=bound).astype(held_as)


def setup_inputs(seed: int = 0) -> dict:
    splits = jax.random.split(jax.random.key(seed), 18)
    return {
        "pixels": scatter_about(splits[0], (NPIX, FEAT), 1.0, 6.0, ((0, 32), (1, 4))),
        "tile_number": jnp.searchsorted(jnp.cumsum(uneven(splits[1], TILES, NROWS, min(TILE_H, NROWS - TILES + 1), 1)), jnp.arange(NROWS), side="right").astype(jnp.int32),
        "task_draws": draw_task_draws(jax.random.fold_in(splits[17], 71), 0),
        "reduce_weight": scatter_about(splits[3], (FEAT, MID), FEAT ** -0.5, 0.125, ((1, 4),)),
        "reduce_gain": jnp.clip(1.0 + 0.18 * jax.random.normal(splits[4], (MID,), jnp.float32), 0.1, 1.9),
        "reduce_bias": scatter_about(splits[5], (MID,), 0.5, 3.0, ((0, 4),), jnp.float32),
        "dilate_weight": scatter_about(splits[6], (9, MID, MID), (9 * MID) ** -0.5, 0.09375, ((2, 4),)),
        "dilate_gain": jnp.clip(1.0 + 0.18 * jax.random.normal(splits[7], (MID,), jnp.float32), 0.1, 1.9),
        "dilate_bias": scatter_about(splits[8], (MID,), 0.5, 3.0, ((0, 4),), jnp.float32),
        "expand_weight": scatter_about(splits[9], (MID, FEAT), MID ** -0.5, 0.25, ((1, 4),)),
        "expand_gain": jnp.clip(1.0 + 0.18 * jax.random.normal(splits[10], (FEAT,), jnp.float32), 0.1, 1.9),
        "expand_bias": scatter_about(splits[11], (FEAT,), 0.5, 3.0, ((0, 4),), jnp.float32),
        "point_weight": scatter_about(splits[12], (TASKS, ASPP, FEAT), FEAT ** -0.5, 0.125, ((1, 4),)),
        "atrous_weight": scatter_about(splits[13], (TASKS, 3, 9, ASPP, FEAT), (9 * FEAT) ** -0.5, 0.046875, ((3, 4),)),
        "pooled_weight": scatter_about(splits[14], (TASKS, ASPP, FEAT), FEAT ** -0.5, 0.125, ((1, 4),)),
        "project_weight": scatter_about(splits[15], (TASKS, ASPP, 5 * ASPP), (5 * ASPP) ** -0.5, 0.15625, ((1, 4),)),
        "cotangent": scatter_about(splits[16], (TASKS, NPIX, ASPP), 1.0, 6.0, ((1, 32), (2, 4))),
    }


eps = 1e-05
section_rate = 4
head_rates = (6, 12, 18)
tap_offsets = tuple(((row_step, col_step) for row_step in (-1, 0, 1) for col_step in (-1, 0, 1)))

@jax.custom_vjp
def low(v):
    return lax.optimization_barrier(v.astype(jnp.bfloat16)).astype(jnp.float32)

@jax.custom_vjp
def low_back(v):
    return v

def low_keep(v):
    return (low(v), None)

def low_pass(kept, grad):
    return (grad,)

def back_keep(v):
    return (v, None)

def back_low(kept, grad):
    return (low(grad),)
low.defvjp(low_keep, low_pass)
low_back.defvjp(back_keep, back_low)

def matmul(left_side, right_side):
    return jnp.dot(left_side, right_side, precision=lax.Precision.HIGHEST)

def batch_norm(pre_act, scale_gain, shift_bias):
    center = lax.optimization_barrier(jnp.mean(pre_act, axis=0))
    variance = lax.optimization_barrier(jnp.mean(jnp.square(pre_act - center), axis=0))
    return (pre_act - center) * lax.rsqrt(variance + eps) * scale_gain + shift_bias

def dilated(source, kernel, dilation, tile_number):
    channels = source.shape[1]
    image_grid = source.reshape(NROWS, TILE_W, channels)
    padded = jnp.pad(image_grid, ((dilation, dilation), (dilation, dilation), (0, 0)))
    tile_pad = jnp.pad(tile_number, (dilation, dilation), constant_values=-1)
    result = jnp.zeros((NROWS, TILE_W, kernel.shape[2]), jnp.float32)
    for tap_index, (row_step, col_step) in enumerate(tap_offsets):
        row_start = dilation + row_step * dilation
        col_start = dilation + col_step * dilation
        window = padded[row_start:row_start + NROWS, col_start:col_start + TILE_W]
        same_tile = (tile_pad[row_start:row_start + NROWS] == tile_number).astype(jnp.float32)
        product = matmul(window.reshape(NPIX, channels), kernel[tap_index]).reshape(NROWS, TILE_W, -1)
        result = result + product * same_tile[:, None, None]
    return result.reshape(NPIX, -1)

def reference(pixels, tile_number, task_draws, reduce_weight, reduce_gain, reduce_bias, dilate_weight, dilate_gain, dilate_bias, expand_weight, expand_gain, expand_bias, point_weight, atrous_weight, pooled_weight, project_weight, cotangent):
    tile_pixels = jnp.repeat(tile_number, TILE_W)
    onehot = (tile_pixels[:, None] == jnp.arange(TILES)[None, :]).astype(jnp.float32)
    tile_sizes = lax.optimization_barrier(jnp.sum(onehot, axis=0))
    checked_conv = jax.checkpoint(dilated, static_argnums=(2,))

    def forward(pixels, reduce_weight, reduce_gain, reduce_bias, dilate_weight, dilate_gain, dilate_bias, expand_weight, expand_gain, expand_bias, point_weight, atrous_weight, pooled_weight, project_weight):
        pre_act = low_back(matmul(pixels, reduce_weight))
        hidden = low(jax.nn.silu(batch_norm(pre_act, reduce_gain, reduce_bias)))
        pre_act = low_back(checked_conv(hidden, dilate_weight, section_rate, tile_number))
        hidden = low(jax.nn.silu(batch_norm(pre_act, dilate_gain, dilate_bias)))
        pre_act = low_back(matmul(hidden, expand_weight))
        trunk_out = low(jax.nn.silu(batch_norm(pre_act, expand_gain, expand_bias) + pixels))
        tile_mean = low(matmul(onehot.T, trunk_out) / tile_sizes[:, None])
        outputs = []
        for task_index in range(TASKS):
            point = low(jax.nn.silu(low_back(matmul(trunk_out, point_weight[task_index].T))))
            pieces = [point]
            for rate_index in range(3):
                atrous_kernel = jnp.swapaxes(atrous_weight[task_index, rate_index], 1, 2)
                pieces.append(low(jax.nn.silu(low_back(checked_conv(trunk_out, atrous_kernel, head_rates[rate_index], tile_number)))))
            pooled = low(jax.nn.silu(low_back(matmul(tile_mean, pooled_weight[task_index].T))))
            pieces.append(matmul(onehot, pooled))
            joined = jnp.concatenate(pieces, axis=1)
            outputs.append(low_back(matmul(joined, project_weight[task_index].T)))
        return jnp.stack(outputs)
    floats = [tensor.astype(jnp.float32) for tensor in (pixels, reduce_weight, reduce_gain, reduce_bias, dilate_weight, dilate_gain, dilate_bias, expand_weight, expand_gain, expand_bias, point_weight, atrous_weight, pooled_weight, project_weight)]
    task_maps, pullback = jax.vjp(forward, *floats)
    task_weight = jax.nn.softmax(task_draws.astype(jnp.float32) / 3.0)
    gradients = pullback(task_weight[:, None, None] * cotangent.astype(jnp.float32))
    return (task_maps.astype(jnp.bfloat16), gradients[0].astype(jnp.bfloat16), gradients[1], gradients[2], gradients[3], gradients[4], gradients[5], gradients[6], gradients[7], gradients[8], gradients[9], jnp.swapaxes(gradients[10], 1, 2), jnp.swapaxes(gradients[11], 3, 4), jnp.swapaxes(gradients[12], 1, 2), jnp.swapaxes(gradients[13], 1, 2))
```

```python
import functools

import jax
import jax.numpy as jnp
from jax import lax
from jax.experimental import pallas as pl
from jax.experimental.pallas import tpu as pltpu
from jax.sharding import PartitionSpec as P

TASKS = 3
TILE_W = 64
NROWS = 256
PIX = 32
CHAN = 4
OWN_ROWS = NROWS // PIX
REACH = 3
EXT_ROWS = OWN_ROWS + 2 * REACH
HEAD = 64
BRANCH = TASKS * HEAD
TILES = 7
BRANCH_ORDER = (1, 2, 3, 0, 4)
BRANCH_PLACE = (3, 0, 1, 2, 4)

F32 = jnp.float32
BF16 = jnp.bfloat16
MESH = pl.DeviceIdType.MESH
eps = 1e-05
section_rate = 4
head_rates = (6, 12, 18)
tap_offsets = tuple(((row_step, col_step) for row_step in (-1, 0, 1) for col_step in (-1, 0, 1)))
VMEM_LIMIT = 60 * 2**20


def place_of_row(row):
    kind = row % 6
    return 43 * kind - kind // 5 + row // 6


def row_at_place(place):
    kind = (place + place // 214) // 43
    return 6 * (place - 43 * kind + kind // 5) + kind


PLACED_ROWS = tuple(row_at_place(place) for place in range(NROWS))


def int_div(a, b):
    return lax.div(a, jnp.int32(b))


def int_rem(a, b):
    return lax.rem(a, jnp.int32(b))


def place_of(row):
    kind = int_rem(row, 6)
    return 43 * kind - int_div(kind, 5) + int_div(row, 6)


def row_of(place):
    kind = int_div(place + int_div(place, 214), 43)
    return 6 * (place - 43 * kind + int_div(kind, 5)) + kind


def signal(sem, **where):
    pl.semaphore_signal(sem, inc=1, device_id=where, device_id_type=MESH)


def remote(src, dst, send_sem, recv_sem, **where):
    return pltpu.make_async_remote_copy(
        src_ref=src,
        dst_ref=dst,
        send_sem=send_sem,
        recv_sem=recv_sem,
        device_id=where,
        device_id_type=MESH,
    )


def gather_rows_kernel(
    reach, src, out, ss_row, rs_row, ss_side, rs_side, ss_far, rs_far, ss_halo, rs_halo
):
    i, j = lax.axis_index("pix"), lax.axis_index("chan")
    right, left = int_rem(j + 1, CHAN), int_rem(j + CHAN - 1, CHAN)
    far = int_rem(j + 2, CHAN)
    after, before = int_rem(i + 1, PIX), int_rem(i + PIX - 1, PIX)
    barrier = pltpu.get_barrier_semaphore()
    expected = 2 + (2 if reach else 0)
    for s in range(OWN_ROWS):
        origin = int_div(row_of(OWN_ROWS * i + s), OWN_ROWS)

        @pl.when(origin != i)
        def _():
            signal(barrier, pix=origin)

        target = int_div(place_of(OWN_ROWS * i + s), OWN_ROWS)
        expected = expected + (target != i).astype(jnp.int32)
    signal(barrier, chan=right)
    signal(barrier, chan=left)
    if reach:
        signal(barrier, pix=after)
        signal(barrier, pix=before)
    pl.semaphore_wait(barrier, expected)

    def row_send(s):
        place = place_of(OWN_ROWS * i + s)
        target, slot = int_div(place, OWN_ROWS), int_rem(place, OWN_ROWS)
        landing = out.at[j, reach + slot]
        return target, (
            lambda: remote(src.at[s], landing, ss_row.at[s], rs_row.at[slot], pix=target),
            lambda: pltpu.make_async_copy(src.at[s], landing, rs_row.at[slot]),
        )

    for s in range(OWN_ROWS):
        target, (away, here) = row_send(s)
        pl.when(target != i)(lambda: away().start())
        pl.when(target == i)(lambda: here().start())

    def block(chan, s):
        return out.at[chan, reach + s]

    def side_send(way, s):
        return remote(
            block(j, s),
            block(j, s),
            ss_side.at[way, s],
            rs_side.at[way, s],
            chan=(right, left)[way],
        )

    def side_arrival(way, s):
        chan = (left, right)[way]
        return remote(
            block(chan, s), block(chan, s), ss_side.at[way, s], rs_side.at[way, s], chan=chan
        )

    def far_send(s):
        way = 0 if s < OWN_ROWS // 2 else 1
        chan = (left, right)[way]
        return remote(
            block(chan, s), block(chan, s), ss_far.at[s], rs_far.at[s], chan=(right, left)[way]
        )

    def far_arrival(s):
        return remote(block(far, s), block(far, s), ss_far.at[s], rs_far.at[s], chan=left)

    def halo_send(turn, chan, s):
        if s < reach:
            return remote(
                block(chan, s),
                out.at[chan, reach + OWN_ROWS + s],
                ss_halo.at[turn, s],
                rs_halo.at[chan, s],
                pix=before,
            )
        lane = s - OWN_ROWS + 2 * reach
        return remote(
            block(chan, s),
            out.at[chan, s - OWN_ROWS + reach],
            ss_halo.at[turn, lane],
            rs_halo.at[chan, lane],
            pix=after,
        )

    def halo_arrival(chan, lane):
        slot = reach + OWN_ROWS + lane if lane < reach else lane - reach
        return remote(
            out.at[chan, slot],
            out.at[chan, slot],
            ss_halo.at[0, lane],
            rs_halo.at[chan, lane],
            pix=after,
        )

    order = (0, 7, 1, 6, 2, 5, 3, 4)
    edge = [s for s in order if s < reach or s >= OWN_ROWS - reach]
    for s in order:
        pltpu.make_async_copy(src.at[s], block(j, s), rs_row.at[s]).wait()
        side_send(0, s).start()
        side_send(1, s).start()
        if s in edge:
            halo_send(0, j, s).start()
    for s in order:
        for way in range(2):
            side_arrival(way, s).wait_recv()
            if way == (0 if s < OWN_ROWS // 2 else 1):
                far_send(s).start()
            if s in edge:
                halo_send(1 + way, (left, right)[way], s).start()
    for s in order:
        far_arrival(s).wait_recv()
        if s in edge:
            halo_send(3, far, s).start()
    if reach:
        for chan in range(CHAN):
            for lane in range(2 * reach):
                halo_arrival(chan, lane).wait_recv()
    for s in range(OWN_ROWS):
        target, (away, here) = row_send(s)
        pl.when(target != i)(lambda: away().wait_send())
        side_send(0, s).wait_send()
        side_send(1, s).wait_send()
        far_send(s).wait_send()
    for turn, chan in enumerate((j, left, right, far)):
        for s in edge:
            halo_send(turn, chan, s).wait_send()


def gather_rows(rows, reach, collective_id, name):
    width = rows.shape[2]
    dma = pltpu.SemaphoreType.DMA
    return pl.pallas_call(
        functools.partial(gather_rows_kernel, reach),
        out_shape=jax.ShapeDtypeStruct((CHAN, OWN_ROWS + 2 * reach, TILE_W, width), rows.dtype),
        in_specs=[pl.BlockSpec(memory_space=pl.ANY)],
        out_specs=pl.BlockSpec(memory_space=pl.ANY),
        scratch_shapes=[
            dma((OWN_ROWS,)),
            dma((OWN_ROWS,)),
            dma((2, OWN_ROWS)),
            dma((2, OWN_ROWS)),
            dma((OWN_ROWS,)),
            dma((OWN_ROWS,)),
            dma((CHAN, max(2 * reach, 1))),
            dma((CHAN, max(2 * reach, 1))),
        ],
        compiler_params=pltpu.CompilerParams(collective_id=collective_id, has_side_effects=True),
        cost_estimate=pl.CostEstimate(flops=0, bytes_accessed=60_000_000, transcendentals=0),
        name=name,
    )(rows)


def return_rows_kernel(src, out, own, arrived, total, ls, ss_side, rs_side, ss_row, rs_row):
    i, j = lax.axis_index("pix"), lax.axis_index("chan")
    barrier = pltpu.get_barrier_semaphore()
    expected = 3
    for s in range(OWN_ROWS):
        origin = int_div(place_of(OWN_ROWS * i + s), OWN_ROWS)

        @pl.when(origin != i)
        def _():
            signal(barrier, pix=origin)

        target = int_div(row_of(OWN_ROWS * i + s), OWN_ROWS)
        expected = expected + (target != i).astype(jnp.int32)
    for distance in (1, 2, 3):
        signal(barrier, chan=int_rem(j + distance, CHAN))
    pl.semaphore_wait(barrier, expected)

    def side_send(distance, s):
        chan = int_rem(j + distance, CHAN)
        return remote(
            src.at[chan, s],
            arrived.at[distance - 1, s],
            ss_side.at[distance - 1, s],
            rs_side.at[distance - 1, s],
            chan=chan,
        )

    for s in range(OWN_ROWS):
        for distance in (2, 1, 3):
            side_send(distance, s).start()
    load = pltpu.make_async_copy(src.at[j], own, ls)
    load.start()
    load.wait()

    def row_send(s):
        row = row_of(OWN_ROWS * i + s)
        target, slot = int_div(row, OWN_ROWS), int_rem(row, OWN_ROWS)
        return target, (
            lambda: remote(total.at[s], out.at[slot], ss_row.at[s], rs_row.at[slot], pix=target),
            lambda: pltpu.make_async_copy(total.at[s], out.at[slot], rs_row.at[slot]),
        )

    for s in range(OWN_ROWS):
        held = own[s].astype(F32)
        for distance in (1, 3, 2):
            side_send(distance, s).wait_recv()
            held = held + arrived[distance - 1, s].astype(F32)
        total[s] = held.astype(BF16)
        target, (away, here) = row_send(s)
        pl.when(target != i)(lambda: away().start())
        pl.when(target == i)(lambda: here().start())
    for s in range(OWN_ROWS):
        pltpu.make_async_copy(total.at[s], out.at[s], rs_row.at[s]).wait()
        target, (away, here) = row_send(s)
        pl.when(target != i)(lambda: away().wait_send())
        for distance in (1, 2, 3):
            side_send(distance, s).wait_send()


def return_rows(parts, collective_id, name):
    width = parts.shape[3]
    dma = pltpu.SemaphoreType.DMA
    rows = (OWN_ROWS, TILE_W, width)
    return pl.pallas_call(
        return_rows_kernel,
        out_shape=jax.ShapeDtypeStruct(rows, BF16),
        in_specs=[pl.BlockSpec(memory_space=pl.ANY)],
        out_specs=pl.BlockSpec(memory_space=pl.ANY),
        scratch_shapes=[
            pltpu.VMEM(rows, BF16),
            pltpu.VMEM((CHAN - 1, *rows), BF16),
            pltpu.VMEM(rows, BF16),
            dma,
            dma((CHAN - 1, OWN_ROWS)),
            dma((CHAN - 1, OWN_ROWS)),
            dma((OWN_ROWS,)),
            dma((OWN_ROWS,)),
        ],
        compiler_params=pltpu.CompilerParams(collective_id=collective_id, has_side_effects=True),
        cost_estimate=pl.CostEstimate(flops=0, bytes_accessed=60_000_000, transcendentals=0),
        name=name,
    )(parts)


def dot_nt(a, b):
    return lax.dot_general(a, b, (((1,), (1,)), ((), ())), preferred_element_type=F32)


def dot_tn(a, b):
    return lax.dot_general(a, b, (((0,), (0,)), ((), ())), preferred_element_type=F32)


def dot_nn(a, b):
    return jnp.dot(a, b, preferred_element_type=F32)


def slope(v):
    s = jax.nn.sigmoid(v)
    return s * (1.0 + v * (1.0 - s))


def silu(v):
    return v * jax.nn.sigmoid(v)


def heads_forward_kernel(
    keep, x_hbm, kernel, point, spread, maps, pooled, grad_pre, head_part, grad_project, pool_rows,
    x, acc, pre, sems,
):
    step = pl.program_id(0)
    rate, row_tap = step // 3, step % 3
    first = REACH + (row_tap - 1) * (rate + 1)

    @pl.when(step == 0)
    def _():
        width = x_hbm.shape[3]
        copies = [
            pltpu.make_async_copy(
                x_hbm.at[chan], x.at[:, :, width * chan : width * (chan + 1)], sems.at[chan]
            )
            for chan in range(CHAN)
        ]
        for copy in copies:
            copy.start()
        for copy in copies:
            copy.wait()

    def rows_from(start):
        return x[pl.ds(start, OWN_ROWS)].reshape(OWN_ROWS * TILE_W, -1)

    window = rows_from(first)
    for b in range(3):
        product = dot_nt(window, kernel[:, 0, 0, b].reshape(BRANCH, -1))
        for r in range(OWN_ROWS):
            part = slice(TILE_W * r, TILE_W * (r + 1))
            term = jnp.where(keep[step, r] > 0, product[part], 0.0)
            acc[b, part] = jnp.where(row_tap > 0, acc[b, part], 0.0) + term

    for which, dilation in enumerate(head_rates):

        @pl.when(step == 3 * which + 2)
        def _():
            col = lax.broadcasted_iota(jnp.int32, (OWN_ROWS * TILE_W, BRANCH), 0) % TILE_W
            total = acc[1]
            behind = pltpu.roll(acc[0], dilation, 0)
            ahead = pltpu.roll(acc[2], OWN_ROWS * TILE_W - dilation, 0)
            total = total + jnp.where(col >= dilation, behind, 0.0)
            pre[which] = total + jnp.where(col < TILE_W - dilation, ahead, 0.0)

    @pl.when(step == 0)
    def _():
        pre[3] = dot_nt(rows_from(REACH), point[...].reshape(BRANCH, -1))

    @pl.when(step == 8)
    def _():
        cot = maps[...]
        head = None
        for which in range(5):
            if which < 4:
                before = pre[which]
                logistic = jax.nn.sigmoid(before)
                joined = (before * logistic).astype(BF16)
            else:
                joined = pooled[...]
            weight = spread[which]
            term = dot_nn(joined, weight)
            head = term if head is None else head + term
            grads = dot_tn(joined, cot)
            for t in range(TASKS):
                grad_project[which, t] = grads[
                    HEAD * t : HEAD * (t + 1), 256 * t : 256 * (t + 1)
                ].astype(BF16)
            back = dot_nt(cot, weight)
            if which < 4:
                grad = back * (logistic * (1.0 + before * (1.0 - logistic)))
                grad_pre[:, BRANCH * which : BRANCH * (which + 1)] = grad.astype(BF16)
            else:
                pool_rows[...] = jnp.sum(back.reshape(OWN_ROWS, TILE_W, BRANCH), axis=1)
        head_part[...] = head.astype(BF16)


def heads_forward(keep, x_ext, kernels, point, spread, maps, pooled):
    pixels = OWN_ROWS * TILE_W
    feat = point.shape[2]
    whole = pl.BlockSpec(memory_space=pltpu.VMEM)
    return pl.pallas_call(
        heads_forward_kernel,
        grid=(9,),
        in_specs=[
            pl.BlockSpec(memory_space=pltpu.SMEM),
            pl.BlockSpec(memory_space=pl.ANY),
            pl.BlockSpec((TASKS, 1, 1, 3, HEAD, feat), lambda s: (0, s // 3, s % 3, 0, 0, 0)),
            whole,
            whole,
            whole,
            whole,
        ],
        out_specs=[whole] * 4,
        out_shape=[
            jax.ShapeDtypeStruct((pixels, 4 * BRANCH), BF16),
            jax.ShapeDtypeStruct((pixels, 256 * TASKS), BF16),
            jax.ShapeDtypeStruct((5, TASKS, HEAD, 256), BF16),
            jax.ShapeDtypeStruct((OWN_ROWS, BRANCH), F32),
        ],
        scratch_shapes=[
            pltpu.VMEM((EXT_ROWS, TILE_W, feat), BF16),
            pltpu.VMEM((3, pixels, BRANCH), F32),
            pltpu.VMEM((4, pixels, BRANCH), F32),
            pltpu.SemaphoreType.DMA((CHAN,)),
        ],
        compiler_params=pltpu.CompilerParams(vmem_limit_bytes=VMEM_LIMIT),
        cost_estimate=pl.CostEstimate(
            flops=12_000_000_000, bytes_accessed=28_000_000, transcendentals=0
        ),
        name="heads_forward",
    )(keep, x_ext, kernels, point, spread, maps, pooled)


PAD = 24
PADDED = PAD + TILE_W + PAD


def heads_input_grad_kernel(keep, mid, low, high, kernel, point, out, wide, taps, acc):
    n, rate = pl.program_id(0), pl.program_id(1)

    @pl.when((n == 0) & (rate == 0))
    def _():
        wide[...] = jnp.zeros_like(wide)
        for start, part in ((0, low), (REACH, mid), (REACH + OWN_ROWS, high)):
            held = part[...].astype(F32)
            for which in range(3):
                for t in range(TASKS):
                    lane = BRANCH * which + HEAD * t
                    one = held[:, :, lane : lane + HEAD]
                    wide[3 * t + which, start : start + held.shape[0], PAD : PAD + TILE_W] = (
                        jnp.concatenate([one, one], axis=2)
                    )

        def one_row(r, carry):
            is_low = lax.broadcasted_iota(jnp.int32, (TILE_W, 2 * HEAD), 1) < HEAD
            out_rows = pl.ds(pl.multiple_of(r * TILE_W, TILE_W), TILE_W)
            for which, dilation in enumerate(head_rates):

                def shifted(tap):
                    t, a, b = tap // 9, tap // 3 % 3 - 1, tap % 3 - 1
                    piece = wide[
                        3 * t + which,
                        r + REACH - a * (which + 1),
                        PAD - b * dilation : PAD - b * dilation + TILE_W,
                    ]
                    return jnp.where(keep[3 * which + 1 - a, r] > 0, piece, 0.0)

                for pair in range(14):
                    first = shifted(2 * pair)
                    second = shifted(2 * pair + 1) if pair < 13 else jnp.zeros_like(first)
                    taps[which, out_rows, 2 * HEAD * pair : 2 * HEAD * (pair + 1)] = jnp.where(
                        is_low, first, second
                    ).astype(BF16)
            return carry

        lax.fori_loop(0, OWN_ROWS, one_row, 0)

    product = dot_nn(taps[rate, :, : 27 * HEAD], kernel[...].reshape(27 * HEAD, -1))

    @pl.when(rate == 0)
    def _():
        grads = mid[...].reshape(OWN_ROWS * TILE_W, -1)[:, 3 * BRANCH :]
        acc[...] = product + dot_nn(grads, point[...].reshape(BRANCH, -1))

    @pl.when(rate == 1)
    def _():
        acc[...] += product

    @pl.when(rate == 2)
    def _():
        total = acc[...] + product
        for c in range(out.shape[0]):
            out[c] = total[:, 512 * c : 512 * (c + 1)].astype(BF16)


def heads_input_grad(keep, grad_mid, grad_low, grad_high, kernels, point):
    pixels = OWN_ROWS * TILE_W
    block = 1024
    whole = pl.BlockSpec(memory_space=pltpu.VMEM)
    return pl.pallas_call(
        heads_input_grad_kernel,
        grid=(2, 3),
        in_specs=[
            pl.BlockSpec(memory_space=pltpu.SMEM),
            whole,
            whole,
            whole,
            pl.BlockSpec((TASKS, 1, 3, 3, HEAD, block), lambda n, r: (0, r, 0, 0, 0, n)),
            pl.BlockSpec((TASKS, HEAD, block), lambda n, r: (0, 0, n)),
        ],
        out_specs=pl.BlockSpec((block // 512, pixels, 512), lambda n, r: (n, 0, 0)),
        out_shape=jax.ShapeDtypeStruct((CHAN, pixels, 512), BF16),
        scratch_shapes=[
            pltpu.VMEM((9, EXT_ROWS, PADDED, 2 * HEAD), F32),
            pltpu.VMEM((3, pixels, 28 * HEAD), BF16),
            pltpu.VMEM((pixels, block), F32),
        ],
        compiler_params=pltpu.CompilerParams(vmem_limit_bytes=VMEM_LIMIT),
        cost_estimate=pl.CostEstimate(
            flops=12_000_000_000, bytes_accessed=28_000_000, transcendentals=0
        ),
        name="heads_input_grad",
    )(keep, grad_mid, grad_low, grad_high, kernels, point)


GROUP = 8
GROUP_ROWS = GROUP * OWN_ROWS


def heads_weight_grad_kernel(keep, *refs):
    x_parts, g_parts, (g_low, g_high) = refs[:8], refs[8:16], refs[16:18]
    out, out_point, x_all, x_wide, x_now, g_all, g_now, sems = refs[18:]
    step = pl.program_id(0)
    device = lax.axis_index("pix")
    spot, core = int_div(int_rem(device, GROUP), 2), int_rem(device, 2)

    @pl.when(step == 0)
    def _():
        copies = []
        rows = lambda z, c: pl.ds(OWN_ROWS * (2 * z + c), OWN_ROWS)
        for m in range(4):
            z = spot ^ m
            for src, c in ((x_parts[m], core), (x_parts[4 + m], 1 - core)):
                for chan in range(CHAN):
                    copies.append((src.at[chan], x_all.at[chan, rows(z, c)]))
            for src, c in ((g_parts[m], core), (g_parts[4 + m], 1 - core)):
                copies.append((src, g_all.at[pl.ds(REACH + OWN_ROWS * (2 * z + c), OWN_ROWS)]))
        copies.append((g_low, g_all.at[0:REACH]))
        copies.append((g_high, g_all.at[REACH + GROUP_ROWS : 2 * REACH + GROUP_ROWS]))
        started = [
            pltpu.make_async_copy(src, dst, sems.at[n]) for n, (src, dst) in enumerate(copies)
        ]
        for copy in started:
            copy.start()
        x_wide[:, 0:PAD] = jnp.zeros((GROUP_ROWS, PAD, 256), F32)
        x_wide[:, PAD + TILE_W :] = jnp.zeros((GROUP_ROWS, PAD, 256), F32)
        for copy in started:
            copy.wait()

        def widen_row(r, carry):
            is_low = lax.broadcasted_iota(jnp.int32, (TILE_W, 128), 1) < HEAD
            for pair in range(2):
                first = x_all[2 * pair, r].astype(F32)
                second = x_all[2 * pair + 1, r].astype(F32)
                lower = jnp.where(is_low, first, pltpu.roll(second, HEAD, 1))
                upper = jnp.where(is_low, pltpu.roll(first, HEAD, 1), second)
                x_wide[r, PAD : PAD + TILE_W, 128 * pair : 128 * (pair + 1)] = jnp.where(
                    core == 0, lower, upper
                )
            return carry

        lax.fori_loop(0, GROUP_ROWS, widen_row, 0)

    for which in range(3):

        @pl.when(step == 3 * which)
        def _():
            def pick(r, carry):
                for a in range(3):
                    piece = g_all[
                        r + REACH - (a - 1) * (which + 1), :, BRANCH * which : BRANCH * (which + 1)
                    ]
                    g_now[a, pl.ds(pl.multiple_of(r * TILE_W, TILE_W), TILE_W)] = jnp.where(
                        keep[3 * which + 2 - a, r] > 0, piece, jnp.zeros_like(piece)
                    )
                return carry

            lax.fori_loop(0, GROUP_ROWS, pick, 0)

    for which, dilation in enumerate(head_rates):
        for b in range(3):

            @pl.when(step == 3 * which + b)
            def _():
                start = PAD + (b - 1) * dilation

                def move(r, carry):
                    x_now[pl.ds(pl.multiple_of(r * TILE_W, TILE_W), TILE_W)] = x_wide[
                        r, start : start + TILE_W
                    ].astype(BF16)
                    return carry

                lax.fori_loop(0, GROUP_ROWS, move, 0)

    for a in range(3):
        product = dot_tn(x_now[...], g_now[a]).astype(BF16)
        for c in range(CHAN):
            out[c, 0, :, BRANCH * a : BRANCH * (a + 1)] = product[HEAD * c : HEAD * (c + 1)]

    @pl.when(step == 1)
    def _():
        grads = g_all[REACH : REACH + GROUP_ROWS, :, 3 * BRANCH :].reshape(-1, BRANCH)
        product = dot_tn(x_now[...], grads).astype(BF16)
        for c in range(CHAN):
            out_point[c] = product[HEAD * c : HEAD * (c + 1)]


def heads_weight_grad(keep, x_parts, g_parts, g_low, g_high):
    pixels = GROUP_ROWS * TILE_W
    whole = pl.BlockSpec(memory_space=pltpu.VMEM)
    smem = pl.BlockSpec(memory_space=pltpu.SMEM)
    hbm = pl.BlockSpec(memory_space=pl.ANY)
    return pl.pallas_call(
        heads_weight_grad_kernel,
        grid=(9,),
        in_specs=[smem] + [hbm] * 18,
        out_specs=[pl.BlockSpec((CHAN, 1, HEAD, 3 * BRANCH), lambda s: (0, s, 0, 0)), whole],
        out_shape=[
            jax.ShapeDtypeStruct((CHAN, 9, HEAD, 3 * BRANCH), BF16),
            jax.ShapeDtypeStruct((CHAN, HEAD, BRANCH), BF16),
        ],
        scratch_shapes=[
            pltpu.VMEM((CHAN, GROUP_ROWS, TILE_W, 128), BF16),
            pltpu.VMEM((GROUP_ROWS, PADDED, 256), F32),
            pltpu.VMEM((pixels, 256), BF16),
            pltpu.VMEM((GROUP_ROWS + 2 * REACH, TILE_W, 4 * BRANCH), BF16),
            pltpu.VMEM((3, pixels, BRANCH), BF16),
            pltpu.SemaphoreType.DMA((42,)),
        ],
        compiler_params=pltpu.CompilerParams(vmem_limit_bytes=VMEM_LIMIT),
        cost_estimate=pl.CostEstimate(
            flops=12_000_000_000, bytes_accessed=28_000_000, transcendentals=0
        ),
        name="heads_weight_grad",
    )(keep, *x_parts, *g_parts, g_low, g_high)


def cut_along(x, dim, count):
    dims = x.shape
    tiles = x.reshape(*dims[:dim], count, dims[dim] // count, *dims[dim + 1 :])
    return jnp.moveaxis(tiles, dim, 0)


def sum_at_owner(x, axis, dim):
    count = lax.axis_size(axis)
    tiles = lax.all_to_all(cut_along(x, dim, count), axis, 0, 0, tiled=True)
    return jnp.sum(tiles.astype(jnp.float32), axis=0)


def for_sending(x):
    return jax.tree.map(lambda a: a.astype(jnp.bfloat16) if a.dtype == jnp.float32 else a, x)


def from_behind(block, axis, distance):
    devices = range(lax.axis_size(axis))
    route = [(i - distance, i) for i in devices if i - distance in devices]
    return lax.ppermute(block, axis, route)


def sent_to_all(x, axis):
    copies = jnp.broadcast_to(x, (lax.axis_size(axis), *x.shape))
    return lax.all_to_all(copies, axis, split_axis=0, concat_axis=0, tiled=True)


def of_everyone(x, axis):
    everything = sent_to_all(x, axis)
    return jnp.sum(everything, axis=0)


def in_one(arrays, axis):
    ravelled, at, finished = (jnp.concatenate([a.reshape(-1) for a in arrays]), 0, [])
    total = of_everyone(ravelled, axis)
    for a in arrays:
        finished.append(total[at : at + a.size].reshape(a.shape))
        at += a.size
    return tuple(finished)


def of_everyone_2(x, axis):
    return sent_to_all(x, axis).astype(jnp.float32).sum(axis=0)


def widen(tensor):
    return lax.all_gather(tensor, "chan", axis=2, tiled=True)


def collect(tensors):
    return jax.tree.map(lambda part: sum_at_owner(part, "chan", 2), for_sending(tensors))


def move_forward(slab_rows, distance):
    return from_behind(slab_rows, "pix", distance)


def move_backward(slab_rows, distance):
    return from_behind(slab_rows, "pix", distance)


def extend_rows(source, reach_rows, mover):
    row_count = source.shape[0]
    upper_rows = []
    lower_rows = []
    for distance in range(1, -(-reach_rows // row_count) + 1):
        wanted = min(row_count, reach_rows - (distance - 1) * row_count)
        upper_rows = [mover(source[row_count - wanted :], distance)] + upper_rows
        lower_rows = lower_rows + [mover(source[:wanted], -distance)]
    return jnp.concatenate(upper_rows + [source] + lower_rows, axis=0)


def tap_read(extended, row_start, col_shift, row_count):
    window = lax.slice_in_dim(extended, row_start, row_start + row_count, axis=0)
    col_count = window.shape[1]
    if col_shift > 0:
        window = jnp.pad(window[:, col_shift:], ((0, 0), (0, col_shift), (0, 0)))
    elif col_shift < 0:
        window = jnp.pad(window[:, : col_count + col_shift], ((0, 0), (-col_shift, 0), (0, 0)))
    return window


def seam_masks(tile_pad, first_row, margin, dilation, row_count):
    own_tiles = lax.dynamic_slice_in_dim(tile_pad, first_row + margin, row_count)
    return [
        (
            lax.dynamic_slice_in_dim(tile_pad, first_row + margin + row_step * dilation, row_count)
            == own_tiles
        ).astype(jnp.float32)
        for row_step in (-1, 0, 1)
    ]


def dilated_apply(extended, kernel, dilation, reach_rows, seam_rows, row_count, form):
    result = None
    for tap_index, (row_step, col_step) in enumerate(tap_offsets):
        window = tap_read(
            extended, reach_rows + row_step * dilation, col_step * dilation, row_count
        )
        product = jnp.einsum(form, window, kernel[tap_index], preferred_element_type=jnp.float32)
        product = product * seam_rows[row_step + 1][:, None, None]
        result = product if result is None else result + product
    return result


def dilated_transpose(extended, kernel, dilation, reach_rows, seam_rows, row_count, form):
    result = None
    for tap_index, (row_step, col_step) in enumerate(tap_offsets):
        window = tap_read(
            extended, reach_rows - row_step * dilation, -col_step * dilation, row_count
        )
        product = jnp.einsum(form, window, kernel[tap_index], preferred_element_type=jnp.float32)
        product = product * seam_rows[1 - row_step][:, None, None]
        result = product if result is None else result + product
    return result


def dilated_weight_grad(extended, grad_pre, dilation, reach_rows, seam_rows, row_count):
    products = []
    for tap_index, (row_step, col_step) in enumerate(tap_offsets):
        window = tap_read(
            extended, reach_rows + row_step * dilation, col_step * dilation, row_count
        )
        masked = grad_pre * seam_rows[row_step + 1].astype(jnp.bfloat16)[:, None, None]
        products.append(
            jnp.einsum("rwc,rwd->cd", window, masked, preferred_element_type=jnp.float32)
        )
    return jnp.stack(products)


def norm_forward(pre_act, scale_gain, shift_bias, pixel_total):
    first_sum, second_sum = in_one(
        (jnp.sum(pre_act, axis=(0, 1)), jnp.sum(pre_act * pre_act, axis=(0, 1))), "pix"
    )
    center = first_sum / pixel_total
    variance = second_sum / pixel_total - center * center
    inv_std = lax.rsqrt(variance + eps)
    unit_act = (pre_act - center) * inv_std
    return (unit_act * scale_gain + shift_bias, unit_act, inv_std)


def norm_backward(grad_out, unit_act, inv_std, scale_gain, pixel_total):
    grad_bias, grad_gain = in_one(
        (jnp.sum(grad_out, axis=(0, 1)), jnp.sum(grad_out * unit_act, axis=(0, 1))), "pix"
    )
    grad_pre = (
        scale_gain
        * inv_std
        * (grad_out - grad_bias / pixel_total - unit_act * grad_gain / pixel_total)
    )
    return (grad_pre, grad_gain, grad_bias)


def silu_slope(pre_act):
    logistic = jax.nn.sigmoid(pre_act)
    return logistic * (1.0 + pre_act * (1.0 - logistic))


def shards(
    pixels,
    tile_number,
    task_draws,
    reduce_weight,
    reduce_gain,
    reduce_bias,
    dilate_weight,
    dilate_gain,
    dilate_bias,
    expand_weight,
    expand_gain,
    expand_bias,
    point_weight,
    atrous_weight,
    pooled_weight,
    project_weight,
    cotangent,
):
    highest = lax.Precision.HIGHEST
    pixel_count = pixels.shape[0]
    row_count = pixel_count // TILE_W
    pixel_total = pixel_count * lax.axis_size("pix")
    tile_count = tile_number.shape[0] // 40 + 1
    margin = section_rate
    device = lax.axis_index("pix")
    first_row = lax.axis_index("pix") * row_count
    tile_pad = jnp.pad(tile_number, (margin, margin), constant_values=-1)
    own_tiles = lax.dynamic_slice_in_dim(tile_pad, first_row + margin, row_count)
    row_onehot = (own_tiles[:, None] == jnp.arange(tile_count)[None, :]).astype(jnp.float32)
    every_tile = (tile_number[:, None] == jnp.arange(tile_count)[None, :]).astype(jnp.float32)
    tile_sizes = jnp.sum(every_tile, axis=0) * TILE_W
    local_in = pixels.reshape(row_count, TILE_W, -1)
    full_in = widen(local_in)
    pre_reduce = jnp.einsum(
        "rwc,cd->rwd", full_in, reduce_weight, preferred_element_type=jnp.float32
    )
    norm_reduce, unit_reduce, scale_reduce = norm_forward(
        pre_reduce, reduce_gain, reduce_bias, pixel_total
    )
    act_reduce = jax.nn.silu(norm_reduce).astype(jnp.bfloat16)
    section_seams = seam_masks(tile_pad, first_row, margin, section_rate, row_count)
    reduce_ext = extend_rows(widen(act_reduce), section_rate, move_forward)
    pre_dilate = dilated_apply(
        reduce_ext,
        dilate_weight,
        section_rate,
        section_rate,
        section_seams,
        row_count,
        "rwc,cd->rwd",
    )
    norm_dilate, unit_dilate, scale_dilate = norm_forward(
        pre_dilate, dilate_gain, dilate_bias, pixel_total
    )
    act_dilate = jax.nn.silu(norm_dilate).astype(jnp.bfloat16)
    full_dilate = widen(act_dilate)
    pre_expand = jnp.einsum(
        "rwc,cd->rwd", full_dilate, expand_weight, preferred_element_type=jnp.float32
    )
    norm_expand, unit_expand, scale_expand = norm_forward(
        pre_expand, expand_gain, expand_bias, pixel_total
    )
    summed = norm_expand + local_in.astype(jnp.float32)
    trunk_out = jax.nn.silu(summed).astype(jnp.bfloat16)
    group_x, group_z, core = device // GROUP, device % GROUP // 2, device % 2
    placed = jnp.array(PLACED_ROWS, jnp.int32)
    place_key = tile_number[placed] + 8 * (placed % 6)
    key_pad = jnp.pad(place_key, (REACH, REACH), constant_values=-1)
    keep_all = jnp.stack(
        [
            key_pad[REACH + a * k : REACH + a * k + NROWS] == place_key
            for k in (1, 2, 3)
            for a in (-1, 0, 1)
        ]
    ).astype(jnp.int32)
    keep_own = lax.dynamic_slice_in_dim(keep_all, device * OWN_ROWS, OWN_ROWS, axis=1)
    keep_group = lax.dynamic_slice_in_dim(keep_all, group_x * GROUP_ROWS, GROUP_ROWS, axis=1)
    place_tiles = lax.dynamic_slice_in_dim(tile_number[placed], device * OWN_ROWS, OWN_ROWS)
    place_onehot = (place_tiles[:, None] == jnp.arange(tile_count)[None, :]).astype(jnp.float32)
    x_ext = gather_rows(trunk_out, REACH, 1, "gather_trunk")
    row_sums = jnp.sum(trunk_out, axis=1, dtype=jnp.float32)
    tile_sums = of_everyone_2(
        jnp.dot(row_onehot.T, row_sums, precision=highest).astype(jnp.bfloat16), "pix"
    )
    tile_mean = lax.all_gather(
        (tile_sums / tile_sizes[:, None]).astype(jnp.bfloat16), "chan", axis=1, tiled=True
    )
    pre_pooled = jnp.einsum("kc,tdc->ktd", tile_mean, pooled_weight, preferred_element_type=F32)
    pooled_act = jax.nn.silu(pre_pooled).astype(jnp.bfloat16).reshape(tile_count, BRANCH)
    pooled_rows = jnp.dot(
        place_onehot.astype(jnp.bfloat16), pooled_act, preferred_element_type=F32
    ).astype(jnp.bfloat16)
    pooled_pixels = jnp.broadcast_to(
        pooled_rows[:, None, :], (OWN_ROWS, TILE_W, BRANCH)
    ).reshape(pixel_count, BRANCH)
    task_weight = jax.nn.softmax(task_draws.astype(jnp.float32) / 3.0)
    grad_maps = (task_weight[:, None, None] * cotangent.astype(jnp.float32)).astype(jnp.bfloat16)
    maps_own = jnp.moveaxis(grad_maps, 0, 1).reshape(OWN_ROWS, TILE_W, BRANCH)
    maps_all = gather_rows(maps_own, 0, 2, "gather_maps")
    maps_all = jnp.moveaxis(
        maps_all.reshape(CHAN, pixel_count, TASKS, HEAD), 0, 2
    ).reshape(pixel_count, 256 * TASKS)
    project_cut = jnp.moveaxis(project_weight.reshape(TASKS, HEAD, 5, CHAN, HEAD), 3, 0)
    project_own = lax.all_to_all(project_cut, "chan", 0, 0, tiled=True)
    project_own = jnp.transpose(project_own, (3, 1, 4, 0, 2)).reshape(5, TASKS, HEAD, 256)
    project_own = project_own[jnp.array(BRANCH_ORDER)]
    spread = (
        project_own[:, :, :, None, :] * jnp.eye(TASKS, dtype=jnp.bfloat16)[None, :, None, :, None]
    ).reshape(5, BRANCH, 256 * TASKS)
    grad_pre, head_part, grad_project, pool_rows = heads_forward(
        keep_own, x_ext, atrous_weight.reshape(TASKS, 3, 3, 3, HEAD, -1), point_weight, spread,
        maps_all, pooled_pixels,
    )
    g_own = grad_pre.reshape(OWN_ROWS, TILE_W, 4 * BRANCH)
    ring = range(PIX)
    g_low = lax.ppermute(g_own[OWN_ROWS - REACH :], "pix", [(p, (p + 1) % PIX) for p in ring])
    g_high = lax.ppermute(g_own[:REACH], "pix", [(p, (p - 1) % PIX) for p in ring])
    mate_route = [(p, p ^ 1) for p in ring]
    x_parts, g_parts = [], []
    for m in range(4):
        block = lax.dynamic_slice(
            x_ext, (0, REACH, 0, 128 * (group_z ^ m)), (CHAN, OWN_ROWS, TILE_W, 128)
        )
        route = [(p, p ^ (2 * m)) for p in ring]
        x_parts.append(lax.ppermute(block, "pix", route) if m else block)
        g_parts.append(lax.ppermute(g_own, "pix", route) if m else g_own)
    x_parts = x_parts + [lax.ppermute(part, "pix", mate_route) for part in x_parts]
    g_parts = g_parts + [lax.ppermute(part, "pix", mate_route) for part in g_parts]

    def group_edge(spot, rows):
        picked = g_parts[0][rows]
        for m in range(4):
            for other in range(2):
                here = (group_z ^ m == spot // 2) & (core ^ other == spot % 2)
                picked = jnp.where(here, g_parts[4 * other + m][rows], picked)
        return picked

    group_low = lax.ppermute(
        group_edge(GROUP - 1, slice(OWN_ROWS - REACH, OWN_ROWS)),
        "pix",
        [(p, (p + GROUP) % PIX) for p in ring],
    )
    group_high = lax.ppermute(
        group_edge(0, slice(0, REACH)), "pix", [(p, (p - GROUP) % PIX) for p in ring]
    )
    trunk_parts = heads_input_grad(
        keep_own, g_own, g_low, g_high, atrous_weight.reshape(TASKS, 3, 3, 3, HEAD, -1), point_weight
    )
    trunk_grad = return_rows(
        trunk_parts.reshape(CHAN, OWN_ROWS, TILE_W, -1), 3, "return_trunk"
    ).astype(jnp.float32)
    maps_parts = jnp.moveaxis(
        head_part.reshape(OWN_ROWS, TILE_W, TASKS, CHAN, HEAD), 3, 0
    ).reshape(CHAN, OWN_ROWS, TILE_W, BRANCH)
    task_maps = jnp.moveaxis(
        return_rows(maps_parts, 4, "return_maps").reshape(pixel_count, TASKS, HEAD), 1, 0
    )
    weight_parts, point_parts = heads_weight_grad(keep_group, x_parts, g_parts, group_low, group_high)

    def sum_over_groups(parts):
        total = lax.dynamic_index_in_dim(parts, group_x, 0, False).astype(jnp.float32)
        for step in range(1, 4):
            sent = lax.dynamic_index_in_dim(parts, (group_x + step) % 4, 0, False)
            route = [(p, (p + GROUP * step) % PIX) for p in ring]
            total = total + lax.ppermute(sent, "pix", route).astype(jnp.float32)
        return total

    grad_atrous_weight = jnp.transpose(
        sum_over_groups(weight_parts).reshape(3, 3, HEAD, 3, TASKS, HEAD), (4, 0, 3, 1, 2, 5)
    ).reshape(TASKS, 3, 9, HEAD, HEAD)
    grad_point_weight = jnp.transpose(
        sum_over_groups(point_parts).reshape(HEAD, TASKS, HEAD), (1, 0, 2)
    )
    pooled_total = of_everyone(jnp.dot(place_onehot.T, pool_rows, precision=highest), "pix")
    grad_pooled_pre = (
        pooled_total.reshape(tile_count, TASKS, HEAD) * silu_slope(pre_pooled)
    ).astype(jnp.bfloat16)
    grad_pooled_weight = jnp.einsum(
        "kc,ktd->tcd", tile_mean, grad_pooled_pre, preferred_element_type=jnp.float32
    )
    mean_part = jnp.einsum(
        "ktd,tdc->kc", grad_pooled_pre, pooled_weight, preferred_element_type=jnp.float32
    )
    (mean_grad,) = collect((mean_part.reshape(tile_count, 1, -1),))
    mean_rows = jnp.dot(row_onehot, mean_grad[:, 0] / tile_sizes[:, None], precision=highest)
    project_sides = lax.all_to_all(
        jnp.moveaxis(
            grad_project[jnp.array(BRANCH_PLACE)].reshape(5, TASKS, HEAD, CHAN, HEAD), 3, 0
        ),
        "chan",
        0,
        0,
        tiled=True,
    )
    grad_project = jnp.transpose(project_sides, (2, 1, 0, 3, 4)).reshape(TASKS, -1, HEAD)
    grad_trunk = trunk_grad + mean_rows[:, None, :]
    grad_summed = grad_trunk * silu_slope(summed)
    grad_expand_pre, grad_expand_gain, grad_expand_bias = norm_backward(
        grad_summed, unit_expand, scale_expand, expand_gain, pixel_total
    )
    grad_expand_pre = grad_expand_pre.astype(jnp.bfloat16)
    expand_grad = jnp.einsum(
        "rwc,rwd->cd", full_dilate, grad_expand_pre, preferred_element_type=jnp.float32
    )
    (grad_dilate_act,) = collect(
        (
            jnp.einsum(
                "rwd,cd->rwc", grad_expand_pre, expand_weight, preferred_element_type=jnp.float32
            ),
        )
    )
    grad_dilate_pre, grad_dilate_gain, grad_dilate_bias = norm_backward(
        grad_dilate_act * silu_slope(norm_dilate),
        unit_dilate,
        scale_dilate,
        dilate_gain,
        pixel_total,
    )
    grad_dilate_pre = grad_dilate_pre.astype(jnp.bfloat16)
    dilate_grad = dilated_weight_grad(
        reduce_ext, grad_dilate_pre, section_rate, section_rate, section_seams, row_count
    )
    dilate_ext = extend_rows(grad_dilate_pre, section_rate, move_backward)
    (grad_reduce_act,) = collect(
        (
            dilated_transpose(
                dilate_ext,
                dilate_weight,
                section_rate,
                section_rate,
                section_seams,
                row_count,
                "rwd,cd->rwc",
            ),
        )
    )
    grad_reduce_pre, grad_reduce_gain, grad_reduce_bias = norm_backward(
        grad_reduce_act * silu_slope(norm_reduce),
        unit_reduce,
        scale_reduce,
        reduce_gain,
        pixel_total,
    )
    grad_reduce_pre = grad_reduce_pre.astype(jnp.bfloat16)
    reduce_grad = jnp.einsum(
        "rwc,rwd->cd", full_in, grad_reduce_pre, preferred_element_type=jnp.float32
    )
    (grad_input,) = collect(
        (
            jnp.einsum(
                "rwd,cd->rwc", grad_reduce_pre, reduce_weight, preferred_element_type=jnp.float32
            ),
        )
    )
    grad_pixels = (grad_input + grad_summed).astype(jnp.bfloat16).reshape(pixel_count, -1)
    summed_grads = (
        lax.psum_scatter(
            reduce_grad[None].astype(jnp.bfloat16), "pix", scatter_dimension=1, tiled=True
        ).astype(jnp.float32),
        lax.psum_scatter(
            dilate_grad.astype(jnp.bfloat16), "pix", scatter_dimension=1, tiled=True
        ).astype(jnp.float32),
        lax.psum_scatter(
            expand_grad[None].astype(jnp.bfloat16), "pix", scatter_dimension=1, tiled=True
        ).astype(jnp.float32),
        lax.psum_scatter(
            grad_project.astype(jnp.bfloat16), "pix", scatter_dimension=1, tiled=True
        ).astype(jnp.float32),
    )
    return (
        task_maps,
        grad_pixels,
        summed_grads[0][0],
        grad_reduce_gain,
        grad_reduce_bias,
        summed_grads[1],
        grad_dilate_gain,
        grad_dilate_bias,
        summed_grads[2][0],
        grad_expand_gain,
        grad_expand_bias,
        grad_point_weight,
        grad_atrous_weight,
        grad_pooled_weight,
        summed_grads[3],
    )


def solution(mesh):
    placed = (
        P("pix", "chan"),
        P(),
        P(),
        P(None, "chan"),
        P("chan"),
        P("chan"),
        P(None, None, "chan"),
        P("chan"),
        P("chan"),
        P(None, "chan"),
        P("chan"),
        P("chan"),
        P(None, "chan", None),
        P(None, None, None, "chan", None),
        P(None, "chan", None),
        P(None, "chan", None),
        P(None, "pix", "chan"),
    )
    return jax.shard_map(
        shards,
        mesh=mesh,
        in_specs=placed,
        out_specs=(
            P(None, "pix", "chan"),
            P("pix", "chan"),
            P("pix", "chan"),
            P("chan"),
            P("chan"),
            P(None, "pix", "chan"),
            P("chan"),
            P("chan"),
            P("pix", "chan"),
            P("chan"),
            P("chan"),
            P(None, "pix", "chan"),
            P(None, None, None, "pix", "chan"),
            P(None, None, "chan"),
            P(None, "pix", "chan"),
        ),
        check_vma=False,
    )
```

```python
import functools

import jax
import jax.numpy as jnp
from jax import lax
from jax.experimental import pallas as pl
from jax.experimental.pallas import tpu as pltpu
from jax.sharding import PartitionSpec as P

TASKS = 3
TILE_W = 64
NROWS = 256
PIX = 32
CHAN = 4
OWN_ROWS = NROWS // PIX
REACH = 3
EXT_ROWS = OWN_ROWS + 2 * REACH
HEAD = 64
BRANCH = TASKS * HEAD
TILES = 7
BRANCH_ORDER = (1, 2, 3, 0, 4)
BRANCH_PLACE = (3, 0, 1, 2, 4)

F32 = jnp.float32
BF16 = jnp.bfloat16
MESH = pl.DeviceIdType.MESH
eps = 1e-05
section_rate = 4
head_rates = (6, 12, 18)
VMEM_LIMIT = 60 * 2**20


def place_of_row(row):
    kind = row % 6
    return 43 * kind - kind // 5 + row // 6


def row_at_place(place):
    kind = (place + place // 214) // 43
    return 6 * (place - 43 * kind + kind // 5) + kind


PLACED_ROWS = tuple(row_at_place(place) for place in range(NROWS))


def int_div(a, b):
    return lax.div(a, jnp.int32(b))


def int_rem(a, b):
    return lax.rem(a, jnp.int32(b))


def place_of(row):
    kind = int_rem(row, 6)
    return 43 * kind - int_div(kind, 5) + int_div(row, 6)


def row_of(place):
    kind = int_div(place + int_div(place, 214), 43)
    return 6 * (place - 43 * kind + int_div(kind, 5)) + kind


def signal(sem, **where):
    pl.semaphore_signal(sem, inc=1, device_id=where, device_id_type=MESH)


def remote(src, dst, send_sem, recv_sem, **where):
    return pltpu.make_async_remote_copy(
        src_ref=src,
        dst_ref=dst,
        send_sem=send_sem,
        recv_sem=recv_sem,
        device_id=where,
        device_id_type=MESH,
    )


def gather_rows_kernel(
    reach, src, out, ss_row, rs_row, ss_side, rs_side, ss_far, rs_far, ss_halo, rs_halo
):
    i, j = lax.axis_index("pix"), lax.axis_index("chan")
    right, left = int_rem(j + 1, CHAN), int_rem(j + CHAN - 1, CHAN)
    far = int_rem(j + 2, CHAN)
    after, before = int_rem(i + 1, PIX), int_rem(i + PIX - 1, PIX)
    barrier = pltpu.get_barrier_semaphore()
    expected = 2 + (2 if reach else 0)
    for s in range(OWN_ROWS):
        origin = int_div(row_of(OWN_ROWS * i + s), OWN_ROWS)

        @pl.when(origin != i)
        def _():
            signal(barrier, pix=origin)

        target = int_div(place_of(OWN_ROWS * i + s), OWN_ROWS)
        expected = expected + (target != i).astype(jnp.int32)
    signal(barrier, chan=right)
    signal(barrier, chan=left)
    if reach:
        signal(barrier, pix=after)
        signal(barrier, pix=before)
    pl.semaphore_wait(barrier, expected)

    def row_send(s):
        place = place_of(OWN_ROWS * i + s)
        target, slot = int_div(place, OWN_ROWS), int_rem(place, OWN_ROWS)
        landing = out.at[j, reach + slot]
        return target, (
            lambda: remote(src.at[s], landing, ss_row.at[s], rs_row.at[slot], pix=target),
            lambda: pltpu.make_async_copy(src.at[s], landing, rs_row.at[slot]),
        )

    for s in range(OWN_ROWS):
        target, (away, here) = row_send(s)
        pl.when(target != i)(lambda: away().start())
        pl.when(target == i)(lambda: here().start())

    def block(chan, s):
        return out.at[chan, reach + s]

    def side_send(way, s):
        return remote(
            block(j, s),
            block(j, s),
            ss_side.at[way, s],
            rs_side.at[way, s],
            chan=(right, left)[way],
        )

    def side_arrival(way, s):
        chan = (left, right)[way]
        return remote(
            block(chan, s), block(chan, s), ss_side.at[way, s], rs_side.at[way, s], chan=chan
        )

    def far_send(s):
        way = 0 if s < OWN_ROWS // 2 else 1
        chan = (left, right)[way]
        return remote(
            block(chan, s), block(chan, s), ss_far.at[s], rs_far.at[s], chan=(right, left)[way]
        )

    def far_arrival(s):
        return remote(block(far, s), block(far, s), ss_far.at[s], rs_far.at[s], chan=left)

    def halo_send(turn, chan, s):
        if s < reach:
            return remote(
                block(chan, s),
                out.at[chan, reach + OWN_ROWS + s],
                ss_halo.at[turn, s],
                rs_halo.at[chan, s],
                pix=before,
            )
        lane = s - OWN_ROWS + 2 * reach
        return remote(
            block(chan, s),
            out.at[chan, s - OWN_ROWS + reach],
            ss_halo.at[turn, lane],
            rs_halo.at[chan, lane],
            pix=after,
        )

    def halo_arrival(chan, lane):
        slot = reach + OWN_ROWS + lane if lane < reach else lane - reach
        return remote(
            out.at[chan, slot],
            out.at[chan, slot],
            ss_halo.at[0, lane],
            rs_halo.at[chan, lane],
            pix=after,
        )

    order = (0, 7, 1, 6, 2, 5, 3, 4)
    edge = [s for s in order if s < reach or s >= OWN_ROWS - reach]
    for s in order:
        pltpu.make_async_copy(src.at[s], block(j, s), rs_row.at[s]).wait()
        side_send(0, s).start()
        side_send(1, s).start()
        if s in edge:
            halo_send(0, j, s).start()
    for s in order:
        for way in range(2):
            side_arrival(way, s).wait_recv()
            if way == (0 if s < OWN_ROWS // 2 else 1):
                far_send(s).start()
            if s in edge:
                halo_send(1 + way, (left, right)[way], s).start()
    for s in order:
        far_arrival(s).wait_recv()
        if s in edge:
            halo_send(3, far, s).start()
    if reach:
        for chan in range(CHAN):
            for lane in range(2 * reach):
                halo_arrival(chan, lane).wait_recv()
    for s in range(OWN_ROWS):
        target, (away, here) = row_send(s)
        pl.when(target != i)(lambda: away().wait_send())
        side_send(0, s).wait_send()
        side_send(1, s).wait_send()
        far_send(s).wait_send()
    for turn, chan in enumerate((j, left, right, far)):
        for s in edge:
            halo_send(turn, chan, s).wait_send()


def gather_rows(rows, reach, collective_id, name):
    width = rows.shape[2]
    dma = pltpu.SemaphoreType.DMA
    return pl.pallas_call(
        functools.partial(gather_rows_kernel, reach),
        out_shape=jax.ShapeDtypeStruct((CHAN, OWN_ROWS + 2 * reach, TILE_W, width), rows.dtype),
        in_specs=[pl.BlockSpec(memory_space=pl.ANY)],
        out_specs=pl.BlockSpec(memory_space=pl.ANY),
        scratch_shapes=[
            dma((OWN_ROWS,)),
            dma((OWN_ROWS,)),
            dma((2, OWN_ROWS)),
            dma((2, OWN_ROWS)),
            dma((OWN_ROWS,)),
            dma((OWN_ROWS,)),
            dma((CHAN, max(2 * reach, 1))),
            dma((CHAN, max(2 * reach, 1))),
        ],
        compiler_params=pltpu.CompilerParams(collective_id=collective_id, has_side_effects=True),
        cost_estimate=pl.CostEstimate(flops=0, bytes_accessed=60_000_000, transcendentals=0),
        name=name,
    )(rows)


def return_rows_kernel(src, out, own, arrived, total, ls, ss_side, rs_side, ss_row, rs_row):
    i, j = lax.axis_index("pix"), lax.axis_index("chan")
    barrier = pltpu.get_barrier_semaphore()
    expected = 3
    for s in range(OWN_ROWS):
        origin = int_div(place_of(OWN_ROWS * i + s), OWN_ROWS)

        @pl.when(origin != i)
        def _():
            signal(barrier, pix=origin)

        target = int_div(row_of(OWN_ROWS * i + s), OWN_ROWS)
        expected = expected + (target != i).astype(jnp.int32)
    for distance in (1, 2, 3):
        signal(barrier, chan=int_rem(j + distance, CHAN))
    pl.semaphore_wait(barrier, expected)

    def side_send(distance, s):
        chan = int_rem(j + distance, CHAN)
        return remote(
            src.at[chan, s],
            arrived.at[distance - 1, s],
            ss_side.at[distance - 1, s],
            rs_side.at[distance - 1, s],
            chan=chan,
        )

    for s in range(OWN_ROWS):
        for distance in (2, 1, 3):
            side_send(distance, s).start()
    load = pltpu.make_async_copy(src.at[j], own, ls)
    load.start()
    load.wait()

    def row_send(s):
        row = row_of(OWN_ROWS * i + s)
        target, slot = int_div(row, OWN_ROWS), int_rem(row, OWN_ROWS)
        return target, (
            lambda: remote(total.at[s], out.at[slot], ss_row.at[s], rs_row.at[slot], pix=target),
            lambda: pltpu.make_async_copy(total.at[s], out.at[slot], rs_row.at[slot]),
        )

    for s in range(OWN_ROWS):
        held = own[s].astype(F32)
        for distance in (1, 3, 2):
            side_send(distance, s).wait_recv()
            held = held + arrived[distance - 1, s].astype(F32)
        total[s] = held.astype(BF16)
        target, (away, here) = row_send(s)
        pl.when(target != i)(lambda: away().start())
        pl.when(target == i)(lambda: here().start())
    for s in range(OWN_ROWS):
        pltpu.make_async_copy(total.at[s], out.at[s], rs_row.at[s]).wait()
        target, (away, here) = row_send(s)
        pl.when(target != i)(lambda: away().wait_send())
        for distance in (1, 2, 3):
            side_send(distance, s).wait_send()


def return_rows(parts, collective_id, name):
    width = parts.shape[3]
    dma = pltpu.SemaphoreType.DMA
    rows = (OWN_ROWS, TILE_W, width)
    return pl.pallas_call(
        return_rows_kernel,
        out_shape=jax.ShapeDtypeStruct(rows, BF16),
        in_specs=[pl.BlockSpec(memory_space=pl.ANY)],
        out_specs=pl.BlockSpec(memory_space=pl.ANY),
        scratch_shapes=[
            pltpu.VMEM(rows, BF16),
            pltpu.VMEM((CHAN - 1, *rows), BF16),
            pltpu.VMEM(rows, BF16),
            dma,
            dma((CHAN - 1, OWN_ROWS)),
            dma((CHAN - 1, OWN_ROWS)),
            dma((OWN_ROWS,)),
            dma((OWN_ROWS,)),
        ],
        compiler_params=pltpu.CompilerParams(collective_id=collective_id, has_side_effects=True),
        cost_estimate=pl.CostEstimate(flops=0, bytes_accessed=60_000_000, transcendentals=0),
        name=name,
    )(parts)


def dot_nt(a, b):
    return lax.dot_general(a, b, (((1,), (1,)), ((), ())), preferred_element_type=F32)


def dot_tn(a, b):
    return lax.dot_general(a, b, (((0,), (0,)), ((), ())), preferred_element_type=F32)


def dot_nn(a, b):
    return jnp.dot(a, b, preferred_element_type=F32)


def slope(v):
    s = jax.nn.sigmoid(v)
    return s * (1.0 + v * (1.0 - s))


def silu(v):
    return v * jax.nn.sigmoid(v)


def heads_forward_kernel(
    keep, x_hbm, kernel, point, spread, maps, pooled, grad_pre, head_part, grad_project, pool_rows,
    x, acc, pre, sems,
):
    step = pl.program_id(0)
    rate, row_tap = step // 3, step % 3
    first = REACH + (row_tap - 1) * (rate + 1)

    @pl.when(step == 0)
    def _():
        width = x_hbm.shape[3]
        copies = [
            pltpu.make_async_copy(
                x_hbm.at[chan], x.at[:, :, width * chan : width * (chan + 1)], sems.at[chan]
            )
            for chan in range(CHAN)
        ]
        for copy in copies:
            copy.start()
        for copy in copies:
            copy.wait()

    def rows_from(start):
        return x[pl.ds(start, OWN_ROWS)].reshape(OWN_ROWS * TILE_W, -1)

    window = rows_from(first)
    for b in range(3):
        product = dot_nt(window, kernel[:, 0, 0, b].reshape(BRANCH, -1))
        for r in range(OWN_ROWS):
            part = slice(TILE_W * r, TILE_W * (r + 1))
            term = jnp.where(keep[step, r] > 0, product[part], 0.0)
            acc[b, part] = jnp.where(row_tap > 0, acc[b, part], 0.0) + term

    for which, dilation in enumerate(head_rates):

        @pl.when(step == 3 * which + 2)
        def _():
            col = lax.broadcasted_iota(jnp.int32, (OWN_ROWS * TILE_W, BRANCH), 0) % TILE_W
            total = acc[1]
            behind = pltpu.roll(acc[0], dilation, 0)
            ahead = pltpu.roll(acc[2], OWN_ROWS * TILE_W - dilation, 0)
            total = total + jnp.where(col >= dilation, behind, 0.0)
            pre[which] = total + jnp.where(col < TILE_W - dilation, ahead, 0.0)

    @pl.when(step == 0)
    def _():
        pre[3] = dot_nt(rows_from(REACH), point[...].reshape(BRANCH, -1))

    @pl.when(step == 8)
    def _():
        cot = maps[...]
        head = None
        for which in range(5):
            if which < 4:
                before = pre[which]
                logistic = jax.nn.sigmoid(before)
                joined = (before * logistic).astype(BF16)
            else:
                joined = pooled[...]
            weight = spread[which]
            term = dot_nn(joined, weight)
            head = term if head is None else head + term
            grads = dot_tn(joined, cot)
            for t in range(TASKS):
                for c in range(CHAN):
                    lane = 256 * t + HEAD * c
                    grad_project[c, which, t] = grads[
                        HEAD * t : HEAD * (t + 1), lane : lane + HEAD
                    ].astype(BF16)
            back = dot_nt(cot, weight)
            if which < 4:
                grad = back * (logistic * (1.0 + before * (1.0 - logistic)))
                grad_pre[:, BRANCH * which : BRANCH * (which + 1)] = grad.astype(BF16)
            else:
                sums = jnp.sum(back.reshape(OWN_ROWS, TILE_W, BRANCH), axis=1)
                pool_rows[:, :BRANCH] = sums
                pool_rows[:, BRANCH:] = jnp.zeros((OWN_ROWS, 256 - BRANCH), F32)
        head_part[...] = head.astype(BF16)


def heads_forward(keep, x_ext, kernels, point, spread, maps, pooled):
    pixels = OWN_ROWS * TILE_W
    feat = point.shape[2]
    whole = pl.BlockSpec(memory_space=pltpu.VMEM)
    return pl.pallas_call(
        heads_forward_kernel,
        grid=(9,),
        in_specs=[
            pl.BlockSpec(memory_space=pltpu.SMEM),
            pl.BlockSpec(memory_space=pl.ANY),
            pl.BlockSpec((TASKS, 1, 1, 3, HEAD, feat), lambda s: (0, s // 3, s % 3, 0, 0, 0)),
            whole,
            whole,
            whole,
            whole,
        ],
        out_specs=[whole] * 4,
        out_shape=[
            jax.ShapeDtypeStruct((pixels, 4 * BRANCH), BF16),
            jax.ShapeDtypeStruct((pixels, 256 * TASKS), BF16),
            jax.ShapeDtypeStruct((CHAN, 5, TASKS, HEAD, HEAD), BF16),
            jax.ShapeDtypeStruct((OWN_ROWS, 256), F32),
        ],
        scratch_shapes=[
            pltpu.VMEM((EXT_ROWS, TILE_W, feat), BF16),
            pltpu.VMEM((3, pixels, BRANCH), F32),
            pltpu.VMEM((4, pixels, BRANCH), F32),
            pltpu.SemaphoreType.DMA((CHAN,)),
        ],
        compiler_params=pltpu.CompilerParams(vmem_limit_bytes=VMEM_LIMIT),
        cost_estimate=pl.CostEstimate(
            flops=12_000_000_000, bytes_accessed=28_000_000, transcendentals=0
        ),
        name="heads_forward",
    )(keep, x_ext, kernels, point, spread, maps, pooled)


PAD = 24
PADDED = PAD + TILE_W + PAD


def heads_input_grad_kernel(keep, mid, low, high, kernel, point, out, wide, taps, acc):
    n, rate = pl.program_id(0), pl.program_id(1)

    @pl.when((n == 0) & (rate == 0))
    def _():
        wide[...] = jnp.zeros_like(wide)
        for start, part in ((0, low), (REACH, mid), (REACH + OWN_ROWS, high)):
            held = part[...].astype(F32)
            for which in range(3):
                for t in range(TASKS):
                    lane = BRANCH * which + HEAD * t
                    one = held[:, :, lane : lane + HEAD]
                    wide[3 * t + which, start : start + held.shape[0], PAD : PAD + TILE_W] = (
                        jnp.concatenate([one, one], axis=2)
                    )

        def one_row(r, carry):
            is_low = lax.broadcasted_iota(jnp.int32, (TILE_W, 2 * HEAD), 1) < HEAD
            out_rows = pl.ds(pl.multiple_of(r * TILE_W, TILE_W), TILE_W)
            for which, dilation in enumerate(head_rates):

                def shifted(tap):
                    t, a, b = tap // 9, tap // 3 % 3 - 1, tap % 3 - 1
                    piece = wide[
                        3 * t + which,
                        r + REACH - a * (which + 1),
                        PAD - b * dilation : PAD - b * dilation + TILE_W,
                    ]
                    return jnp.where(keep[3 * which + 1 - a, r] > 0, piece, 0.0)

                for pair in range(14):
                    first = shifted(2 * pair)
                    second = shifted(2 * pair + 1) if pair < 13 else jnp.zeros_like(first)
                    taps[which, out_rows, 2 * HEAD * pair : 2 * HEAD * (pair + 1)] = jnp.where(
                        is_low, first, second
                    ).astype(BF16)
            return carry

        lax.fori_loop(0, OWN_ROWS, one_row, 0)

    product = dot_nn(taps[rate, :, : 27 * HEAD], kernel[...].reshape(27 * HEAD, -1))

    @pl.when(rate == 0)
    def _():
        grads = mid[...].reshape(OWN_ROWS * TILE_W, -1)[:, 3 * BRANCH :]
        acc[...] = product + dot_nn(grads, point[...].reshape(BRANCH, -1))

    @pl.when(rate == 1)
    def _():
        acc[...] += product

    @pl.when(rate == 2)
    def _():
        total = acc[...] + product
        for c in range(out.shape[0]):
            out[c] = total[:, 512 * c : 512 * (c + 1)].astype(BF16)


def heads_input_grad(keep, grad_mid, grad_low, grad_high, kernels, point):
    pixels = OWN_ROWS * TILE_W
    block = 1024
    whole = pl.BlockSpec(memory_space=pltpu.VMEM)
    return pl.pallas_call(
        heads_input_grad_kernel,
        grid=(2, 3),
        in_specs=[
            pl.BlockSpec(memory_space=pltpu.SMEM),
            whole,
            whole,
            whole,
            pl.BlockSpec((TASKS, 1, 3, 3, HEAD, block), lambda n, r: (0, r, 0, 0, 0, n)),
            pl.BlockSpec((TASKS, HEAD, block), lambda n, r: (0, 0, n)),
        ],
        out_specs=pl.BlockSpec((block // 512, pixels, 512), lambda n, r: (n, 0, 0)),
        out_shape=jax.ShapeDtypeStruct((CHAN, pixels, 512), BF16),
        scratch_shapes=[
            pltpu.VMEM((9, EXT_ROWS, PADDED, 2 * HEAD), F32),
            pltpu.VMEM((3, pixels, 28 * HEAD), BF16),
            pltpu.VMEM((pixels, block), F32),
        ],
        compiler_params=pltpu.CompilerParams(vmem_limit_bytes=VMEM_LIMIT),
        cost_estimate=pl.CostEstimate(
            flops=12_000_000_000, bytes_accessed=28_000_000, transcendentals=0
        ),
        name="heads_input_grad",
    )(keep, grad_mid, grad_low, grad_high, kernels, point)


GROUP = 8
GROUP_ROWS = GROUP * OWN_ROWS


def heads_weight_grad_kernel(keep, *refs):
    x_parts, g_parts, (g_low, g_high) = refs[:8], refs[8:16], refs[16:18]
    out, out_point, x_all, x_wide, x_now, g_all, g_now, sems = refs[18:]
    step = pl.program_id(0)
    device = lax.axis_index("pix")
    spot, core = int_div(int_rem(device, GROUP), 2), int_rem(device, 2)

    @pl.when(step == 0)
    def _():
        copies = []
        rows = lambda z, c: pl.ds(OWN_ROWS * (2 * z + c), OWN_ROWS)
        for m in range(4):
            z = spot ^ m
            for src, c in ((x_parts[m], core), (x_parts[4 + m], 1 - core)):
                for chan in range(CHAN):
                    copies.append((src.at[chan], x_all.at[chan, rows(z, c)]))
            for src, c in ((g_parts[m], core), (g_parts[4 + m], 1 - core)):
                copies.append((src, g_all.at[pl.ds(REACH + OWN_ROWS * (2 * z + c), OWN_ROWS)]))
        copies.append((g_low, g_all.at[0:REACH]))
        copies.append((g_high, g_all.at[REACH + GROUP_ROWS : 2 * REACH + GROUP_ROWS]))
        started = [
            pltpu.make_async_copy(src, dst, sems.at[n]) for n, (src, dst) in enumerate(copies)
        ]
        for copy in started:
            copy.start()
        x_wide[:, 0:PAD] = jnp.zeros((GROUP_ROWS, PAD, 256), F32)
        x_wide[:, PAD + TILE_W :] = jnp.zeros((GROUP_ROWS, PAD, 256), F32)
        for copy in started:
            copy.wait()

        def widen_row(r, carry):
            is_low = lax.broadcasted_iota(jnp.int32, (TILE_W, 128), 1) < HEAD
            for pair in range(2):
                first = x_all[2 * pair, r].astype(F32)
                second = x_all[2 * pair + 1, r].astype(F32)
                lower = jnp.where(is_low, first, pltpu.roll(second, HEAD, 1))
                upper = jnp.where(is_low, pltpu.roll(first, HEAD, 1), second)
                x_wide[r, PAD : PAD + TILE_W, 128 * pair : 128 * (pair + 1)] = jnp.where(
                    core == 0, lower, upper
                )
            return carry

        lax.fori_loop(0, GROUP_ROWS, widen_row, 0)

    for which in range(3):

        @pl.when(step == 3 * which)
        def _():
            def pick(r, carry):
                for a in range(3):
                    piece = g_all[
                        r + REACH - (a - 1) * (which + 1), :, BRANCH * which : BRANCH * (which + 1)
                    ]
                    g_now[a, pl.ds(pl.multiple_of(r * TILE_W, TILE_W), TILE_W)] = jnp.where(
                        keep[3 * which + 2 - a, r] > 0, piece, jnp.zeros_like(piece)
                    )
                return carry

            lax.fori_loop(0, GROUP_ROWS, pick, 0)

    for which, dilation in enumerate(head_rates):
        for b in range(3):

            @pl.when(step == 3 * which + b)
            def _():
                start = PAD + (b - 1) * dilation

                def move(r, carry):
                    x_now[pl.ds(pl.multiple_of(r * TILE_W, TILE_W), TILE_W)] = x_wide[
                        r, start : start + TILE_W
                    ].astype(BF16)
                    return carry

                lax.fori_loop(0, GROUP_ROWS, move, 0)

    for a in range(3):
        product = dot_tn(x_now[...], g_now[a]).astype(BF16)
        for c in range(CHAN):
            out[c, 0, :, BRANCH * a : BRANCH * (a + 1)] = product[HEAD * c : HEAD * (c + 1)]

    @pl.when(step == 1)
    def _():
        grads = g_all[REACH : REACH + GROUP_ROWS, :, 3 * BRANCH :].reshape(-1, BRANCH)
        product = dot_tn(x_now[...], grads).astype(BF16)
        for c in range(CHAN):
            out_point[c] = product[HEAD * c : HEAD * (c + 1)]


def heads_weight_grad(keep, x_parts, g_parts, g_low, g_high):
    pixels = GROUP_ROWS * TILE_W
    whole = pl.BlockSpec(memory_space=pltpu.VMEM)
    smem = pl.BlockSpec(memory_space=pltpu.SMEM)
    hbm = pl.BlockSpec(memory_space=pl.ANY)
    return pl.pallas_call(
        heads_weight_grad_kernel,
        grid=(9,),
        in_specs=[smem] + [hbm] * 18,
        out_specs=[pl.BlockSpec((CHAN, 1, HEAD, 3 * BRANCH), lambda s: (0, s, 0, 0)), whole],
        out_shape=[
            jax.ShapeDtypeStruct((CHAN, 9, HEAD, 3 * BRANCH), BF16),
            jax.ShapeDtypeStruct((CHAN, HEAD, BRANCH), BF16),
        ],
        scratch_shapes=[
            pltpu.VMEM((CHAN, GROUP_ROWS, TILE_W, 128), BF16),
            pltpu.VMEM((GROUP_ROWS, PADDED, 256), F32),
            pltpu.VMEM((pixels, 256), BF16),
            pltpu.VMEM((GROUP_ROWS + 2 * REACH, TILE_W, 4 * BRANCH), BF16),
            pltpu.VMEM((3, pixels, BRANCH), BF16),
            pltpu.SemaphoreType.DMA((42,)),
        ],
        compiler_params=pltpu.CompilerParams(vmem_limit_bytes=VMEM_LIMIT),
        cost_estimate=pl.CostEstimate(
            flops=12_000_000_000, bytes_accessed=28_000_000, transcendentals=0
        ),
        name="heads_weight_grad",
    )(keep, *x_parts, *g_parts, g_low, g_high)


class Links:
    def __init__(self, send_sems, recv_sems):
        self.send_sems, self.recv_sems, self.count, self.sent = send_sems, recv_sems, 0, []

    def send(self, src, dst, **where):
        n = self.count
        self.count += 1
        copy = remote(src, dst, self.send_sems.at[n], self.recv_sems.at[n], **where)
        copy.start()
        self.sent.append(copy)
        return n

    def arrive(self, n, dst):
        beside = {"chan": int_rem(lax.axis_index("chan") + 1, CHAN)}
        remote(dst, dst, self.send_sems.at[n], self.recv_sems.at[n], **beside).wait_recv()

    def finish(self):
        for copy in self.sent:
            copy.wait_send()


def greet(peers, more=0):
    barrier = pltpu.get_barrier_semaphore()
    for where in peers:
        signal(barrier, **where)
    pl.semaphore_wait(barrier, len(peers) + more)


class Spot:
    def __init__(self):
        self.i, self.j = lax.axis_index("pix"), lax.axis_index("chan")
        self.group, self.k = int_div(self.i, GROUP), int_rem(self.i, GROUP)
        self.z, self.core = int_div(self.k, 2), int_rem(self.k, 2)
        self.before, self.after = int_rem(self.i + PIX - 1, PIX), int_rem(self.i + 1, PIX)
        self.mate = self.i + 1 - 2 * self.core

    def chan(self, distance):
        return int_rem(self.j + CHAN + distance, CHAN)

    def in_group(self, distance):
        return int_rem(self.k + GROUP + distance, GROUP)

    def pix_in_group(self, distance):
        return GROUP * self.group + self.in_group(distance)

    def x_of(self, distance):
        return int_rem(self.group + 4 + distance, 4)

    def pix_in_x(self, distance):
        return GROUP * self.x_of(distance) + self.k

    def z_of(self, distance):
        return int_rem(self.z + 4 + distance, 4)

    def pix_in_z(self, distance):
        return GROUP * self.group + 2 * self.z_of(distance) + self.core

    def sum_peers(self):
        return [{"pix": self.pix_in_group(d)} for d in range(1, GROUP)] + [
            {"pix": self.pix_in_x(d)} for d in range(1, 4)
        ]


def sum_over_pix(value, near, across, spot, links):
    near[spot.k] = value
    sent = [
        links.send(near.at[spot.k], near.at[spot.k], pix=spot.pix_in_group(d))
        for d in range(1, GROUP)
    ]
    for d, n in zip(range(1, GROUP), sent):
        links.arrive(n, near.at[spot.in_group(-d)])
    total = near[0]
    for k in range(1, GROUP):
        total = total + near[k]
    across[spot.group] = total
    sent = [
        links.send(across.at[spot.group], across.at[spot.group], pix=spot.pix_in_x(d))
        for d in range(1, 4)
    ]
    for d, n in zip(range(1, 4), sent):
        links.arrive(n, across.at[spot.x_of(-d)])
    return across[0] + across[1] + across[2] + across[3]


def two_sums(first, second):
    width = first.shape[1]
    rows = [jnp.sum(first, axis=0, keepdims=True), jnp.sum(second, axis=0, keepdims=True)]
    return jnp.concatenate(rows + [jnp.zeros((6, width), F32)], axis=0)


PIXELS = NROWS * TILE_W
OWN = OWN_ROWS * TILE_W
MID_OWN = 128
FEAT_OWN = 512
ROW_COLS = OWN_ROWS * TILE_W


def col_shift(value, distance):
    col = lax.broadcasted_iota(jnp.int32, value.shape, 0) % TILE_W
    rows = value.shape[0]
    moved = pltpu.roll(value, (rows - distance) % rows, 0)
    inside = (col < TILE_W - distance) if distance > 0 else (col >= -distance)
    return jnp.where(inside, moved, 0.0)


def section_forward_kernel(
    pixels, wr, wd, we, vec_mid, vec_feat, keep, tile_rows, sizes,
    trunk, unit_r, unit_d, unit_e, act_r, act_d, wr_all, inv_mid, inv_feat, mean_all,
    part_out, part_in, near_m, across_m, near_f, across_f, near_t, across_t, send_sems, recv_sems,
):
    spot = Spot()
    links = Links(send_sems, recv_sems)
    j = spot.j
    peers = [{"chan": spot.chan(d)} for d in (1, 2, 3)] + spot.sum_peers()
    for d in range(CHAN):
        peers += [{"pix": p, "chan": spot.chan(d)} for p in (spot.before, spot.after)]
    greet(peers)

    def block(chan):
        return pl.ds(pl.multiple_of(FEAT_OWN * chan, FEAT_OWN), FEAT_OWN)

    sent = {
        d: links.send(wr.at[block(spot.chan(d))], wr_all.at[j], chan=spot.chan(d)) for d in (2, 1, 3)
    }
    wr_all[j] = wr[block(j)]
    pre = dot_nn(pixels[...], wr_all[j])
    back = {}
    for d in (1, 3, 2):
        source = spot.chan(-d)
        links.arrive(sent[d], wr_all.at[source])
        part_out[d - 1] = dot_nn(pixels[...], wr_all[source]).astype(BF16)
        back[d] = links.send(part_out.at[d - 1], part_in.at[d - 1], chan=source)
    for d in (1, 3, 2):
        links.arrive(back[d], part_in.at[d - 1])
        pre = pre + part_in[d - 1].astype(F32)

    def norm(value, near, across, gain, bias):
        sums = sum_over_pix(two_sums(value, value * value), near, across, spot, links)
        center = sums[0:1] / PIXELS
        inv = lax.rsqrt(sums[1:2] / PIXELS - center * center + eps)
        unit = (value - center) * inv
        return unit, unit * gain + bias, inv

    unit, normed, inv_r = norm(pre, near_m.at[0], across_m.at[0], vec_mid[0:1], vec_mid[1:2])
    unit_r[...] = unit
    own = slice(section_rate, section_rate + OWN_ROWS)
    act_r[j, own] = silu(normed).astype(BF16).reshape(OWN_ROWS, TILE_W, MID_OWN)
    low, high = slice(0, section_rate), slice(section_rate + OWN_ROWS, 2 * section_rate + OWN_ROWS)
    first, last = slice(section_rate, 2 * section_rate), slice(OWN_ROWS, section_rate + OWN_ROWS)
    arrivals = []
    for d in (2, 1, 3, 0):
        to, source = spot.chan(d), spot.chan(-d)
        if d:
            n = links.send(act_r.at[j, own], act_r.at[j, own], chan=to)
            arrivals.append((n, act_r.at[source, own]))
        n = links.send(act_r.at[j, first], act_r.at[j, high], pix=spot.before, chan=to)
        arrivals.append((n, act_r.at[source, high]))
        n = links.send(act_r.at[j, last], act_r.at[j, low], pix=spot.after, chan=to)
        arrivals.append((n, act_r.at[source, low]))
    for n, dst in arrivals:
        links.arrive(n, dst)
    pre = jnp.zeros((OWN, MID_OWN), F32)
    for a in range(3):
        rows = slice(section_rate * a, section_rate * a + OWN_ROWS)
        window = jnp.concatenate(
            [act_r[c, rows].reshape(OWN, MID_OWN) for c in range(CHAN)], axis=1
        )
        terms = [dot_nn(window, wd[3 * a + b]) for b in range(3)]
        term = terms[1] + col_shift(terms[0], -section_rate) + col_shift(terms[2], section_rate)
        pre = pre + (term if a == 1 else term * keep[a // 2])

    unit, normed, inv_d = norm(pre, near_m.at[1], across_m.at[1], vec_mid[2:3], vec_mid[3:4])
    unit_d[...] = unit
    inv_mid[...] = jnp.concatenate([inv_r, inv_d, jnp.zeros((6, MID_OWN), F32)], axis=0)
    act_d[j] = silu(normed).astype(BF16)
    sent = {d: links.send(act_d.at[j], act_d.at[j], chan=spot.chan(d)) for d in (2, 1, 3)}
    for d in (1, 3, 2):
        links.arrive(sent[d], act_d.at[spot.chan(-d)])
    full = jnp.concatenate([act_d[c] for c in range(CHAN)], axis=1)
    unit, normed, inv_e = norm(
        dot_nn(full, we[...]), near_f, across_f, vec_feat[0:1], vec_feat[1:2]
    )
    unit_e[...] = unit
    inv_feat[...] = jnp.concatenate([inv_e, jnp.zeros((7, FEAT_OWN), F32)], axis=0)
    out = silu(normed + pixels[...].astype(F32)).astype(BF16)
    trunk[...] = out.reshape(OWN_ROWS, TILE_W, FEAT_OWN)
    row_sums = jnp.sum(out.astype(F32).reshape(OWN_ROWS, TILE_W, FEAT_OWN), axis=1)
    sums = jnp.zeros((8, FEAT_OWN), F32)
    for r in range(OWN_ROWS):
        sums = sums + tile_rows[:, r : r + 1] * row_sums[r : r + 1]
    sums = sum_over_pix(sums, near_t, across_t, spot, links)
    mean = jnp.concatenate([sums / sizes[:, 0:1], jnp.zeros((8, FEAT_OWN), F32)], axis=0)
    mean_all[j] = mean.astype(BF16)
    sent = {d: links.send(mean_all.at[j], mean_all.at[j], chan=spot.chan(d)) for d in (2, 1, 3)}
    for d in (1, 3, 2):
        links.arrive(sent[d], mean_all.at[spot.chan(-d)])
    links.finish()


def section_forward(pixels, wr, wd, we, vec_mid, vec_feat, keep, tile_rows, sizes):
    whole = pl.BlockSpec(memory_space=pltpu.VMEM)
    shape = jax.ShapeDtypeStruct
    mid, feat = (OWN, MID_OWN), (OWN, FEAT_OWN)
    dma = pltpu.SemaphoreType.DMA
    return pl.pallas_call(
        section_forward_kernel,
        in_specs=[whole] * 9,
        out_specs=[whole] * 10,
        out_shape=[
            shape((OWN_ROWS, TILE_W, FEAT_OWN), BF16),
            shape(mid, F32),
            shape(mid, F32),
            shape(feat, F32),
            shape((CHAN, OWN_ROWS + 2 * section_rate, TILE_W, MID_OWN), BF16),
            shape((CHAN, *mid), BF16),
            shape((CHAN, FEAT_OWN, MID_OWN), BF16),
            shape((8, MID_OWN), F32),
            shape((8, FEAT_OWN), F32),
            shape((CHAN, 16, FEAT_OWN), BF16),
        ],
        scratch_shapes=[
            pltpu.VMEM((3, *mid), BF16),
            pltpu.VMEM((3, *mid), BF16),
            pltpu.VMEM((2, GROUP, 8, MID_OWN), F32),
            pltpu.VMEM((2, 4, 8, MID_OWN), F32),
            pltpu.VMEM((GROUP, 8, FEAT_OWN), F32),
            pltpu.VMEM((4, 8, FEAT_OWN), F32),
            pltpu.VMEM((GROUP, 8, FEAT_OWN), F32),
            pltpu.VMEM((4, 8, FEAT_OWN), F32),
            dma((64,)),
            dma((64,)),
        ],
        compiler_params=pltpu.CompilerParams(
            collective_id=5, has_side_effects=True, vmem_limit_bytes=VMEM_LIMIT
        ),
        cost_estimate=pl.CostEstimate(
            flops=2_000_000_000, bytes_accessed=120_000_000, transcendentals=0
        ),
        name="section_forward",
    )(pixels, wr, wd, we, vec_mid, vec_feat, keep, tile_rows, sizes)


class Scatter:
    def __init__(self, parts, mate_in, near, near_in, far, far_in, spot, links):
        self.parts, self.mate_in, self.near, self.near_in = parts, mate_in, near, near_in
        self.far, self.far_in, self.spot, self.links = far, far_in, spot, links

    def start(self):
        spot = self.spot
        self.sent = self.links.send(self.parts.at[1 - spot.core], self.mate_in, pix=spot.mate)

    def along_z(self):
        spot, links = self.spot, self.links
        links.arrive(self.sent, self.mate_in)
        for z in range(4):
            self.near[z] = (
                self.parts[spot.core, z].astype(F32) + self.mate_in[z].astype(F32)
            ).astype(BF16)
        self.sent = {
            d: links.send(
                self.near.at[spot.z_of(d)], self.near_in.at[d - 1], pix=spot.pix_in_z(d)
            )
            for d in (2, 1, 3)
        }

    def along_x(self):
        spot, links = self.spot, self.links
        total = self.near[spot.z].astype(F32)
        for d in (1, 3, 2):
            links.arrive(self.sent[d], self.near_in.at[d - 1])
            total = total + self.near_in[d - 1].astype(F32)
        self.far[...] = total.astype(BF16)
        self.sent = {
            d: links.send(self.far.at[spot.x_of(d)], self.far_in.at[d - 1], pix=spot.pix_in_x(d))
            for d in (2, 1, 3)
        }

    def finish(self):
        spot, links = self.spot, self.links
        total = self.far[spot.group].astype(F32)
        for d in (1, 3, 2):
            links.arrive(self.sent[d], self.far_in.at[d - 1])
            total = total + self.far_in[d - 1].astype(F32)
        return total


def scatter_scratch(*shape):
    return [
        pltpu.VMEM((2, 4, 4, *shape), BF16),
        pltpu.VMEM((4, 4, *shape), BF16),
        pltpu.VMEM((4, 4, *shape), BF16),
        pltpu.VMEM((3, 4, *shape), BF16),
        pltpu.VMEM((4, *shape), BF16),
        pltpu.VMEM((3, *shape), BF16),
    ]


def spot_of(device):
    return device % 2, device % GROUP // 2, device // GROUP


def section_backward_kernel(
    trunk_grad, pixels, unit_r, unit_d, unit_e, act_r, act_d, wr_all, wd_cat, we, vec_mid, vec_feat,
    inv_mid, inv_feat, keep, pool_rows, place_rows, tile_cols, sizes, pre_pooled, pooled, projects,
    grad_pixels, mid_grads, feat_grads, grad_reduce, grad_dilate, grad_expand, grad_project, grad_pooled,
    *scratch,
):
    (
        side_out, side_in, halo, taps, full, mean_out, mean_in, project_in, project_wide, reduce_out,
        near_m, across_m, near_f, across_f, near_p, across_p,
    ) = scratch[:16]
    send_sems, recv_sems, last_sems = scratch[-3:]
    buffers = scratch[16:-3]
    spot = Spot()
    links = Links(send_sems, recv_sems)
    i, j = spot.i, spot.j
    by_expand, by_dilate, by_project, by_reduce = [
        Scatter(*buffers[6 * n : 6 * n + 6], spot, links) for n in range(4)
    ]
    owner_i, owner_j = GROUP * j + int_div(i, 4), int_rem(i, 4)
    maker_i, maker_j = 4 * int_rem(i, GROUP) + j, spot.group
    stays = (owner_i == i) & (owner_j == j)
    barrier = pltpu.get_barrier_semaphore()

    @pl.when(jnp.logical_not(stays))
    def _():
        signal(barrier, pix=maker_i, chan=maker_j)

    peers = [{"chan": spot.chan(d)} for d in (1, 2, 3)] + spot.sum_peers()
    peers += [{"pix": spot.before}, {"pix": spot.after}]
    greet(peers, 1 - stays.astype(jnp.int32))

    project_sent = {
        d: links.send(projects.at[spot.chan(d)], project_in.at[d - 1], chan=spot.chan(d))
        for d in (2, 1, 3)
    }

    sums = jnp.zeros((8, 2 * MID_OWN), F32)
    for r in range(OWN_ROWS):
        sums = sums + place_rows[:, r : r + 1] * pool_rows[r : r + 1]
    sums = sum_over_pix(sums, near_p, across_p, spot, links)
    pooled_pre = (sums[:, :BRANCH] * slope(pre_pooled[...])).astype(BF16)
    grad_pooled[...] = pooled_pre.astype(F32)
    wide = jnp.concatenate([pooled_pre.astype(F32), jnp.zeros((8, BRANCH), F32)], axis=0).astype(BF16)
    for c in range(CHAN):
        mean_out[c] = dot_nn(wide, pooled[:, FEAT_OWN * c : FEAT_OWN * (c + 1)]).astype(BF16)
    sent = {
        d: links.send(mean_out.at[spot.chan(d)], mean_in.at[d - 1], chan=spot.chan(d))
        for d in (2, 1, 3)
    }
    mean = mean_out[j].astype(F32)
    for d in (1, 3, 2):
        links.arrive(sent[d], mean_in.at[d - 1])
        mean = mean + mean_in[d - 1].astype(F32)
    mean = mean[0:8] / sizes[:, 0:1]
    mean_rows = jnp.zeros((OWN_ROWS, FEAT_OWN), F32)
    for k in range(8):
        mean_rows = mean_rows + tile_cols[:, k : k + 1] * mean[k : k + 1]

    def norm_back(grad, unit, near, across, scale):
        sums = sum_over_pix(two_sums(grad, grad * unit), near, across, spot, links)
        pre = scale * (grad - sums[0:1] / PIXELS - unit * (sums[1:2] / PIXELS))
        return pre.astype(BF16), sums

    grad_trunk = trunk_grad[...].astype(F32) + mean_rows[:, None, :]
    grad_trunk = grad_trunk.reshape(OWN, FEAT_OWN)
    unit = unit_e[...]
    summed = unit * vec_feat[0:1] + vec_feat[1:2] + pixels[...].astype(F32)
    grad_summed = grad_trunk * slope(summed)
    g_expand, sums = norm_back(grad_summed, unit, near_f, across_f, vec_feat[0:1] * inv_feat[0:1])
    feat_grads[...] = sums

    def sides(turn, make):
        sent = {}
        for d in (2, 1, 3):
            side_out[turn, d - 1] = make(spot.chan(d)).astype(BF16)
            sent[d] = links.send(
                side_out.at[turn, d - 1], side_in.at[turn, d - 1], chan=spot.chan(d)
            )
        return sent

    def side_sum(turn, own, sent):
        for d in (1, 3, 2):
            links.arrive(sent[d], side_in.at[turn, d - 1])
            own = own + side_in[turn, d - 1].astype(F32)
        return own

    def mid_rows(chan):
        return pl.ds(pl.multiple_of(MID_OWN * chan, MID_OWN), MID_OWN)

    sent = sides(0, lambda c: dot_nt(g_expand, we[mid_rows(c)]))
    own = dot_nt(g_expand, we[mid_rows(j)])
    part = 16
    for c in range(CHAN):
        grads = dot_tn(act_d[c], g_expand).astype(BF16)
        for n in range(8):
            by_expand.parts[spot_of(8 * c + n)] = grads[part * n : part * (n + 1)]
    by_expand.start()
    grad_act = side_sum(0, own, sent)

    unit = unit_d[...]
    grad = grad_act * slope(unit * vec_mid[2:3] + vec_mid[3:4])
    g_dilate, sums_d = norm_back(
        grad, unit, near_m.at[0], across_m.at[0], vec_mid[2:3] * inv_mid[1:2]
    )
    own_rows = slice(section_rate, section_rate + OWN_ROWS)
    halo[own_rows] = g_dilate.reshape(OWN_ROWS, TILE_W, MID_OWN)
    low, high = slice(0, section_rate), slice(section_rate + OWN_ROWS, 2 * section_rate + OWN_ROWS)
    first, last = slice(section_rate, 2 * section_rate), slice(OWN_ROWS, section_rate + OWN_ROWS)
    to_before = links.send(halo.at[first], halo.at[high], pix=spot.before)
    to_after = links.send(halo.at[last], halo.at[low], pix=spot.after)
    by_expand.along_z()
    for d in (1, 3, 2):
        links.arrive(project_sent[d], project_in.at[d - 1])
        project_wide[spot.chan(-d)] = project_in[d - 1].astype(F32)
    project_wide[j] = projects[j].astype(F32)
    links.arrive(to_before, halo.at[high])
    links.arrive(to_after, halo.at[low])
    for a in range(3):
        rows = halo[section_rate * (2 - a) : section_rate * (2 - a) + OWN_ROWS]
        rows = rows.reshape(OWN, MID_OWN).astype(F32)
        if a != 1:
            rows = rows * keep[1 - a // 2]
        for b in range(3):
            moved = rows if b == 1 else col_shift(rows, -section_rate * (b - 1))
            tap = 3 * a + b
            taps[:, MID_OWN * tap : MID_OWN * (tap + 1)] = moved.astype(BF16)
    sent = sides(1, lambda c: dot_nt(taps[...], wd_cat[mid_rows(c)]))
    own = dot_nt(taps[...], wd_cat[mid_rows(j)])
    for c in range(CHAN):
        act = act_r[c, own_rows].reshape(OWN, MID_OWN)
        grads = dot_tn(act, taps[...]).astype(BF16)
        for n in range(8):
            for tap in range(9):
                by_dilate.parts[(*spot_of(8 * c + n), tap)] = grads[
                    part * n : part * (n + 1), MID_OWN * tap : MID_OWN * (tap + 1)
                ]
    by_dilate.start()
    grad_act = side_sum(1, own, sent)
    by_expand.along_x()

    unit = unit_r[...]
    grad = grad_act * slope(unit * vec_mid[0:1] + vec_mid[1:2])
    g_reduce, sums_r = norm_back(
        grad, unit, near_m.at[1], across_m.at[1], vec_mid[0:1] * inv_mid[0:1]
    )
    mid_grads[...] = jnp.concatenate([sums_r[0:2], sums_d[0:2], jnp.zeros((4, MID_OWN), F32)], axis=0)
    full[j] = g_reduce
    sent = {d: links.send(full.at[j], full.at[j], chan=spot.chan(d)) for d in (2, 1, 3)}
    by_dilate.along_z()
    for t in range(TASKS):
        for device in range(PIX):
            rows = []
            for start in range(40 * device, 40 * device + 40, 8):
                b, src, d = start // 256, start // HEAD % CHAN, start % HEAD
                rows.append(project_wide[src, BRANCH_PLACE[b], t, d : d + 8])
            rows.append(jnp.zeros((8, HEAD), F32))
            by_project.parts[(*spot_of(device), t)] = jnp.concatenate(rows, axis=0).astype(BF16)
    by_project.start()
    grad_expand[...] = by_expand.finish()
    for d in (1, 3, 2):
        links.arrive(sent[d], full.at[spot.chan(-d)])
    g_reduce = jnp.concatenate([full[c] for c in range(CHAN)], axis=1)
    weight = jnp.concatenate([wr_all[c] for c in range(CHAN)], axis=1)
    grads = dot_tn(pixels[...], g_reduce).astype(BF16)
    for c in range(CHAN):
        for n in range(8):
            by_reduce.parts[spot_of(4 * n + c)] = grads[
                HEAD * n : HEAD * (n + 1), MID_OWN * c : MID_OWN * (c + 1)
            ]
    by_reduce.start()
    grad_pixels[...] = (grad_summed + dot_nt(g_reduce, weight)).astype(BF16)
    by_project.along_z()
    by_reduce.along_z()
    by_dilate.along_x()
    by_reduce.along_x()
    by_project.along_x()
    reduce_out[...] = by_reduce.finish()

    def last_copies():
        return (
            lambda: remote(
                reduce_out, grad_reduce, last_sems.at[0], last_sems.at[1], pix=owner_i, chan=owner_j
            ),
            lambda: pltpu.make_async_copy(reduce_out, grad_reduce, last_sems.at[1]),
        )

    away, here = last_copies()
    pl.when(jnp.logical_not(stays))(lambda: away().start())
    pl.when(stays)(lambda: here().start())
    grad_dilate[...] = by_dilate.finish()
    grad_project[...] = by_project.finish()
    pltpu.make_async_copy(reduce_out, grad_reduce, last_sems.at[1]).wait()
    pl.when(jnp.logical_not(stays))(lambda: away().wait_send())
    links.finish()


def section_backward(*operands):
    whole = pl.BlockSpec(memory_space=pltpu.VMEM)
    shape = jax.ShapeDtypeStruct
    dma = pltpu.SemaphoreType.DMA
    mid, feat = (OWN, MID_OWN), (OWN, FEAT_OWN)
    return pl.pallas_call(
        section_backward_kernel,
        in_specs=[whole] * len(operands),
        out_specs=[whole] * 8,
        out_shape=[
            shape(feat, BF16),
            shape((8, MID_OWN), F32),
            shape((8, FEAT_OWN), F32),
            shape((HEAD, MID_OWN), F32),
            shape((9, 16, MID_OWN), F32),
            shape((16, FEAT_OWN), F32),
            shape((TASKS, 48, HEAD), F32),
            shape((8, BRANCH), F32),
        ],
        scratch_shapes=[
            pltpu.VMEM((2, 3, *mid), BF16),
            pltpu.VMEM((2, 3, *mid), BF16),
            pltpu.VMEM((OWN_ROWS + 2 * section_rate, TILE_W, MID_OWN), BF16),
            pltpu.VMEM((OWN, 9 * MID_OWN), BF16),
            pltpu.VMEM((CHAN, *mid), BF16),
            pltpu.VMEM((CHAN, 16, FEAT_OWN), BF16),
            pltpu.VMEM((3, 16, FEAT_OWN), BF16),
            pltpu.VMEM((3, 5, TASKS, HEAD, HEAD), BF16),
            pltpu.VMEM((CHAN, 5, TASKS, HEAD, HEAD), F32),
            pltpu.VMEM((HEAD, MID_OWN), F32),
            pltpu.VMEM((2, GROUP, 8, MID_OWN), F32),
            pltpu.VMEM((2, 4, 8, MID_OWN), F32),
            pltpu.VMEM((GROUP, 8, FEAT_OWN), F32),
            pltpu.VMEM((4, 8, FEAT_OWN), F32),
            pltpu.VMEM((GROUP, 8, 2 * MID_OWN), F32),
            pltpu.VMEM((4, 8, 2 * MID_OWN), F32),
            *scatter_scratch(16, FEAT_OWN),
            *scatter_scratch(9, 16, MID_OWN),
            *scatter_scratch(TASKS, 48, HEAD),
            *scatter_scratch(HEAD, MID_OWN),
            dma((96,)),
            dma((96,)),
            dma((2,)),
        ],
        compiler_params=pltpu.CompilerParams(
            collective_id=6, has_side_effects=True, vmem_limit_bytes=VMEM_LIMIT
        ),
        cost_estimate=pl.CostEstimate(
            flops=4_000_000_000, bytes_accessed=250_000_000, transcendentals=0
        ),
        name="section_backward",
    )(*operands)


def shards(
    pixels,
    tile_number,
    task_draws,
    reduce_weight,
    reduce_gain,
    reduce_bias,
    dilate_weight,
    dilate_gain,
    dilate_bias,
    expand_weight,
    expand_gain,
    expand_bias,
    point_weight,
    atrous_weight,
    pooled_weight,
    project_weight,
    cotangent,
):
    pixel_count = pixels.shape[0]
    device = lax.axis_index("pix")
    first_row = device * OWN_ROWS
    tile_count = 8
    tiles = jnp.arange(tile_count)
    tile_sizes = jnp.sum((tile_number[:, None] == tiles[None, :]).astype(F32), axis=0) * TILE_W
    sizes = jnp.broadcast_to(jnp.maximum(tile_sizes, 1.0)[:, None], (tile_count, 128))
    tile_pad = jnp.pad(tile_number, (section_rate, section_rate), constant_values=-1)
    tiles_at = [
        lax.dynamic_slice_in_dim(tile_pad, first_row + section_rate * (1 + step), OWN_ROWS)
        for step in (-1, 0, 1)
    ]
    row_onehot = (tiles_at[1][:, None] == tiles[None, :]).astype(F32)
    keep_rows = jnp.stack([tiles_at[0] == tiles_at[1], tiles_at[2] == tiles_at[1]]).astype(F32)
    keep_section = jnp.broadcast_to(
        keep_rows[:, :, None, None], (2, OWN_ROWS, TILE_W, MID_OWN)
    ).reshape(2, OWN, MID_OWN)
    vec_mid = jnp.pad(
        jnp.stack([reduce_gain, reduce_bias, dilate_gain, dilate_bias]), ((0, 4), (0, 0))
    )
    vec_feat = jnp.pad(jnp.stack([expand_gain, expand_bias]), ((0, 6), (0, 0)))
    (
        trunk_out, unit_reduce, unit_dilate, unit_expand, act_reduce, act_dilate, reduce_all, inv_mid,
        inv_feat, mean_all,
    ) = section_forward(
        pixels, reduce_weight, dilate_weight, expand_weight, vec_mid, vec_feat, keep_section,
        row_onehot.T, sizes,
    )
    tile_mean = jnp.moveaxis(mean_all[:, :tile_count], 0, 1).reshape(tile_count, -1)
    group_x, group_z, core = device // GROUP, device % GROUP // 2, device % 2
    placed = jnp.array(PLACED_ROWS, jnp.int32)
    place_key = tile_number[placed] + 8 * (placed % 6)
    key_pad = jnp.pad(place_key, (REACH, REACH), constant_values=-1)
    keep_all = jnp.stack(
        [
            key_pad[REACH + a * k : REACH + a * k + NROWS] == place_key
            for k in (1, 2, 3)
            for a in (-1, 0, 1)
        ]
    ).astype(jnp.int32)
    keep_own = lax.dynamic_slice_in_dim(keep_all, device * OWN_ROWS, OWN_ROWS, axis=1)
    keep_group = lax.dynamic_slice_in_dim(keep_all, group_x * GROUP_ROWS, GROUP_ROWS, axis=1)
    place_tiles = lax.dynamic_slice_in_dim(tile_number[placed], device * OWN_ROWS, OWN_ROWS)
    place_onehot = (place_tiles[:, None] == tiles[None, :]).astype(F32)
    x_ext = gather_rows(trunk_out, REACH, 1, "gather_trunk")
    pre_pooled = jnp.einsum("kc,tdc->ktd", tile_mean, pooled_weight, preferred_element_type=F32)
    pooled_act = jax.nn.silu(pre_pooled).astype(jnp.bfloat16).reshape(tile_count, BRANCH)
    pooled_rows = jnp.dot(
        place_onehot.astype(jnp.bfloat16), pooled_act, preferred_element_type=F32
    ).astype(jnp.bfloat16)
    pooled_pixels = jnp.broadcast_to(
        pooled_rows[:, None, :], (OWN_ROWS, TILE_W, BRANCH)
    ).reshape(pixel_count, BRANCH)
    task_weight = jax.nn.softmax(task_draws.astype(jnp.float32) / 3.0)
    grad_maps = (task_weight[:, None, None] * cotangent.astype(jnp.float32)).astype(jnp.bfloat16)
    maps_own = jnp.moveaxis(grad_maps, 0, 1).reshape(OWN_ROWS, TILE_W, BRANCH)
    maps_all = gather_rows(maps_own, 0, 2, "gather_maps")
    maps_all = jnp.moveaxis(
        maps_all.reshape(CHAN, pixel_count, TASKS, HEAD), 0, 2
    ).reshape(pixel_count, 256 * TASKS)
    project_cut = jnp.moveaxis(project_weight.reshape(TASKS, HEAD, 5, CHAN, HEAD), 3, 0)
    project_own = lax.all_to_all(project_cut, "chan", 0, 0, tiled=True)
    project_own = jnp.transpose(project_own, (3, 1, 4, 0, 2)).reshape(5, TASKS, HEAD, 256)
    project_own = project_own[jnp.array(BRANCH_ORDER)]
    spread = (
        project_own[:, :, :, None, :] * jnp.eye(TASKS, dtype=jnp.bfloat16)[None, :, None, :, None]
    ).reshape(5, BRANCH, 256 * TASKS)
    grad_pre, head_part, grad_project, pool_rows = heads_forward(
        keep_own, x_ext, atrous_weight.reshape(TASKS, 3, 3, 3, HEAD, -1), point_weight, spread,
        maps_all, pooled_pixels,
    )
    g_own = grad_pre.reshape(OWN_ROWS, TILE_W, 4 * BRANCH)
    ring = range(PIX)
    g_low = lax.ppermute(g_own[OWN_ROWS - REACH :], "pix", [(p, (p + 1) % PIX) for p in ring])
    g_high = lax.ppermute(g_own[:REACH], "pix", [(p, (p - 1) % PIX) for p in ring])
    mate_route = [(p, p ^ 1) for p in ring]
    x_parts, g_parts = [], []
    for m in range(4):
        block = lax.dynamic_slice(
            x_ext, (0, REACH, 0, 128 * (group_z ^ m)), (CHAN, OWN_ROWS, TILE_W, 128)
        )
        route = [(p, p ^ (2 * m)) for p in ring]
        x_parts.append(lax.ppermute(block, "pix", route) if m else block)
        g_parts.append(lax.ppermute(g_own, "pix", route) if m else g_own)
    x_parts = x_parts + [lax.ppermute(part, "pix", mate_route) for part in x_parts]
    g_parts = g_parts + [lax.ppermute(part, "pix", mate_route) for part in g_parts]

    def group_edge(spot, rows):
        picked = g_parts[0][rows]
        for m in range(4):
            for other in range(2):
                here = (group_z ^ m == spot // 2) & (core ^ other == spot % 2)
                picked = jnp.where(here, g_parts[4 * other + m][rows], picked)
        return picked

    group_low = lax.ppermute(
        group_edge(GROUP - 1, slice(OWN_ROWS - REACH, OWN_ROWS)),
        "pix",
        [(p, (p + GROUP) % PIX) for p in ring],
    )
    group_high = lax.ppermute(
        group_edge(0, slice(0, REACH)), "pix", [(p, (p - GROUP) % PIX) for p in ring]
    )
    trunk_parts = heads_input_grad(
        keep_own, g_own, g_low, g_high, atrous_weight.reshape(TASKS, 3, 3, 3, HEAD, -1), point_weight
    )
    trunk_grad = return_rows(trunk_parts.reshape(CHAN, OWN_ROWS, TILE_W, -1), 3, "return_trunk")
    maps_parts = jnp.moveaxis(
        head_part.reshape(OWN_ROWS, TILE_W, TASKS, CHAN, HEAD), 3, 0
    ).reshape(CHAN, OWN_ROWS, TILE_W, BRANCH)
    task_maps = jnp.moveaxis(
        return_rows(maps_parts, 4, "return_maps").reshape(pixel_count, TASKS, HEAD), 1, 0
    )
    weight_parts, point_parts = heads_weight_grad(keep_group, x_parts, g_parts, group_low, group_high)

    def sum_over_groups(parts):
        total = lax.dynamic_index_in_dim(parts, group_x, 0, False).astype(jnp.float32)
        for step in range(1, 4):
            sent = lax.dynamic_index_in_dim(parts, (group_x + step) % 4, 0, False)
            route = [(p, (p + GROUP * step) % PIX) for p in ring]
            total = total + lax.ppermute(sent, "pix", route).astype(jnp.float32)
        return total

    grad_atrous_weight = jnp.transpose(
        sum_over_groups(weight_parts).reshape(3, 3, HEAD, 3, TASKS, HEAD), (4, 0, 3, 1, 2, 5)
    ).reshape(TASKS, 3, 9, HEAD, HEAD)
    grad_point_weight = jnp.transpose(
        sum_over_groups(point_parts).reshape(HEAD, TASKS, HEAD), (1, 0, 2)
    )
    (
        grad_pixels, mid_grads, feat_grads, grad_reduce, grad_dilate, grad_expand, grad_project,
        grad_pooled,
    ) = section_backward(
        trunk_grad, pixels, unit_reduce, unit_dilate, unit_expand, act_reduce, act_dilate, reduce_all,
        jnp.moveaxis(dilate_weight, 0, 1).reshape(-1, 9 * MID_OWN), expand_weight, vec_mid, vec_feat,
        inv_mid, inv_feat, keep_section, pool_rows, place_onehot.T, row_onehot, sizes,
        pre_pooled.reshape(tile_count, BRANCH), pooled_weight.reshape(BRANCH, -1), grad_project,
    )
    grad_pooled_weight = jnp.einsum(
        "kc,ktd->tcd",
        tile_mean,
        grad_pooled.reshape(tile_count, TASKS, HEAD).astype(BF16),
        preferred_element_type=F32,
    )
    return (
        task_maps,
        grad_pixels,
        grad_reduce,
        mid_grads[1],
        mid_grads[0],
        grad_dilate,
        mid_grads[3],
        mid_grads[2],
        grad_expand,
        feat_grads[1],
        feat_grads[0],
        grad_point_weight,
        grad_atrous_weight,
        grad_pooled_weight,
        grad_project[:, :40],
    )


def solution(mesh):
    placed = (
        P("pix", "chan"),
        P(),
        P(),
        P(None, "chan"),
        P("chan"),
        P("chan"),
        P(None, None, "chan"),
        P("chan"),
        P("chan"),
        P(None, "chan"),
        P("chan"),
        P("chan"),
        P(None, "chan", None),
        P(None, None, None, "chan", None),
        P(None, "chan", None),
        P(None, "chan", None),
        P(None, "pix", "chan"),
    )
    return jax.shard_map(
        shards,
        mesh=mesh,
        in_specs=placed,
        out_specs=(
            P(None, "pix", "chan"),
            P("pix", "chan"),
            P("pix", "chan"),
            P("chan"),
            P("chan"),
            P(None, "pix", "chan"),
            P("chan"),
            P("chan"),
            P("pix", "chan"),
            P("chan"),
            P("chan"),
            P(None, "pix", "chan"),
            P(None, None, None, "pix", "chan"),
            P(None, None, "chan"),
            P(None, "pix", "chan"),
        ),
        check_vma=False,
    )
```

```python
import functools

import jax
import jax.numpy as jnp
from jax import lax
from jax.experimental import pallas as pl
from jax.experimental.pallas import tpu as pltpu
from jax.sharding import PartitionSpec as P

TASKS = 3
TILE_W = 64
NROWS = 256
PIX = 32
CHAN = 4
OWN_ROWS = NROWS // PIX
REACH = 3
EXT_ROWS = OWN_ROWS + 2 * REACH
HEAD = 64
BRANCH = TASKS * HEAD
TILES = 7
BRANCH_ORDER = (1, 2, 3, 0, 4)
BRANCH_PLACE = (3, 0, 1, 2, 4)

F32 = jnp.float32
BF16 = jnp.bfloat16
MESH = pl.DeviceIdType.MESH
eps = 1e-05
section_rate = 4
head_rates = (6, 12, 18)
VMEM_LIMIT = 60 * 2**20


def place_of_row(row):
    kind = row % 6
    return 43 * kind - kind // 5 + row // 6


def row_at_place(place):
    kind = (place + place // 214) // 43
    return 6 * (place - 43 * kind + kind // 5) + kind


PLACED_ROWS = tuple(row_at_place(place) for place in range(NROWS))


def int_div(a, b):
    return lax.div(a, jnp.int32(b))


def int_rem(a, b):
    return lax.rem(a, jnp.int32(b))


def place_of(row):
    kind = int_rem(row, 6)
    return 43 * kind - int_div(kind, 5) + int_div(row, 6)


def row_of(place):
    kind = int_div(place + int_div(place, 214), 43)
    return 6 * (place - 43 * kind + int_div(kind, 5)) + kind


def signal(sem, **where):
    pl.semaphore_signal(sem, inc=1, device_id=where, device_id_type=MESH)


def remote(src, dst, send_sem, recv_sem, **where):
    return pltpu.make_async_remote_copy(
        src_ref=src,
        dst_ref=dst,
        send_sem=send_sem,
        recv_sem=recv_sem,
        device_id=where,
        device_id_type=MESH,
    )


def gather_rows_kernel(
    reach, src, out, ss_row, rs_row, ss_side, rs_side, ss_far, rs_far, ss_halo, rs_halo
):
    i, j = lax.axis_index("pix"), lax.axis_index("chan")
    right, left = int_rem(j + 1, CHAN), int_rem(j + CHAN - 1, CHAN)
    far = int_rem(j + 2, CHAN)
    after, before = int_rem(i + 1, PIX), int_rem(i + PIX - 1, PIX)
    barrier = pltpu.get_barrier_semaphore()
    expected = 2 + (2 if reach else 0)
    for s in range(OWN_ROWS):
        origin = int_div(row_of(OWN_ROWS * i + s), OWN_ROWS)

        @pl.when(origin != i)
        def _():
            signal(barrier, pix=origin)

        target = int_div(place_of(OWN_ROWS * i + s), OWN_ROWS)
        expected = expected + (target != i).astype(jnp.int32)
    signal(barrier, chan=right)
    signal(barrier, chan=left)
    if reach:
        signal(barrier, pix=after)
        signal(barrier, pix=before)
    pl.semaphore_wait(barrier, expected)

    def row_send(s):
        place = place_of(OWN_ROWS * i + s)
        target, slot = int_div(place, OWN_ROWS), int_rem(place, OWN_ROWS)
        landing = out.at[j, reach + slot]
        return target, (
            lambda: remote(src.at[s], landing, ss_row.at[s], rs_row.at[slot], pix=target),
            lambda: pltpu.make_async_copy(src.at[s], landing, rs_row.at[slot]),
        )

    for s in range(OWN_ROWS):
        target, (away, here) = row_send(s)
        pl.when(target != i)(lambda: away().start())
        pl.when(target == i)(lambda: here().start())

    def block(chan, s):
        return out.at[chan, reach + s]

    def side_send(way, s):
        return remote(
            block(j, s),
            block(j, s),
            ss_side.at[way, s],
            rs_side.at[way, s],
            chan=(right, left)[way],
        )

    def side_arrival(way, s):
        chan = (left, right)[way]
        return remote(
            block(chan, s), block(chan, s), ss_side.at[way, s], rs_side.at[way, s], chan=chan
        )

    def far_send(s):
        way = 0 if s < OWN_ROWS // 2 else 1
        chan = (left, right)[way]
        return remote(
            block(chan, s), block(chan, s), ss_far.at[s], rs_far.at[s], chan=(right, left)[way]
        )

    def far_arrival(s):
        return remote(block(far, s), block(far, s), ss_far.at[s], rs_far.at[s], chan=left)

    def halo_send(turn, chan, s):
        if s < reach:
            return remote(
                block(chan, s),
                out.at[chan, reach + OWN_ROWS + s],
                ss_halo.at[turn, s],
                rs_halo.at[chan, s],
                pix=before,
            )
        lane = s - OWN_ROWS + 2 * reach
        return remote(
            block(chan, s),
            out.at[chan, s - OWN_ROWS + reach],
            ss_halo.at[turn, lane],
            rs_halo.at[chan, lane],
            pix=after,
        )

    def halo_arrival(chan, lane):
        slot = reach + OWN_ROWS + lane if lane < reach else lane - reach
        return remote(
            out.at[chan, slot],
            out.at[chan, slot],
            ss_halo.at[0, lane],
            rs_halo.at[chan, lane],
            pix=after,
        )

    order = (0, 7, 1, 6, 2, 5, 3, 4)
    edge = [s for s in order if s < reach or s >= OWN_ROWS - reach]
    for s in order:
        pltpu.make_async_copy(src.at[s], block(j, s), rs_row.at[s]).wait()
        side_send(0, s).start()
        side_send(1, s).start()
        if s in edge:
            halo_send(0, j, s).start()
    for s in order:
        for way in range(2):
            side_arrival(way, s).wait_recv()
            if way == (0 if s < OWN_ROWS // 2 else 1):
                far_send(s).start()
            if s in edge:
                halo_send(1 + way, (left, right)[way], s).start()
    for s in order:
        far_arrival(s).wait_recv()
        if s in edge:
            halo_send(3, far, s).start()
    if reach:
        for chan in range(CHAN):
            for lane in range(2 * reach):
                halo_arrival(chan, lane).wait_recv()
    for s in range(OWN_ROWS):
        target, (away, here) = row_send(s)
        pl.when(target != i)(lambda: away().wait_send())
        side_send(0, s).wait_send()
        side_send(1, s).wait_send()
        far_send(s).wait_send()
    for turn, chan in enumerate((j, left, right, far)):
        for s in edge:
            halo_send(turn, chan, s).wait_send()


def gather_rows(rows, reach, collective_id, name):
    width = rows.shape[2]
    dma = pltpu.SemaphoreType.DMA
    return pl.pallas_call(
        functools.partial(gather_rows_kernel, reach),
        out_shape=jax.ShapeDtypeStruct((CHAN, OWN_ROWS + 2 * reach, TILE_W, width), rows.dtype),
        in_specs=[pl.BlockSpec(memory_space=pl.ANY)],
        out_specs=pl.BlockSpec(memory_space=pl.ANY),
        scratch_shapes=[
            dma((OWN_ROWS,)),
            dma((OWN_ROWS,)),
            dma((2, OWN_ROWS)),
            dma((2, OWN_ROWS)),
            dma((OWN_ROWS,)),
            dma((OWN_ROWS,)),
            dma((CHAN, max(2 * reach, 1))),
            dma((CHAN, max(2 * reach, 1))),
        ],
        compiler_params=pltpu.CompilerParams(collective_id=collective_id, has_side_effects=True),
        cost_estimate=pl.CostEstimate(flops=0, bytes_accessed=60_000_000, transcendentals=0),
        name=name,
    )(rows)


def return_rows_kernel(src, out, own, arrived, total, ls, ss_side, rs_side, ss_row, rs_row):
    i, j = lax.axis_index("pix"), lax.axis_index("chan")
    barrier = pltpu.get_barrier_semaphore()
    expected = 3
    for s in range(OWN_ROWS):
        origin = int_div(place_of(OWN_ROWS * i + s), OWN_ROWS)

        @pl.when(origin != i)
        def _():
            signal(barrier, pix=origin)

        target = int_div(row_of(OWN_ROWS * i + s), OWN_ROWS)
        expected = expected + (target != i).astype(jnp.int32)
    for distance in (1, 2, 3):
        signal(barrier, chan=int_rem(j + distance, CHAN))
    pl.semaphore_wait(barrier, expected)

    def side_send(distance, s):
        chan = int_rem(j + distance, CHAN)
        return remote(
            src.at[chan, s],
            arrived.at[distance - 1, s],
            ss_side.at[distance - 1, s],
            rs_side.at[distance - 1, s],
            chan=chan,
        )

    for s in range(OWN_ROWS):
        for distance in (2, 1, 3):
            side_send(distance, s).start()
    load = pltpu.make_async_copy(src.at[j], own, ls)
    load.start()
    load.wait()

    def row_send(s):
        row = row_of(OWN_ROWS * i + s)
        target, slot = int_div(row, OWN_ROWS), int_rem(row, OWN_ROWS)
        return target, (
            lambda: remote(total.at[s], out.at[slot], ss_row.at[s], rs_row.at[slot], pix=target),
            lambda: pltpu.make_async_copy(total.at[s], out.at[slot], rs_row.at[slot]),
        )

    for s in range(OWN_ROWS):
        held = own[s].astype(F32)
        for distance in (1, 3, 2):
            side_send(distance, s).wait_recv()
            held = held + arrived[distance - 1, s].astype(F32)
        total[s] = held.astype(BF16)
        target, (away, here) = row_send(s)
        pl.when(target != i)(lambda: away().start())
        pl.when(target == i)(lambda: here().start())
    for s in range(OWN_ROWS):
        pltpu.make_async_copy(total.at[s], out.at[s], rs_row.at[s]).wait()
        target, (away, here) = row_send(s)
        pl.when(target != i)(lambda: away().wait_send())
        for distance in (1, 2, 3):
            side_send(distance, s).wait_send()


def return_rows(parts, collective_id, name):
    width = parts.shape[3]
    dma = pltpu.SemaphoreType.DMA
    rows = (OWN_ROWS, TILE_W, width)
    return pl.pallas_call(
        return_rows_kernel,
        out_shape=jax.ShapeDtypeStruct(rows, BF16),
        in_specs=[pl.BlockSpec(memory_space=pl.ANY)],
        out_specs=pl.BlockSpec(memory_space=pl.ANY),
        scratch_shapes=[
            pltpu.VMEM(rows, BF16),
            pltpu.VMEM((CHAN - 1, *rows), BF16),
            pltpu.VMEM(rows, BF16),
            dma,
            dma((CHAN - 1, OWN_ROWS)),
            dma((CHAN - 1, OWN_ROWS)),
            dma((OWN_ROWS,)),
            dma((OWN_ROWS,)),
        ],
        compiler_params=pltpu.CompilerParams(collective_id=collective_id, has_side_effects=True),
        cost_estimate=pl.CostEstimate(flops=0, bytes_accessed=60_000_000, transcendentals=0),
        name=name,
    )(parts)


GROUP = 8
GROUP_ROWS = GROUP * OWN_ROWS


class Posts:
    def __init__(self, send_sems, recv_sems):
        self.send_sems, self.recv_sems, self.made = send_sems, recv_sems, []

    def copy(self, n, make):
        src, dst, where = make()
        return remote(src, dst, self.send_sems.at[n], self.recv_sems.at[n], **where)

    def post(self, make):
        n = len(self.made)
        self.made.append(make)
        self.copy(n, make).start()
        return n

    def arrive(self, n, dst):
        beside = {"chan": int_rem(lax.axis_index("chan") + 1, CHAN)}
        remote(dst, dst, self.send_sems.at[n], self.recv_sems.at[n], **beside).wait_recv()

    def finish(self):
        for n, make in enumerate(self.made):
            self.copy(n, make).wait_send()


def greet(peers, more=0):
    barrier = pltpu.get_barrier_semaphore()
    for where in peers:
        signal(barrier, **where)
    pl.semaphore_wait(barrier, len(peers) + more)


class Spot:
    def __init__(self):
        self.i, self.j = lax.axis_index("pix"), lax.axis_index("chan")
        self.group, self.k = int_div(self.i, GROUP), int_rem(self.i, GROUP)
        self.z, self.core = int_div(self.k, 2), int_rem(self.k, 2)
        self.before, self.after = int_rem(self.i + PIX - 1, PIX), int_rem(self.i + 1, PIX)
        self.mate = self.i + 1 - 2 * self.core

    def chan(self, distance):
        return int_rem(self.j + CHAN + distance, CHAN)

    def in_group(self, distance):
        return int_rem(self.k + GROUP + distance, GROUP)

    def pix_in_group(self, distance):
        return GROUP * self.group + self.in_group(distance)

    def x_of(self, distance):
        return int_rem(self.group + 4 + distance, 4)

    def pix_in_x(self, distance):
        return GROUP * self.x_of(distance) + self.k

    def z_of(self, distance):
        return int_rem(self.z + 4 + distance, 4)

    def pix_in_z(self, distance):
        return GROUP * self.group + 2 * self.z_of(distance) + self.core

    def sum_peers(self):
        return [{"pix": self.pix_in_group(d)} for d in range(1, GROUP)] + [
            {"pix": self.pix_in_x(d)} for d in range(1, 4)
        ]


def dot_nt(a, b):
    return lax.dot_general(a, b, (((1,), (1,)), ((), ())), preferred_element_type=F32)


def dot_tn(a, b):
    return lax.dot_general(a, b, (((0,), (0,)), ((), ())), preferred_element_type=F32)


def dot_nn(a, b):
    return jnp.dot(a, b, preferred_element_type=F32)


def slope(v):
    s = jax.nn.sigmoid(v)
    return s * (1.0 + v * (1.0 - s))


def silu(v):
    return v * jax.nn.sigmoid(v)


def heads_forward_kernel(
    keep, x_hbm, maps_own, kernel, point, spread, pooled,
    grad_pre, head_part, grad_project, pool_rows, x_group,
    x, acc, pre, maps_in, relay, sems, ss_row, rs_row, send_sems, recv_sems, own_sem,
):
    step = pl.program_id(0)
    rate, row_tap = step // 3, step % 3
    first = REACH + (row_tap - 1) * (rate + 1)
    spot = Spot()
    posts = Posts(send_sems, recv_sems)
    i, j = spot.i, spot.j
    halves = (slice(0, OWN_ROWS // 2), slice(OWN_ROWS // 2, OWN_ROWS))
    chans = (slice(0, 2), slice(2, 4))

    def x_slice(distance, which=slice(0, CHAN)):
        lanes = pl.ds(pl.multiple_of(128 * spot.z_of(distance), 128), 128)
        return x_hbm.at[which, REACH : REACH + OWN_ROWS, :, lanes]

    def x_rows(distance, core, which=slice(0, CHAN)):
        return x_group.at[which, pl.ds(OWN_ROWS * (2 * spot.z_of(distance) + core), OWN_ROWS)]

    def own_copy():
        return pltpu.make_async_copy(x_slice(0), x_rows(0, spot.core), own_sem.at[0])

    def row_send(s):
        place = place_of(OWN_ROWS * i + s)
        target, slot = int_div(place, OWN_ROWS), int_rem(place, OWN_ROWS)
        return target, (
            lambda: remote(
                maps_own.at[s], maps_in.at[j, slot], ss_row.at[s], rs_row.at[slot], pix=target
            ),
            lambda: pltpu.make_async_copy(maps_own.at[s], maps_in.at[j, slot], rs_row.at[slot]),
        )

    ways = ((1, {"chan": spot.chan(1)}), (-1, {"chan": spot.chan(-1)}))
    marks = {}

    @pl.when(step == 0)
    def _():
        width = x_hbm.shape[3]
        copies = [
            pltpu.make_async_copy(
                x_hbm.at[chan], x.at[:, :, width * chan : width * (chan + 1)], sems.at[chan]
            )
            for chan in range(CHAN)
        ]
        for copy in copies:
            copy.start()
        own_copy().start()
        barrier = pltpu.get_barrier_semaphore()
        expected = 0
        for s in range(OWN_ROWS):
            origin = int_div(row_of(OWN_ROWS * i + s), OWN_ROWS)

            @pl.when(origin != i)
            def _():
                signal(barrier, pix=origin)

            target = int_div(place_of(OWN_ROWS * i + s), OWN_ROWS)
            expected = expected + (target != i).astype(jnp.int32)
        greet(
            [where for _, where in ways]
            + [{"pix": spot.pix_in_z(d)} for d in (1, -1)]
            + [{"pix": spot.mate}],
            expected,
        )
        for s in range(OWN_ROWS):
            target, (away, here) = row_send(s)
            pl.when(target != i)(lambda: away().start())
            pl.when(target == i)(lambda: here().start())
        for way, d in enumerate((1, -1)):
            marks["relay", way] = posts.post(
                lambda way=way, d=d: (
                    x_slice(2, chans[way]), relay.at[way], {"pix": spot.pix_in_z(d)}
                )
            )
        for d in (1, -1):
            marks["z", d] = posts.post(
                lambda d=d: (x_slice(d), x_rows(0, spot.core), {"pix": spot.pix_in_z(d)})
            )
        marks["mate", 0] = posts.post(
            lambda: (x_slice(0), x_rows(0, spot.core), {"pix": spot.mate})
        )
        for copy in copies:
            copy.wait()

    @pl.when(step == 1)
    def _():
        for s in range(OWN_ROWS):
            pltpu.make_async_copy(maps_own.at[s], maps_in.at[j, s], rs_row.at[s]).wait()
        for half in range(2):
            for d, where in ways:
                marks["maps", d, half] = posts.post(
                    lambda half=half, where=where: (
                        maps_in.at[j, halves[half]], maps_in.at[j, halves[half]], where
                    )
                )

    @pl.when(step == 3)
    def _():
        for way, d in enumerate((1, -1)):
            posts.arrive(marks["relay", way], relay.at[way])
            marks["far", way] = posts.post(
                lambda way=way, d=d: (
                    relay.at[way],
                    x_rows(-d, spot.core, chans[way]),
                    {"pix": spot.pix_in_z(d)},
                )
            )

    @pl.when(step == 4)
    def _():
        for d, _ in ways:
            for half in range(2):
                source = spot.chan(-d)
                posts.arrive(marks["maps", d, half], maps_in.at[source, halves[half]])
        for half, (d, where) in enumerate(ways):
            marks["maps far", half] = posts.post(
                lambda d=d, half=half, where=where: (
                    maps_in.at[spot.chan(-d), halves[half]],
                    maps_in.at[spot.chan(-d), halves[half]],
                    where,
                )
            )

    @pl.when(step == 6)
    def _():
        for d in (1, -1):
            posts.arrive(marks["z", d], x_rows(-d, spot.core))
            marks["mate", d] = posts.post(
                lambda d=d: (x_rows(-d, spot.core), x_rows(-d, spot.core), {"pix": spot.mate})
            )

    def rows_from(start):
        return x[pl.ds(start, OWN_ROWS)].reshape(OWN_ROWS * TILE_W, -1)

    window = rows_from(first)
    for b in range(3):
        product = dot_nt(window, kernel[:, 0, 0, b].reshape(BRANCH, -1))
        for r in range(OWN_ROWS):
            part = slice(TILE_W * r, TILE_W * (r + 1))
            term = jnp.where(keep[step, r] > 0, product[part], 0.0)
            acc[b, part] = jnp.where(row_tap > 0, acc[b, part], 0.0) + term

    for which, dilation in enumerate(head_rates):

        @pl.when(step == 3 * which + 2)
        def _():
            col = lax.broadcasted_iota(jnp.int32, (OWN_ROWS * TILE_W, BRANCH), 0) % TILE_W
            total = acc[1]
            behind = pltpu.roll(acc[0], dilation, 0)
            ahead = pltpu.roll(acc[2], OWN_ROWS * TILE_W - dilation, 0)
            total = total + jnp.where(col >= dilation, behind, 0.0)
            pre[which] = total + jnp.where(col < TILE_W - dilation, ahead, 0.0)

    @pl.when(step == 0)
    def _():
        pre[3] = dot_nt(rows_from(REACH), point[...].reshape(BRANCH, -1))

    @pl.when(step == 8)
    def _():
        for half in range(2):
            posts.arrive(marks["maps far", half], maps_in.at[spot.chan(2), halves[half]])
        for way in range(2):
            posts.arrive(marks["far", way], x_rows(2, spot.core, chans[way]))
        marks["mate", 2] = posts.post(
            lambda: (x_rows(2, spot.core), x_rows(2, spot.core), {"pix": spot.mate})
        )
        cot = jnp.concatenate([maps_in[c].reshape(-1, BRANCH) for c in range(CHAN)], axis=1)
        head = None
        for which in range(5):
            if which < 4:
                before = pre[which]
                logistic = jax.nn.sigmoid(before)
                joined = (before * logistic).astype(BF16)
            else:
                joined = pooled[...]
            weight = spread[which]
            term = dot_nn(joined, weight)
            head = term if head is None else head + term
            grads = dot_tn(joined, cot)
            for t in range(TASKS):
                for c in range(CHAN):
                    lane = BRANCH * c + HEAD * t
                    grad_project[c, which, t] = grads[
                        HEAD * t : HEAD * (t + 1), lane : lane + HEAD
                    ].astype(BF16)
            back = dot_nt(cot, weight)
            if which < 4:
                grad = back * (logistic * (1.0 + before * (1.0 - logistic)))
                grad_pre[:, BRANCH * which : BRANCH * (which + 1)] = grad.astype(BF16)
            else:
                sums = jnp.sum(back.reshape(OWN_ROWS, TILE_W, BRANCH), axis=1)
                pool_rows[:, :BRANCH] = sums
                pool_rows[:, BRANCH:] = jnp.zeros((OWN_ROWS, 256 - BRANCH), F32)
        for c in range(CHAN):
            head_part[c] = head[:, BRANCH * c : BRANCH * (c + 1)].astype(BF16)
        for d in (0, 1, -1, 2):
            other = 1 - spot.core
            posts.arrive(marks["mate", d], x_rows(-d, other))
        own_copy().wait()
        for s in range(OWN_ROWS):
            target, (away, here) = row_send(s)
            pl.when(target != i)(lambda: away().wait_send())
        posts.finish()


def heads_forward(keep, x_ext, maps_own, kernels, point, spread, pooled):
    pixels = OWN_ROWS * TILE_W
    feat = point.shape[2]
    whole = pl.BlockSpec(memory_space=pltpu.VMEM)
    hbm = pl.BlockSpec(memory_space=pl.ANY)
    dma = pltpu.SemaphoreType.DMA
    return pl.pallas_call(
        heads_forward_kernel,
        grid=(9,),
        in_specs=[
            pl.BlockSpec(memory_space=pltpu.SMEM),
            hbm,
            whole,
            pl.BlockSpec((TASKS, 1, 1, 3, HEAD, feat), lambda s: (0, s // 3, s % 3, 0, 0, 0)),
            whole,
            whole,
            whole,
        ],
        out_specs=[whole] * 4 + [hbm],
        out_shape=[
            jax.ShapeDtypeStruct((pixels, 4 * BRANCH), BF16),
            jax.ShapeDtypeStruct((CHAN, pixels, BRANCH), BF16),
            jax.ShapeDtypeStruct((CHAN, 5, TASKS, HEAD, HEAD), BF16),
            jax.ShapeDtypeStruct((OWN_ROWS, 256), F32),
            jax.ShapeDtypeStruct((CHAN, GROUP_ROWS, TILE_W, 128), BF16),
        ],
        scratch_shapes=[
            pltpu.VMEM((EXT_ROWS, TILE_W, feat), BF16),
            pltpu.VMEM((3, pixels, BRANCH), F32),
            pltpu.VMEM((4, pixels, BRANCH), F32),
            pltpu.VMEM((CHAN, OWN_ROWS, TILE_W, BRANCH), BF16),
            pltpu.VMEM((2, 2, OWN_ROWS, TILE_W, 128), BF16),
            dma((CHAN,)),
            dma((OWN_ROWS,)),
            dma((OWN_ROWS,)),
            dma((16,)),
            dma((16,)),
            dma((1,)),
        ],
        compiler_params=pltpu.CompilerParams(
            collective_id=2, has_side_effects=True, vmem_limit_bytes=VMEM_LIMIT
        ),
        cost_estimate=pl.CostEstimate(
            flops=12_000_000_000, bytes_accessed=28_000_000, transcendentals=0
        ),
        name="heads_forward",
    )(keep, x_ext, maps_own, kernels, point, spread, pooled)


PAD = 24
PADDED = PAD + TILE_W + PAD


def heads_input_grad_kernel(
    keep, mid, parts, kernel, point, out, g_group, maps_out,
    wide, taps, acc, edges, maps_in, maps_sum, ss_row, rs_row, send_sems, recv_sems, own_sem,
):
    n, rate = pl.program_id(0), pl.program_id(1)
    step = 3 * n + rate
    spot = Spot()
    posts = Posts(send_sems, recv_sems)
    i, j = spot.i, spot.j
    low, high = edges.at[0], edges.at[1]
    half_rows = OWN_ROWS // 2
    marks = {}

    def g_rows(distance, core, half=None):
        start = OWN_ROWS * (2 * spot.z_of(distance) + core)
        if half is None:
            return g_group.at[pl.ds(start, OWN_ROWS)]
        return g_group.at[pl.ds(start + half_rows * half, half_rows)]

    def own_copy():
        return pltpu.make_async_copy(mid, g_rows(0, spot.core), own_sem.at[0])

    def row_send(s):
        row = row_of(OWN_ROWS * i + s)
        target, slot = int_div(row, OWN_ROWS), int_rem(row, OWN_ROWS)
        return target, (
            lambda: remote(
                maps_sum.at[s], maps_out.at[slot], ss_row.at[s], rs_row.at[slot], pix=target
            ),
            lambda: pltpu.make_async_copy(maps_sum.at[s], maps_out.at[slot], rs_row.at[slot]),
        )

    @pl.when(step == 0)
    def _():
        own_copy().start()
        barrier = pltpu.get_barrier_semaphore()
        expected = 0
        for s in range(OWN_ROWS):
            origin = int_div(place_of(OWN_ROWS * i + s), OWN_ROWS)

            @pl.when(origin != i)
            def _():
                signal(barrier, pix=origin)

            target = int_div(row_of(OWN_ROWS * i + s), OWN_ROWS)
            expected = expected + (target != i).astype(jnp.int32)
        greet(
            [{"chan": spot.chan(d)} for d in (1, 2, 3)]
            + [{"pix": spot.pix_in_z(d)} for d in (1, -1)]
            + [{"pix": p} for p in (spot.mate, spot.before, spot.after)],
            expected,
        )
        marks["low"] = posts.post(
            lambda: (mid.at[OWN_ROWS - REACH :], low, {"pix": spot.after})
        )
        marks["high"] = posts.post(lambda: (mid.at[:REACH], high, {"pix": spot.before}))
        for d in (2, 1, 3):
            marks["maps", d] = posts.post(
                lambda d=d: (parts.at[spot.chan(d)], maps_in.at[d - 1], {"chan": spot.chan(d)})
            )
        for half in range(2):
            for d in (1, -1):
                marks["z", d, half] = posts.post(
                    lambda half=half, d=d: (
                        mid.at[half_rows * half : half_rows * (half + 1)],
                        g_rows(0, spot.core, half),
                        {"pix": spot.pix_in_z(d)},
                    )
                )
        marks["mate", 0] = posts.post(lambda: (mid, g_rows(0, spot.core), {"pix": spot.mate}))
        wide[...] = jnp.zeros_like(wide)
        posts.arrive(marks["low"], low)
        posts.arrive(marks["high"], high)
        for start, part in ((0, low), (REACH, mid), (REACH + OWN_ROWS, high)):
            held = part[...].astype(F32)
            for which in range(3):
                for t in range(TASKS):
                    lane = BRANCH * which + HEAD * t
                    one = held[:, :, lane : lane + HEAD]
                    wide[3 * t + which, start : start + held.shape[0], PAD : PAD + TILE_W] = (
                        jnp.concatenate([one, one], axis=2)
                    )

        def one_row(r, carry):
            is_low = lax.broadcasted_iota(jnp.int32, (TILE_W, 2 * HEAD), 1) < HEAD
            out_rows = pl.ds(pl.multiple_of(r * TILE_W, TILE_W), TILE_W)
            for which, dilation in enumerate(head_rates):

                def shifted(tap):
                    t, a, b = tap // 9, tap // 3 % 3 - 1, tap % 3 - 1
                    piece = wide[
                        3 * t + which,
                        r + REACH - a * (which + 1),
                        PAD - b * dilation : PAD - b * dilation + TILE_W,
                    ]
                    return jnp.where(keep[3 * which + 1 - a, r] > 0, piece, 0.0)

                for pair in range(14):
                    first = shifted(2 * pair)
                    second = shifted(2 * pair + 1) if pair < 13 else jnp.zeros_like(first)
                    taps[which, out_rows, 2 * HEAD * pair : 2 * HEAD * (pair + 1)] = jnp.where(
                        is_low, first, second
                    ).astype(BF16)
            return carry

        lax.fori_loop(0, OWN_ROWS, one_row, 0)

    @pl.when(step == 3)
    def _():
        for d in (1, 3, 2):
            posts.arrive(marks["maps", d], maps_in.at[d - 1])
        for s in range(OWN_ROWS):
            held = parts[j, s].astype(F32)
            for d in (1, 2, 3):
                held = held + maps_in[d - 1, s].astype(F32)
            maps_sum[s] = held.astype(BF16)
            target, (away, here) = row_send(s)
            pl.when(target != i)(lambda: away().start())
            pl.when(target == i)(lambda: here().start())

    @pl.when(step == 4)
    def _():
        for half, d in enumerate((1, -1)):
            posts.arrive(marks["z", d, half], g_rows(-d, spot.core, half))
            marks["far", half] = posts.post(
                lambda half=half, d=d: (
                    g_rows(-d, spot.core, half),
                    g_rows(-d, spot.core, half),
                    {"pix": spot.pix_in_z(d)},
                )
            )
        for half, d in enumerate((-1, 1)):
            posts.arrive(marks["z", d, half], g_rows(-d, spot.core, half))
        for d in (1, -1):
            marks["mate", d] = posts.post(
                lambda d=d: (g_rows(-d, spot.core), g_rows(-d, spot.core), {"pix": spot.mate})
            )

    product = dot_nn(taps[rate, :, : 27 * HEAD], kernel[...].reshape(27 * HEAD, -1))

    @pl.when(rate == 0)
    def _():
        grads = mid[...].reshape(OWN_ROWS * TILE_W, -1)[:, 3 * BRANCH :]
        acc[...] = product + dot_nn(grads, point[...].reshape(BRANCH, -1))

    @pl.when(rate == 1)
    def _():
        acc[...] += product

    @pl.when(rate == 2)
    def _():
        total = acc[...] + product
        for c in range(out.shape[0]):
            out[c] = total[:, 512 * c : 512 * (c + 1)].astype(BF16)

    @pl.when(step == 5)
    def _():
        for half in range(2):
            posts.arrive(marks["far", half], g_rows(2, spot.core, half))
        marks["mate", 2] = posts.post(
            lambda: (g_rows(2, spot.core), g_rows(2, spot.core), {"pix": spot.mate})
        )
        for d in (0, 1, -1, 2):
            posts.arrive(marks["mate", d], g_rows(-d, 1 - spot.core))
        own_copy().wait()
        for s in range(OWN_ROWS):
            pltpu.make_async_copy(maps_sum.at[s], maps_out.at[s], rs_row.at[s]).wait()
            target, (away, here) = row_send(s)
            pl.when(target != i)(lambda: away().wait_send())
        posts.finish()


def heads_input_grad(keep, grad_mid, head_part, kernels, point):
    pixels = OWN_ROWS * TILE_W
    block = 1024
    whole = pl.BlockSpec(memory_space=pltpu.VMEM)
    hbm = pl.BlockSpec(memory_space=pl.ANY)
    dma = pltpu.SemaphoreType.DMA
    maps = (OWN_ROWS, TILE_W, BRANCH)
    return pl.pallas_call(
        heads_input_grad_kernel,
        grid=(2, 3),
        in_specs=[
            pl.BlockSpec(memory_space=pltpu.SMEM),
            whole,
            whole,
            pl.BlockSpec((TASKS, 1, 3, 3, HEAD, block), lambda n, r: (0, r, 0, 0, 0, n)),
            pl.BlockSpec((TASKS, HEAD, block), lambda n, r: (0, 0, n)),
        ],
        out_specs=[
            pl.BlockSpec((block // 512, pixels, 512), lambda n, r: (n, 0, 0)),
            hbm,
            hbm,
        ],
        out_shape=[
            jax.ShapeDtypeStruct((CHAN, pixels, 512), BF16),
            jax.ShapeDtypeStruct((GROUP_ROWS, TILE_W, 4 * BRANCH), BF16),
            jax.ShapeDtypeStruct(maps, BF16),
        ],
        scratch_shapes=[
            pltpu.VMEM((9, EXT_ROWS, PADDED, 2 * HEAD), F32),
            pltpu.VMEM((3, pixels, 28 * HEAD), BF16),
            pltpu.VMEM((pixels, block), F32),
            pltpu.VMEM((2, REACH, TILE_W, 4 * BRANCH), BF16),
            pltpu.VMEM((CHAN - 1, *maps), BF16),
            pltpu.VMEM(maps, BF16),
            dma((OWN_ROWS,)),
            dma((OWN_ROWS,)),
            dma((16,)),
            dma((16,)),
            dma((1,)),
        ],
        compiler_params=pltpu.CompilerParams(
            collective_id=3, has_side_effects=True, vmem_limit_bytes=VMEM_LIMIT
        ),
        cost_estimate=pl.CostEstimate(
            flops=12_000_000_000, bytes_accessed=28_000_000, transcendentals=0
        ),
        name="heads_input_grad",
    )(keep, grad_mid, head_part, kernels, point)


class GroupSum:
    def __init__(self, out, relay_in, side_in, spot, links):
        self.out, self.relay_in, self.side_in, self.spot, self.links = out, relay_in, side_in, spot, links
        self.open, self.arrivals = [], []

    def send(self, n, way):
        spot, links, out = self.spot, self.links, self.out
        relay = links.send(out.at[n, spot.x_of(2)], self.relay_in.at[n], pix=spot.pix_in_x(way))
        side = links.send(
            out.at[n, spot.x_of(-way)], self.side_in.at[n, 0], pix=spot.pix_in_x(-way)
        )
        self.arrivals.append((side, n, 0))
        self.open.append((n, way, relay))

    def relay(self):
        for n, way, relay in self.open:
            self.links.arrive(relay, self.relay_in.at[n])
            target = self.spot.x_of(way)
            both = self.out[n, target].astype(F32) + self.relay_in[n].astype(F32)
            self.out[n, target] = both.astype(BF16)
            side = self.links.send(
                self.out.at[n, target], self.side_in.at[n, 1], pix=self.spot.pix_in_x(way)
            )
            self.arrivals.append((side, n, 1))
        self.open = []

    def finish(self, total):
        for side, n, which in self.arrivals:
            self.links.arrive(side, self.side_in.at[n, which])
        for n in range(self.out.shape[0]):
            total[n] = (
                self.out[n, self.spot.group].astype(F32)
                + self.side_in[n, 0].astype(F32)
                + self.side_in[n, 1].astype(F32)
            )


class Links:
    def __init__(self, send_sems, recv_sems):
        self.send_sems, self.recv_sems, self.count, self.sent = send_sems, recv_sems, 0, []

    def send(self, src, dst, **where):
        n = self.count
        self.count += 1
        copy = remote(src, dst, self.send_sems.at[n], self.recv_sems.at[n], **where)
        copy.start()
        self.sent.append(copy)
        return n

    def arrive(self, n, dst):
        beside = {"chan": int_rem(lax.axis_index("chan") + 1, CHAN)}
        remote(dst, dst, self.send_sems.at[n], self.recv_sems.at[n], **beside).wait_recv()

    def finish(self):
        for copy in self.sent:
            copy.wait_send()


def sum_over_pix(value, near, across, spot, links, meanwhile=lambda: None):
    near[spot.k] = value
    sent = [
        links.send(near.at[spot.k], near.at[spot.k], pix=spot.pix_in_group(d))
        for d in range(1, GROUP)
    ]
    meanwhile()
    for d, n in zip(range(1, GROUP), sent):
        links.arrive(n, near.at[spot.in_group(-d)])
    total = near[0]
    for k in range(1, GROUP):
        total = total + near[k]
    across[spot.group] = total
    sent = [
        links.send(across.at[spot.group], across.at[spot.group], pix=spot.pix_in_x(d))
        for d in range(1, 4)
    ]
    meanwhile()
    for d, n in zip(range(1, 4), sent):
        links.arrive(n, across.at[spot.x_of(-d)])
    return across[0] + across[1] + across[2] + across[3]


def two_sums(first, second):
    width = first.shape[1]
    rows = [jnp.sum(first, axis=0, keepdims=True), jnp.sum(second, axis=0, keepdims=True)]
    return jnp.concatenate(rows + [jnp.zeros((6, width), F32)], axis=0)


PIXELS = NROWS * TILE_W
OWN = OWN_ROWS * TILE_W
MID_OWN = 128
FEAT_OWN = 512
ROW_COLS = OWN_ROWS * TILE_W


def col_shift(value, distance):
    col = lax.broadcasted_iota(jnp.int32, value.shape, 0) % TILE_W
    rows = value.shape[0]
    moved = pltpu.roll(value, (rows - distance) % rows, 0)
    inside = (col < TILE_W - distance) if distance > 0 else (col >= -distance)
    return jnp.where(inside, moved, 0.0)


def section_forward_kernel(
    pixels, wr, wd, we, vec_mid, vec_feat, keep, tile_rows, sizes,
    trunk, unit_r, unit_d, unit_e, act_r, act_d, wr_all, inv_mid, inv_feat, mean_all,
    part_out, part_in, near_m, across_m, near_f, across_f, near_t, across_t, send_sems, recv_sems,
):
    spot = Spot()
    links = Links(send_sems, recv_sems)
    j = spot.j
    peers = [{"chan": spot.chan(d)} for d in (1, 2, 3)] + spot.sum_peers()
    for d in range(CHAN):
        peers += [{"pix": p, "chan": spot.chan(d)} for p in (spot.before, spot.after)]
    greet(peers)

    def block(chan):
        return pl.ds(pl.multiple_of(FEAT_OWN * chan, FEAT_OWN), FEAT_OWN)

    sent = {
        d: links.send(wr.at[block(spot.chan(d))], wr_all.at[j], chan=spot.chan(d)) for d in (2, 1, 3)
    }
    wr_all[j] = wr[block(j)]
    pre = dot_nn(pixels[...], wr_all[j])
    back = {}
    for d in (1, 3, 2):
        source = spot.chan(-d)
        links.arrive(sent[d], wr_all.at[source])
        part_out[d - 1] = dot_nn(pixels[...], wr_all[source]).astype(BF16)
        back[d] = links.send(part_out.at[d - 1], part_in.at[d - 1], chan=source)
    for d in (1, 3, 2):
        links.arrive(back[d], part_in.at[d - 1])
        pre = pre + part_in[d - 1].astype(F32)

    def norm(value, near, across, gain, bias):
        sums = sum_over_pix(two_sums(value, value * value), near, across, spot, links)
        center = sums[0:1] / PIXELS
        inv = lax.rsqrt(sums[1:2] / PIXELS - center * center + eps)
        unit = (value - center) * inv
        return unit, unit * gain + bias, inv

    unit, normed, inv_r = norm(pre, near_m.at[0], across_m.at[0], vec_mid[0:1], vec_mid[1:2])
    unit_r[...] = unit
    own = slice(section_rate, section_rate + OWN_ROWS)
    act_r[j, own] = silu(normed).astype(BF16).reshape(OWN_ROWS, TILE_W, MID_OWN)
    low, high = slice(0, section_rate), slice(section_rate + OWN_ROWS, 2 * section_rate + OWN_ROWS)
    first, last = slice(section_rate, 2 * section_rate), slice(OWN_ROWS, section_rate + OWN_ROWS)
    arrivals = []
    for d in (2, 1, 3, 0):
        to, source = spot.chan(d), spot.chan(-d)
        if d:
            n = links.send(act_r.at[j, own], act_r.at[j, own], chan=to)
            arrivals.append((n, act_r.at[source, own]))
        n = links.send(act_r.at[j, first], act_r.at[j, high], pix=spot.before, chan=to)
        arrivals.append((n, act_r.at[source, high]))
        n = links.send(act_r.at[j, last], act_r.at[j, low], pix=spot.after, chan=to)
        arrivals.append((n, act_r.at[source, low]))
    for n, dst in arrivals:
        links.arrive(n, dst)
    pre = jnp.zeros((OWN, MID_OWN), F32)
    for a in range(3):
        rows = slice(section_rate * a, section_rate * a + OWN_ROWS)
        window = jnp.concatenate(
            [act_r[c, rows].reshape(OWN, MID_OWN) for c in range(CHAN)], axis=1
        )
        terms = [dot_nn(window, wd[3 * a + b]) for b in range(3)]
        term = terms[1] + col_shift(terms[0], -section_rate) + col_shift(terms[2], section_rate)
        pre = pre + (term if a == 1 else term * keep[a // 2])

    unit, normed, inv_d = norm(pre, near_m.at[1], across_m.at[1], vec_mid[2:3], vec_mid[3:4])
    unit_d[...] = unit
    inv_mid[...] = jnp.concatenate([inv_r, inv_d, jnp.zeros((6, MID_OWN), F32)], axis=0)
    act_d[j] = silu(normed).astype(BF16)
    sent = {d: links.send(act_d.at[j], act_d.at[j], chan=spot.chan(d)) for d in (2, 1, 3)}
    for d in (1, 3, 2):
        links.arrive(sent[d], act_d.at[spot.chan(-d)])
    full = jnp.concatenate([act_d[c] for c in range(CHAN)], axis=1)
    unit, normed, inv_e = norm(
        dot_nn(full, we[...]), near_f, across_f, vec_feat[0:1], vec_feat[1:2]
    )
    unit_e[...] = unit
    inv_feat[...] = jnp.concatenate([inv_e, jnp.zeros((7, FEAT_OWN), F32)], axis=0)
    out = silu(normed + pixels[...].astype(F32)).astype(BF16)
    trunk[...] = out.reshape(OWN_ROWS, TILE_W, FEAT_OWN)
    row_sums = jnp.sum(out.astype(F32).reshape(OWN_ROWS, TILE_W, FEAT_OWN), axis=1)
    sums = jnp.zeros((8, FEAT_OWN), F32)
    for r in range(OWN_ROWS):
        sums = sums + tile_rows[:, r : r + 1] * row_sums[r : r + 1]
    sums = sum_over_pix(sums, near_t, across_t, spot, links)
    mean = jnp.concatenate([sums / sizes[:, 0:1], jnp.zeros((8, FEAT_OWN), F32)], axis=0)
    mean_all[j] = mean.astype(BF16)
    sent = {d: links.send(mean_all.at[j], mean_all.at[j], chan=spot.chan(d)) for d in (2, 1, 3)}
    for d in (1, 3, 2):
        links.arrive(sent[d], mean_all.at[spot.chan(-d)])
    links.finish()


def section_forward(pixels, wr, wd, we, vec_mid, vec_feat, keep, tile_rows, sizes):
    whole = pl.BlockSpec(memory_space=pltpu.VMEM)
    shape = jax.ShapeDtypeStruct
    mid, feat = (OWN, MID_OWN), (OWN, FEAT_OWN)
    dma = pltpu.SemaphoreType.DMA
    return pl.pallas_call(
        section_forward_kernel,
        in_specs=[whole] * 9,
        out_specs=[whole] * 10,
        out_shape=[
            shape((OWN_ROWS, TILE_W, FEAT_OWN), BF16),
            shape(mid, F32),
            shape(mid, F32),
            shape(feat, F32),
            shape((CHAN, OWN_ROWS + 2 * section_rate, TILE_W, MID_OWN), BF16),
            shape((CHAN, *mid), BF16),
            shape((CHAN, FEAT_OWN, MID_OWN), BF16),
            shape((8, MID_OWN), F32),
            shape((8, FEAT_OWN), F32),
            shape((CHAN, 16, FEAT_OWN), BF16),
        ],
        scratch_shapes=[
            pltpu.VMEM((3, *mid), BF16),
            pltpu.VMEM((3, *mid), BF16),
            pltpu.VMEM((2, GROUP, 8, MID_OWN), F32),
            pltpu.VMEM((2, 4, 8, MID_OWN), F32),
            pltpu.VMEM((GROUP, 8, FEAT_OWN), F32),
            pltpu.VMEM((4, 8, FEAT_OWN), F32),
            pltpu.VMEM((GROUP, 8, FEAT_OWN), F32),
            pltpu.VMEM((4, 8, FEAT_OWN), F32),
            dma((64,)),
            dma((64,)),
        ],
        compiler_params=pltpu.CompilerParams(
            collective_id=5, has_side_effects=True, vmem_limit_bytes=VMEM_LIMIT
        ),
        cost_estimate=pl.CostEstimate(
            flops=2_000_000_000, bytes_accessed=120_000_000, transcendentals=0
        ),
        name="section_forward",
    )(pixels, wr, wd, we, vec_mid, vec_feat, keep, tile_rows, sizes)


class Scatter:
    def __init__(self, parts, mate_in, near, near_in, far, far_in, spot, links):
        self.parts, self.mate_in, self.near, self.near_in = parts, mate_in, near, near_in
        self.far, self.far_in, self.spot, self.links = far, far_in, spot, links

    def start(self):
        spot = self.spot
        self.sent = self.links.send(self.parts.at[1 - spot.core], self.mate_in, pix=spot.mate)

    def along_z(self):
        spot, links = self.spot, self.links
        links.arrive(self.sent, self.mate_in)
        for z in range(4):
            self.near[z] = (
                self.parts[spot.core, z].astype(F32) + self.mate_in[z].astype(F32)
            ).astype(BF16)
        self.sent = {
            d: links.send(
                self.near.at[spot.z_of(d)], self.near_in.at[d - 1], pix=spot.pix_in_z(d)
            )
            for d in (2, 1, 3)
        }

    def along_x(self):
        spot, links = self.spot, self.links
        total = self.near[spot.z].astype(F32)
        for d in (1, 3, 2):
            links.arrive(self.sent[d], self.near_in.at[d - 1])
            total = total + self.near_in[d - 1].astype(F32)
        self.far[...] = total.astype(BF16)
        self.sent = {
            d: links.send(self.far.at[spot.x_of(d)], self.far_in.at[d - 1], pix=spot.pix_in_x(d))
            for d in (2, 1, 3)
        }

    def finish(self):
        spot, links = self.spot, self.links
        total = self.far[spot.group].astype(F32)
        for d in (1, 3, 2):
            links.arrive(self.sent[d], self.far_in.at[d - 1])
            total = total + self.far_in[d - 1].astype(F32)
        return total


def scatter_scratch(*shape):
    return [
        pltpu.VMEM((2, 4, 4, *shape), BF16),
        pltpu.VMEM((4, 4, *shape), BF16),
        pltpu.VMEM((4, 4, *shape), BF16),
        pltpu.VMEM((3, 4, *shape), BF16),
        pltpu.VMEM((4, *shape), BF16),
        pltpu.VMEM((3, *shape), BF16),
    ]


def spot_of(device):
    return device % 2, device % GROUP // 2, device // GROUP


def section_backward_kernel(
    trunk_grad, pixels, unit_r, unit_d, unit_e, act_r, act_d, wr_all, wd_cat, we, vec_mid, vec_feat,
    inv_mid, inv_feat, keep, pool_rows, place_rows, tile_cols, sizes, pre_pooled, pooled, projects,
    keep_group, x_group, g_group, *refs,
):
    (
        grad_pixels, mid_grads, feat_grads, grad_reduce, grad_dilate, grad_expand, grad_project,
        grad_pooled, grad_atrous, grad_point,
    ) = refs[:10]
    scratch = refs[10:]
    (
        side_out, side_in, halo, taps, full, mean_out, mean_in, project_in, project_wide, reduce_out,
        near_m, across_m, near_f, across_f, near_p, across_p, x_all, x_base, x_now, g_all, g_now,
    ) = scratch[:21]
    send_sems, recv_sems, last_sems, load_sems = scratch[-4:]
    buffers = scratch[21:-4]
    spot = Spot()
    links = Links(send_sems, recv_sems)
    i, j = spot.i, spot.j
    by_expand, by_dilate, by_project, by_reduce = [
        Scatter(*buffers[6 * n : 6 * n + 6], spot, links) for n in range(4)
    ]
    owner_i, owner_j = GROUP * j + int_div(i, 4), int_rem(i, 4)
    maker_i, maker_j = 4 * int_rem(i, GROUP) + j, spot.group
    stays = (owner_i == i) & (owner_j == j)
    barrier = pltpu.get_barrier_semaphore()

    @pl.when(jnp.logical_not(stays))
    def _():
        signal(barrier, pix=maker_i, chan=maker_j)

    peers = [{"chan": spot.chan(d)} for d in (1, 2, 3)] + spot.sum_peers()
    peers += [{"pix": spot.before}, {"pix": spot.after}]
    greet(peers, 1 - stays.astype(jnp.int32))

    atrous_sum = GroupSum(*buffers[24:27], spot, links)
    point_sum = GroupSum(*buffers[27:30], spot, links)
    loads = [
        pltpu.make_async_copy(x_group, x_all, load_sems.at[0]),
        pltpu.make_async_copy(g_group, g_all.at[REACH : REACH + GROUP_ROWS], load_sems.at[1]),
    ]
    for load in loads:
        load.start()
    edges = [
        (g_group.at[GROUP_ROWS - REACH :], g_all.at[:REACH], 1),
        (g_group.at[:REACH], g_all.at[REACH + GROUP_ROWS :], -1),
    ]
    edges = [(links.send(src, dst, pix=spot.pix_in_x(d)), dst) for src, dst, d in edges]

    def row_block(r):
        return pl.ds(pl.multiple_of(r * TILE_W, TILE_W), TILE_W)

    def take():
        for load in loads:
            load.wait()
        for n, dst in edges:
            links.arrive(n, dst)

        def one_row(r, carry):
            is_low = lax.broadcasted_iota(jnp.int32, (TILE_W, 2 * HEAD), 1) < HEAD
            for pair in range(2):
                first = x_all[2 * pair, r].astype(F32)
                second = x_all[2 * pair + 1, r].astype(F32)
                lower = jnp.where(is_low, first, pltpu.roll(second, HEAD, 1))
                upper = jnp.where(is_low, pltpu.roll(first, HEAD, 1), second)
                x_base[row_block(r), 2 * HEAD * pair : 2 * HEAD * (pair + 1)] = jnp.where(
                    spot.core == 0, lower, upper
                ).astype(BF16)
            return carry

        lax.fori_loop(0, GROUP_ROWS, one_row, 0, unroll=4)

    def pick(which):
        def one_row(r, carry):
            pieces = []
            for a in range(3):
                piece = g_all[
                    r + REACH - (a - 1) * (which + 1), :, BRANCH * which : BRANCH * (which + 1)
                ]
                pieces.append(
                    jnp.where(keep_group[3 * which + 2 - a, r] > 0, piece, jnp.zeros_like(piece))
                )
            g_now[row_block(r)] = jnp.concatenate(pieces, axis=1)
            return carry

        lax.fori_loop(0, GROUP_ROWS, one_row, 0, unroll=4)

    def multiply(which, b):
        held = x_base
        if b != 1:
            held = x_now

            def one_row(r, carry):
                row = x_base[row_block(r)].astype(F32)
                x_now[row_block(r)] = col_shift(row, (b - 1) * head_rates[which]).astype(BF16)
                return carry

            lax.fori_loop(0, GROUP_ROWS, one_row, 0, unroll=4)
        product = dot_tn(g_now[...], held[...]).T.astype(BF16)
        n = 3 * which + b
        for c in range(CHAN):
            atrous_sum.out[n, c] = product[HEAD * c : HEAD * (c + 1)]
        atrous_sum.relay()
        atrous_sum.send(n, 1 if n % 2 else -1)

    def multiply_point():
        grads = g_all[REACH : REACH + GROUP_ROWS, :, 3 * BRANCH :].reshape(-1, BRANCH)
        product = dot_tn(grads, x_base[...]).T.astype(BF16)
        for c in range(CHAN):
            point_sum.out[0, c] = product[HEAD * c : HEAD * (c + 1)]
        point_sum.send(0, 1)

    tasks = [take]
    for which in range(3):
        tasks.append(functools.partial(pick, which))
        tasks += [functools.partial(multiply, which, b) for b in range(3)]
    tasks += [multiply_point, point_sum.relay, atrous_sum.relay]
    queue = iter(tasks)

    def meanwhile(count=1):
        for _ in range(count):
            task = next(queue, None)
            if task is not None:
                task()

    project_sent = {
        d: links.send(projects.at[spot.chan(d)], project_in.at[d - 1], chan=spot.chan(d))
        for d in (2, 1, 3)
    }

    sums = jnp.zeros((8, 2 * MID_OWN), F32)
    for r in range(OWN_ROWS):
        sums = sums + place_rows[:, r : r + 1] * pool_rows[r : r + 1]
    sums = sum_over_pix(sums, near_p, across_p, spot, links, meanwhile)
    pooled_pre = (sums[:, :BRANCH] * slope(pre_pooled[...])).astype(BF16)
    grad_pooled[...] = pooled_pre.astype(F32)
    wide = jnp.concatenate([pooled_pre.astype(F32), jnp.zeros((8, BRANCH), F32)], axis=0).astype(BF16)
    for c in range(CHAN):
        mean_out[c] = dot_nn(wide, pooled[:, FEAT_OWN * c : FEAT_OWN * (c + 1)]).astype(BF16)
    sent = {
        d: links.send(mean_out.at[spot.chan(d)], mean_in.at[d - 1], chan=spot.chan(d))
        for d in (2, 1, 3)
    }
    meanwhile()
    mean = mean_out[j].astype(F32)
    for d in (1, 3, 2):
        links.arrive(sent[d], mean_in.at[d - 1])
        mean = mean + mean_in[d - 1].astype(F32)
    mean = mean[0:8] / sizes[:, 0:1]
    mean_rows = jnp.zeros((OWN_ROWS, FEAT_OWN), F32)
    for k in range(8):
        mean_rows = mean_rows + tile_cols[:, k : k + 1] * mean[k : k + 1]

    def norm_back(grad, unit, near, across, scale):
        sums = sum_over_pix(two_sums(grad, grad * unit), near, across, spot, links, meanwhile)
        pre = scale * (grad - sums[0:1] / PIXELS - unit * (sums[1:2] / PIXELS))
        return pre.astype(BF16), sums

    grad_trunk = trunk_grad[...].astype(F32) + mean_rows[:, None, :]
    grad_trunk = grad_trunk.reshape(OWN, FEAT_OWN)
    unit = unit_e[...]
    summed = unit * vec_feat[0:1] + vec_feat[1:2] + pixels[...].astype(F32)
    grad_summed = grad_trunk * slope(summed)
    g_expand, sums = norm_back(grad_summed, unit, near_f, across_f, vec_feat[0:1] * inv_feat[0:1])
    feat_grads[...] = sums

    def sides(turn, make):
        sent = {}
        for d in (2, 1, 3):
            side_out[turn, d - 1] = make(spot.chan(d)).astype(BF16)
            sent[d] = links.send(
                side_out.at[turn, d - 1], side_in.at[turn, d - 1], chan=spot.chan(d)
            )
        return sent

    def side_sum(turn, own, sent):
        for d in (1, 3, 2):
            links.arrive(sent[d], side_in.at[turn, d - 1])
            own = own + side_in[turn, d - 1].astype(F32)
        return own

    def mid_rows(chan):
        return pl.ds(pl.multiple_of(MID_OWN * chan, MID_OWN), MID_OWN)

    sent = sides(0, lambda c: dot_nt(g_expand, we[mid_rows(c)]))
    own = dot_nt(g_expand, we[mid_rows(j)])
    part = 16
    for c in range(CHAN):
        grads = dot_tn(act_d[c], g_expand).astype(BF16)
        for n in range(8):
            by_expand.parts[spot_of(8 * c + n)] = grads[part * n : part * (n + 1)]
    by_expand.start()
    meanwhile()
    grad_act = side_sum(0, own, sent)

    unit = unit_d[...]
    grad = grad_act * slope(unit * vec_mid[2:3] + vec_mid[3:4])
    g_dilate, sums_d = norm_back(
        grad, unit, near_m.at[0], across_m.at[0], vec_mid[2:3] * inv_mid[1:2]
    )
    own_rows = slice(section_rate, section_rate + OWN_ROWS)
    halo[own_rows] = g_dilate.reshape(OWN_ROWS, TILE_W, MID_OWN)
    low, high = slice(0, section_rate), slice(section_rate + OWN_ROWS, 2 * section_rate + OWN_ROWS)
    first, last = slice(section_rate, 2 * section_rate), slice(OWN_ROWS, section_rate + OWN_ROWS)
    to_before = links.send(halo.at[first], halo.at[high], pix=spot.before)
    to_after = links.send(halo.at[last], halo.at[low], pix=spot.after)
    by_expand.along_z()
    meanwhile()
    for d in (1, 3, 2):
        links.arrive(project_sent[d], project_in.at[d - 1])
        project_wide[spot.chan(-d)] = project_in[d - 1].astype(F32)
    project_wide[j] = projects[j].astype(F32)
    links.arrive(to_before, halo.at[high])
    links.arrive(to_after, halo.at[low])
    for a in range(3):
        rows = halo[section_rate * (2 - a) : section_rate * (2 - a) + OWN_ROWS]
        rows = rows.reshape(OWN, MID_OWN).astype(F32)
        if a != 1:
            rows = rows * keep[1 - a // 2]
        for b in range(3):
            moved = rows if b == 1 else col_shift(rows, -section_rate * (b - 1))
            tap = 3 * a + b
            taps[:, MID_OWN * tap : MID_OWN * (tap + 1)] = moved.astype(BF16)
    sent = sides(1, lambda c: dot_nt(taps[...], wd_cat[mid_rows(c)]))
    own = dot_nt(taps[...], wd_cat[mid_rows(j)])
    for c in range(CHAN):
        act = act_r[c, own_rows].reshape(OWN, MID_OWN)
        grads = dot_tn(act, taps[...]).astype(BF16)
        for n in range(8):
            for tap in range(9):
                by_dilate.parts[(*spot_of(8 * c + n), tap)] = grads[
                    part * n : part * (n + 1), MID_OWN * tap : MID_OWN * (tap + 1)
                ]
    by_dilate.start()
    meanwhile()
    grad_act = side_sum(1, own, sent)
    by_expand.along_x()

    unit = unit_r[...]
    grad = grad_act * slope(unit * vec_mid[0:1] + vec_mid[1:2])
    g_reduce, sums_r = norm_back(
        grad, unit, near_m.at[1], across_m.at[1], vec_mid[0:1] * inv_mid[0:1]
    )
    mid_grads[...] = jnp.concatenate([sums_r[0:2], sums_d[0:2], jnp.zeros((4, MID_OWN), F32)], axis=0)
    full[j] = g_reduce
    sent = {d: links.send(full.at[j], full.at[j], chan=spot.chan(d)) for d in (2, 1, 3)}
    by_dilate.along_z()
    for t in range(TASKS):
        for device in range(PIX):
            rows = []
            for start in range(40 * device, 40 * device + 40, 8):
                b, src, d = start // 256, start // HEAD % CHAN, start % HEAD
                rows.append(project_wide[src, BRANCH_PLACE[b], t, d : d + 8])
            rows.append(jnp.zeros((8, HEAD), F32))
            by_project.parts[(*spot_of(device), t)] = jnp.concatenate(rows, axis=0).astype(BF16)
    by_project.start()
    grad_expand[...] = by_expand.finish()
    meanwhile()
    for d in (1, 3, 2):
        links.arrive(sent[d], full.at[spot.chan(-d)])
    g_reduce = jnp.concatenate([full[c] for c in range(CHAN)], axis=1)
    weight = jnp.concatenate([wr_all[c] for c in range(CHAN)], axis=1)
    grads = dot_tn(pixels[...], g_reduce).astype(BF16)
    for c in range(CHAN):
        for n in range(8):
            by_reduce.parts[spot_of(4 * n + c)] = grads[
                HEAD * n : HEAD * (n + 1), MID_OWN * c : MID_OWN * (c + 1)
            ]
    by_reduce.start()
    grad_pixels[...] = (grad_summed + dot_nt(g_reduce, weight)).astype(BF16)
    by_project.along_z()
    meanwhile(2)
    by_reduce.along_z()
    meanwhile(2)
    by_dilate.along_x()
    by_reduce.along_x()
    by_project.along_x()
    meanwhile(len(tasks))
    reduce_out[...] = by_reduce.finish()

    def last_copies():
        return (
            lambda: remote(
                reduce_out, grad_reduce, last_sems.at[0], last_sems.at[1], pix=owner_i, chan=owner_j
            ),
            lambda: pltpu.make_async_copy(reduce_out, grad_reduce, last_sems.at[1]),
        )

    away, here = last_copies()
    pl.when(jnp.logical_not(stays))(lambda: away().start())
    pl.when(stays)(lambda: here().start())
    grad_dilate[...] = by_dilate.finish()
    grad_project[...] = by_project.finish()
    pltpu.make_async_copy(reduce_out, grad_reduce, last_sems.at[1]).wait()
    pl.when(jnp.logical_not(stays))(lambda: away().wait_send())
    atrous_sum.finish(grad_atrous)
    point_sum.finish(grad_point)
    links.finish()


def group_scratch(count, *shape):
    return [
        pltpu.VMEM((count, 4, *shape), BF16),
        pltpu.VMEM((count, *shape), BF16),
        pltpu.VMEM((count, 2, *shape), BF16),
    ]


def section_backward(*operands):
    whole = pl.BlockSpec(memory_space=pltpu.VMEM)
    shape = jax.ShapeDtypeStruct
    dma = pltpu.SemaphoreType.DMA
    mid, feat = (OWN, MID_OWN), (OWN, FEAT_OWN)
    return pl.pallas_call(
        section_backward_kernel,
        in_specs=[whole] * 22
        + [pl.BlockSpec(memory_space=pltpu.SMEM)]
        + [pl.BlockSpec(memory_space=pl.ANY)] * 2,
        out_specs=[whole] * 10,
        out_shape=[
            shape(feat, BF16),
            shape((8, MID_OWN), F32),
            shape((8, FEAT_OWN), F32),
            shape((HEAD, MID_OWN), F32),
            shape((9, 16, MID_OWN), F32),
            shape((16, FEAT_OWN), F32),
            shape((TASKS, 48, HEAD), F32),
            shape((8, BRANCH), F32),
            shape((9, HEAD, 3 * BRANCH), F32),
            shape((1, HEAD, BRANCH), F32),
        ],
        scratch_shapes=[
            pltpu.VMEM((2, 3, *mid), BF16),
            pltpu.VMEM((2, 3, *mid), BF16),
            pltpu.VMEM((OWN_ROWS + 2 * section_rate, TILE_W, MID_OWN), BF16),
            pltpu.VMEM((OWN, 9 * MID_OWN), BF16),
            pltpu.VMEM((CHAN, *mid), BF16),
            pltpu.VMEM((CHAN, 16, FEAT_OWN), BF16),
            pltpu.VMEM((3, 16, FEAT_OWN), BF16),
            pltpu.VMEM((3, 5, TASKS, HEAD, HEAD), BF16),
            pltpu.VMEM((CHAN, 5, TASKS, HEAD, HEAD), F32),
            pltpu.VMEM((HEAD, MID_OWN), F32),
            pltpu.VMEM((2, GROUP, 8, MID_OWN), F32),
            pltpu.VMEM((2, 4, 8, MID_OWN), F32),
            pltpu.VMEM((GROUP, 8, FEAT_OWN), F32),
            pltpu.VMEM((4, 8, FEAT_OWN), F32),
            pltpu.VMEM((GROUP, 8, 2 * MID_OWN), F32),
            pltpu.VMEM((4, 8, 2 * MID_OWN), F32),
            pltpu.VMEM((CHAN, GROUP_ROWS, TILE_W, 128), BF16),
            pltpu.VMEM((GROUP_ROWS * TILE_W, 256), BF16),
            pltpu.VMEM((GROUP_ROWS * TILE_W, 256), BF16),
            pltpu.VMEM((GROUP_ROWS + 2 * REACH, TILE_W, 4 * BRANCH), BF16),
            pltpu.VMEM((GROUP_ROWS * TILE_W, 3 * BRANCH), BF16),
            *scatter_scratch(16, FEAT_OWN),
            *scatter_scratch(9, 16, MID_OWN),
            *scatter_scratch(TASKS, 48, HEAD),
            *scatter_scratch(HEAD, MID_OWN),
            *group_scratch(9, HEAD, 3 * BRANCH),
            *group_scratch(1, HEAD, BRANCH),
            dma((128,)),
            dma((128,)),
            dma((2,)),
            dma((2,)),
        ],
        compiler_params=pltpu.CompilerParams(
            collective_id=6, has_side_effects=True, vmem_limit_bytes=VMEM_LIMIT
        ),
        cost_estimate=pl.CostEstimate(
            flops=16_000_000_000, bytes_accessed=250_000_000, transcendentals=0
        ),
        name="section_backward",
    )(*operands)


def shards(
    pixels,
    tile_number,
    task_draws,
    reduce_weight,
    reduce_gain,
    reduce_bias,
    dilate_weight,
    dilate_gain,
    dilate_bias,
    expand_weight,
    expand_gain,
    expand_bias,
    point_weight,
    atrous_weight,
    pooled_weight,
    project_weight,
    cotangent,
):
    pixel_count = pixels.shape[0]
    device = lax.axis_index("pix")
    first_row = device * OWN_ROWS
    tile_count = 8
    tiles = jnp.arange(tile_count)
    tile_sizes = jnp.sum((tile_number[:, None] == tiles[None, :]).astype(F32), axis=0) * TILE_W
    sizes = jnp.broadcast_to(jnp.maximum(tile_sizes, 1.0)[:, None], (tile_count, 128))
    tile_pad = jnp.pad(tile_number, (section_rate, section_rate), constant_values=-1)
    tiles_at = [
        lax.dynamic_slice_in_dim(tile_pad, first_row + section_rate * (1 + step), OWN_ROWS)
        for step in (-1, 0, 1)
    ]
    row_onehot = (tiles_at[1][:, None] == tiles[None, :]).astype(F32)
    keep_rows = jnp.stack([tiles_at[0] == tiles_at[1], tiles_at[2] == tiles_at[1]]).astype(F32)
    keep_section = jnp.broadcast_to(
        keep_rows[:, :, None, None], (2, OWN_ROWS, TILE_W, MID_OWN)
    ).reshape(2, OWN, MID_OWN)
    vec_mid = jnp.pad(
        jnp.stack([reduce_gain, reduce_bias, dilate_gain, dilate_bias]), ((0, 4), (0, 0))
    )
    vec_feat = jnp.pad(jnp.stack([expand_gain, expand_bias]), ((0, 6), (0, 0)))
    (
        trunk_out, unit_reduce, unit_dilate, unit_expand, act_reduce, act_dilate, reduce_all, inv_mid,
        inv_feat, mean_all,
    ) = section_forward(
        pixels, reduce_weight, dilate_weight, expand_weight, vec_mid, vec_feat, keep_section,
        row_onehot.T, sizes,
    )
    tile_mean = jnp.moveaxis(mean_all[:, :tile_count], 0, 1).reshape(tile_count, -1)
    group_x = device // GROUP
    placed = jnp.array(PLACED_ROWS, jnp.int32)
    place_key = tile_number[placed] + 8 * (placed % 6)
    key_pad = jnp.pad(place_key, (REACH, REACH), constant_values=-1)
    keep_all = jnp.stack(
        [
            key_pad[REACH + a * k : REACH + a * k + NROWS] == place_key
            for k in (1, 2, 3)
            for a in (-1, 0, 1)
        ]
    ).astype(jnp.int32)
    keep_own = lax.dynamic_slice_in_dim(keep_all, device * OWN_ROWS, OWN_ROWS, axis=1)
    keep_group = lax.dynamic_slice_in_dim(keep_all, group_x * GROUP_ROWS, GROUP_ROWS, axis=1)
    place_tiles = lax.dynamic_slice_in_dim(tile_number[placed], device * OWN_ROWS, OWN_ROWS)
    place_onehot = (place_tiles[:, None] == tiles[None, :]).astype(F32)
    x_ext = gather_rows(trunk_out, REACH, 1, "gather_trunk")
    pre_pooled = jnp.einsum("kc,tdc->ktd", tile_mean, pooled_weight, preferred_element_type=F32)
    pooled_act = jax.nn.silu(pre_pooled).astype(jnp.bfloat16).reshape(tile_count, BRANCH)
    pooled_rows = jnp.dot(
        place_onehot.astype(jnp.bfloat16), pooled_act, preferred_element_type=F32
    ).astype(jnp.bfloat16)
    pooled_pixels = jnp.broadcast_to(
        pooled_rows[:, None, :], (OWN_ROWS, TILE_W, BRANCH)
    ).reshape(pixel_count, BRANCH)
    task_weight = jax.nn.softmax(task_draws.astype(jnp.float32) / 3.0)
    grad_maps = (task_weight[:, None, None] * cotangent.astype(jnp.float32)).astype(jnp.bfloat16)
    maps_own = jnp.moveaxis(grad_maps, 0, 1).reshape(OWN_ROWS, TILE_W, BRANCH)
    project_cut = jnp.moveaxis(project_weight.reshape(TASKS, HEAD, 5, CHAN, HEAD), 3, 0)
    project_own = lax.all_to_all(project_cut, "chan", 0, 0, tiled=True)
    project_own = jnp.transpose(project_own, (3, 1, 4, 0, 2))[jnp.array(BRANCH_ORDER)]
    same = jnp.eye(TASKS, dtype=jnp.bfloat16)[None, :, None, None, :, None]
    spread = (project_own[:, :, :, :, None, :] * same).reshape(5, BRANCH, 256 * TASKS)
    kernels = atrous_weight.reshape(TASKS, 3, 3, 3, HEAD, -1)
    grad_pre, head_part, grad_project, pool_rows, x_group = heads_forward(
        keep_own, x_ext, maps_own, kernels, point_weight, spread, pooled_pixels
    )
    trunk_parts, g_group, task_maps = heads_input_grad(
        keep_own, grad_pre.reshape(OWN_ROWS, TILE_W, 4 * BRANCH),
        head_part.reshape(CHAN, OWN_ROWS, TILE_W, BRANCH), kernels, point_weight,
    )
    task_maps = jnp.moveaxis(task_maps.reshape(pixel_count, TASKS, HEAD), 1, 0)
    trunk_grad = return_rows(trunk_parts.reshape(CHAN, OWN_ROWS, TILE_W, -1), 4, "return_trunk")
    (
        grad_pixels, mid_grads, feat_grads, grad_reduce, grad_dilate, grad_expand, grad_project,
        grad_pooled, grad_atrous, grad_point,
    ) = section_backward(
        trunk_grad, pixels, unit_reduce, unit_dilate, unit_expand, act_reduce, act_dilate, reduce_all,
        jnp.moveaxis(dilate_weight, 0, 1).reshape(-1, 9 * MID_OWN), expand_weight, vec_mid, vec_feat,
        inv_mid, inv_feat, keep_section, pool_rows, place_onehot.T, row_onehot, sizes,
        pre_pooled.reshape(tile_count, BRANCH), pooled_weight.reshape(BRANCH, -1), grad_project,
        keep_group, x_group, g_group,
    )
    grad_atrous_weight = jnp.transpose(
        grad_atrous.reshape(3, 3, HEAD, 3, TASKS, HEAD), (4, 0, 3, 1, 2, 5)
    ).reshape(TASKS, 3, 9, HEAD, HEAD)
    grad_point_weight = jnp.transpose(grad_point.reshape(HEAD, TASKS, HEAD), (1, 0, 2))
    grad_pooled_weight = jnp.einsum(
        "kc,ktd->tcd",
        tile_mean,
        grad_pooled.reshape(tile_count, TASKS, HEAD).astype(BF16),
        preferred_element_type=F32,
    )
    return (
        task_maps,
        grad_pixels,
        grad_reduce,
        mid_grads[1],
        mid_grads[0],
        grad_dilate,
        mid_grads[3],
        mid_grads[2],
        grad_expand,
        feat_grads[1],
        feat_grads[0],
        grad_point_weight,
        grad_atrous_weight,
        grad_pooled_weight,
        grad_project[:, :40],
    )


def solution(mesh):
    placed = (
        P("pix", "chan"),
        P(),
        P(),
        P(None, "chan"),
        P("chan"),
        P("chan"),
        P(None, None, "chan"),
        P("chan"),
        P("chan"),
        P(None, "chan"),
        P("chan"),
        P("chan"),
        P(None, "chan", None),
        P(None, None, None, "chan", None),
        P(None, "chan", None),
        P(None, "chan", None),
        P(None, "pix", "chan"),
    )
    return jax.shard_map(
        shards,
        mesh=mesh,
        in_specs=placed,
        out_specs=(
            P(None, "pix", "chan"),
            P("pix", "chan"),
            P("pix", "chan"),
            P("chan"),
            P("chan"),
            P(None, "pix", "chan"),
            P("chan"),
            P("chan"),
            P("pix", "chan"),
            P("chan"),
            P("chan"),
            P(None, "pix", "chan"),
            P(None, None, None, "pix", "chan"),
            P(None, None, "chan"),
            P(None, "pix", "chan"),
        ),
        check_vma=False,
    )
```

```python
import functools

import jax
import jax.numpy as jnp
from jax import lax
from jax.experimental import pallas as pl
from jax.experimental.pallas import tpu as pltpu
from jax.sharding import PartitionSpec as P

TASKS = 3
TILE_W = 64
NROWS = 256
PIX = 32
CHAN = 4
OWN_ROWS = NROWS // PIX
REACH = 3
EXT_ROWS = OWN_ROWS + 2 * REACH
HEAD = 64
BRANCH = TASKS * HEAD
TILES = 7
BRANCH_ORDER = (1, 2, 3, 0, 4)
BRANCH_PLACE = (3, 0, 1, 2, 4)

F32 = jnp.float32
BF16 = jnp.bfloat16
MESH = pl.DeviceIdType.MESH
eps = 1e-05
section_rate = 4
head_rates = (6, 12, 18)
VMEM_LIMIT = 60 * 2**20


def place_of_row(row):
    kind = row % 6
    return 43 * kind - kind // 5 + row // 6


def row_at_place(place):
    kind = (place + place // 214) // 43
    return 6 * (place - 43 * kind + kind // 5) + kind


PLACED_ROWS = tuple(row_at_place(place) for place in range(NROWS))


def int_div(a, b):
    return lax.div(a, jnp.int32(b))


def int_rem(a, b):
    return lax.rem(a, jnp.int32(b))


def place_of(row):
    kind = int_rem(row, 6)
    return 43 * kind - int_div(kind, 5) + int_div(row, 6)


def row_of(place):
    kind = int_div(place + int_div(place, 214), 43)
    return 6 * (place - 43 * kind + int_div(kind, 5)) + kind


def signal(sem, **where):
    pl.semaphore_signal(sem, inc=1, device_id=where, device_id_type=MESH)


def remote(src, dst, send_sem, recv_sem, **where):
    return pltpu.make_async_remote_copy(
        src_ref=src,
        dst_ref=dst,
        send_sem=send_sem,
        recv_sem=recv_sem,
        device_id=where,
        device_id_type=MESH,
    )


class RowGather:
    def __init__(self, reach, src, out, spot, sems):
        self.reach, self.src, self.out, self.spot = reach, src, out, spot
        (
            self.ss_row, self.rs_row, self.ss_side, self.rs_side, self.ss_far, self.rs_far, self.ss_halo,
            self.rs_halo,
        ) = sems
        self.order = (0, 7, 1, 6, 2, 5, 3, 4)
        self.edge = [s for s in self.order if s < reach or s >= OWN_ROWS - reach]

    def greet(self):
        barrier = pltpu.get_barrier_semaphore()
        i, expected = self.spot.i, 0
        for s in range(OWN_ROWS):
            origin = int_div(row_of(OWN_ROWS * i + s), OWN_ROWS)

            @pl.when(origin != i)
            def _():
                signal(barrier, pix=origin)

            target = int_div(place_of(OWN_ROWS * i + s), OWN_ROWS)
            expected = expected + (target != i).astype(jnp.int32)
        return expected

    def row_send(self, s):
        place = place_of(OWN_ROWS * self.spot.i + s)
        target, slot = int_div(place, OWN_ROWS), int_rem(place, OWN_ROWS)
        src, landing = self.src.at[s], self.out.at[self.spot.j, self.reach + slot]
        return target, (
            lambda: remote(src, landing, self.ss_row.at[s], self.rs_row.at[slot], pix=target),
            lambda: pltpu.make_async_copy(src, landing, self.rs_row.at[slot]),
        )

    def block(self, chan, s):
        return self.out.at[chan, self.reach + s]

    def side(self, way):
        return self.spot.chan((1, -1)[way])

    def side_copy(self, way, s, chan):
        block = self.block(chan, s)
        return remote(
            block, block, self.ss_side.at[way, s], self.rs_side.at[way, s], chan=self.side(way)
        )

    def far_way(self, s):
        return 0 if s < OWN_ROWS // 2 else 1

    def far_copy(self, s, chan):
        block = self.block(chan, s)
        return remote(
            block, block, self.ss_far.at[s], self.rs_far.at[s], chan=self.side(self.far_way(s))
        )

    def halo_copy(self, turn, chan, s):
        reach = self.reach
        if s < reach:
            lane, slot, target = s, reach + OWN_ROWS + s, self.spot.before
        else:
            lane, slot, target = s - OWN_ROWS + 2 * reach, s - OWN_ROWS + reach, self.spot.after
        return remote(
            self.block(chan, s),
            self.out.at[chan, slot],
            self.ss_halo.at[turn, lane],
            self.rs_halo.at[chan, lane],
            pix=target,
        )

    def halo_arrival(self, chan, lane):
        slot = self.reach + OWN_ROWS + lane if lane < self.reach else lane - self.reach
        dst = self.out.at[chan, slot]
        return remote(
            dst, dst, self.ss_halo.at[0, lane], self.rs_halo.at[chan, lane], pix=self.spot.after
        )

    def send_rows(self):
        for s in range(OWN_ROWS):
            target, (away, here) = self.row_send(s)
            pl.when(target != self.spot.i)(lambda: away().start())
            pl.when(target == self.spot.i)(lambda: here().start())

    def pass_own(self):
        j = self.spot.j
        for s in self.order:
            pltpu.make_async_copy(self.src.at[s], self.block(j, s), self.rs_row.at[s]).wait()
            self.side_copy(0, s, j).start()
            self.side_copy(1, s, j).start()
            if s in self.edge:
                self.halo_copy(0, j, s).start()

    def pass_sides(self):
        for s in self.order:
            for way in range(2):
                chan = self.side(1 - way)
                self.side_copy(way, s, chan).wait_recv()
                if way == self.far_way(s):
                    self.far_copy(s, chan).start()
                if s in self.edge:
                    self.halo_copy(1 + way, chan, s).start()

    def finish(self):
        spot, far = self.spot, self.spot.chan(2)
        for s in self.order:
            self.far_copy(s, far).wait_recv()
            if s in self.edge:
                self.halo_copy(3, far, s).start()
        for chan in range(CHAN):
            for lane in range(2 * self.reach):
                self.halo_arrival(chan, lane).wait_recv()
        for s in range(OWN_ROWS):
            target, (away, here) = self.row_send(s)
            pl.when(target != spot.i)(lambda: away().wait_send())
            self.side_copy(0, s, spot.j).wait_send()
            self.side_copy(1, s, spot.j).wait_send()
            self.far_copy(s, self.side(1 - self.far_way(s))).wait_send()
        for turn, chan in enumerate((spot.j, self.side(1), self.side(0), far)):
            for s in self.edge:
                self.halo_copy(turn, chan, s).wait_send()


def gather_sems(reach):
    dma = pltpu.SemaphoreType.DMA
    return [
        dma((OWN_ROWS,)),
        dma((OWN_ROWS,)),
        dma((2, OWN_ROWS)),
        dma((2, OWN_ROWS)),
        dma((OWN_ROWS,)),
        dma((OWN_ROWS,)),
        dma((CHAN, 2 * reach)),
        dma((CHAN, 2 * reach)),
    ]


GROUP = 8
GROUP_ROWS = GROUP * OWN_ROWS


class Posts:
    def __init__(self, send_sems, recv_sems):
        self.send_sems, self.recv_sems, self.made = send_sems, recv_sems, []

    def copy(self, n, make):
        src, dst, where = make()
        return remote(src, dst, self.send_sems.at[n], self.recv_sems.at[n], **where)

    def post(self, make):
        n = len(self.made)
        self.made.append(make)
        self.copy(n, make).start()
        return n

    def arrive(self, n, dst):
        beside = {"chan": int_rem(lax.axis_index("chan") + 1, CHAN)}
        remote(dst, dst, self.send_sems.at[n], self.recv_sems.at[n], **beside).wait_recv()

    def finish(self):
        for n, make in enumerate(self.made):
            self.copy(n, make).wait_send()


def greet(peers, more=0):
    barrier = pltpu.get_barrier_semaphore()
    for where in peers:
        signal(barrier, **where)
    pl.semaphore_wait(barrier, len(peers) + more)


class Spot:
    def __init__(self):
        self.i, self.j = lax.axis_index("pix"), lax.axis_index("chan")
        self.group, self.k = int_div(self.i, GROUP), int_rem(self.i, GROUP)
        self.z, self.core = int_div(self.k, 2), int_rem(self.k, 2)
        self.before, self.after = int_rem(self.i + PIX - 1, PIX), int_rem(self.i + 1, PIX)
        self.mate = self.i + 1 - 2 * self.core

    def chan(self, distance):
        return int_rem(self.j + CHAN + distance, CHAN)

    def in_group(self, distance):
        return int_rem(self.k + GROUP + distance, GROUP)

    def pix_in_group(self, distance):
        return GROUP * self.group + self.in_group(distance)

    def x_of(self, distance):
        return int_rem(self.group + 4 + distance, 4)

    def pix_in_x(self, distance):
        return GROUP * self.x_of(distance) + self.k

    def z_of(self, distance):
        return int_rem(self.z + 4 + distance, 4)

    def pix_in_z(self, distance):
        return GROUP * self.group + 2 * self.z_of(distance) + self.core

    def sum_peers(self):
        return [{"pix": self.pix_in_group(d)} for d in range(1, GROUP)] + [
            {"pix": self.pix_in_x(d)} for d in range(1, 4)
        ]


def dot_nt(a, b):
    return lax.dot_general(a, b, (((1,), (1,)), ((), ())), preferred_element_type=F32)


def dot_tn(a, b):
    return lax.dot_general(a, b, (((0,), (0,)), ((), ())), preferred_element_type=F32)


def dot_nn(a, b):
    return jnp.dot(a, b, preferred_element_type=F32)


def slope(v):
    s = jax.nn.sigmoid(v)
    return s * (1.0 + v * (1.0 - s))


def silu(v):
    return v * jax.nn.sigmoid(v)


def heads_forward_kernel(
    keep, x_hbm, maps_own, kernel, point, project, pooled,
    grad_pre, head_part, grad_project, pool_rows, x_group,
    x, acc, pre, maps_in, relay, spread, sems, ss_row, rs_row, send_sems, recv_sems, own_sem,
):
    step = pl.program_id(0)
    rate, row_tap = step // 3, step % 3
    first = REACH + (row_tap - 1) * (rate + 1)
    spot = Spot()
    posts = Posts(send_sems, recv_sems)
    i, j = spot.i, spot.j
    halves = (slice(0, OWN_ROWS // 2), slice(OWN_ROWS // 2, OWN_ROWS))
    chans = (slice(0, 2), slice(2, 4))

    def x_slice(distance, which=slice(0, CHAN)):
        lanes = pl.ds(pl.multiple_of(128 * spot.z_of(distance), 128), 128)
        return x_hbm.at[which, REACH : REACH + OWN_ROWS, :, lanes]

    def x_rows(distance, core, which=slice(0, CHAN)):
        return x_group.at[which, pl.ds(OWN_ROWS * (2 * spot.z_of(distance) + core), OWN_ROWS)]

    def own_copy():
        return pltpu.make_async_copy(x_slice(0), x_rows(0, spot.core), own_sem.at[0])

    def row_send(s):
        place = place_of(OWN_ROWS * i + s)
        target, slot = int_div(place, OWN_ROWS), int_rem(place, OWN_ROWS)
        return target, (
            lambda: remote(
                maps_own.at[s], maps_in.at[j, slot], ss_row.at[s], rs_row.at[slot], pix=target
            ),
            lambda: pltpu.make_async_copy(maps_own.at[s], maps_in.at[j, slot], rs_row.at[slot]),
        )

    ways = ((1, {"chan": spot.chan(1)}), (-1, {"chan": spot.chan(-1)}))
    marks = {}

    @pl.when(step == 0)
    def _():
        width = x_hbm.shape[3]
        copies = [
            pltpu.make_async_copy(
                x_hbm.at[chan], x.at[:, :, width * chan : width * (chan + 1)], sems.at[chan]
            )
            for chan in range(CHAN)
        ]
        for copy in copies:
            copy.start()
        own_copy().start()
        barrier = pltpu.get_barrier_semaphore()
        expected = 0
        for s in range(OWN_ROWS):
            origin = int_div(row_of(OWN_ROWS * i + s), OWN_ROWS)

            @pl.when(origin != i)
            def _():
                signal(barrier, pix=origin)

            target = int_div(place_of(OWN_ROWS * i + s), OWN_ROWS)
            expected = expected + (target != i).astype(jnp.int32)
        greet(
            [where for _, where in ways]
            + [{"pix": spot.pix_in_z(d)} for d in (1, -1)]
            + [{"pix": spot.mate}],
            expected,
        )
        for s in range(OWN_ROWS):
            target, (away, here) = row_send(s)
            pl.when(target != i)(lambda: away().start())
            pl.when(target == i)(lambda: here().start())
        for way, d in enumerate((1, -1)):
            marks["relay", way] = posts.post(
                lambda way=way, d=d: (
                    x_slice(2, chans[way]), relay.at[way], {"pix": spot.pix_in_z(d)}
                )
            )
        for d in (1, -1):
            marks["z", d] = posts.post(
                lambda d=d: (x_slice(d), x_rows(0, spot.core), {"pix": spot.pix_in_z(d)})
            )
        marks["mate", 0] = posts.post(
            lambda: (x_slice(0), x_rows(0, spot.core), {"pix": spot.mate})
        )
        spread[...] = jnp.zeros_like(spread)
        for which, b in enumerate(BRANCH_ORDER):
            for c in range(CHAN):
                for t in range(TASKS):
                    start = BRANCH * c + HEAD * t
                    spread[which, start : start + HEAD, HEAD * t : HEAD * (t + 1)] = project[
                        c, b // 2, t, :, HEAD * (b % 2) : HEAD * (b % 2 + 1)
                    ]
        for copy in copies:
            copy.wait()

    @pl.when(step == 1)
    def _():
        for s in range(OWN_ROWS):
            pltpu.make_async_copy(maps_own.at[s], maps_in.at[j, s], rs_row.at[s]).wait()
        for half in range(2):
            for d, where in ways:
                marks["maps", d, half] = posts.post(
                    lambda half=half, where=where: (
                        maps_in.at[j, halves[half]], maps_in.at[j, halves[half]], where
                    )
                )

    @pl.when(step == 3)
    def _():
        for way, d in enumerate((1, -1)):
            posts.arrive(marks["relay", way], relay.at[way])
            marks["far", way] = posts.post(
                lambda way=way, d=d: (
                    relay.at[way],
                    x_rows(-d, spot.core, chans[way]),
                    {"pix": spot.pix_in_z(d)},
                )
            )

    @pl.when(step == 4)
    def _():
        for d, _ in ways:
            for half in range(2):
                source = spot.chan(-d)
                posts.arrive(marks["maps", d, half], maps_in.at[source, halves[half]])
        for half, (d, where) in enumerate(ways):
            marks["maps far", half] = posts.post(
                lambda d=d, half=half, where=where: (
                    maps_in.at[spot.chan(-d), halves[half]],
                    maps_in.at[spot.chan(-d), halves[half]],
                    where,
                )
            )

    @pl.when(step == 6)
    def _():
        for d in (1, -1):
            posts.arrive(marks["z", d], x_rows(-d, spot.core))
            marks["mate", d] = posts.post(
                lambda d=d: (x_rows(-d, spot.core), x_rows(-d, spot.core), {"pix": spot.mate})
            )

    def rows_from(start):
        return x[pl.ds(start, OWN_ROWS)].reshape(OWN_ROWS * TILE_W, -1)

    window = rows_from(first)
    for b in range(3):
        product = dot_nt(window, kernel[:, 0, 0, b].reshape(BRANCH, -1))
        for r in range(OWN_ROWS):
            part = slice(TILE_W * r, TILE_W * (r + 1))
            term = jnp.where(keep[step, r] > 0, product[part], 0.0)
            acc[b, part] = jnp.where(row_tap > 0, acc[b, part], 0.0) + term

    for which, dilation in enumerate(head_rates):

        @pl.when(step == 3 * which + 2)
        def _():
            col = lax.broadcasted_iota(jnp.int32, (OWN_ROWS * TILE_W, BRANCH), 0) % TILE_W
            total = acc[1]
            behind = pltpu.roll(acc[0], dilation, 0)
            ahead = pltpu.roll(acc[2], OWN_ROWS * TILE_W - dilation, 0)
            total = total + jnp.where(col >= dilation, behind, 0.0)
            pre[which] = total + jnp.where(col < TILE_W - dilation, ahead, 0.0)

    @pl.when(step == 0)
    def _():
        pre[3] = dot_nt(rows_from(REACH), point[...].reshape(BRANCH, -1))

    @pl.when(step == 8)
    def _():
        for half in range(2):
            posts.arrive(marks["maps far", half], maps_in.at[spot.chan(2), halves[half]])
        for way in range(2):
            posts.arrive(marks["far", way], x_rows(2, spot.core, chans[way]))
        marks["mate", 2] = posts.post(
            lambda: (x_rows(2, spot.core), x_rows(2, spot.core), {"pix": spot.mate})
        )
        cot = jnp.concatenate([maps_in[c].reshape(-1, BRANCH) for c in range(CHAN)], axis=1)
        head = None
        for which in range(5):
            if which < 4:
                before = pre[which]
                logistic = jax.nn.sigmoid(before)
                joined = (before * logistic).astype(BF16)
            else:
                joined = pooled[...]
            weight = spread[which]
            term = dot_nt(joined, weight)
            head = term if head is None else head + term
            grads = dot_tn(joined, cot)
            for t in range(TASKS):
                for c in range(CHAN):
                    lane = BRANCH * c + HEAD * t
                    grad_project[c, which, t] = grads[
                        HEAD * t : HEAD * (t + 1), lane : lane + HEAD
                    ].astype(BF16)
            back = dot_nn(cot, weight)
            if which < 4:
                grad = back * (logistic * (1.0 + before * (1.0 - logistic)))
                grad_pre[:, BRANCH * which : BRANCH * (which + 1)] = grad.astype(BF16)
            else:
                sums = jnp.sum(back.reshape(OWN_ROWS, TILE_W, BRANCH), axis=1)
                pool_rows[:, :BRANCH] = sums
                pool_rows[:, BRANCH:] = jnp.zeros((OWN_ROWS, 256 - BRANCH), F32)
        for c in range(CHAN):
            head_part[c] = head[:, BRANCH * c : BRANCH * (c + 1)].astype(BF16)
        for d in (0, 1, -1, 2):
            other = 1 - spot.core
            posts.arrive(marks["mate", d], x_rows(-d, other))
        own_copy().wait()
        for s in range(OWN_ROWS):
            target, (away, here) = row_send(s)
            pl.when(target != i)(lambda: away().wait_send())
        posts.finish()


def heads_forward(keep, x_ext, maps_own, kernels, point, project, pooled):
    pixels = OWN_ROWS * TILE_W
    feat = point.shape[2]
    whole = pl.BlockSpec(memory_space=pltpu.VMEM)
    hbm = pl.BlockSpec(memory_space=pl.ANY)
    dma = pltpu.SemaphoreType.DMA
    return pl.pallas_call(
        heads_forward_kernel,
        grid=(9,),
        in_specs=[
            pl.BlockSpec(memory_space=pltpu.SMEM),
            hbm,
            whole,
            pl.BlockSpec((TASKS, 1, 1, 3, HEAD, feat), lambda s: (0, s // 3, s % 3, 0, 0, 0)),
            whole,
            whole,
            whole,
        ],
        out_specs=[whole] * 4 + [hbm],
        out_shape=[
            jax.ShapeDtypeStruct((pixels, 4 * BRANCH), BF16),
            jax.ShapeDtypeStruct((CHAN, pixels, BRANCH), BF16),
            jax.ShapeDtypeStruct((CHAN, 5, TASKS, HEAD, HEAD), BF16),
            jax.ShapeDtypeStruct((OWN_ROWS, 256), F32),
            jax.ShapeDtypeStruct((CHAN, GROUP_ROWS, TILE_W, 128), BF16),
        ],
        scratch_shapes=[
            pltpu.VMEM((EXT_ROWS, TILE_W, feat), BF16),
            pltpu.VMEM((3, pixels, BRANCH), F32),
            pltpu.VMEM((4, pixels, BRANCH), F32),
            pltpu.VMEM((CHAN, OWN_ROWS, TILE_W, BRANCH), BF16),
            pltpu.VMEM((2, 2, OWN_ROWS, TILE_W, 128), BF16),
            pltpu.VMEM((5, 256 * TASKS, BRANCH), BF16),
            dma((CHAN,)),
            dma((OWN_ROWS,)),
            dma((OWN_ROWS,)),
            dma((16,)),
            dma((16,)),
            dma((1,)),
        ],
        compiler_params=pltpu.CompilerParams(
            collective_id=2, has_side_effects=True, vmem_limit_bytes=VMEM_LIMIT
        ),
        cost_estimate=pl.CostEstimate(
            flops=12_000_000_000, bytes_accessed=28_000_000, transcendentals=0
        ),
        name="heads_forward",
    )(keep, x_ext, maps_own, kernels, point, project, pooled)


PAD = 24
PADDED = PAD + TILE_W + PAD


def heads_input_grad_kernel(
    keep, mid, parts, kernel, point, pool_rows, place_rows, tile_cols, sizes, pre_pooled, pooled,
    trunk_grad, g_group, maps_out, mean_rows, grad_pooled,
    wide, taps, acc, edges, maps_in, maps_sum, out, out_in, out_sum, near, across, mean_out, mean_in,
    ss_row, rs_row, send_sems, recv_sems, own_sem, ss_side, rs_side, ss_back, rs_back,
):
    n, rate = pl.program_id(0), pl.program_id(1)
    step = 3 * n + rate
    spot = Spot()
    posts = Posts(send_sems, recv_sems)
    i, j = spot.i, spot.j
    low, high = edges.at[0], edges.at[1]
    half_rows = OWN_ROWS // 2
    marks = {}

    def g_rows(distance, core, half=None):
        start = OWN_ROWS * (2 * spot.z_of(distance) + core)
        if half is None:
            return g_group.at[pl.ds(start, OWN_ROWS)]
        return g_group.at[pl.ds(start + half_rows * half, half_rows)]

    def own_copy():
        return pltpu.make_async_copy(mid, g_rows(0, spot.core), own_sem.at[0])

    def row_send(s):
        row = row_of(OWN_ROWS * i + s)
        target, slot = int_div(row, OWN_ROWS), int_rem(row, OWN_ROWS)
        return target, (
            lambda: remote(
                maps_sum.at[s], maps_out.at[slot], ss_row.at[s], rs_row.at[slot], pix=target
            ),
            lambda: pltpu.make_async_copy(maps_sum.at[s], maps_out.at[slot], rs_row.at[slot]),
        )

    @pl.when(step == 0)
    def _():
        own_copy().start()
        barrier = pltpu.get_barrier_semaphore()
        expected = 0
        for s in range(OWN_ROWS):
            origin = int_div(place_of(OWN_ROWS * i + s), OWN_ROWS)

            @pl.when(origin != i)
            def _():
                signal(barrier, pix=origin)

            target = int_div(row_of(OWN_ROWS * i + s), OWN_ROWS)
            expected = expected + (target != i).astype(jnp.int32)
        greet(
            [{"chan": spot.chan(d)} for d in (1, 2, 3)]
            + [{"pix": spot.pix_in_z(d)} for d in (1, -1)]
            + spot.sum_peers()
            + [{"pix": p} for p in (spot.mate, spot.before, spot.after)],
            expected,
        )
        marks["low"] = posts.post(
            lambda: (mid.at[OWN_ROWS - REACH :], low, {"pix": spot.after})
        )
        marks["high"] = posts.post(lambda: (mid.at[:REACH], high, {"pix": spot.before}))
        for d in (2, 1, 3):
            marks["maps", d] = posts.post(
                lambda d=d: (parts.at[spot.chan(d)], maps_in.at[d - 1], {"chan": spot.chan(d)})
            )
        for half in range(2):
            for d in (1, -1):
                marks["z", d, half] = posts.post(
                    lambda half=half, d=d: (
                        mid.at[half_rows * half : half_rows * (half + 1)],
                        g_rows(0, spot.core, half),
                        {"pix": spot.pix_in_z(d)},
                    )
                )
        marks["mate", 0] = posts.post(lambda: (mid, g_rows(0, spot.core), {"pix": spot.mate}))
        sums = jnp.zeros((8, 256), F32)
        for r in range(OWN_ROWS):
            sums = sums + place_rows[:, r : r + 1] * pool_rows[r : r + 1]
        near[spot.k] = sums
        for d in range(1, GROUP):
            marks["near", d] = posts.post(
                lambda d=d: (near.at[spot.k], near.at[spot.k], {"pix": spot.pix_in_group(d)})
            )
        wide[...] = jnp.zeros_like(wide)
        posts.arrive(marks["low"], low)
        posts.arrive(marks["high"], high)
        for start, part in ((0, low), (REACH, mid), (REACH + OWN_ROWS, high)):
            held = part[...].astype(F32)
            for which in range(3):
                for t in range(TASKS):
                    lane = BRANCH * which + HEAD * t
                    one = held[:, :, lane : lane + HEAD]
                    wide[3 * t + which, start : start + held.shape[0], PAD : PAD + TILE_W] = (
                        jnp.concatenate([one, one], axis=2)
                    )

        def one_row(r, carry):
            is_low = lax.broadcasted_iota(jnp.int32, (TILE_W, 2 * HEAD), 1) < HEAD
            out_rows = pl.ds(pl.multiple_of(r * TILE_W, TILE_W), TILE_W)
            for which, dilation in enumerate(head_rates):

                def shifted(tap):
                    t, a, b = tap // 9, tap // 3 % 3 - 1, tap % 3 - 1
                    piece = wide[
                        3 * t + which,
                        r + REACH - a * (which + 1),
                        PAD - b * dilation : PAD - b * dilation + TILE_W,
                    ]
                    return jnp.where(keep[3 * which + 1 - a, r] > 0, piece, 0.0)

                for pair in range(14):
                    first = shifted(2 * pair)
                    second = shifted(2 * pair + 1) if pair < 13 else jnp.zeros_like(first)
                    taps[which, out_rows, 2 * HEAD * pair : 2 * HEAD * (pair + 1)] = jnp.where(
                        is_low, first, second
                    ).astype(BF16)
            return carry

        lax.fori_loop(0, OWN_ROWS, one_row, 0)

    @pl.when(step == 1)
    def _():
        for d in range(1, GROUP):
            posts.arrive(marks["near", d], near.at[spot.in_group(-d)])
        total = near[0]
        for k in range(1, GROUP):
            total = total + near[k]
        across[spot.group] = total
        for d in range(1, 4):
            marks["across", d] = posts.post(
                lambda d=d: (
                    across.at[spot.group], across.at[spot.group], {"pix": spot.pix_in_x(d)}
                )
            )

    @pl.when(step == 2)
    def _():
        for d in range(1, 4):
            posts.arrive(marks["across", d], across.at[spot.x_of(-d)])
        sums = across[0] + across[1] + across[2] + across[3]
        pooled_pre = (sums[:, :BRANCH] * slope(pre_pooled[...])).astype(BF16).astype(F32)
        grad_pooled[...] = pooled_pre
        tall = jnp.concatenate([pooled_pre, jnp.zeros((8, BRANCH), F32)], axis=0).astype(BF16)
        for c in range(CHAN):
            mean_out[c] = dot_nn(tall, pooled[:, 512 * c : 512 * (c + 1)]).astype(BF16)
        for d in (2, 1, 3):
            marks["mean", d] = posts.post(
                lambda d=d: (mean_out.at[spot.chan(d)], mean_in.at[d - 1], {"chan": spot.chan(d)})
            )

    @pl.when(step == 3)
    def _():
        mean = mean_out[j].astype(F32)
        for d in (1, 3, 2):
            posts.arrive(marks["mean", d], mean_in.at[d - 1])
            mean = mean + mean_in[d - 1].astype(F32)
        mean = mean[0:8] / sizes[:, 0:1]
        rows = jnp.zeros((OWN_ROWS, 512), F32)
        for k in range(8):
            rows = rows + tile_cols[:, k : k + 1] * mean[k : k + 1]
        mean_rows[...] = rows
        for d in (1, 3, 2):
            posts.arrive(marks["maps", d], maps_in.at[d - 1])
        for s in range(OWN_ROWS):
            held = parts[j, s].astype(F32)
            for d in (1, 2, 3):
                held = held + maps_in[d - 1, s].astype(F32)
            maps_sum[s] = held.astype(BF16)
            target, (away, here) = row_send(s)
            pl.when(target != i)(lambda: away().start())
            pl.when(target == i)(lambda: here().start())

    @pl.when(step == 4)
    def _():
        for half, d in enumerate((1, -1)):
            posts.arrive(marks["z", d, half], g_rows(-d, spot.core, half))
            marks["far", half] = posts.post(
                lambda half=half, d=d: (
                    g_rows(-d, spot.core, half),
                    g_rows(-d, spot.core, half),
                    {"pix": spot.pix_in_z(d)},
                )
            )
        for half, d in enumerate((-1, 1)):
            posts.arrive(marks["z", d, half], g_rows(-d, spot.core, half))
        for d in (1, -1):
            marks["mate", d] = posts.post(
                lambda d=d: (g_rows(-d, spot.core), g_rows(-d, spot.core), {"pix": spot.mate})
            )

    product = dot_nn(taps[rate, :, : 27 * HEAD], kernel[...].reshape(27 * HEAD, -1))

    @pl.when(rate == 0)
    def _():
        grads = mid[...].reshape(OWN_ROWS * TILE_W, -1)[:, 3 * BRANCH :]
        acc[...] = product + dot_nn(grads, point[...].reshape(BRANCH, -1))

    @pl.when(rate == 1)
    def _():
        acc[...] += product

    @pl.when(rate == 2)
    def _():
        total = acc[...] + product
        for c in range(2):
            chan = 2 * pair_at(n, j) + c
            out[chan] = total[:, 512 * c : 512 * (c + 1)].astype(BF16).reshape(
                OWN_ROWS, TILE_W, 512
            )

    def side_send(chan, s):
        turn = int_rem(chan + CHAN - j, CHAN) - 1
        return remote(
            out.at[chan, s], out_in.at[turn, s], ss_side.at[turn, s], rs_side.at[turn, s], chan=chan
        )

    away_pair = 2 * pair_at(0, j)
    beside = j + 1 - 2 * int_rem(j, 2)

    @pl.when(step == 2)
    def _():
        for s in range(OWN_ROWS):
            for c in range(2):
                side_send(away_pair + c, s).start()

    def back_send(s):
        row = row_of(OWN_ROWS * i + s)
        target, slot = int_div(row, OWN_ROWS), int_rem(row, OWN_ROWS)
        return target, (
            lambda: remote(
                out_sum.at[s], trunk_grad.at[slot], ss_back.at[s], rs_back.at[slot], pix=target
            ),
            lambda: pltpu.make_async_copy(out_sum.at[s], trunk_grad.at[slot], rs_back.at[slot]),
        )

    def side_arrival(turn, s):
        dst = out_in.at[turn, s]
        return remote(dst, dst, ss_side.at[turn, s], rs_side.at[turn, s], chan=beside)

    @pl.when(step == 5)
    def _():
        for s in range(OWN_ROWS):
            side_send(beside, s).start()
        for half in range(2):
            posts.arrive(marks["far", half], g_rows(2, spot.core, half))
        marks["mate", 2] = posts.post(
            lambda: (g_rows(2, spot.core), g_rows(2, spot.core), {"pix": spot.mate})
        )
        for s in range(OWN_ROWS):
            held = out[j, s].astype(F32)
            for turn in range(3):
                side_arrival(turn, s).wait_recv()
                held = held + out_in[turn, s].astype(F32)
            out_sum[s] = held.astype(BF16)
            target, (away, here) = back_send(s)
            pl.when(target != i)(lambda: away().start())
            pl.when(target == i)(lambda: here().start())
        for d in (0, 1, -1, 2):
            posts.arrive(marks["mate", d], g_rows(-d, 1 - spot.core))
        own_copy().wait()
        for s in range(OWN_ROWS):
            pltpu.make_async_copy(out_sum.at[s], trunk_grad.at[s], rs_back.at[s]).wait()
            target, (away, here) = back_send(s)
            pl.when(target != i)(lambda: away().wait_send())
            for c in range(2):
                side_send(away_pair + c, s).wait_send()
            side_send(beside, s).wait_send()
            pltpu.make_async_copy(maps_sum.at[s], maps_out.at[s], rs_row.at[s]).wait()
            target, (away, here) = row_send(s)
            pl.when(target != i)(lambda: away().wait_send())
        posts.finish()


def pair_at(n, chan):
    return int_rem(1 + n - int_div(chan, 2) + 2, 2)


def heads_input_grad(keep, grad_mid, head_part, kernels, point, *pool_operands):
    pixels = OWN_ROWS * TILE_W
    block = 1024
    whole = pl.BlockSpec(memory_space=pltpu.VMEM)
    hbm = pl.BlockSpec(memory_space=pl.ANY)
    dma = pltpu.SemaphoreType.DMA
    maps, trunk = (OWN_ROWS, TILE_W, BRANCH), (OWN_ROWS, TILE_W, 512)
    return pl.pallas_call(
        heads_input_grad_kernel,
        grid=(2, 3),
        in_specs=[
            pl.BlockSpec(memory_space=pltpu.SMEM),
            whole,
            whole,
            pl.BlockSpec((TASKS, 1, 3, 3, HEAD, block), lambda n, r: (0, r, 0, 0, 0, pair_at(n, lax.axis_index("chan")))),
            pl.BlockSpec(
                (TASKS, HEAD, block), lambda n, r: (0, 0, pair_at(n, lax.axis_index("chan")))
            ),
        ]
        + [whole] * 6,
        out_specs=[hbm, hbm, hbm, whole, whole],
        out_shape=[
            jax.ShapeDtypeStruct(trunk, BF16),
            jax.ShapeDtypeStruct((GROUP_ROWS, TILE_W, 4 * BRANCH), BF16),
            jax.ShapeDtypeStruct(maps, BF16),
            jax.ShapeDtypeStruct((OWN_ROWS, 512), F32),
            jax.ShapeDtypeStruct((8, BRANCH), F32),
        ],
        scratch_shapes=[
            pltpu.VMEM((9, EXT_ROWS, PADDED, 2 * HEAD), F32),
            pltpu.VMEM((3, pixels, 28 * HEAD), BF16),
            pltpu.VMEM((pixels, block), F32),
            pltpu.VMEM((2, REACH, TILE_W, 4 * BRANCH), BF16),
            pltpu.VMEM((CHAN - 1, *maps), BF16),
            pltpu.VMEM(maps, BF16),
            pltpu.VMEM((CHAN, *trunk), BF16),
            pltpu.VMEM((CHAN - 1, *trunk), BF16),
            pltpu.VMEM(trunk, BF16),
            pltpu.VMEM((GROUP, 8, 256), F32),
            pltpu.VMEM((4, 8, 256), F32),
            pltpu.VMEM((CHAN, 16, 512), BF16),
            pltpu.VMEM((CHAN - 1, 16, 512), BF16),
            dma((OWN_ROWS,)),
            dma((OWN_ROWS,)),
            dma((32,)),
            dma((32,)),
            dma((1,)),
            dma((CHAN - 1, OWN_ROWS)),
            dma((CHAN - 1, OWN_ROWS)),
            dma((OWN_ROWS,)),
            dma((OWN_ROWS,)),
        ],
        compiler_params=pltpu.CompilerParams(
            collective_id=3, has_side_effects=True, vmem_limit_bytes=VMEM_LIMIT
        ),
        cost_estimate=pl.CostEstimate(
            flops=12_000_000_000, bytes_accessed=28_000_000, transcendentals=0
        ),
        name="heads_input_grad",
    )(keep, grad_mid, head_part, kernels, point, *pool_operands)


class GroupSum:
    def __init__(self, out, relay_in, side_in, spot, links):
        self.out, self.relay_in, self.side_in, self.spot, self.links = out, relay_in, side_in, spot, links
        self.open, self.arrivals = [], []

    def send(self, n, way):
        spot, links, out = self.spot, self.links, self.out
        relay = links.send(out.at[n, spot.x_of(2)], self.relay_in.at[n], pix=spot.pix_in_x(way))
        side = links.send(
            out.at[n, spot.x_of(-way)], self.side_in.at[n, 0], pix=spot.pix_in_x(-way)
        )
        self.arrivals.append((side, n, 0))
        self.open.append((n, way, relay))

    def relay(self):
        for n, way, relay in self.open:
            self.links.arrive(relay, self.relay_in.at[n])
            target = self.spot.x_of(way)
            both = self.out[n, target].astype(F32) + self.relay_in[n].astype(F32)
            self.out[n, target] = both.astype(BF16)
            side = self.links.send(
                self.out.at[n, target], self.side_in.at[n, 1], pix=self.spot.pix_in_x(way)
            )
            self.arrivals.append((side, n, 1))
        self.open = []

    def finish(self, total):
        for side, n, which in self.arrivals:
            self.links.arrive(side, self.side_in.at[n, which])
        for n in range(self.out.shape[0]):
            total[n] = (
                self.out[n, self.spot.group].astype(F32)
                + self.side_in[n, 0].astype(F32)
                + self.side_in[n, 1].astype(F32)
            )


class Links:
    def __init__(self, send_sems, recv_sems):
        self.send_sems, self.recv_sems, self.count, self.sent = send_sems, recv_sems, 0, []

    def send(self, src, dst, **where):
        n = self.count
        self.count += 1
        copy = remote(src, dst, self.send_sems.at[n], self.recv_sems.at[n], **where)
        copy.start()
        self.sent.append(copy)
        return n

    def arrive(self, n, dst):
        beside = {"chan": int_rem(lax.axis_index("chan") + 1, CHAN)}
        remote(dst, dst, self.send_sems.at[n], self.recv_sems.at[n], **beside).wait_recv()

    def finish(self):
        for copy in self.sent:
            copy.wait_send()


def sum_over_pix(value, near, across, spot, links, meanwhile=lambda: None):
    near[spot.k] = value
    sent = [
        links.send(near.at[spot.k], near.at[spot.k], pix=spot.pix_in_group(d))
        for d in range(1, GROUP)
    ]
    meanwhile()
    for d, n in zip(range(1, GROUP), sent):
        links.arrive(n, near.at[spot.in_group(-d)])
    total = near[0]
    for k in range(1, GROUP):
        total = total + near[k]
    across[spot.group] = total
    sent = [
        links.send(across.at[spot.group], across.at[spot.group], pix=spot.pix_in_x(d))
        for d in range(1, 4)
    ]
    meanwhile()
    for d, n in zip(range(1, 4), sent):
        links.arrive(n, across.at[spot.x_of(-d)])
    return across[0] + across[1] + across[2] + across[3]


def two_sums(first, second):
    width = first.shape[1]
    rows = [jnp.sum(first, axis=0, keepdims=True), jnp.sum(second, axis=0, keepdims=True)]
    return jnp.concatenate(rows + [jnp.zeros((6, width), F32)], axis=0)


PIXELS = NROWS * TILE_W
OWN = OWN_ROWS * TILE_W
MID_OWN = 128
FEAT_OWN = 512
ROW_COLS = OWN_ROWS * TILE_W


def col_shift(value, distance):
    col = lax.broadcasted_iota(jnp.int32, value.shape, 0) % TILE_W
    rows = value.shape[0]
    moved = pltpu.roll(value, (rows - distance) % rows, 0)
    inside = (col < TILE_W - distance) if distance > 0 else (col >= -distance)
    return jnp.where(inside, moved, 0.0)


def section_forward_kernel(
    pixels, wr, wd, we, vec_mid, vec_feat, keep, tile_rows, sizes, project,
    x_ext, unit_r, unit_d, unit_e, act_r, act_d, wr_all, inv_mid, inv_feat, mean_all, project_all,
    trunk, project_out, part_out, part_in, near_m, across_m, near_f, across_f, near_t, across_t,
    *sems,
):
    send_sems, recv_sems, sems = sems[0], sems[1], sems[2:]
    spot = Spot()
    links = Links(send_sems, recv_sems)
    rows_out = RowGather(REACH, trunk, x_ext, spot, sems)
    j = spot.j
    expected = rows_out.greet()
    greet(
        [{"chan": spot.chan(d)} for d in (1, 2, 3)]
        + spot.sum_peers()
        + [{"pix": p} for p in (spot.before, spot.after, spot.mate)],
        expected,
    )
    half = FEAT_OWN // 2

    def half_of(chan, core):
        return pl.ds(pl.multiple_of(FEAT_OWN * chan + half * core, half), half)

    own_half = half_of(0, spot.core)
    other_half = half_of(0, 1 - spot.core)
    sent = {
        d: links.send(
            wr.at[half_of(spot.chan(d), spot.core)], wr_all.at[j, own_half], chan=spot.chan(d)
        )
        for d in (2, 1, 3)
    }
    wr_all[j] = wr[pl.ds(pl.multiple_of(FEAT_OWN * j, FEAT_OWN), FEAT_OWN)]
    pre = dot_nn(pixels[...], wr_all[j])
    for c in range(CHAN):
        for b in range(5):
            lane = HEAD * (b % 2)
            project_out[c, b // 2, :, :, lane : lane + HEAD] = project[
                :, :, 256 * b + HEAD * c : 256 * b + HEAD * (c + 1)
            ]
        project_out[c, 2, :, :, HEAD:] = jnp.zeros((TASKS, HEAD, HEAD), BF16)
    mates = {}
    for d in (1, 3, 2):
        source = spot.chan(-d)
        links.arrive(sent[d], wr_all.at[source, own_half])
        mates[d] = links.send(
            wr_all.at[source, own_half], wr_all.at[source, own_half], pix=spot.mate
        )
    back = {}
    for d in (1, 3, 2):
        source = spot.chan(-d)
        links.arrive(mates[d], wr_all.at[source, other_half])
        part_out[d - 1] = dot_nn(pixels[...], wr_all[source]).astype(BF16)
        back[d] = links.send(part_out.at[d - 1], part_in.at[d - 1], chan=source)
    for d in (1, 3, 2):
        links.arrive(back[d], part_in.at[d - 1])
        pre = pre + part_in[d - 1].astype(F32)

    project_sent = {}

    def send_project():
        for d in (2, 1, 3):
            for last, part in ((False, spot.core), (True, 2)):
                project_sent[d, last] = links.send(
                    project_out.at[spot.chan(d), part], project_all.at[j, part], chan=spot.chan(d)
                )

    def swap_project():
        for d in (1, 3, 2):
            source = spot.chan(-d)
            links.arrive(project_sent[d, False], project_all.at[source, spot.core])
            links.arrive(project_sent[d, True], project_all.at[source, 2])
            project_sent[d] = links.send(
                project_all.at[source, spot.core], project_all.at[source, spot.core], pix=spot.mate
            )

    todo = [send_project, lambda: None, swap_project]

    def meanwhile():
        if todo:
            todo.pop(0)()

    def norm(value, near, across, gain, bias):
        sums = sum_over_pix(two_sums(value, value * value), near, across, spot, links, meanwhile)
        center = sums[0:1] / PIXELS
        inv = lax.rsqrt(sums[1:2] / PIXELS - center * center + eps)
        unit = (value - center) * inv
        return unit, unit * gain + bias, inv

    unit, normed, inv_r = norm(pre, near_m.at[0], across_m.at[0], vec_mid[0:1], vec_mid[1:2])
    unit_r[...] = unit
    own = slice(section_rate, section_rate + OWN_ROWS)
    act_r[j, own] = silu(normed).astype(BF16).reshape(OWN_ROWS, TILE_W, MID_OWN)
    low, high = slice(0, section_rate), slice(section_rate + OWN_ROWS, 2 * section_rate + OWN_ROWS)
    first, last = slice(section_rate, 2 * section_rate), slice(OWN_ROWS, section_rate + OWN_ROWS)
    sent = {
        d: links.send(act_r.at[j, own], act_r.at[j, own], chan=spot.chan(d)) for d in (2, 1, 3)
    }
    arrivals = []
    for d in (0, 1, 3, 2):
        source = spot.chan(-d)
        if d:
            links.arrive(sent[d], act_r.at[source, own])
        n = links.send(act_r.at[source, first], act_r.at[source, high], pix=spot.before)
        arrivals.append((n, act_r.at[source, high]))
        n = links.send(act_r.at[source, last], act_r.at[source, low], pix=spot.after)
        arrivals.append((n, act_r.at[source, low]))
    for n, dst in arrivals:
        links.arrive(n, dst)
    pre = jnp.zeros((OWN, MID_OWN), F32)
    for a in range(3):
        rows = slice(section_rate * a, section_rate * a + OWN_ROWS)
        window = jnp.concatenate(
            [act_r[c, rows].reshape(OWN, MID_OWN) for c in range(CHAN)], axis=1
        )
        terms = [dot_nn(window, wd[3 * a + b]) for b in range(3)]
        term = terms[1] + col_shift(terms[0], -section_rate) + col_shift(terms[2], section_rate)
        pre = pre + (term if a == 1 else term * keep[a // 2])

    unit, normed, inv_d = norm(pre, near_m.at[1], across_m.at[1], vec_mid[2:3], vec_mid[3:4])
    unit_d[...] = unit
    inv_mid[...] = jnp.concatenate([inv_r, inv_d, jnp.zeros((6, MID_OWN), F32)], axis=0)
    act_d[j] = silu(normed).astype(BF16)
    sent = {d: links.send(act_d.at[j], act_d.at[j], chan=spot.chan(d)) for d in (2, 1, 3)}
    for d in (1, 3, 2):
        links.arrive(sent[d], act_d.at[spot.chan(-d)])
    full = jnp.concatenate([act_d[c] for c in range(CHAN)], axis=1)
    unit, normed, inv_e = norm(
        dot_nn(full, we[...]), near_f, across_f, vec_feat[0:1], vec_feat[1:2]
    )
    unit_e[...] = unit
    inv_feat[...] = jnp.concatenate([inv_e, jnp.zeros((7, FEAT_OWN), F32)], axis=0)
    out = silu(normed + pixels[...].astype(F32)).astype(BF16)
    trunk[...] = out.reshape(OWN_ROWS, TILE_W, FEAT_OWN)
    rows_out.send_rows()
    row_sums = jnp.sum(out.astype(F32).reshape(OWN_ROWS, TILE_W, FEAT_OWN), axis=1)
    sums = jnp.zeros((8, FEAT_OWN), F32)
    for r in range(OWN_ROWS):
        sums = sums + tile_rows[:, r : r + 1] * row_sums[r : r + 1]
    todo[:] = [rows_out.pass_own]
    sums = sum_over_pix(sums, near_t, across_t, spot, links, meanwhile)
    mean = jnp.concatenate([sums / sizes[:, 0:1], jnp.zeros((8, FEAT_OWN), F32)], axis=0)
    mean_all[j] = mean.astype(BF16)
    sent = {d: links.send(mean_all.at[j], mean_all.at[j], chan=spot.chan(d)) for d in (2, 1, 3)}
    rows_out.pass_sides()
    for d in (1, 3, 2):
        links.arrive(sent[d], mean_all.at[spot.chan(-d)])
        links.arrive(project_sent[d], project_all.at[spot.chan(-d), 1 - spot.core])
    project_all[j] = project_out[j]
    rows_out.finish()
    links.finish()


def section_forward(*operands):
    whole = pl.BlockSpec(memory_space=pltpu.VMEM)
    shape = jax.ShapeDtypeStruct
    mid, feat = (OWN, MID_OWN), (OWN, FEAT_OWN)
    dma = pltpu.SemaphoreType.DMA
    return pl.pallas_call(
        section_forward_kernel,
        in_specs=[whole] * 10,
        out_specs=[pl.BlockSpec(memory_space=pl.ANY)] + [whole] * 10,
        out_shape=[
            shape((CHAN, EXT_ROWS, TILE_W, FEAT_OWN), BF16),
            shape(mid, F32),
            shape(mid, F32),
            shape(feat, F32),
            shape((CHAN, OWN_ROWS + 2 * section_rate, TILE_W, MID_OWN), BF16),
            shape((CHAN, *mid), BF16),
            shape((CHAN, FEAT_OWN, MID_OWN), BF16),
            shape((8, MID_OWN), F32),
            shape((8, FEAT_OWN), F32),
            shape((CHAN, 16, FEAT_OWN), BF16),
            shape((CHAN, 3, TASKS, HEAD, 2 * HEAD), BF16),
        ],
        scratch_shapes=[
            pltpu.VMEM((OWN_ROWS, TILE_W, FEAT_OWN), BF16),
            pltpu.VMEM((CHAN, 3, TASKS, HEAD, 2 * HEAD), BF16),
            pltpu.VMEM((3, *mid), BF16),
            pltpu.VMEM((3, *mid), BF16),
            pltpu.VMEM((2, GROUP, 8, MID_OWN), F32),
            pltpu.VMEM((2, 4, 8, MID_OWN), F32),
            pltpu.VMEM((GROUP, 8, FEAT_OWN), F32),
            pltpu.VMEM((4, 8, FEAT_OWN), F32),
            pltpu.VMEM((GROUP, 8, FEAT_OWN), F32),
            pltpu.VMEM((4, 8, FEAT_OWN), F32),
            dma((80,)),
            dma((80,)),
            *gather_sems(REACH),
        ],
        compiler_params=pltpu.CompilerParams(
            collective_id=5, has_side_effects=True, vmem_limit_bytes=VMEM_LIMIT
        ),
        cost_estimate=pl.CostEstimate(
            flops=2_000_000_000, bytes_accessed=120_000_000, transcendentals=0
        ),
        name="section_forward",
    )(*operands)


class Scatter:
    def __init__(self, parts, mate_in, near, near_in, far, far_in, spot, links):
        self.parts, self.mate_in, self.near, self.near_in = parts, mate_in, near, near_in
        self.far, self.far_in, self.spot, self.links = far, far_in, spot, links

    def start(self):
        spot = self.spot
        self.sent = self.links.send(self.parts.at[1 - spot.core], self.mate_in, pix=spot.mate)

    def along_z(self):
        spot, links = self.spot, self.links
        links.arrive(self.sent, self.mate_in)
        for z in range(4):
            self.near[z] = (
                self.parts[spot.core, z].astype(F32) + self.mate_in[z].astype(F32)
            ).astype(BF16)
        self.sent = {
            d: links.send(
                self.near.at[spot.z_of(d)], self.near_in.at[d - 1], pix=spot.pix_in_z(d)
            )
            for d in (2, 1, 3)
        }

    def along_x(self):
        spot, links = self.spot, self.links
        total = self.near[spot.z].astype(F32)
        for d in (1, 3, 2):
            links.arrive(self.sent[d], self.near_in.at[d - 1])
            total = total + self.near_in[d - 1].astype(F32)
        self.far[...] = total.astype(BF16)
        self.sent = {
            d: links.send(self.far.at[spot.x_of(d)], self.far_in.at[d - 1], pix=spot.pix_in_x(d))
            for d in (2, 1, 3)
        }

    def finish(self):
        spot, links = self.spot, self.links
        total = self.far[spot.group].astype(F32)
        for d in (1, 3, 2):
            links.arrive(self.sent[d], self.far_in.at[d - 1])
            total = total + self.far_in[d - 1].astype(F32)
        return total


def scatter_scratch(*shape):
    return [
        pltpu.VMEM((2, 4, 4, *shape), BF16),
        pltpu.VMEM((4, 4, *shape), BF16),
        pltpu.VMEM((4, 4, *shape), BF16),
        pltpu.VMEM((3, 4, *shape), BF16),
        pltpu.VMEM((4, *shape), BF16),
        pltpu.VMEM((3, *shape), BF16),
    ]


def spot_of(device):
    return device % 2, device % GROUP // 2, device // GROUP


def section_backward_kernel(
    trunk_grad, pixels, unit_r, unit_d, unit_e, act_r, act_d, wr_all, wd_cat, we, vec_mid, vec_feat,
    inv_mid, inv_feat, keep, mean_rows, projects, keep_group, x_group, g_group, *refs,
):
    (
        grad_pixels, mid_grads, feat_grads, grad_reduce, grad_dilate, grad_expand, grad_project,
        grad_atrous, grad_point,
    ) = refs[:9]
    scratch = refs[9:]
    (
        side_out, side_in, halo, taps, full, project_in, project_wide, reduce_out,
        near_m, across_m, near_f, across_f, x_all, x_base, x_now, g_all, g_now,
    ) = scratch[:17]
    send_sems, recv_sems, last_sems, load_sems = scratch[-4:]
    buffers = scratch[17:-4]
    spot = Spot()
    links = Links(send_sems, recv_sems)
    i, j = spot.i, spot.j
    by_expand, by_dilate, by_project, by_reduce = [
        Scatter(*buffers[6 * n : 6 * n + 6], spot, links) for n in range(4)
    ]
    owner_i, owner_j = GROUP * j + int_div(i, 4), int_rem(i, 4)
    maker_i, maker_j = 4 * int_rem(i, GROUP) + j, spot.group
    stays = (owner_i == i) & (owner_j == j)
    barrier = pltpu.get_barrier_semaphore()

    @pl.when(jnp.logical_not(stays))
    def _():
        signal(barrier, pix=maker_i, chan=maker_j)

    peers = [{"chan": spot.chan(d)} for d in (1, 2, 3)] + spot.sum_peers()
    peers += [{"pix": spot.before}, {"pix": spot.after}]
    greet(peers, 1 - stays.astype(jnp.int32))

    atrous_sum = GroupSum(*buffers[24:27], spot, links)
    point_sum = GroupSum(*buffers[27:30], spot, links)
    loads = [
        pltpu.make_async_copy(x_group, x_all, load_sems.at[0]),
        pltpu.make_async_copy(g_group, g_all.at[REACH : REACH + GROUP_ROWS], load_sems.at[1]),
    ]
    for load in loads:
        load.start()
    edges = [
        (g_group.at[GROUP_ROWS - REACH :], g_all.at[:REACH], 1),
        (g_group.at[:REACH], g_all.at[REACH + GROUP_ROWS :], -1),
    ]
    edges = [(links.send(src, dst, pix=spot.pix_in_x(d)), dst) for src, dst, d in edges]

    def row_block(r):
        return pl.ds(pl.multiple_of(r * TILE_W, TILE_W), TILE_W)

    def take():
        for load in loads:
            load.wait()
        for n, dst in edges:
            links.arrive(n, dst)

        def one_row(r, carry):
            is_low = lax.broadcasted_iota(jnp.int32, (TILE_W, 2 * HEAD), 1) < HEAD
            for pair in range(2):
                first = x_all[2 * pair, r].astype(F32)
                second = x_all[2 * pair + 1, r].astype(F32)
                lower = jnp.where(is_low, first, pltpu.roll(second, HEAD, 1))
                upper = jnp.where(is_low, pltpu.roll(first, HEAD, 1), second)
                x_base[row_block(r), 2 * HEAD * pair : 2 * HEAD * (pair + 1)] = jnp.where(
                    spot.core == 0, lower, upper
                ).astype(BF16)
            return carry

        lax.fori_loop(0, GROUP_ROWS, one_row, 0, unroll=4)

    def pick(which):
        def one_row(r, carry):
            pieces = []
            for a in range(3):
                piece = g_all[
                    r + REACH - (a - 1) * (which + 1), :, BRANCH * which : BRANCH * (which + 1)
                ]
                pieces.append(
                    jnp.where(keep_group[3 * which + 2 - a, r] > 0, piece, jnp.zeros_like(piece))
                )
            g_now[row_block(r)] = jnp.concatenate(pieces, axis=1)
            return carry

        lax.fori_loop(0, GROUP_ROWS, one_row, 0, unroll=4)

    def multiply(which, b):
        held = x_base
        if b != 1:
            held = x_now

            def one_row(r, carry):
                row = x_base[row_block(r)].astype(F32)
                x_now[row_block(r)] = col_shift(row, (b - 1) * head_rates[which]).astype(BF16)
                return carry

            lax.fori_loop(0, GROUP_ROWS, one_row, 0, unroll=4)
        product = dot_tn(g_now[...], held[...]).T.astype(BF16)
        n = 3 * which + b
        for c in range(CHAN):
            atrous_sum.out[n, c] = product[HEAD * c : HEAD * (c + 1)]
        atrous_sum.relay()
        atrous_sum.send(n, 1 if n % 2 else -1)

    def multiply_point():
        grads = g_all[REACH : REACH + GROUP_ROWS, :, 3 * BRANCH :].reshape(-1, BRANCH)
        product = dot_tn(grads, x_base[...]).T.astype(BF16)
        for c in range(CHAN):
            point_sum.out[0, c] = product[HEAD * c : HEAD * (c + 1)]
        point_sum.send(0, 1)

    tasks = [take]
    for which in range(3):
        tasks.append(functools.partial(pick, which))
        tasks += [functools.partial(multiply, which, b) for b in range(3)]
    tasks += [multiply_point, point_sum.relay, atrous_sum.relay]
    queue = iter(tasks)

    def meanwhile(count=1):
        for _ in range(count):
            task = next(queue, None)
            if task is not None:
                task()

    project_sent = {
        d: links.send(projects.at[spot.chan(d)], project_in.at[d - 1], chan=spot.chan(d))
        for d in (2, 1, 3)
    }

    def norm_back(grad, unit, near, across, scale):
        sums = sum_over_pix(two_sums(grad, grad * unit), near, across, spot, links, meanwhile)
        pre = scale * (grad - sums[0:1] / PIXELS - unit * (sums[1:2] / PIXELS))
        return pre.astype(BF16), sums

    grad_trunk = trunk_grad[...].astype(F32) + mean_rows[...][:, None, :]
    grad_trunk = grad_trunk.reshape(OWN, FEAT_OWN)
    unit = unit_e[...]
    summed = unit * vec_feat[0:1] + vec_feat[1:2] + pixels[...].astype(F32)
    grad_summed = grad_trunk * slope(summed)
    g_expand, sums = norm_back(grad_summed, unit, near_f, across_f, vec_feat[0:1] * inv_feat[0:1])
    feat_grads[...] = sums

    def sides(turn, make):
        sent = {}
        for d in (2, 1, 3):
            side_out[turn, d - 1] = make(spot.chan(d)).astype(BF16)
            sent[d] = links.send(
                side_out.at[turn, d - 1], side_in.at[turn, d - 1], chan=spot.chan(d)
            )
        return sent

    def side_sum(turn, own, sent):
        for d in (1, 3, 2):
            links.arrive(sent[d], side_in.at[turn, d - 1])
            own = own + side_in[turn, d - 1].astype(F32)
        return own

    def mid_rows(chan):
        return pl.ds(pl.multiple_of(MID_OWN * chan, MID_OWN), MID_OWN)

    sent = sides(0, lambda c: dot_nt(g_expand, we[mid_rows(c)]))
    own = dot_nt(g_expand, we[mid_rows(j)])
    part = 16
    for c in range(CHAN):
        grads = dot_tn(act_d[c], g_expand).astype(BF16)
        for n in range(8):
            by_expand.parts[spot_of(8 * c + n)] = grads[part * n : part * (n + 1)]
    by_expand.start()
    meanwhile()
    grad_act = side_sum(0, own, sent)

    unit = unit_d[...]
    grad = grad_act * slope(unit * vec_mid[2:3] + vec_mid[3:4])
    g_dilate, sums_d = norm_back(
        grad, unit, near_m.at[0], across_m.at[0], vec_mid[2:3] * inv_mid[1:2]
    )
    own_rows = slice(section_rate, section_rate + OWN_ROWS)
    halo[own_rows] = g_dilate.reshape(OWN_ROWS, TILE_W, MID_OWN)
    low, high = slice(0, section_rate), slice(section_rate + OWN_ROWS, 2 * section_rate + OWN_ROWS)
    first, last = slice(section_rate, 2 * section_rate), slice(OWN_ROWS, section_rate + OWN_ROWS)
    to_before = links.send(halo.at[first], halo.at[high], pix=spot.before)
    to_after = links.send(halo.at[last], halo.at[low], pix=spot.after)
    by_expand.along_z()
    meanwhile()
    for d in (1, 3, 2):
        links.arrive(project_sent[d], project_in.at[d - 1])
        project_wide[spot.chan(-d)] = project_in[d - 1].astype(F32)
    project_wide[j] = projects[j].astype(F32)
    links.arrive(to_before, halo.at[high])
    links.arrive(to_after, halo.at[low])
    for a in range(3):
        rows = halo[section_rate * (2 - a) : section_rate * (2 - a) + OWN_ROWS]
        rows = rows.reshape(OWN, MID_OWN).astype(F32)
        if a != 1:
            rows = rows * keep[1 - a // 2]
        for b in range(3):
            moved = rows if b == 1 else col_shift(rows, -section_rate * (b - 1))
            tap = 3 * a + b
            taps[:, MID_OWN * tap : MID_OWN * (tap + 1)] = moved.astype(BF16)
    sent = sides(1, lambda c: dot_nt(taps[...], wd_cat[mid_rows(c)]))
    own = dot_nt(taps[...], wd_cat[mid_rows(j)])
    for c in range(CHAN):
        act = act_r[c, own_rows].reshape(OWN, MID_OWN)
        grads = dot_tn(act, taps[...]).astype(BF16)
        for n in range(8):
            for tap in range(9):
                by_dilate.parts[(*spot_of(8 * c + n), tap)] = grads[
                    part * n : part * (n + 1), MID_OWN * tap : MID_OWN * (tap + 1)
                ]
    by_dilate.start()
    meanwhile()
    grad_act = side_sum(1, own, sent)
    by_expand.along_x()

    unit = unit_r[...]
    grad = grad_act * slope(unit * vec_mid[0:1] + vec_mid[1:2])
    g_reduce, sums_r = norm_back(
        grad, unit, near_m.at[1], across_m.at[1], vec_mid[0:1] * inv_mid[0:1]
    )
    mid_grads[...] = jnp.concatenate([sums_r[0:2], sums_d[0:2], jnp.zeros((4, MID_OWN), F32)], axis=0)
    full[j] = g_reduce
    sent = {d: links.send(full.at[j], full.at[j], chan=spot.chan(d)) for d in (2, 1, 3)}
    by_dilate.along_z()
    for t in range(TASKS):
        for device in range(PIX):
            rows = []
            for start in range(40 * device, 40 * device + 40, 8):
                b, src, d = start // 256, start // HEAD % CHAN, start % HEAD
                rows.append(project_wide[src, BRANCH_PLACE[b], t, d : d + 8])
            rows.append(jnp.zeros((8, HEAD), F32))
            by_project.parts[(*spot_of(device), t)] = jnp.concatenate(rows, axis=0).astype(BF16)
    by_project.start()
    grad_expand[...] = by_expand.finish()
    meanwhile()
    for d in (1, 3, 2):
        links.arrive(sent[d], full.at[spot.chan(-d)])
    g_reduce = jnp.concatenate([full[c] for c in range(CHAN)], axis=1)
    weight = jnp.concatenate([wr_all[c] for c in range(CHAN)], axis=1)
    grads = dot_tn(pixels[...], g_reduce).astype(BF16)
    for c in range(CHAN):
        for n in range(8):
            by_reduce.parts[spot_of(4 * n + c)] = grads[
                HEAD * n : HEAD * (n + 1), MID_OWN * c : MID_OWN * (c + 1)
            ]
    by_reduce.start()
    grad_pixels[...] = (grad_summed + dot_nt(g_reduce, weight)).astype(BF16)
    by_project.along_z()
    meanwhile(2)
    by_reduce.along_z()
    meanwhile(2)
    by_dilate.along_x()
    by_reduce.along_x()
    by_project.along_x()
    meanwhile(len(tasks))
    reduce_out[...] = by_reduce.finish()

    def last_copies():
        return (
            lambda: remote(
                reduce_out, grad_reduce, last_sems.at[0], last_sems.at[1], pix=owner_i, chan=owner_j
            ),
            lambda: pltpu.make_async_copy(reduce_out, grad_reduce, last_sems.at[1]),
        )

    away, here = last_copies()
    pl.when(jnp.logical_not(stays))(lambda: away().start())
    pl.when(stays)(lambda: here().start())
    grad_dilate[...] = by_dilate.finish()
    grad_project[...] = by_project.finish()
    pltpu.make_async_copy(reduce_out, grad_reduce, last_sems.at[1]).wait()
    pl.when(jnp.logical_not(stays))(lambda: away().wait_send())
    atrous_sum.finish(grad_atrous)
    point_sum.finish(grad_point)
    links.finish()


def group_scratch(count, *shape):
    return [
        pltpu.VMEM((count, 4, *shape), BF16),
        pltpu.VMEM((count, *shape), BF16),
        pltpu.VMEM((count, 2, *shape), BF16),
    ]


def section_backward(*operands):
    whole = pl.BlockSpec(memory_space=pltpu.VMEM)
    shape = jax.ShapeDtypeStruct
    dma = pltpu.SemaphoreType.DMA
    mid, feat = (OWN, MID_OWN), (OWN, FEAT_OWN)
    return pl.pallas_call(
        section_backward_kernel,
        in_specs=[whole] * 17
        + [pl.BlockSpec(memory_space=pltpu.SMEM)]
        + [pl.BlockSpec(memory_space=pl.ANY)] * 2,
        out_specs=[whole] * 9,
        out_shape=[
            shape(feat, BF16),
            shape((8, MID_OWN), F32),
            shape((8, FEAT_OWN), F32),
            shape((HEAD, MID_OWN), F32),
            shape((9, 16, MID_OWN), F32),
            shape((16, FEAT_OWN), F32),
            shape((TASKS, 48, HEAD), F32),
            shape((9, HEAD, 3 * BRANCH), F32),
            shape((1, HEAD, BRANCH), F32),
        ],
        scratch_shapes=[
            pltpu.VMEM((2, 3, *mid), BF16),
            pltpu.VMEM((2, 3, *mid), BF16),
            pltpu.VMEM((OWN_ROWS + 2 * section_rate, TILE_W, MID_OWN), BF16),
            pltpu.VMEM((OWN, 9 * MID_OWN), BF16),
            pltpu.VMEM((CHAN, *mid), BF16),
            pltpu.VMEM((3, 5, TASKS, HEAD, HEAD), BF16),
            pltpu.VMEM((CHAN, 5, TASKS, HEAD, HEAD), F32),
            pltpu.VMEM((HEAD, MID_OWN), F32),
            pltpu.VMEM((2, GROUP, 8, MID_OWN), F32),
            pltpu.VMEM((2, 4, 8, MID_OWN), F32),
            pltpu.VMEM((GROUP, 8, FEAT_OWN), F32),
            pltpu.VMEM((4, 8, FEAT_OWN), F32),
            pltpu.VMEM((CHAN, GROUP_ROWS, TILE_W, 128), BF16),
            pltpu.VMEM((GROUP_ROWS * TILE_W, 256), BF16),
            pltpu.VMEM((GROUP_ROWS * TILE_W, 256), BF16),
            pltpu.VMEM((GROUP_ROWS + 2 * REACH, TILE_W, 4 * BRANCH), BF16),
            pltpu.VMEM((GROUP_ROWS * TILE_W, 3 * BRANCH), BF16),
            *scatter_scratch(16, FEAT_OWN),
            *scatter_scratch(9, 16, MID_OWN),
            *scatter_scratch(TASKS, 48, HEAD),
            *scatter_scratch(HEAD, MID_OWN),
            *group_scratch(9, HEAD, 3 * BRANCH),
            *group_scratch(1, HEAD, BRANCH),
            dma((128,)),
            dma((128,)),
            dma((2,)),
            dma((2,)),
        ],
        compiler_params=pltpu.CompilerParams(
            collective_id=6, has_side_effects=True, vmem_limit_bytes=VMEM_LIMIT
        ),
        cost_estimate=pl.CostEstimate(
            flops=16_000_000_000, bytes_accessed=250_000_000, transcendentals=0
        ),
        name="section_backward",
    )(*operands)


def shards(
    pixels,
    tile_number,
    task_draws,
    reduce_weight,
    reduce_gain,
    reduce_bias,
    dilate_weight,
    dilate_gain,
    dilate_bias,
    expand_weight,
    expand_gain,
    expand_bias,
    point_weight,
    atrous_weight,
    pooled_weight,
    project_weight,
    cotangent,
):
    pixel_count = pixels.shape[0]
    device = lax.axis_index("pix")
    first_row = device * OWN_ROWS
    tile_count = 8
    tiles = jnp.arange(tile_count)
    tile_sizes = jnp.sum((tile_number[:, None] == tiles[None, :]).astype(F32), axis=0) * TILE_W
    sizes = jnp.broadcast_to(jnp.maximum(tile_sizes, 1.0)[:, None], (tile_count, 128))
    tile_pad = jnp.pad(tile_number, (section_rate, section_rate), constant_values=-1)
    tiles_at = [
        lax.dynamic_slice_in_dim(tile_pad, first_row + section_rate * (1 + step), OWN_ROWS)
        for step in (-1, 0, 1)
    ]
    row_onehot = (tiles_at[1][:, None] == tiles[None, :]).astype(F32)
    keep_rows = jnp.stack([tiles_at[0] == tiles_at[1], tiles_at[2] == tiles_at[1]]).astype(F32)
    keep_section = jnp.broadcast_to(
        keep_rows[:, :, None, None], (2, OWN_ROWS, TILE_W, MID_OWN)
    ).reshape(2, OWN, MID_OWN)
    vec_mid = jnp.pad(
        jnp.stack([reduce_gain, reduce_bias, dilate_gain, dilate_bias]), ((0, 4), (0, 0))
    )
    vec_feat = jnp.pad(jnp.stack([expand_gain, expand_bias]), ((0, 6), (0, 0)))
    (
        x_ext, unit_reduce, unit_dilate, unit_expand, act_reduce, act_dilate, reduce_all, inv_mid,
        inv_feat, mean_all, project_all,
    ) = section_forward(
        pixels, reduce_weight, dilate_weight, expand_weight, vec_mid, vec_feat, keep_section,
        row_onehot.T, sizes, project_weight,
    )
    tile_mean = jnp.moveaxis(mean_all[:, :tile_count], 0, 1).reshape(tile_count, -1)
    group_x = device // GROUP
    placed = jnp.array(PLACED_ROWS, jnp.int32)
    place_key = tile_number[placed] + 8 * (placed % 6)
    key_pad = jnp.pad(place_key, (REACH, REACH), constant_values=-1)
    keep_all = jnp.stack(
        [
            key_pad[REACH + a * k : REACH + a * k + NROWS] == place_key
            for k in (1, 2, 3)
            for a in (-1, 0, 1)
        ]
    ).astype(jnp.int32)
    keep_own = lax.dynamic_slice_in_dim(keep_all, device * OWN_ROWS, OWN_ROWS, axis=1)
    keep_group = lax.dynamic_slice_in_dim(keep_all, group_x * GROUP_ROWS, GROUP_ROWS, axis=1)
    place_tiles = lax.dynamic_slice_in_dim(tile_number[placed], device * OWN_ROWS, OWN_ROWS)
    place_onehot = (place_tiles[:, None] == tiles[None, :]).astype(F32)
    pre_pooled = jnp.einsum("kc,tdc->ktd", tile_mean, pooled_weight, preferred_element_type=F32)
    pooled_act = jax.nn.silu(pre_pooled).astype(jnp.bfloat16).reshape(tile_count, BRANCH)
    pooled_rows = jnp.dot(
        place_onehot.astype(jnp.bfloat16), pooled_act, preferred_element_type=F32
    ).astype(jnp.bfloat16)
    pooled_pixels = jnp.broadcast_to(
        pooled_rows[:, None, :], (OWN_ROWS, TILE_W, BRANCH)
    ).reshape(pixel_count, BRANCH)
    task_weight = jax.nn.softmax(task_draws.astype(jnp.float32) / 3.0)
    grad_maps = (task_weight[:, None, None] * cotangent.astype(jnp.float32)).astype(jnp.bfloat16)
    maps_own = jnp.moveaxis(grad_maps, 0, 1).reshape(OWN_ROWS, TILE_W, BRANCH)
    kernels = atrous_weight.reshape(TASKS, 3, 3, 3, HEAD, -1)
    grad_pre, head_part, grad_project, pool_rows, x_group = heads_forward(
        keep_own, x_ext, maps_own, kernels, point_weight, project_all, pooled_pixels
    )
    trunk_grad, g_group, task_maps, mean_rows, grad_pooled = heads_input_grad(
        keep_own, grad_pre.reshape(OWN_ROWS, TILE_W, 4 * BRANCH),
        head_part.reshape(CHAN, OWN_ROWS, TILE_W, BRANCH), kernels, point_weight, pool_rows,
        place_onehot.T, row_onehot, sizes, pre_pooled.reshape(tile_count, BRANCH),
        pooled_weight.reshape(BRANCH, -1),
    )
    task_maps = jnp.moveaxis(task_maps.reshape(pixel_count, TASKS, HEAD), 1, 0)
    (
        grad_pixels, mid_grads, feat_grads, grad_reduce, grad_dilate, grad_expand, grad_project,
        grad_atrous, grad_point,
    ) = section_backward(
        trunk_grad, pixels, unit_reduce, unit_dilate, unit_expand, act_reduce, act_dilate, reduce_all,
        jnp.moveaxis(dilate_weight, 0, 1).reshape(-1, 9 * MID_OWN), expand_weight, vec_mid, vec_feat,
        inv_mid, inv_feat, keep_section, mean_rows, grad_project, keep_group, x_group, g_group,
    )
    grad_atrous_weight = jnp.transpose(
        grad_atrous.reshape(3, 3, HEAD, 3, TASKS, HEAD), (4, 0, 3, 1, 2, 5)
    ).reshape(TASKS, 3, 9, HEAD, HEAD)
    grad_point_weight = jnp.transpose(grad_point.reshape(HEAD, TASKS, HEAD), (1, 0, 2))
    grad_pooled_weight = jnp.einsum(
        "kc,ktd->tcd",
        tile_mean,
        grad_pooled.reshape(tile_count, TASKS, HEAD).astype(BF16),
        preferred_element_type=F32,
    )
    return (
        task_maps,
        grad_pixels,
        grad_reduce,
        mid_grads[1],
        mid_grads[0],
        grad_dilate,
        mid_grads[3],
        mid_grads[2],
        grad_expand,
        feat_grads[1],
        feat_grads[0],
        grad_point_weight,
        grad_atrous_weight,
        grad_pooled_weight,
        grad_project[:, :40],
    )


def solution(mesh):
    placed = (
        P("pix", "chan"),
        P(),
        P(),
        P(None, "chan"),
        P("chan"),
        P("chan"),
        P(None, None, "chan"),
        P("chan"),
        P("chan"),
        P(None, "chan"),
        P("chan"),
        P("chan"),
        P(None, "chan", None),
        P(None, None, None, "chan", None),
        P(None, "chan", None),
        P(None, "chan", None),
        P(None, "pix", "chan"),
    )
    return jax.shard_map(
        shards,
        mesh=mesh,
        in_specs=placed,
        out_specs=(
            P(None, "pix", "chan"),
            P("pix", "chan"),
            P("pix", "chan"),
            P("chan"),
            P("chan"),
            P(None, "pix", "chan"),
            P("chan"),
            P("chan"),
            P("pix", "chan"),
            P("chan"),
            P("chan"),
            P(None, "pix", "chan"),
            P(None, None, None, "pix", "chan"),
            P(None, None, "chan"),
            P(None, "pix", "chan"),
        ),
        check_vma=False,
    )
```

```python
import functools

import jax
import jax.numpy as jnp
from jax import lax
from jax.experimental import pallas as pl
from jax.experimental.pallas import tpu as pltpu
from jax.sharding import PartitionSpec as P

TASKS = 3
TILE_W = 64
NROWS = 256
PIX = 32
CHAN = 4
OWN_ROWS = NROWS // PIX
REACH = 3
EXT_ROWS = OWN_ROWS + 2 * REACH
HEAD = 64
BRANCH = TASKS * HEAD
BRANCH_ORDER = (1, 2, 3, 0, 4)
BRANCH_PLACE = (3, 0, 1, 2, 4)

F32 = jnp.float32
BF16 = jnp.bfloat16
MESH = pl.DeviceIdType.MESH
eps = 1e-05
section_rate = 4
head_rates = (6, 12, 18)
VMEM_LIMIT = 60 * 2**20


def int_div(a, b):
    if b & (b - 1) == 0:
        return lax.shift_right_logical(a, jnp.int32(b.bit_length() - 1))
    return lax.shift_right_logical(a * (2**16 // b + 1), jnp.int32(16))


def int_rem(a, b):
    return a - b * int_div(a, b)


def place_of(row):
    kind = int_rem(row, 6)
    return 43 * kind - int_div(kind, 5) + int_div(row, 6)


def row_of(place):
    kind = int_div(place + int_div(place, 214), 43)
    return 6 * (place - 43 * kind + int_div(kind, 5)) + kind


def tile_at(tiles, row):
    return jnp.where((row >= 0) & (row < NROWS), tiles[jnp.clip(row, 0, NROWS - 1)], -1)


def fill_keys(tiles, keys, first, count):
    start = row_of(jnp.maximum(first, 0))

    def one(n, carry):
        row, kind = carry
        inside = (first + n >= 0) & (first + n < NROWS)
        keys[n] = jnp.where(inside, tiles[row] + 8 * kind, -1)
        end = row + 6 >= NROWS
        next_kind = jnp.where(end, jnp.minimum(kind + 1, 5), kind)
        next_row = jnp.where(end, next_kind, row + 6)
        return jnp.where(inside, next_row, row), jnp.where(inside, next_kind, kind)

    lax.fori_loop(0, count, one, (start, int_rem(start, 6)))


def fill_keep(tiles, keep, i):
    for r in range(OWN_ROWS):
        here = tile_at(tiles, OWN_ROWS * i + r)
        for side, step in enumerate((-section_rate, section_rate)):
            same = jnp.where(tile_at(tiles, OWN_ROWS * i + r + step) == here, 1.0, 0.0)
            keep[side, TILE_W * r : TILE_W * (r + 1)] = jnp.full((TILE_W, 128), same, F32)


def rows_at(value, tile):
    row = lax.broadcasted_iota(jnp.int32, value.shape, 0)
    return jnp.sum(jnp.where(row == tile, value, 0.0), axis=0, keepdims=True)


def add_at(sums, row, tile):
    return sums + jnp.where(lax.broadcasted_iota(jnp.int32, sums.shape, 0) == tile, row, 0.0)


def tile_sizes(grid):
    sizes = jnp.zeros((8, 128), F32)
    for tile in range(8):
        here = jnp.sum(jnp.where(grid == tile, 1.0, 0.0), axis=1, keepdims=True)
        sizes = add_at(sizes, TILE_W * jnp.sum(here, axis=0, keepdims=True), tile)
    return jnp.maximum(sizes, 1.0)


def signal(sem, **where):
    pl.semaphore_signal(sem, inc=1, device_id=where, device_id_type=MESH)


def remote(src, dst, send_sem, recv_sem, **where):
    return pltpu.make_async_remote_copy(
        src_ref=src,
        dst_ref=dst,
        send_sem=send_sem,
        recv_sem=recv_sem,
        device_id=where,
        device_id_type=MESH,
    )


class RowGather:
    def __init__(self, reach, src, out, spot, sems):
        self.reach, self.src, self.out, self.spot = reach, src, out, spot
        (
            self.ss_row, self.rs_row, self.ss_side, self.rs_side, self.ss_far, self.rs_far, self.ss_halo,
            self.rs_halo,
        ) = sems
        self.order = (0, 7, 1, 6, 2, 5, 3, 4)
        self.edge = [s for s in self.order if s < reach or s >= OWN_ROWS - reach]

    def greet(self):
        barrier = pltpu.get_barrier_semaphore()
        i, expected = self.spot.i, 0
        for s in range(OWN_ROWS):
            origin = int_div(row_of(OWN_ROWS * i + s), OWN_ROWS)

            @pl.when(origin != i)
            def _():
                signal(barrier, pix=origin)

            target = int_div(place_of(OWN_ROWS * i + s), OWN_ROWS)
            expected = expected + (target != i).astype(jnp.int32)
        return expected

    def row_send(self, s):
        place = place_of(OWN_ROWS * self.spot.i + s)
        target, slot = int_div(place, OWN_ROWS), int_rem(place, OWN_ROWS)
        src, landing = self.src.at[s], self.out.at[self.spot.j, self.reach + slot]
        return target, (
            lambda: remote(src, landing, self.ss_row.at[s], self.rs_row.at[slot], pix=target),
            lambda: pltpu.make_async_copy(src, landing, self.rs_row.at[slot]),
        )

    def block(self, chan, s):
        return self.out.at[chan, self.reach + s]

    def side(self, way):
        return self.spot.chan((1, -1)[way])

    def side_copy(self, way, s, chan):
        block = self.block(chan, s)
        return remote(
            block, block, self.ss_side.at[way, s], self.rs_side.at[way, s], chan=self.side(way)
        )

    def far_way(self, s):
        return 0 if s < OWN_ROWS // 2 else 1

    def far_copy(self, s, chan):
        block = self.block(chan, s)
        return remote(
            block, block, self.ss_far.at[s], self.rs_far.at[s], chan=self.side(self.far_way(s))
        )

    def halo_copy(self, turn, chan, s):
        reach = self.reach
        if s < reach:
            lane, slot, target = s, reach + OWN_ROWS + s, self.spot.before
        else:
            lane, slot, target = s - OWN_ROWS + 2 * reach, s - OWN_ROWS + reach, self.spot.after
        return remote(
            self.block(chan, s),
            self.out.at[chan, slot],
            self.ss_halo.at[turn, lane],
            self.rs_halo.at[chan, lane],
            pix=target,
        )

    def halo_arrival(self, chan, lane):
        slot = self.reach + OWN_ROWS + lane if lane < self.reach else lane - self.reach
        dst = self.out.at[chan, slot]
        return remote(
            dst, dst, self.ss_halo.at[0, lane], self.rs_halo.at[chan, lane], pix=self.spot.after
        )

    def send_rows(self):
        for s in range(OWN_ROWS):
            target, (away, here) = self.row_send(s)
            pl.when(target != self.spot.i)(lambda: away().start())
            pl.when(target == self.spot.i)(lambda: here().start())

    def pass_own(self):
        j = self.spot.j
        for s in self.order:
            pltpu.make_async_copy(self.src.at[s], self.block(j, s), self.rs_row.at[s]).wait()
            self.side_copy(0, s, j).start()
            self.side_copy(1, s, j).start()
            if s in self.edge:
                self.halo_copy(0, j, s).start()

    def pass_sides(self):
        for s in self.order:
            for way in range(2):
                chan = self.side(1 - way)
                self.side_copy(way, s, chan).wait_recv()
                if way == self.far_way(s):
                    self.far_copy(s, chan).start()
                if s in self.edge:
                    self.halo_copy(1 + way, chan, s).start()

    def finish(self):
        spot, far = self.spot, self.spot.chan(2)
        for s in self.order:
            self.far_copy(s, far).wait_recv()
            if s in self.edge:
                self.halo_copy(3, far, s).start()
        for chan in range(CHAN):
            for lane in range(2 * self.reach):
                self.halo_arrival(chan, lane).wait_recv()
        for s in range(OWN_ROWS):
            target, (away, here) = self.row_send(s)
            pl.when(target != spot.i)(lambda: away().wait_send())
            self.side_copy(0, s, spot.j).wait_send()
            self.side_copy(1, s, spot.j).wait_send()
            self.far_copy(s, self.side(1 - self.far_way(s))).wait_send()
        for turn, chan in enumerate((spot.j, self.side(1), self.side(0), far)):
            for s in self.edge:
                self.halo_copy(turn, chan, s).wait_send()


def gather_sems(reach):
    dma = pltpu.SemaphoreType.DMA
    return [
        dma((OWN_ROWS,)),
        dma((OWN_ROWS,)),
        dma((2, OWN_ROWS)),
        dma((2, OWN_ROWS)),
        dma((OWN_ROWS,)),
        dma((OWN_ROWS,)),
        dma((CHAN, 2 * reach)),
        dma((CHAN, 2 * reach)),
    ]


GROUP = 8
GROUP_ROWS = GROUP * OWN_ROWS


class Posts:
    def __init__(self, send_sems, recv_sems):
        self.send_sems, self.recv_sems, self.made = send_sems, recv_sems, []

    def copy(self, n, make):
        src, dst, where = make()
        return remote(src, dst, self.send_sems.at[n], self.recv_sems.at[n], **where)

    def post(self, make):
        n = len(self.made)
        self.made.append(make)
        self.copy(n, make).start()
        return n

    def arrive(self, n, dst):
        beside = {"chan": int_rem(lax.axis_index("chan") + 1, CHAN)}
        remote(dst, dst, self.send_sems.at[n], self.recv_sems.at[n], **beside).wait_recv()

    def finish(self):
        for n, make in enumerate(self.made):
            self.copy(n, make).wait_send()


def greet(peers, more=0, meanwhile=lambda: None):
    barrier = pltpu.get_barrier_semaphore()
    for where in peers:
        signal(barrier, **where)
    meanwhile()
    pl.semaphore_wait(barrier, len(peers) + more)


class Spot:
    def __init__(self):
        self.i, self.j = lax.axis_index("pix"), lax.axis_index("chan")
        self.group, self.k = int_div(self.i, GROUP), int_rem(self.i, GROUP)
        self.z, self.core = int_div(self.k, 2), int_rem(self.k, 2)
        self.before, self.after = int_rem(self.i + PIX - 1, PIX), int_rem(self.i + 1, PIX)
        self.mate = self.i + 1 - 2 * self.core

    def chan(self, distance):
        return int_rem(self.j + CHAN + distance, CHAN)

    def in_group(self, distance):
        return int_rem(self.k + GROUP + distance, GROUP)

    def pix_in_group(self, distance):
        return GROUP * self.group + self.in_group(distance)

    def x_of(self, distance):
        return int_rem(self.group + 4 + distance, 4)

    def pix_in_x(self, distance):
        return GROUP * self.x_of(distance) + self.k

    def z_of(self, distance):
        return int_rem(self.z + 4 + distance, 4)

    def pix_in_z(self, distance):
        return GROUP * self.group + 2 * self.z_of(distance) + self.core

    def sum_peers(self):
        return [{"pix": self.pix_in_group(d)} for d in range(1, GROUP)] + [
            {"pix": self.pix_in_x(d)} for d in range(1, 4)
        ]


def dot_nt(a, b):
    return lax.dot_general(a, b, (((1,), (1,)), ((), ())), preferred_element_type=F32)


def dot_tn(a, b):
    return lax.dot_general(a, b, (((0,), (0,)), ((), ())), preferred_element_type=F32)


def dot_nn(a, b):
    return jnp.dot(a, b, preferred_element_type=F32)


def slope(v):
    s = jax.nn.sigmoid(v)
    return s * (1.0 + v * (1.0 - s))


def silu(v):
    return v * jax.nn.sigmoid(v)


def heads_forward_kernel(
    tiles, draws, x_hbm, cotangent, kernel, point, project, mean_all, pooled_weight,
    grad_pre, head_part, grad_project, pool_rows, x_group, pre_pooled,
    keys, maps_own, pooled, x, acc, pre, maps_in, relay, spread, sems, ss_row, rs_row, send_sems, recv_sems, own_sem,
):
    step = pl.program_id(0)
    rate, row_tap = step // 3, step % 3
    first = REACH + (row_tap - 1) * (rate + 1)
    spot = Spot()
    posts = Posts(send_sems, recv_sems)
    i, j = spot.i, spot.j
    halves = (slice(0, OWN_ROWS // 2), slice(OWN_ROWS // 2, OWN_ROWS))
    chans = (slice(0, 2), slice(2, 4))

    def x_slice(distance, which=slice(0, CHAN)):
        lanes = pl.ds(pl.multiple_of(128 * spot.z_of(distance), 128), 128)
        return x_hbm.at[which, REACH : REACH + OWN_ROWS, :, lanes]

    def x_rows(distance, core, which=slice(0, CHAN)):
        return x_group.at[which, pl.ds(OWN_ROWS * (2 * spot.z_of(distance) + core), OWN_ROWS)]

    def own_copy():
        return pltpu.make_async_copy(x_slice(0), x_rows(0, spot.core), own_sem.at[0])

    def row_send(s):
        place = place_of(OWN_ROWS * i + s)
        target, slot = int_div(place, OWN_ROWS), int_rem(place, OWN_ROWS)
        return target, (
            lambda: remote(
                maps_own.at[s], maps_in.at[j, slot], ss_row.at[s], rs_row.at[slot], pix=target
            ),
            lambda: pltpu.make_async_copy(maps_own.at[s], maps_in.at[j, slot], rs_row.at[slot]),
        )

    ways = ((1, {"chan": spot.chan(1)}), (-1, {"chan": spot.chan(-1)}))
    marks = {}

    @pl.when(step == 0)
    def _():
        width = x_hbm.shape[3]
        copies = [
            pltpu.make_async_copy(
                x_hbm.at[chan], x.at[:, :, width * chan : width * (chan + 1)], sems.at[chan]
            )
            for chan in range(CHAN)
        ]
        for copy in copies:
            copy.start()
        own_copy().start()
        barrier = pltpu.get_barrier_semaphore()
        expected = 0
        for s in range(OWN_ROWS):
            origin = int_div(row_of(OWN_ROWS * i + s), OWN_ROWS)

            @pl.when(origin != i)
            def _():
                signal(barrier, pix=origin)

            target = int_div(place_of(OWN_ROWS * i + s), OWN_ROWS)
            expected = expected + (target != i).astype(jnp.int32)

        def prepare():
            lane = lax.broadcasted_iota(jnp.int32, (8, 128), 1)
            drawn = jnp.full((8, 128), -1e30, F32)
            for t in range(TASKS):
                drawn = jnp.where(lane == t, draws[t].astype(F32) / 3.0, drawn)
            grown = jnp.where(lane < TASKS, jnp.exp(drawn - jnp.max(drawn, axis=1, keepdims=True)), 0.0)
            grown = grown / jnp.sum(grown, axis=1, keepdims=True)
            for t in range(TASKS):
                weight = jnp.sum(jnp.where(lane == t, grown, 0.0), axis=1, keepdims=True)[0:1]
                scaled = (cotangent[t].astype(F32).T * weight).astype(BF16)
                maps_own[:, :, HEAD * t : HEAD * (t + 1)] = scaled.reshape(OWN_ROWS, TILE_W, HEAD)
            fill_keys(tiles, keys, OWN_ROWS * i - REACH, EXT_ROWS)
            act = None
            for c in range(CHAN):
                term = dot_nt(mean_all[c], pooled_weight[:, 512 * c : 512 * (c + 1)])
                act = term if act is None else act + term
            pre_pooled[...] = act
            act = silu(act).astype(BF16).astype(F32)
            for r in range(OWN_ROWS):
                row = rows_at(act, tiles[row_of(OWN_ROWS * i + r)])
                pooled[TILE_W * r : TILE_W * (r + 1)] = jnp.broadcast_to(row, (TILE_W, BRANCH)).astype(
                    BF16
                )
            spread[...] = jnp.zeros_like(spread)
            for which, b in enumerate(BRANCH_ORDER):
                for c in range(CHAN):
                    for t in range(TASKS):
                        start = BRANCH * c + HEAD * t
                        spread[which, start : start + HEAD, HEAD * t : HEAD * (t + 1)] = project[
                            c, b // 2, t, :, HEAD * (b % 2) : HEAD * (b % 2 + 1)
                        ]

        greet(
            [where for _, where in ways]
            + [{"pix": spot.pix_in_z(d)} for d in (1, -1)]
            + [{"pix": spot.mate}],
            expected,
            prepare,
        )
        for s in range(OWN_ROWS):
            target, (away, here) = row_send(s)
            pl.when(target != i)(lambda: away().start())
            pl.when(target == i)(lambda: here().start())
        for way, d in enumerate((1, -1)):
            marks["relay", way] = posts.post(
                lambda way=way, d=d: (
                    x_slice(2, chans[way]), relay.at[way], {"pix": spot.pix_in_z(d)}
                )
            )
        for d in (1, -1):
            marks["z", d] = posts.post(
                lambda d=d: (x_slice(d), x_rows(0, spot.core), {"pix": spot.pix_in_z(d)})
            )
        marks["mate", 0] = posts.post(
            lambda: (x_slice(0), x_rows(0, spot.core), {"pix": spot.mate})
        )
        for copy in copies:
            copy.wait()

    @pl.when(step == 1)
    def _():
        for s in range(OWN_ROWS):
            pltpu.make_async_copy(maps_own.at[s], maps_in.at[j, s], rs_row.at[s]).wait()
        for half in range(2):
            for d, where in ways:
                marks["maps", d, half] = posts.post(
                    lambda half=half, where=where: (
                        maps_in.at[j, halves[half]], maps_in.at[j, halves[half]], where
                    )
                )

    @pl.when(step == 3)
    def _():
        for way, d in enumerate((1, -1)):
            posts.arrive(marks["relay", way], relay.at[way])
            marks["far", way] = posts.post(
                lambda way=way, d=d: (
                    relay.at[way],
                    x_rows(-d, spot.core, chans[way]),
                    {"pix": spot.pix_in_z(d)},
                )
            )

    @pl.when(step == 4)
    def _():
        for d, _ in ways:
            for half in range(2):
                source = spot.chan(-d)
                posts.arrive(marks["maps", d, half], maps_in.at[source, halves[half]])
        for half, (d, where) in enumerate(ways):
            marks["maps far", half] = posts.post(
                lambda d=d, half=half, where=where: (
                    maps_in.at[spot.chan(-d), halves[half]],
                    maps_in.at[spot.chan(-d), halves[half]],
                    where,
                )
            )

    @pl.when(step == 6)
    def _():
        for d in (1, -1):
            posts.arrive(marks["z", d], x_rows(-d, spot.core))
            marks["mate", d] = posts.post(
                lambda d=d: (x_rows(-d, spot.core), x_rows(-d, spot.core), {"pix": spot.mate})
            )

    def rows_from(start):
        return x[pl.ds(start, OWN_ROWS)].reshape(OWN_ROWS * TILE_W, -1)

    window = rows_from(first)
    for b in range(3):
        product = dot_nt(window, kernel[:, 0, 0, b].reshape(BRANCH, -1))
        for r in range(OWN_ROWS):
            part = slice(TILE_W * r, TILE_W * (r + 1))
            same = keys[REACH + r] == keys[first + r]
            term = jnp.where(same, product[part], 0.0)
            acc[b, part] = jnp.where(row_tap > 0, acc[b, part], 0.0) + term

    for which, dilation in enumerate(head_rates):

        @pl.when(step == 3 * which + 2)
        def _():
            col = lax.broadcasted_iota(jnp.int32, (OWN_ROWS * TILE_W, BRANCH), 0) % TILE_W
            total = acc[1]
            behind = pltpu.roll(acc[0], dilation, 0)
            ahead = pltpu.roll(acc[2], OWN_ROWS * TILE_W - dilation, 0)
            total = total + jnp.where(col >= dilation, behind, 0.0)
            pre[which] = total + jnp.where(col < TILE_W - dilation, ahead, 0.0)

    @pl.when(step == 0)
    def _():
        pre[3] = dot_nt(rows_from(REACH), point[...].reshape(BRANCH, -1))

    @pl.when(step == 8)
    def _():
        for half in range(2):
            posts.arrive(marks["maps far", half], maps_in.at[spot.chan(2), halves[half]])
        for way in range(2):
            posts.arrive(marks["far", way], x_rows(2, spot.core, chans[way]))
        marks["mate", 2] = posts.post(
            lambda: (x_rows(2, spot.core), x_rows(2, spot.core), {"pix": spot.mate})
        )
        cot = jnp.concatenate([maps_in[c].reshape(-1, BRANCH) for c in range(CHAN)], axis=1)
        head = None
        for which in range(5):
            if which < 4:
                before = pre[which]
                logistic = jax.nn.sigmoid(before)
                joined = (before * logistic).astype(BF16)
            else:
                joined = pooled[...]
            weight = spread[which]
            term = dot_nt(joined, weight)
            head = term if head is None else head + term
            grads = dot_tn(joined, cot)
            for t in range(TASKS):
                for c in range(CHAN):
                    lane = BRANCH * c + HEAD * t
                    grad_project[c, which, t] = grads[
                        HEAD * t : HEAD * (t + 1), lane : lane + HEAD
                    ].astype(BF16)
            back = dot_nn(cot, weight)
            if which < 4:
                grad = back * (logistic * (1.0 + before * (1.0 - logistic)))
                grad_pre[:, BRANCH * which : BRANCH * (which + 1)] = grad.astype(BF16)
            else:
                sums = jnp.sum(back.reshape(OWN_ROWS, TILE_W, BRANCH), axis=1)
                pool_rows[:, :BRANCH] = sums
                pool_rows[:, BRANCH:] = jnp.zeros((OWN_ROWS, 256 - BRANCH), F32)
        for c in range(CHAN):
            head_part[c] = head[:, BRANCH * c : BRANCH * (c + 1)].astype(BF16)
        for d in (0, 1, -1, 2):
            other = 1 - spot.core
            posts.arrive(marks["mate", d], x_rows(-d, other))
        own_copy().wait()
        for s in range(OWN_ROWS):
            target, (away, here) = row_send(s)
            pl.when(target != i)(lambda: away().wait_send())
        posts.finish()


def heads_forward(tiles, draws, x_ext, cotangent, kernels, point, project, mean_all, pooled_weight):
    pixels = OWN_ROWS * TILE_W
    feat = point.shape[2]
    whole = pl.BlockSpec(memory_space=pltpu.VMEM)
    hbm = pl.BlockSpec(memory_space=pl.ANY)
    dma = pltpu.SemaphoreType.DMA
    return pl.pallas_call(
        heads_forward_kernel,
        grid=(9,),
        in_specs=[
            pl.BlockSpec(memory_space=pltpu.SMEM),
            pl.BlockSpec(memory_space=pltpu.SMEM),
            hbm,
            whole,
            pl.BlockSpec((TASKS, 1, 1, 3, HEAD, feat), lambda s: (0, s // 3, s % 3, 0, 0, 0)),
            whole,
            whole,
            whole,
            whole,
        ],
        out_specs=[whole] * 4 + [hbm, whole],
        out_shape=[
            jax.ShapeDtypeStruct((pixels, 4 * BRANCH), BF16),
            jax.ShapeDtypeStruct((CHAN, pixels, BRANCH), BF16),
            jax.ShapeDtypeStruct((CHAN, 5, TASKS, HEAD, HEAD), BF16),
            jax.ShapeDtypeStruct((OWN_ROWS, 256), F32),
            jax.ShapeDtypeStruct((CHAN, GROUP_ROWS, TILE_W, 128), BF16),
            jax.ShapeDtypeStruct((16, BRANCH), F32),
        ],
        scratch_shapes=[
            pltpu.SMEM((EXT_ROWS,), jnp.int32),
            pltpu.VMEM((OWN_ROWS, TILE_W, BRANCH), BF16),
            pltpu.VMEM((pixels, BRANCH), BF16),
            pltpu.VMEM((EXT_ROWS, TILE_W, feat), BF16),
            pltpu.VMEM((3, pixels, BRANCH), F32),
            pltpu.VMEM((4, pixels, BRANCH), F32),
            pltpu.VMEM((CHAN, OWN_ROWS, TILE_W, BRANCH), BF16),
            pltpu.VMEM((2, 2, OWN_ROWS, TILE_W, 128), BF16),
            pltpu.VMEM((5, 256 * TASKS, BRANCH), BF16),
            dma((CHAN,)),
            dma((OWN_ROWS,)),
            dma((OWN_ROWS,)),
            dma((16,)),
            dma((16,)),
            dma((1,)),
        ],
        compiler_params=pltpu.CompilerParams(
            collective_id=2, has_side_effects=True, vmem_limit_bytes=VMEM_LIMIT
        ),
        cost_estimate=pl.CostEstimate(
            flops=12_000_000_000, bytes_accessed=28_000_000, transcendentals=0
        ),
        name="heads_forward",
    )(tiles, draws, x_ext, cotangent, kernels, point, project, mean_all, pooled_weight)


PAD = 24
PADDED = PAD + TILE_W + PAD


def heads_input_grad_kernel(
    tiles, tile_grid, mid, parts, kernel, point, pool_rows, pre_pooled, pooled,
    trunk_grad, g_group, maps_out, mean_rows, tall,
    keys, wide, taps, acc, edges, maps_in, maps_sum, out, out_in, out_sum, near, across, mean_out, mean_in,
    ss_row, rs_row, send_sems, recv_sems, own_sem, ss_side, rs_side, ss_back, rs_back,
):
    n, rate = pl.program_id(0), pl.program_id(1)
    step = 3 * n + rate
    spot = Spot()
    posts = Posts(send_sems, recv_sems)
    i, j = spot.i, spot.j
    low, high = edges.at[0], edges.at[1]
    half_rows = OWN_ROWS // 2
    marks = {}

    def g_rows(distance, core, half=None):
        start = OWN_ROWS * (2 * spot.z_of(distance) + core)
        if half is None:
            return g_group.at[pl.ds(start, OWN_ROWS)]
        return g_group.at[pl.ds(start + half_rows * half, half_rows)]

    def own_copy():
        return pltpu.make_async_copy(mid, g_rows(0, spot.core), own_sem.at[0])

    def row_send(s):
        row = row_of(OWN_ROWS * i + s)
        target, slot = int_div(row, OWN_ROWS), int_rem(row, OWN_ROWS)
        return target, (
            lambda: remote(
                maps_sum.at[s], maps_out.at[:, slot], ss_row.at[s], rs_row.at[slot], pix=target
            ),
            lambda: pltpu.make_async_copy(
                maps_sum.at[s], maps_out.at[:, slot], rs_row.at[slot]
            ),
        )

    def widen(start, part):
        held = part[...].astype(F32)
        for which in range(3):
            for t in range(TASKS):
                lane = BRANCH * which + HEAD * t
                one = held[:, :, lane : lane + HEAD]
                wide[3 * t + which, start : start + held.shape[0], PAD : PAD + TILE_W] = (
                    jnp.concatenate([one, one], axis=2)
                )

    def prepare():
        fill_keys(tiles, keys, OWN_ROWS * i - REACH, EXT_ROWS)
        wide[...] = jnp.zeros_like(wide)
        widen(REACH, mid)

    @pl.when(step == 0)
    def _():
        own_copy().start()
        barrier = pltpu.get_barrier_semaphore()
        expected = 0
        for s in range(OWN_ROWS):
            origin = int_div(place_of(OWN_ROWS * i + s), OWN_ROWS)

            @pl.when(origin != i)
            def _():
                signal(barrier, pix=origin)

            target = int_div(row_of(OWN_ROWS * i + s), OWN_ROWS)
            expected = expected + (target != i).astype(jnp.int32)
        greet(
            [{"chan": spot.chan(d)} for d in (1, 2, 3)]
            + [{"pix": spot.pix_in_z(d)} for d in (1, -1)]
            + spot.sum_peers()
            + [{"pix": p} for p in (spot.mate, spot.before, spot.after)],
            expected,
            prepare,
        )
        marks["low"] = posts.post(
            lambda: (mid.at[OWN_ROWS - REACH :], low, {"pix": spot.after})
        )
        marks["high"] = posts.post(lambda: (mid.at[:REACH], high, {"pix": spot.before}))
        for d in (2, 1, 3):
            marks["maps", d] = posts.post(
                lambda d=d: (parts.at[spot.chan(d)], maps_in.at[d - 1], {"chan": spot.chan(d)})
            )
        for turn in range(2):
            for d in (1, -1):
                half = turn if d == 1 else 1 - turn
                marks["z", d, half] = posts.post(
                    lambda half=half, d=d: (
                        mid.at[half_rows * half : half_rows * (half + 1)],
                        g_rows(0, spot.core, half),
                        {"pix": spot.pix_in_z(d)},
                    )
                )
        marks["mate", 0] = posts.post(lambda: (mid, g_rows(0, spot.core), {"pix": spot.mate}))
        sums = jnp.zeros((8, 256), F32)
        for r in range(OWN_ROWS):
            sums = add_at(sums, pool_rows[r : r + 1], tiles[row_of(OWN_ROWS * i + r)])
        near[spot.k] = sums
        for d in range(1, GROUP):
            marks["near", d] = posts.post(
                lambda d=d: (near.at[spot.k], near.at[spot.k], {"pix": spot.pix_in_group(d)})
            )
        posts.arrive(marks["low"], low)
        posts.arrive(marks["high"], high)
        widen(0, low)
        widen(REACH + OWN_ROWS, high)

        def one_row(r, carry):
            is_low = lax.broadcasted_iota(jnp.int32, (TILE_W, 2 * HEAD), 1) < HEAD
            out_rows = pl.ds(pl.multiple_of(r * TILE_W, TILE_W), TILE_W)
            for which, dilation in enumerate(head_rates):

                def shifted(tap):
                    t, a, b = tap // 9, tap // 3 % 3 - 1, tap % 3 - 1
                    piece = wide[
                        3 * t + which,
                        r + REACH - a * (which + 1),
                        PAD - b * dilation : PAD - b * dilation + TILE_W,
                    ]
                    same = keys[REACH + r] == keys[REACH + r - a * (which + 1)]
                    return jnp.where(same, piece, 0.0)

                for pair in range(14):
                    first = shifted(2 * pair)
                    second = shifted(2 * pair + 1) if pair < 13 else jnp.zeros_like(first)
                    taps[which, out_rows, 2 * HEAD * pair : 2 * HEAD * (pair + 1)] = jnp.where(
                        is_low, first, second
                    ).astype(BF16)
            return carry

        lax.fori_loop(0, OWN_ROWS, one_row, 0)

    @pl.when(step == 2)
    def _():
        for d in range(1, GROUP):
            posts.arrive(marks["near", d], near.at[spot.in_group(-d)])
        total = near[0]
        for k in range(1, GROUP):
            total = total + near[k]
        across[spot.group] = total
        for d in range(1, 4):
            marks["across", d] = posts.post(
                lambda d=d: (
                    across.at[spot.group], across.at[spot.group], {"pix": spot.pix_in_x(d)}
                )
            )

    @pl.when(step == 4)
    def _():
        for d in range(1, 4):
            posts.arrive(marks["across", d], across.at[spot.x_of(-d)])
        sums = across[0] + across[1] + across[2] + across[3]
        pooled_pre = sums[:, :BRANCH] * slope(pre_pooled[0:8])
        tall[...] = jnp.concatenate([pooled_pre, jnp.zeros((8, BRANCH), F32)], axis=0).astype(BF16)
        for c in range(CHAN):
            mean_out[c] = dot_nn(tall[...], pooled[:, 512 * c : 512 * (c + 1)]).astype(BF16)
        for d in (2, 1, 3):
            marks["mean", d] = posts.post(
                lambda d=d: (mean_out.at[spot.chan(d)], mean_in.at[d - 1], {"chan": spot.chan(d)})
            )

    @pl.when(step == 8)
    def _():
        mean = mean_out[j].astype(F32)
        for d in (1, 3, 2):
            posts.arrive(marks["mean", d], mean_in.at[d - 1])
            mean = mean + mean_in[d - 1].astype(F32)
        mean = mean[0:8] / tile_sizes(tile_grid[...])[:, 0:1]
        for r in range(OWN_ROWS):
            mean_rows[r : r + 1] = rows_at(mean, tiles[OWN_ROWS * i + r])
        for d in (1, 3, 2):
            posts.arrive(marks["maps", d], maps_in.at[d - 1])
        for s in range(OWN_ROWS):
            held = parts[j, s].astype(F32)
            for d in (1, 2, 3):
                held = held + maps_in[d - 1, s].astype(F32)
            for t in range(TASKS):
                maps_sum[s, t] = held[:, HEAD * t : HEAD * (t + 1)].astype(BF16)
            target, (away, here) = row_send(s)
            pl.when(target != i)(lambda: away().start())
            pl.when(target == i)(lambda: here().start())

    @pl.when(step == 5)
    def _():
        for half, d in enumerate((1, -1)):
            posts.arrive(marks["z", d, half], g_rows(-d, spot.core, half))
            marks["far", half] = posts.post(
                lambda half=half, d=d: (
                    g_rows(-d, spot.core, half),
                    g_rows(-d, spot.core, half),
                    {"pix": spot.pix_in_z(d)},
                )
            )

    @pl.when(step == 10)
    def _():
        for half, d in enumerate((-1, 1)):
            posts.arrive(marks["z", d, half], g_rows(-d, spot.core, half))
        for d in (1, -1):
            marks["mate", d] = posts.post(
                lambda d=d: (g_rows(-d, spot.core), g_rows(-d, spot.core), {"pix": spot.mate})
            )

    product = dot_nn(taps[rate, :, : 27 * HEAD], kernel[...].reshape(27 * HEAD, -1))

    @pl.when(rate == 0)
    def _():
        grads = mid[...].reshape(OWN_ROWS * TILE_W, -1)[:, 3 * BRANCH :]
        acc[...] = product + dot_nn(grads, point[...].reshape(BRANCH, -1))

    @pl.when(rate == 1)
    def _():
        acc[...] += product

    @pl.when(rate == 2)
    def _():
        total = acc[...] + product
        out[block_at(n, j)] = total.astype(BF16).reshape(OWN_ROWS, TILE_W, 512)

    def side_send(chan, s):
        turn = int_rem(chan + CHAN - j, CHAN) - 1
        return remote(
            out.at[chan, s], out_in.at[turn, s], ss_side.at[turn, s], rs_side.at[turn, s], chan=chan
        )

    @pl.when((rate == 2) & (n < 3))
    def _():
        for s in range(OWN_ROWS):
            side_send(block_at(n, j), s).start()

    def back_send(s):
        row = row_of(OWN_ROWS * i + s)
        target, slot = int_div(row, OWN_ROWS), int_rem(row, OWN_ROWS)
        return target, (
            lambda: remote(
                out_sum.at[s], trunk_grad.at[slot], ss_back.at[s], rs_back.at[slot], pix=target
            ),
            lambda: pltpu.make_async_copy(out_sum.at[s], trunk_grad.at[slot], rs_back.at[slot]),
        )

    def side_arrival(turn, s):
        dst = out_in.at[turn, s]
        return remote(dst, dst, ss_side.at[turn, s], rs_side.at[turn, s], chan=spot.chan(1))

    @pl.when(step == 11)
    def _():
        for s in range(OWN_ROWS):
            held = out[j, s].astype(F32)
            for turn in range(3):
                side_arrival(turn, s).wait_recv()
                held = held + out_in[turn, s].astype(F32)
            out_sum[s] = held.astype(BF16)
            target, (away, here) = back_send(s)
            pl.when(target != i)(lambda: away().start())
            pl.when(target == i)(lambda: here().start())
        for half in range(2):
            posts.arrive(marks["far", half], g_rows(2, spot.core, half))
        marks["mate", 2] = posts.post(
            lambda: (g_rows(2, spot.core), g_rows(2, spot.core), {"pix": spot.mate})
        )
        for d in (0, 1, -1, 2):
            posts.arrive(marks["mate", d], g_rows(-d, 1 - spot.core))
        own_copy().wait()
        for s in range(OWN_ROWS):
            pltpu.make_async_copy(out_sum.at[s], trunk_grad.at[s], rs_back.at[s]).wait()
            target, (away, here) = back_send(s)
            pl.when(target != i)(lambda: away().wait_send())
            for d in (1, 2, 3):
                side_send(spot.chan(d), s).wait_send()
            pltpu.make_async_copy(maps_sum.at[s], maps_out.at[:, s], rs_row.at[s]).wait()
            target, (away, here) = row_send(s)
            pl.when(target != i)(lambda: away().wait_send())
        posts.finish()


def block_at(n, chan):
    ahead = jnp.where(n == 0, 2, jnp.where(n == 1, 1, jnp.where(n == 2, 3, 0)))
    return int_rem(chan + ahead, CHAN)


def heads_input_grad(tiles, tile_grid, grad_mid, head_part, kernels, point, *pool_operands):
    pixels = OWN_ROWS * TILE_W
    block = 512
    whole = pl.BlockSpec(memory_space=pltpu.VMEM)
    hbm = pl.BlockSpec(memory_space=pl.ANY)
    dma = pltpu.SemaphoreType.DMA
    maps, trunk = (OWN_ROWS, TILE_W, BRANCH), (OWN_ROWS, TILE_W, 512)
    return pl.pallas_call(
        heads_input_grad_kernel,
        grid=(4, 3),
        in_specs=[
            pl.BlockSpec(memory_space=pltpu.SMEM),
            whole,
            whole,
            whole,
            pl.BlockSpec(
                (TASKS, 1, 3, 3, HEAD, block),
                lambda n, r: (0, r, 0, 0, 0, block_at(n, lax.axis_index("chan"))),
            ),
            pl.BlockSpec(
                (TASKS, HEAD, block), lambda n, r: (0, 0, block_at(n, lax.axis_index("chan")))
            ),
        ]
        + [whole] * 3,
        out_specs=[hbm, hbm, hbm, whole, whole],
        out_shape=[
            jax.ShapeDtypeStruct(trunk, BF16),
            jax.ShapeDtypeStruct((GROUP_ROWS, TILE_W, 4 * BRANCH), BF16),
            jax.ShapeDtypeStruct((TASKS, OWN_ROWS, TILE_W, HEAD), BF16),
            jax.ShapeDtypeStruct((OWN_ROWS, 512), F32),
            jax.ShapeDtypeStruct((16, BRANCH), BF16),
        ],
        scratch_shapes=[
            pltpu.SMEM((EXT_ROWS,), jnp.int32),
            pltpu.VMEM((9, EXT_ROWS, PADDED, 2 * HEAD), F32),
            pltpu.VMEM((3, pixels, 28 * HEAD), BF16),
            pltpu.VMEM((pixels, block), F32),
            pltpu.VMEM((2, REACH, TILE_W, 4 * BRANCH), BF16),
            pltpu.VMEM((CHAN - 1, *maps), BF16),
            pltpu.VMEM((OWN_ROWS, TASKS, TILE_W, HEAD), BF16),
            pltpu.VMEM((CHAN, *trunk), BF16),
            pltpu.VMEM((CHAN - 1, *trunk), BF16),
            pltpu.VMEM(trunk, BF16),
            pltpu.VMEM((GROUP, 8, 256), F32),
            pltpu.VMEM((4, 8, 256), F32),
            pltpu.VMEM((CHAN, 16, 512), BF16),
            pltpu.VMEM((CHAN - 1, 16, 512), BF16),
            dma((OWN_ROWS,)),
            dma((OWN_ROWS,)),
            dma((32,)),
            dma((32,)),
            dma((1,)),
            dma((CHAN - 1, OWN_ROWS)),
            dma((CHAN - 1, OWN_ROWS)),
            dma((OWN_ROWS,)),
            dma((OWN_ROWS,)),
        ],
        compiler_params=pltpu.CompilerParams(
            collective_id=3, has_side_effects=True, vmem_limit_bytes=VMEM_LIMIT
        ),
        cost_estimate=pl.CostEstimate(
            flops=12_000_000_000, bytes_accessed=28_000_000, transcendentals=0
        ),
        name="heads_input_grad",
    )(tiles, tile_grid, grad_mid, head_part, kernels, point, *pool_operands)


class GroupSum:
    def __init__(self, out, relay_in, side_in, spot, links):
        self.out, self.relay_in, self.side_in, self.spot, self.links = out, relay_in, side_in, spot, links
        self.ready, self.open, self.arrivals = [], [], []

    def flush(self):
        self.relay()
        for n, way in self.ready:
            self.send(n, way)
        self.ready = []

    def send(self, n, way):
        spot, links, out = self.spot, self.links, self.out
        relay = links.send(out.at[n, spot.x_of(2)], self.relay_in.at[n], pix=spot.pix_in_x(way))
        side = links.send(
            out.at[n, spot.x_of(-way)], self.side_in.at[n, 0], pix=spot.pix_in_x(-way)
        )
        self.arrivals.append((side, n, 0))
        self.open.append((n, way, relay))

    def relay(self):
        for n, way, relay in self.open:
            self.links.arrive(relay, self.relay_in.at[n])
            target = self.spot.x_of(way)
            both = self.out[n, target].astype(F32) + self.relay_in[n].astype(F32)
            self.out[n, target] = both.astype(BF16)
            side = self.links.send(
                self.out.at[n, target], self.side_in.at[n, 1], pix=self.spot.pix_in_x(way)
            )
            self.arrivals.append((side, n, 1))
        self.open = []

    def finish(self, place):
        for side, n, which in self.arrivals:
            self.links.arrive(side, self.side_in.at[n, which])
        for n in range(self.out.shape[0]):
            total = self.out[n, self.spot.group].astype(F32)
            place(n, total + self.side_in[n, 0].astype(F32) + self.side_in[n, 1].astype(F32))


class Links:
    def __init__(self, send_sems, recv_sems):
        self.send_sems, self.recv_sems, self.count, self.sent = send_sems, recv_sems, 0, []

    def send(self, src, dst, **where):
        n = self.count
        self.count += 1
        copy = remote(src, dst, self.send_sems.at[n], self.recv_sems.at[n], **where)
        copy.start()
        self.sent.append(copy)
        return n

    def arrive(self, n, dst):
        beside = {"chan": int_rem(lax.axis_index("chan") + 1, CHAN)}
        remote(dst, dst, self.send_sems.at[n], self.recv_sems.at[n], **beside).wait_recv()

    def finish(self):
        for copy in self.sent:
            copy.wait_send()


def sum_over_pix(value, near, across, spot, links, meanwhile=lambda: None):
    near[spot.k] = value
    sent = [
        links.send(near.at[spot.k], near.at[spot.k], pix=spot.pix_in_group(d))
        for d in range(1, GROUP)
    ]
    meanwhile()
    for d, n in zip(range(1, GROUP), sent):
        links.arrive(n, near.at[spot.in_group(-d)])
    total = near[0]
    for k in range(1, GROUP):
        total = total + near[k]
    across[spot.group] = total
    sent = [
        links.send(across.at[spot.group], across.at[spot.group], pix=spot.pix_in_x(d))
        for d in range(1, 4)
    ]
    meanwhile()
    for d, n in zip(range(1, 4), sent):
        links.arrive(n, across.at[spot.x_of(-d)])
    return across[0] + across[1] + across[2] + across[3]


def two_sums(first, second):
    width = first.shape[1]
    rows = [jnp.sum(first, axis=0, keepdims=True), jnp.sum(second, axis=0, keepdims=True)]
    return jnp.concatenate(rows + [jnp.zeros((6, width), F32)], axis=0)


PIXELS = NROWS * TILE_W
OWN = OWN_ROWS * TILE_W
MID_OWN = 128
FEAT_OWN = 512


def col_shift(value, distance):
    col = lax.broadcasted_iota(jnp.int32, value.shape, 0) % TILE_W
    rows = value.shape[0]
    moved = pltpu.roll(value, (rows - distance) % rows, 0)
    inside = (col < TILE_W - distance) if distance > 0 else (col >= -distance)
    return jnp.where(inside, moved, 0.0)


def section_forward_kernel(
    tiles, tile_grid, pixels, wr, wd, we, gain_r, bias_r, gain_d, bias_d, gain_e, bias_e, project,
    x_ext, unit_r, unit_d, unit_e, act_r, act_d, wr_all, inv_mid, inv_feat, mean_all, project_all,
    keep, trunk, project_out, part_out, part_in, near_m, across_m, near_f, across_f, near_t, across_t,
    *sems,
):
    send_sems, recv_sems, sems = sems[0], sems[1], sems[2:]
    spot = Spot()
    links = Links(send_sems, recv_sems)
    rows_out = RowGather(REACH, trunk, x_ext, spot, sems)
    j = spot.j
    expected = rows_out.greet()

    def prepare():
        fill_keep(tiles, keep, spot.i)
        for c in range(CHAN):
            for b in range(5):
                lane = HEAD * (b % 2)
                project_out[c, b // 2, :, :, lane : lane + HEAD] = project[
                    :, :, 256 * b + HEAD * c : 256 * b + HEAD * (c + 1)
                ]
            project_out[c, 2, :, :, HEAD:] = jnp.zeros((TASKS, HEAD, HEAD), BF16)

    greet(
        [{"chan": spot.chan(d)} for d in (1, 2, 3)]
        + spot.sum_peers()
        + [{"pix": p} for p in (spot.before, spot.after, spot.mate)],
        expected,
        prepare,
    )
    half = FEAT_OWN // 2

    def half_of(chan, core):
        return pl.ds(pl.multiple_of(FEAT_OWN * chan + half * core, half), half)

    own_half = half_of(0, spot.core)
    other_half = half_of(0, 1 - spot.core)
    sent = {
        d: links.send(
            wr.at[half_of(spot.chan(d), spot.core)], wr_all.at[j, own_half], chan=spot.chan(d)
        )
        for d in (2, 1, 3)
    }
    wr_all[j] = wr[pl.ds(pl.multiple_of(FEAT_OWN * j, FEAT_OWN), FEAT_OWN)]
    pre = dot_nn(pixels[...], wr_all[j])
    mates = {}
    for d in (1, 3, 2):
        source = spot.chan(-d)
        links.arrive(sent[d], wr_all.at[source, own_half])
        mates[d] = links.send(
            wr_all.at[source, own_half], wr_all.at[source, own_half], pix=spot.mate
        )
    back = {}
    for d in (1, 3, 2):
        source = spot.chan(-d)
        links.arrive(mates[d], wr_all.at[source, other_half])
        part_out[d - 1] = dot_nn(pixels[...], wr_all[source]).astype(BF16)
        back[d] = links.send(part_out.at[d - 1], part_in.at[d - 1], chan=source)
    for d in (1, 3, 2):
        links.arrive(back[d], part_in.at[d - 1])
        pre = pre + part_in[d - 1].astype(F32)

    project_sent = {}

    def send_project():
        for d in (2, 1, 3):
            for last, part in ((False, spot.core), (True, 2)):
                project_sent[d, last] = links.send(
                    project_out.at[spot.chan(d), part], project_all.at[j, part], chan=spot.chan(d)
                )

    def swap_project():
        for d in (1, 3, 2):
            source = spot.chan(-d)
            links.arrive(project_sent[d, False], project_all.at[source, spot.core])
            links.arrive(project_sent[d, True], project_all.at[source, 2])
            project_sent[d] = links.send(
                project_all.at[source, spot.core], project_all.at[source, spot.core], pix=spot.mate
            )

    todo = [send_project, lambda: None, swap_project]

    def meanwhile():
        if todo:
            todo.pop(0)()

    def norm(value, near, across, gain, bias):
        sums = sum_over_pix(two_sums(value, value * value), near, across, spot, links, meanwhile)
        center = sums[0:1] / PIXELS
        inv = lax.rsqrt(sums[1:2] / PIXELS - center * center + eps)
        unit = (value - center) * inv
        return unit, unit * gain + bias, inv

    unit, normed, inv_r = norm(pre, near_m.at[0], across_m.at[0], gain_r[...], bias_r[...])
    unit_r[...] = unit
    own = slice(section_rate, section_rate + OWN_ROWS)
    act_r[j, own] = silu(normed).astype(BF16).reshape(OWN_ROWS, TILE_W, MID_OWN)
    low, high = slice(0, section_rate), slice(section_rate + OWN_ROWS, 2 * section_rate + OWN_ROWS)
    first, last = slice(section_rate, 2 * section_rate), slice(OWN_ROWS, section_rate + OWN_ROWS)
    sent = {
        d: links.send(act_r.at[j, own], act_r.at[j, own], chan=spot.chan(d)) for d in (2, 1, 3)
    }
    arrivals = []
    for d in (0, 1, 3, 2):
        source = spot.chan(-d)
        if d:
            links.arrive(sent[d], act_r.at[source, own])
        n = links.send(act_r.at[source, first], act_r.at[source, high], pix=spot.before)
        arrivals.append((n, act_r.at[source, high]))
        n = links.send(act_r.at[source, last], act_r.at[source, low], pix=spot.after)
        arrivals.append((n, act_r.at[source, low]))
    for n, dst in arrivals:
        links.arrive(n, dst)
    pre = jnp.zeros((OWN, MID_OWN), F32)
    for a in range(3):
        rows = slice(section_rate * a, section_rate * a + OWN_ROWS)
        window = jnp.concatenate(
            [act_r[c, rows].reshape(OWN, MID_OWN) for c in range(CHAN)], axis=1
        )
        terms = [dot_nn(window, wd[3 * a + b]) for b in range(3)]
        term = terms[1] + col_shift(terms[0], -section_rate) + col_shift(terms[2], section_rate)
        pre = pre + (term if a == 1 else term * keep[a // 2])

    unit, normed, inv_d = norm(pre, near_m.at[1], across_m.at[1], gain_d[...], bias_d[...])
    unit_d[...] = unit
    inv_mid[...] = jnp.concatenate([inv_r, inv_d, jnp.zeros((6, MID_OWN), F32)], axis=0)
    act_d[j] = silu(normed).astype(BF16)
    sent = {d: links.send(act_d.at[j], act_d.at[j], chan=spot.chan(d)) for d in (2, 1, 3)}
    for d in (1, 3, 2):
        links.arrive(sent[d], act_d.at[spot.chan(-d)])
    full = jnp.concatenate([act_d[c] for c in range(CHAN)], axis=1)
    unit, normed, inv_e = norm(
        dot_nn(full, we[...]), near_f, across_f, gain_e[...], bias_e[...]
    )
    unit_e[...] = unit
    inv_feat[...] = jnp.concatenate([inv_e, jnp.zeros((7, FEAT_OWN), F32)], axis=0)
    out = silu(normed + pixels[...].astype(F32)).astype(BF16)
    trunk[...] = out.reshape(OWN_ROWS, TILE_W, FEAT_OWN)
    rows_out.send_rows()
    row_sums = jnp.sum(out.astype(F32).reshape(OWN_ROWS, TILE_W, FEAT_OWN), axis=1)
    sums = jnp.zeros((8, FEAT_OWN), F32)
    for r in range(OWN_ROWS):
        sums = add_at(sums, row_sums[r : r + 1], tile_at(tiles, OWN_ROWS * spot.i + r))
    todo[:] = [rows_out.pass_own]
    sums = sum_over_pix(sums, near_t, across_t, spot, links, meanwhile)
    mean = jnp.concatenate([sums / tile_sizes(tile_grid[...])[:, 0:1], jnp.zeros((8, FEAT_OWN), F32)], axis=0)
    mean_all[j] = mean.astype(BF16)
    sent = {d: links.send(mean_all.at[j], mean_all.at[j], chan=spot.chan(d)) for d in (2, 1, 3)}
    rows_out.pass_sides()
    for d in (1, 3, 2):
        links.arrive(sent[d], mean_all.at[spot.chan(-d)])
        links.arrive(project_sent[d], project_all.at[spot.chan(-d), 1 - spot.core])
    project_all[j] = project_out[j]
    rows_out.finish()
    links.finish()


def section_forward(*operands):
    whole = pl.BlockSpec(memory_space=pltpu.VMEM)
    shape = jax.ShapeDtypeStruct
    mid, feat = (OWN, MID_OWN), (OWN, FEAT_OWN)
    dma = pltpu.SemaphoreType.DMA
    return pl.pallas_call(
        section_forward_kernel,
        in_specs=[pl.BlockSpec(memory_space=pltpu.SMEM)] + [whole] * 12,
        out_specs=[pl.BlockSpec(memory_space=pl.ANY)] + [whole] * 10,
        out_shape=[
            shape((CHAN, EXT_ROWS, TILE_W, FEAT_OWN), BF16),
            shape(mid, F32),
            shape(mid, F32),
            shape(feat, F32),
            shape((CHAN, OWN_ROWS + 2 * section_rate, TILE_W, MID_OWN), BF16),
            shape((CHAN, *mid), BF16),
            shape((CHAN, FEAT_OWN, MID_OWN), BF16),
            shape((8, MID_OWN), F32),
            shape((8, FEAT_OWN), F32),
            shape((CHAN, 16, FEAT_OWN), BF16),
            shape((CHAN, 3, TASKS, HEAD, 2 * HEAD), BF16),
        ],
        scratch_shapes=[
            pltpu.VMEM((2, OWN, MID_OWN), F32),
            pltpu.VMEM((OWN_ROWS, TILE_W, FEAT_OWN), BF16),
            pltpu.VMEM((CHAN, 3, TASKS, HEAD, 2 * HEAD), BF16),
            pltpu.VMEM((3, *mid), BF16),
            pltpu.VMEM((3, *mid), BF16),
            pltpu.VMEM((2, GROUP, 8, MID_OWN), F32),
            pltpu.VMEM((2, 4, 8, MID_OWN), F32),
            pltpu.VMEM((GROUP, 8, FEAT_OWN), F32),
            pltpu.VMEM((4, 8, FEAT_OWN), F32),
            pltpu.VMEM((GROUP, 8, FEAT_OWN), F32),
            pltpu.VMEM((4, 8, FEAT_OWN), F32),
            dma((80,)),
            dma((80,)),
            *gather_sems(REACH),
        ],
        compiler_params=pltpu.CompilerParams(
            collective_id=5, has_side_effects=True, vmem_limit_bytes=VMEM_LIMIT
        ),
        cost_estimate=pl.CostEstimate(
            flops=2_000_000_000, bytes_accessed=120_000_000, transcendentals=0
        ),
        name="section_forward",
    )(*operands)


class Scatter:
    def __init__(self, parts, mate_in, near, near_in, far, far_in, spot, links):
        self.parts, self.mate_in, self.near, self.near_in = parts, mate_in, near, near_in
        self.far, self.far_in, self.spot, self.links = far, far_in, spot, links

    def start(self):
        spot = self.spot
        self.sent = self.links.send(self.parts.at[1 - spot.core], self.mate_in, pix=spot.mate)

    def along_z(self):
        spot, links = self.spot, self.links
        links.arrive(self.sent, self.mate_in)
        for z in range(4):
            self.near[z] = (
                self.parts[spot.core, z].astype(F32) + self.mate_in[z].astype(F32)
            ).astype(BF16)
        self.sent = {
            d: links.send(
                self.near.at[spot.z_of(d)], self.near_in.at[d - 1], pix=spot.pix_in_z(d)
            )
            for d in (2, 1, 3)
        }

    def along_x(self):
        spot, links = self.spot, self.links
        total = self.near[spot.z].astype(F32)
        for d in (1, 3, 2):
            links.arrive(self.sent[d], self.near_in.at[d - 1])
            total = total + self.near_in[d - 1].astype(F32)
        self.far[...] = total.astype(BF16)
        self.sent = {
            d: links.send(self.far.at[spot.x_of(d)], self.far_in.at[d - 1], pix=spot.pix_in_x(d))
            for d in (2, 1, 3)
        }

    def finish(self):
        spot, links = self.spot, self.links
        total = self.far[spot.group].astype(F32)
        for d in (1, 3, 2):
            links.arrive(self.sent[d], self.far_in.at[d - 1])
            total = total + self.far_in[d - 1].astype(F32)
        return total


def scatter_scratch(*shape):
    return [
        pltpu.VMEM((2, 4, 4, *shape), BF16),
        pltpu.VMEM((4, 4, *shape), BF16),
        pltpu.VMEM((4, 4, *shape), BF16),
        pltpu.VMEM((3, 4, *shape), BF16),
        pltpu.VMEM((4, *shape), BF16),
        pltpu.VMEM((3, *shape), BF16),
    ]


def spot_of(device):
    return device % 2, device % GROUP // 2, device // GROUP


def section_backward_kernel(
    tiles, trunk_grad, pixels, unit_r, unit_d, unit_e, act_r, act_d, wr_all, wd, we,
    gain_r, bias_r, gain_d, bias_d, gain_e, bias_e, inv_mid, inv_feat, mean_rows, projects, x_group,
    g_group, *refs,
):
    (
        grad_pixels, grad_reduce, grad_gain_r, grad_bias_r, grad_dilate, grad_gain_d, grad_bias_d,
        grad_expand, grad_gain_e, grad_bias_e, grad_point, grad_atrous, grad_project,
    ) = refs[:13]
    scratch = refs[13:]
    (
        keys, keep, wd_cat, side_out, side_in, halo, taps, full, project_in, project_wide, reduce_out,
        near_m, across_m, near_f, across_f, x_all, x_base, x_now, g_all, g_now,
    ) = scratch[:20]
    send_sems, recv_sems, ss_reduce, rs_reduce, load_sems = scratch[-5:]
    buffers = scratch[20:-5]
    spot = Spot()
    links = Links(send_sems, recv_sems)
    i, j = spot.i, spot.j
    by_expand, by_dilate, by_project, by_reduce = [
        Scatter(*buffers[6 * n : 6 * n + 6], spot, links) for n in range(4)
    ]
    owner_i, owner_j = GROUP * j + int_div(i, 4), int_rem(i, 4)
    maker_i, maker_j = 4 * int_rem(i, GROUP) + j, spot.group
    stays = (owner_i == i) & (owner_j == j)
    barrier = pltpu.get_barrier_semaphore()

    @pl.when(jnp.logical_not(stays))
    def _():
        signal(barrier, pix=maker_i, chan=maker_j)

    peers = [{"chan": spot.chan(d)} for d in (1, 2, 3)] + spot.sum_peers()
    peers += [{"pix": spot.before}, {"pix": spot.after}]

    loads = [
        pltpu.make_async_copy(x_group, x_all, load_sems.at[0]),
        pltpu.make_async_copy(g_group, g_all.at[REACH : REACH + GROUP_ROWS], load_sems.at[1]),
    ]

    def prepare():
        for load in loads:
            load.start()
        fill_keep(tiles, keep, i)
        fill_keys(tiles, keys, GROUP_ROWS * spot.group - REACH, GROUP_ROWS + 2 * REACH)
        for tap in range(9):
            wd_cat[:, MID_OWN * tap : MID_OWN * (tap + 1)] = wd[tap]

    greet(peers, 1 - stays.astype(jnp.int32), prepare)

    atrous_sum = GroupSum(*buffers[24:27], spot, links)
    point_sum = GroupSum(*buffers[27:30], spot, links)
    edges = [
        (g_group.at[GROUP_ROWS - REACH :], g_all.at[:REACH], 1),
        (g_group.at[:REACH], g_all.at[REACH + GROUP_ROWS :], -1),
    ]
    edges = [(links.send(src, dst, pix=spot.pix_in_x(d)), dst) for src, dst, d in edges]

    def row_block(r):
        return pl.ds(pl.multiple_of(r * TILE_W, TILE_W), TILE_W)

    def take():
        for load in loads:
            load.wait()
        for n, dst in edges:
            links.arrive(n, dst)

        def one_row(r, carry):
            is_low = lax.broadcasted_iota(jnp.int32, (TILE_W, 2 * HEAD), 1) < HEAD
            for pair in range(2):
                first = x_all[2 * pair, r].astype(F32)
                second = x_all[2 * pair + 1, r].astype(F32)
                lower = jnp.where(is_low, first, pltpu.roll(second, HEAD, 1))
                upper = jnp.where(is_low, pltpu.roll(first, HEAD, 1), second)
                x_base[row_block(r), 2 * HEAD * pair : 2 * HEAD * (pair + 1)] = jnp.where(
                    spot.core == 0, lower, upper
                ).astype(BF16)
            return carry

        lax.fori_loop(0, GROUP_ROWS, one_row, 0, unroll=4)

    def pick(which):
        def one_row(r, carry):
            pieces = []
            for a in range(3):
                piece = g_all[
                    r + REACH - (a - 1) * (which + 1), :, BRANCH * which : BRANCH * (which + 1)
                ]
                same = keys[r + REACH] == keys[r + REACH - (a - 1) * (which + 1)]
                pieces.append(jnp.where(same, piece, jnp.zeros_like(piece)))
            g_now[row_block(r)] = jnp.concatenate(pieces, axis=1)
            return carry

        lax.fori_loop(0, GROUP_ROWS, one_row, 0, unroll=4)

    def multiply(which, b):
        held = x_base
        if b != 1:
            held = x_now

            def one_row(r, carry):
                row = x_base[row_block(r)].astype(F32)
                x_now[row_block(r)] = col_shift(row, (b - 1) * head_rates[which]).astype(BF16)
                return carry

            lax.fori_loop(0, GROUP_ROWS, one_row, 0, unroll=4)
        product = dot_tn(g_now[...], held[...]).T.astype(BF16)
        n = 3 * which + b
        for c in range(CHAN):
            atrous_sum.out[n, c] = product[HEAD * c : HEAD * (c + 1)]
        atrous_sum.ready.append((n, 1 if n % 2 else -1))

    def multiply_point():
        grads = g_all[REACH : REACH + GROUP_ROWS, :, 3 * BRANCH :].reshape(-1, BRANCH)
        product = dot_tn(grads, x_base[...]).T.astype(BF16)
        for c in range(CHAN):
            point_sum.out[0, c] = product[HEAD * c : HEAD * (c + 1)]
        point_sum.ready.append((0, 1))

    tasks = [take]
    for which in range(3):
        tasks.append(functools.partial(pick, which))
        tasks += [functools.partial(multiply, which, b) for b in range(3)]
    tasks += [multiply_point]
    queue = iter(tasks)

    def flush():
        atrous_sum.flush()
        point_sum.flush()

    def meanwhile(count=1):
        for _ in range(count):
            task = next(queue, None)
            if task is not None:
                task()

    project_sent = {
        d: links.send(projects.at[spot.chan(d)], project_in.at[d - 1], chan=spot.chan(d))
        for d in (2, 1, 3)
    }

    def norm_back(grad, unit, near, across, scale):
        sums = sum_over_pix(two_sums(grad, grad * unit), near, across, spot, links, meanwhile)
        pre = scale * (grad - sums[0:1] / PIXELS - unit * (sums[1:2] / PIXELS))
        return pre.astype(BF16), sums

    grad_trunk = trunk_grad[...].astype(F32) + mean_rows[...][:, None, :]
    grad_trunk = grad_trunk.reshape(OWN, FEAT_OWN)
    unit = unit_e[...]
    summed = unit * gain_e[...] + bias_e[...] + pixels[...].astype(F32)
    grad_summed = grad_trunk * slope(summed)
    g_expand, sums = norm_back(grad_summed, unit, near_f, across_f, gain_e[...] * inv_feat[0:1])
    grad_bias_e[...] = sums[0:1]
    grad_gain_e[...] = sums[1:2]

    def sides(turn, make):
        sent = {}
        for d in (2, 1, 3):
            side_out[turn, d - 1] = make(spot.chan(d)).astype(BF16)
            sent[d] = links.send(
                side_out.at[turn, d - 1], side_in.at[turn, d - 1], chan=spot.chan(d)
            )
        return sent

    def side_sum(turn, own, sent):
        for d in (1, 3, 2):
            links.arrive(sent[d], side_in.at[turn, d - 1])
            own = own + side_in[turn, d - 1].astype(F32)
        return own

    def mid_rows(chan):
        return pl.ds(pl.multiple_of(MID_OWN * chan, MID_OWN), MID_OWN)

    sent = sides(0, lambda c: dot_nt(g_expand, we[mid_rows(c)]))
    own = dot_nt(g_expand, we[mid_rows(j)])
    part = 16
    for c in range(CHAN):
        grads = dot_tn(act_d[c], g_expand).astype(BF16)
        for n in range(8):
            by_expand.parts[spot_of(8 * c + n)] = grads[part * n : part * (n + 1)]
    by_expand.start()
    flush()
    meanwhile(2)
    grad_act = side_sum(0, own, sent)

    unit = unit_d[...]
    grad = grad_act * slope(unit * gain_d[...] + bias_d[...])
    g_dilate, sums = norm_back(
        grad, unit, near_m.at[0], across_m.at[0], gain_d[...] * inv_mid[1:2]
    )
    grad_bias_d[...] = sums[0:1]
    grad_gain_d[...] = sums[1:2]
    own_rows = slice(section_rate, section_rate + OWN_ROWS)
    halo[own_rows] = g_dilate.reshape(OWN_ROWS, TILE_W, MID_OWN)
    low, high = slice(0, section_rate), slice(section_rate + OWN_ROWS, 2 * section_rate + OWN_ROWS)
    first, last = slice(section_rate, 2 * section_rate), slice(OWN_ROWS, section_rate + OWN_ROWS)
    to_before = links.send(halo.at[first], halo.at[high], pix=spot.before)
    to_after = links.send(halo.at[last], halo.at[low], pix=spot.after)
    by_expand.along_z()
    flush()
    meanwhile()
    for d in (1, 3, 2):
        links.arrive(project_sent[d], project_in.at[d - 1])
        project_wide[spot.chan(-d)] = project_in[d - 1].astype(F32)
    project_wide[j] = projects[j].astype(F32)
    links.arrive(to_before, halo.at[high])
    links.arrive(to_after, halo.at[low])
    for a in range(3):
        rows = halo[section_rate * (2 - a) : section_rate * (2 - a) + OWN_ROWS]
        rows = rows.reshape(OWN, MID_OWN).astype(F32)
        if a != 1:
            rows = rows * keep[1 - a // 2]
        for b in range(3):
            moved = rows if b == 1 else col_shift(rows, -section_rate * (b - 1))
            tap = 3 * a + b
            taps[:, MID_OWN * tap : MID_OWN * (tap + 1)] = moved.astype(BF16)
    sent = sides(1, lambda c: dot_nt(taps[...], wd_cat[mid_rows(c)]))
    own = dot_nt(taps[...], wd_cat[mid_rows(j)])
    for c in range(CHAN):
        act = act_r[c, own_rows].reshape(OWN, MID_OWN)
        grads = dot_tn(act, taps[...]).astype(BF16)
        for n in range(8):
            for tap in range(9):
                by_dilate.parts[(*spot_of(8 * c + n), tap)] = grads[
                    part * n : part * (n + 1), MID_OWN * tap : MID_OWN * (tap + 1)
                ]
    by_dilate.start()
    flush()
    meanwhile(2)
    grad_act = side_sum(1, own, sent)
    by_expand.along_x()

    unit = unit_r[...]
    grad = grad_act * slope(unit * gain_r[...] + bias_r[...])
    g_reduce, sums = norm_back(
        grad, unit, near_m.at[1], across_m.at[1], gain_r[...] * inv_mid[0:1]
    )
    grad_bias_r[...] = sums[0:1]
    grad_gain_r[...] = sums[1:2]
    full[j] = g_reduce
    sent = {d: links.send(full.at[j], full.at[j], chan=spot.chan(d)) for d in (2, 1, 3)}
    by_dilate.along_z()
    flush()
    for t in range(TASKS):
        for device in range(PIX):
            rows = []
            for start in range(40 * device, 40 * device + 40, 8):
                b, src, d = start // 256, start // HEAD % CHAN, start % HEAD
                rows.append(project_wide[src, BRANCH_PLACE[b], t, d : d + 8])
            rows.append(jnp.zeros((8, HEAD), F32))
            by_project.parts[(*spot_of(device), t)] = jnp.concatenate(rows, axis=0).astype(BF16)
    by_project.start()
    grad_expand[...] = by_expand.finish()
    meanwhile(2)
    for d in (1, 3, 2):
        links.arrive(sent[d], full.at[spot.chan(-d)])
    g_reduce = jnp.concatenate([full[c] for c in range(CHAN)], axis=1)
    weight = jnp.concatenate([wr_all[c] for c in range(CHAN)], axis=1)
    grads = dot_tn(pixels[...], g_reduce).astype(BF16)
    for c in range(CHAN):
        for n in range(8):
            by_reduce.parts[spot_of(4 * n + c)] = grads[
                HEAD * n : HEAD * (n + 1), MID_OWN * c : MID_OWN * (c + 1)
            ]
    by_reduce.start()
    grad_pixels[...] = (grad_summed + dot_nt(g_reduce, weight)).astype(BF16)
    by_reduce.along_z()
    by_project.along_z()
    meanwhile(2)
    by_reduce.along_x()
    flush()
    by_dilate.along_x()
    meanwhile(len(tasks))
    by_project.along_x()
    flush()
    reduce_out[...] = by_reduce.finish()

    def reduce_copies():
        return (
            lambda: remote(
                reduce_out, grad_reduce, ss_reduce.at[0], rs_reduce.at[0], pix=owner_i, chan=owner_j
            ),
            lambda: pltpu.make_async_copy(reduce_out, grad_reduce, rs_reduce.at[0]),
        )

    away, here = reduce_copies()
    pl.when(jnp.logical_not(stays))(lambda: away().start())
    pl.when(stays)(lambda: here().start())
    flush()
    grad_dilate[...] = by_dilate.finish()
    grad_project[...] = by_project.finish()[:, :40]

    def place(n, total):
        which, b = n // 3, n % 3
        for a in range(3):
            for t in range(TASKS):
                lane = BRANCH * a + HEAD * t
                grad_atrous[t, which, 3 * a + b] = total[:, lane : lane + HEAD]

    def place_point(n, total):
        for t in range(TASKS):
            grad_point[t] = total[:, HEAD * t : HEAD * (t + 1)]

    atrous_sum.finish(place)
    point_sum.finish(place_point)

    pltpu.make_async_copy(reduce_out, grad_reduce, rs_reduce.at[0]).wait()
    pl.when(jnp.logical_not(stays))(lambda: away().wait_send())
    links.finish()


def group_scratch(count, *shape):
    return [
        pltpu.VMEM((count, 4, *shape), BF16),
        pltpu.VMEM((count, *shape), BF16),
        pltpu.VMEM((count, 2, *shape), BF16),
    ]


def section_backward(*operands):
    whole = pl.BlockSpec(memory_space=pltpu.VMEM)
    shape = jax.ShapeDtypeStruct
    dma = pltpu.SemaphoreType.DMA
    mid, feat = (OWN, MID_OWN), (OWN, FEAT_OWN)
    return pl.pallas_call(
        section_backward_kernel,
        in_specs=[pl.BlockSpec(memory_space=pltpu.SMEM)]
        + [whole] * 20
        + [pl.BlockSpec(memory_space=pl.ANY)] * 2,
        out_specs=[whole] * 13,
        out_shape=[
            shape(feat, BF16),
            shape((HEAD, MID_OWN), F32),
            shape((1, MID_OWN), F32),
            shape((1, MID_OWN), F32),
            shape((9, 16, MID_OWN), F32),
            shape((1, MID_OWN), F32),
            shape((1, MID_OWN), F32),
            shape((16, FEAT_OWN), F32),
            shape((1, FEAT_OWN), F32),
            shape((1, FEAT_OWN), F32),
            shape((TASKS, HEAD, HEAD), F32),
            shape((TASKS, 3, 9, HEAD, HEAD), F32),
            shape((TASKS, 40, HEAD), F32),
        ],
        scratch_shapes=[
            pltpu.SMEM((GROUP_ROWS + 2 * REACH,), jnp.int32),
            pltpu.VMEM((2, OWN, MID_OWN), F32),
            pltpu.VMEM((FEAT_OWN, 9 * MID_OWN), BF16),
            pltpu.VMEM((2, 3, *mid), BF16),
            pltpu.VMEM((2, 3, *mid), BF16),
            pltpu.VMEM((OWN_ROWS + 2 * section_rate, TILE_W, MID_OWN), BF16),
            pltpu.VMEM((OWN, 9 * MID_OWN), BF16),
            pltpu.VMEM((CHAN, *mid), BF16),
            pltpu.VMEM((3, 5, TASKS, HEAD, HEAD), BF16),
            pltpu.VMEM((CHAN, 5, TASKS, HEAD, HEAD), F32),
            pltpu.VMEM((HEAD, MID_OWN), F32),
            pltpu.VMEM((2, GROUP, 8, MID_OWN), F32),
            pltpu.VMEM((2, 4, 8, MID_OWN), F32),
            pltpu.VMEM((GROUP, 8, FEAT_OWN), F32),
            pltpu.VMEM((4, 8, FEAT_OWN), F32),
            pltpu.VMEM((CHAN, GROUP_ROWS, TILE_W, 128), BF16),
            pltpu.VMEM((GROUP_ROWS * TILE_W, 256), BF16),
            pltpu.VMEM((GROUP_ROWS * TILE_W, 256), BF16),
            pltpu.VMEM((GROUP_ROWS + 2 * REACH, TILE_W, 4 * BRANCH), BF16),
            pltpu.VMEM((GROUP_ROWS * TILE_W, 3 * BRANCH), BF16),
            *scatter_scratch(16, FEAT_OWN),
            *scatter_scratch(9, 16, MID_OWN),
            *scatter_scratch(TASKS, 48, HEAD),
            *scatter_scratch(HEAD, MID_OWN),
            *group_scratch(9, HEAD, 3 * BRANCH),
            *group_scratch(1, HEAD, BRANCH),
            dma((112,)),
            dma((112,)),
            dma((1,)),
            dma((1,)),
            dma((2,)),
        ],
        compiler_params=pltpu.CompilerParams(
            collective_id=6, has_side_effects=True, vmem_limit_bytes=VMEM_LIMIT
        ),
        cost_estimate=pl.CostEstimate(
            flops=16_000_000_000, bytes_accessed=250_000_000, transcendentals=0
        ),
        name="section_backward",
    )(*operands)


def hand_out_kernel(maps, tall, mean_all, *refs):
    count = (len(refs) - 3) // 2
    grads, (task_maps, grad_pooled), outs, sems = (
        refs[:count], refs[count : count + 2], refs[count + 2 : -1], refs[-1],
    )
    copies = [pltpu.make_async_copy(src, dst, sems.at[n]) for n, (src, dst) in enumerate(zip(grads, outs))]
    for copy in copies:
        copy.start()
    for c in range(CHAN):
        part = dot_tn(tall[...], mean_all[c])
        for t in range(TASKS):
            grad_pooled[t, :, 512 * c : 512 * (c + 1)] = part[HEAD * t : HEAD * (t + 1)]
    for t in range(TASKS):
        task_maps[t] = maps[t].reshape(OWN, HEAD).astype(F32).T.astype(BF16)
    for copy in copies:
        copy.wait()


def hand_out(maps, pooled_grad, mean_all, *grads):
    whole = pl.BlockSpec(memory_space=pltpu.VMEM)
    shape = jax.ShapeDtypeStruct
    return pl.pallas_call(
        hand_out_kernel,
        in_specs=[whole] * (3 + len(grads)),
        out_specs=[whole] * 2 + [pl.BlockSpec(memory_space=pl.ANY)] * len(grads),
        out_shape=[shape((TASKS, HEAD, OWN), BF16), shape((TASKS, HEAD, CHAN * 512), F32)]
        + [shape(grad.shape, grad.dtype) for grad in grads],
        scratch_shapes=[pltpu.SemaphoreType.DMA((len(grads),))],
        compiler_params=pltpu.CompilerParams(vmem_limit_bytes=VMEM_LIMIT),
        cost_estimate=pl.CostEstimate(flops=0, bytes_accessed=10_000_000, transcendentals=0),
        name="hand_out",
    )(maps, pooled_grad, mean_all, *grads)


def shards(
    pixels,
    tile_number,
    task_draws,
    reduce_weight,
    reduce_gain,
    reduce_bias,
    dilate_weight,
    dilate_gain,
    dilate_bias,
    expand_weight,
    expand_gain,
    expand_bias,
    point_weight,
    atrous_weight,
    pooled_weight,
    project_weight,
    cotangent,
):
    tile_grid = tile_number.reshape(2, 128)
    norms = [
        v.reshape(1, -1)
        for v in (reduce_gain, reduce_bias, dilate_gain, dilate_bias, expand_gain, expand_bias)
    ]
    pooled_rows = pooled_weight.reshape(BRANCH, -1)
    (
        x_ext, unit_reduce, unit_dilate, unit_expand, act_reduce, act_dilate, reduce_all, inv_mid,
        inv_feat, mean_all, project_all,
    ) = section_forward(
        tile_number, tile_grid, pixels, reduce_weight, dilate_weight, expand_weight, *norms,
        project_weight,
    )
    kernels = atrous_weight.reshape(TASKS, 3, 3, 3, HEAD, -1)
    grad_pre, head_part, grad_project, pool_rows, x_group, pre_pooled = heads_forward(
        tile_number, task_draws, x_ext, jnp.swapaxes(cotangent, 1, 2), kernels, point_weight, project_all, mean_all,
        pooled_rows,
    )
    trunk_grad, g_group, maps, mean_rows, pooled_grad = heads_input_grad(
        tile_number, tile_grid, grad_pre.reshape(OWN_ROWS, TILE_W, 4 * BRANCH),
        head_part.reshape(CHAN, OWN_ROWS, TILE_W, BRANCH), kernels, point_weight, pool_rows,
        pre_pooled, pooled_rows,
    )
    grads = section_backward(
        tile_number, trunk_grad, pixels, unit_reduce, unit_dilate, unit_expand, act_reduce, act_dilate,
        reduce_all, dilate_weight, expand_weight, *norms, inv_mid, inv_feat, mean_rows, grad_project,
        x_group, g_group,
    )
    (
        task_maps, grad_pooled, grad_pixels, grad_reduce, grad_gain_r, grad_bias_r, grad_dilate,
        grad_gain_d, grad_bias_d, grad_expand, grad_gain_e, grad_bias_e, grad_point, grad_atrous,
        grad_project,
    ) = hand_out(maps, pooled_grad, mean_all, *grads)
    return (
        jnp.swapaxes(task_maps, 1, 2),
        grad_pixels,
        grad_reduce,
        grad_gain_r[0],
        grad_bias_r[0],
        grad_dilate,
        grad_gain_d[0],
        grad_bias_d[0],
        grad_expand,
        grad_gain_e[0],
        grad_bias_e[0],
        grad_point,
        grad_atrous,
        jnp.swapaxes(grad_pooled, 1, 2),
        grad_project,
    )


def solution(mesh):
    placed = (
        P("pix", "chan"),
        P(),
        P(),
        P(None, "chan"),
        P("chan"),
        P("chan"),
        P(None, None, "chan"),
        P("chan"),
        P("chan"),
        P(None, "chan"),
        P("chan"),
        P("chan"),
        P(None, "chan", None),
        P(None, None, None, "chan", None),
        P(None, "chan", None),
        P(None, "chan", None),
        P(None, "pix", "chan"),
    )
    return jax.shard_map(
        shards,
        mesh=mesh,
        in_specs=placed,
        out_specs=(
            P(None, "pix", "chan"),
            P("pix", "chan"),
            P("pix", "chan"),
            P("chan"),
            P("chan"),
            P(None, "pix", "chan"),
            P("chan"),
            P("chan"),
            P("pix", "chan"),
            P("chan"),
            P("chan"),
            P(None, "pix", "chan"),
            P(None, None, None, "pix", "chan"),
            P(None, None, "chan"),
            P(None, "pix", "chan"),
        ),
        check_vma=False,
    )
```

```python
import functools

import jax
import jax.numpy as jnp
from jax import lax
from jax.experimental import pallas as pl
from jax.experimental.pallas import tpu as pltpu
from jax.sharding import PartitionSpec as P

TASKS = 3
TILE_W = 64
NROWS = 256
PIX = 32
CHAN = 4
OWN_ROWS = NROWS // PIX
REACH = 3
EXT_ROWS = OWN_ROWS + 2 * REACH
HEAD = 64
BRANCH = TASKS * HEAD
BRANCH_ORDER = (1, 2, 3, 0, 4)
BRANCH_PLACE = (3, 0, 1, 2, 4)

F32 = jnp.float32
BF16 = jnp.bfloat16
MESH = pl.DeviceIdType.MESH
eps = 1e-05
section_rate = 4
head_rates = (6, 12, 18)
VMEM_LIMIT = 60 * 2**20


def int_div(a, b):
    if b & (b - 1) == 0:
        return lax.shift_right_logical(a, jnp.int32(b.bit_length() - 1))
    return lax.shift_right_logical(a * (2**16 // b + 1), jnp.int32(16))


def int_rem(a, b):
    return a - b * int_div(a, b)


def place_of(row):
    kind = int_rem(row, 6)
    return 43 * kind - int_div(kind, 5) + int_div(row, 6)


def row_of(place):
    kind = int_div(place + int_div(place, 214), 43)
    return 6 * (place - 43 * kind + int_div(kind, 5)) + kind


def tile_at(tiles, row):
    return jnp.where((row >= 0) & (row < NROWS), tiles[jnp.clip(row, 0, NROWS - 1)], -1)


def fill_keys(tiles, keys, first, count):
    start = row_of(jnp.maximum(first, 0))

    def one(n, carry):
        row, kind = carry
        inside = (first + n >= 0) & (first + n < NROWS)
        keys[n] = jnp.where(inside, tiles[row] + 8 * kind, -1)
        end = row + 6 >= NROWS
        next_kind = jnp.where(end, jnp.minimum(kind + 1, 5), kind)
        next_row = jnp.where(end, next_kind, row + 6)
        return jnp.where(inside, next_row, row), jnp.where(inside, next_kind, kind)

    lax.fori_loop(0, count, one, (start, int_rem(start, 6)))


def fill_keep(tiles, keep, i):
    for r in range(OWN_ROWS):
        here = tile_at(tiles, OWN_ROWS * i + r)
        for side, step in enumerate((-section_rate, section_rate)):
            same = jnp.where(tile_at(tiles, OWN_ROWS * i + r + step) == here, 1.0, 0.0)
            keep[side, TILE_W * r : TILE_W * (r + 1)] = jnp.full((TILE_W, 128), same, F32)


def rows_at(value, tile):
    row = lax.broadcasted_iota(jnp.int32, value.shape, 0)
    return jnp.sum(jnp.where(row == tile, value, 0.0), axis=0, keepdims=True)


def add_at(sums, row, tile):
    return sums + jnp.where(lax.broadcasted_iota(jnp.int32, sums.shape, 0) == tile, row, 0.0)


def tile_sizes(grid):
    sizes = jnp.zeros((8, 128), F32)
    for tile in range(8):
        here = jnp.sum(jnp.where(grid == tile, 1.0, 0.0), axis=1, keepdims=True)
        sizes = add_at(sizes, TILE_W * jnp.sum(here, axis=0, keepdims=True), tile)
    return jnp.maximum(sizes, 1.0)


def signal(sem, **where):
    pl.semaphore_signal(sem, inc=1, device_id=where, device_id_type=MESH)


def remote(src, dst, send_sem, recv_sem, **where):
    return pltpu.make_async_remote_copy(
        src_ref=src,
        dst_ref=dst,
        send_sem=send_sem,
        recv_sem=recv_sem,
        device_id=where,
        device_id_type=MESH,
    )


def greet_origins(i):
    barrier, expected = pltpu.get_barrier_semaphore(), 0
    for s in range(OWN_ROWS):
        origin = int_div(row_of(OWN_ROWS * i + s), OWN_ROWS)

        @pl.when(origin != i)
        def _():
            signal(barrier, pix=origin)

        target = int_div(place_of(OWN_ROWS * i + s), OWN_ROWS)
        expected = expected + (target != i).astype(jnp.int32)
    return expected


class RowGather:
    def __init__(self, reach, src, out, spot, sems):
        self.reach, self.src, self.out, self.spot = reach, src, out, spot
        (
            self.ss_row, self.rs_row, self.ss_side, self.rs_side, self.ss_far, self.rs_far, self.ss_halo,
            self.rs_halo,
        ) = sems
        self.order = (0, 7, 1, 6, 2, 5, 3, 4)
        self.edge = [s for s in self.order if s < reach or s >= OWN_ROWS - reach]

    def row_send(self, s):
        place = place_of(OWN_ROWS * self.spot.i + s)
        target, slot = int_div(place, OWN_ROWS), int_rem(place, OWN_ROWS)
        src, landing = self.src.at[s], self.out.at[self.spot.j, self.reach + slot]
        return target, (
            lambda: remote(src, landing, self.ss_row.at[s], self.rs_row.at[slot], pix=target),
            lambda: pltpu.make_async_copy(src, landing, self.rs_row.at[slot]),
        )

    def block(self, chan, s):
        return self.out.at[chan, self.reach + s]

    def side(self, way):
        return self.spot.chan((1, -1)[way])

    def side_copy(self, way, s, chan):
        block = self.block(chan, s)
        return remote(
            block, block, self.ss_side.at[way, s], self.rs_side.at[way, s], chan=self.side(way)
        )

    def far_way(self, s):
        return 0 if s < OWN_ROWS // 2 else 1

    def far_copy(self, s, chan):
        block = self.block(chan, s)
        return remote(
            block, block, self.ss_far.at[s], self.rs_far.at[s], chan=self.side(self.far_way(s))
        )

    def halo_copy(self, turn, chan, s):
        reach = self.reach
        if s < reach:
            lane, slot, target = s, reach + OWN_ROWS + s, self.spot.before
        else:
            lane, slot, target = s - OWN_ROWS + 2 * reach, s - OWN_ROWS + reach, self.spot.after
        return remote(
            self.block(chan, s),
            self.out.at[chan, slot],
            self.ss_halo.at[turn, lane],
            self.rs_halo.at[chan, lane],
            pix=target,
        )

    def halo_arrival(self, chan, lane):
        slot = self.reach + OWN_ROWS + lane if lane < self.reach else lane - self.reach
        dst = self.out.at[chan, slot]
        return remote(
            dst, dst, self.ss_halo.at[0, lane], self.rs_halo.at[chan, lane], pix=self.spot.after
        )

    def send_rows(self):
        for s in range(OWN_ROWS):
            target, (away, here) = self.row_send(s)
            pl.when(target != self.spot.i)(lambda: away().start())
            pl.when(target == self.spot.i)(lambda: here().start())

    def pass_own(self):
        j = self.spot.j
        for s in self.order:
            pltpu.make_async_copy(self.src.at[s], self.block(j, s), self.rs_row.at[s]).wait()
            self.side_copy(0, s, j).start()
            self.side_copy(1, s, j).start()
            if s in self.edge:
                self.halo_copy(0, j, s).start()

    def pass_sides(self):
        for s in self.order:
            for way in range(2):
                chan = self.side(1 - way)
                self.side_copy(way, s, chan).wait_recv()
                if way == self.far_way(s):
                    self.far_copy(s, chan).start()
                if s in self.edge:
                    self.halo_copy(1 + way, chan, s).start()

    def pass_far(self):
        far = self.spot.chan(2)
        for s in self.order:
            self.far_copy(s, far).wait_recv()
            if s in self.edge:
                self.halo_copy(3, far, s).start()

    def await_halo(self, chan):
        for lane in range(2 * self.reach):
            self.halo_arrival(chan, lane).wait_recv()

    def drain(self):
        spot, far = self.spot, self.spot.chan(2)
        for s in range(OWN_ROWS):
            target, (away, here) = self.row_send(s)
            pl.when(target != spot.i)(lambda: away().wait_send())
            self.side_copy(0, s, spot.j).wait_send()
            self.side_copy(1, s, spot.j).wait_send()
            self.far_copy(s, self.side(1 - self.far_way(s))).wait_send()
        for turn, chan in enumerate((spot.j, self.side(1), self.side(0), far)):
            for s in self.edge:
                self.halo_copy(turn, chan, s).wait_send()


def gather_sems(reach):
    dma = pltpu.SemaphoreType.DMA
    return [
        dma((OWN_ROWS,)),
        dma((OWN_ROWS,)),
        dma((2, OWN_ROWS)),
        dma((2, OWN_ROWS)),
        dma((OWN_ROWS,)),
        dma((OWN_ROWS,)),
        dma((CHAN, 2 * reach)),
        dma((CHAN, 2 * reach)),
    ]


GROUP = 8
GROUP_ROWS = GROUP * OWN_ROWS


class Posts:
    def __init__(self, send_sems, recv_sems):
        self.send_sems, self.recv_sems, self.made = send_sems, recv_sems, []

    def copy(self, n, make):
        src, dst, where = make()
        return remote(src, dst, self.send_sems.at[n], self.recv_sems.at[n], **where)

    def post(self, make):
        n = len(self.made)
        self.made.append(make)
        self.copy(n, make).start()
        return n

    def arrive(self, n, dst):
        beside = {"chan": int_rem(lax.axis_index("chan") + 1, CHAN)}
        remote(dst, dst, self.send_sems.at[n], self.recv_sems.at[n], **beside).wait_recv()

    def finish(self):
        for n, make in enumerate(self.made):
            self.copy(n, make).wait_send()


def greet(peers, more=0, meanwhile=lambda: None):
    barrier = pltpu.get_barrier_semaphore()
    for where in peers:
        signal(barrier, **where)
    meanwhile()
    pl.semaphore_wait(barrier, len(peers) + more)


class Spot:
    def __init__(self):
        self.i, self.j = lax.axis_index("pix"), lax.axis_index("chan")
        self.group, self.k = int_div(self.i, GROUP), int_rem(self.i, GROUP)
        self.z, self.core = int_div(self.k, 2), int_rem(self.k, 2)
        self.before, self.after = int_rem(self.i + PIX - 1, PIX), int_rem(self.i + 1, PIX)
        self.mate = self.i + 1 - 2 * self.core

    def chan(self, distance):
        return int_rem(self.j + CHAN + distance, CHAN)

    def in_group(self, distance):
        return int_rem(self.k + GROUP + distance, GROUP)

    def pix_in_group(self, distance):
        return GROUP * self.group + self.in_group(distance)

    def x_of(self, distance):
        return int_rem(self.group + 4 + distance, 4)

    def pix_in_x(self, distance):
        return GROUP * self.x_of(distance) + self.k

    def z_of(self, distance):
        return int_rem(self.z + 4 + distance, 4)

    def pix_in_z(self, distance):
        return GROUP * self.group + 2 * self.z_of(distance) + self.core

    def sum_peers(self):
        return [{"pix": self.pix_in_group(d)} for d in range(1, GROUP)] + [
            {"pix": self.pix_in_x(d)} for d in range(1, 4)
        ]


def dot_nt(a, b):
    return lax.dot_general(a, b, (((1,), (1,)), ((), ())), preferred_element_type=F32)


def dot_tn(a, b):
    return lax.dot_general(a, b, (((0,), (0,)), ((), ())), preferred_element_type=F32)


def dot_nn(a, b):
    return jnp.dot(a, b, preferred_element_type=F32)


def slope(v):
    s = jax.nn.sigmoid(v)
    return s * (1.0 + v * (1.0 - s))


def silu(v):
    return v * jax.nn.sigmoid(v)


def order_at(turn, chan):
    ahead = jnp.where(turn == 0, 0, jnp.where(turn == 1, 3, jnp.where(turn == 2, 1, 2)))
    return int_rem(chan + ahead, CHAN)


def greet_returns(i):
    barrier, expected = pltpu.get_barrier_semaphore(), 0
    for s in range(OWN_ROWS):
        origin = int_div(place_of(OWN_ROWS * i + s), OWN_ROWS)

        @pl.when(origin != i)
        def _():
            signal(barrier, pix=origin)

        target = int_div(row_of(OWN_ROWS * i + s), OWN_ROWS)
        expected = expected + (target != i).astype(jnp.int32)
    return expected


PAD = 24
PADDED = PAD + TILE_W + PAD


def block_at(n, chan):
    ahead = jnp.where(n == 0, 2, jnp.where(n == 1, 1, jnp.where(n == 2, 3, 0)))
    return int_rem(chan + ahead, CHAN)


def heads_kernel(
    tiles, tile_grid, trunk, maps_in, kernel, point, project, pooled_weight, kernel_b,
    grad_project, x_group, mean_kept, trunk_grad, g_group, maps_out, mean_rows, tall,
    keys, mean_all, pooled, x, lhs, acc, pre, relay, spread, near, across, mid, parts, pool_rows, pre_pooled,
    wide, taps, acc_b, edges, head_in, maps_sum, out, out_in, out_sum, near_b, across_b, mean_out, mean_in,
    send_sems, recv_sems, own_sem, ss_row, rs_row, ss_side, rs_side, ss_back, rs_back, *gather,
):
    turn, rate = pl.program_id(0), pl.program_id(1)
    step = 3 * turn + rate
    n, grad_step = turn - 4, step - 12
    spot = Spot()
    posts = Posts(send_sems, recv_sems)
    rows = RowGather(REACH, trunk, x, spot, gather)
    i, j = spot.i, spot.j
    grad_pre, head_part = mid, parts
    blocks = (j, spot.chan(-1), spot.chan(1), spot.chan(2))
    relay_way = (1, 1, -1, -1)
    half_rows = OWN_ROWS // 2
    marks = {}

    low, high = edges.at[0], edges.at[1]

    def g_rows(distance, core, half=None):
        start = OWN_ROWS * (2 * spot.z_of(distance) + core)
        if half is None:
            return g_group.at[pl.ds(start, OWN_ROWS)]
        return g_group.at[pl.ds(start + half_rows * half, half_rows)]

    def g_copy():
        return pltpu.make_async_copy(mid, g_rows(0, spot.core), own_sem.at[1])

    def row_send(s):
        row = row_of(OWN_ROWS * i + s)
        target, slot = int_div(row, OWN_ROWS), int_rem(row, OWN_ROWS)
        return target, (
            lambda: remote(
                maps_sum.at[s], maps_out.at[:, slot], ss_row.at[s], rs_row.at[slot], pix=target
            ),
            lambda: pltpu.make_async_copy(
                maps_sum.at[s], maps_out.at[:, slot], rs_row.at[slot]
            ),
        )

    def widen(start, part):
        held = part[...].astype(F32)
        for which in range(3):
            for t in range(TASKS):
                lane = BRANCH * which + HEAD * t
                one = held[:, :, lane : lane + HEAD]
                wide[3 * t + which, start : start + held.shape[0], PAD : PAD + TILE_W] = (
                    jnp.concatenate([one, one], axis=2)
                )

    def start_grads():
        g_copy().start()
        marks["low"] = posts.post(
            lambda: (mid.at[OWN_ROWS - REACH :], low, {"pix": spot.after})
        )
        marks["high"] = posts.post(lambda: (mid.at[:REACH], high, {"pix": spot.before}))
        for d in (2, 1, 3):
            marks["head", d] = posts.post(
                lambda d=d: (parts.at[spot.chan(d)], head_in.at[d - 1], {"chan": spot.chan(d)})
            )
        for turn in range(2):
            for d in (1, -1):
                half = turn if d == 1 else 1 - turn
                marks["z", d, half] = posts.post(
                    lambda half=half, d=d: (
                        mid.at[half_rows * half : half_rows * (half + 1)],
                        g_rows(0, spot.core, half),
                        {"pix": spot.pix_in_z(d)},
                    )
                )
        sums = jnp.zeros((8, 256), F32)
        for r in range(OWN_ROWS):
            sums = add_at(sums, pool_rows[r : r + 1], tiles[row_of(OWN_ROWS * i + r)])
        near_b[spot.k] = sums
        for d in range(1, GROUP):
            marks["near b", d] = posts.post(
                lambda d=d: (near_b.at[spot.k], near_b.at[spot.k], {"pix": spot.pix_in_group(d)})
            )
        wide[...] = jnp.zeros_like(wide)
        widen(REACH, mid)

    def x_slice(distance, chan=slice(0, CHAN)):
        lanes = pl.ds(pl.multiple_of(128 * spot.z_of(distance), 128), 128)
        return x.at[chan, REACH : REACH + OWN_ROWS, :, lanes]

    def x_rows(distance, core, chan=slice(0, CHAN)):
        return x_group.at[chan, pl.ds(OWN_ROWS * (2 * spot.z_of(distance) + core), OWN_ROWS)]

    def own_copy():
        return pltpu.make_async_copy(x_slice(0), x_rows(0, spot.core), own_sem.at[0])

    def post_x(q):
        way = relay_way[q]
        marks["relay", q] = posts.post(
            lambda: (x_slice(2, blocks[q]), relay.at[q], {"pix": spot.pix_in_z(way)})
        )
        for d in (1, -1):
            marks["x", d, q] = posts.post(
                lambda d=d: (
                    x_slice(d, blocks[q]), x_rows(0, spot.core, blocks[q]), {"pix": spot.pix_in_z(d)}
                )
            )

    def pass_x(q):
        way = relay_way[q]
        posts.arrive(marks["relay", q], relay.at[q])
        marks["far", q] = posts.post(
            lambda: (relay.at[q], x_rows(-way, spot.core, blocks[q]), {"pix": spot.pix_in_z(way)})
        )

    @pl.when(step == 0)
    def _():
        expected = greet_origins(i) + greet_returns(i)

        def prepare():
            fill_keys(tiles, keys, OWN_ROWS * i - REACH, EXT_ROWS)
            spread[...] = jnp.zeros_like(spread)
            for which, b in enumerate(BRANCH_ORDER):
                for c in range(CHAN):
                    for t in range(TASKS):
                        start = BRANCH * c + HEAD * t
                        spread[which, start : start + HEAD, HEAD * t : HEAD * (t + 1)] = project[
                            c, b // 2, t, :, HEAD * (b % 2) : HEAD * (b % 2 + 1)
                        ]

        greet(
            [{"chan": spot.chan(d)} for d in (1, 2, 3)]
            + [{"pix": spot.pix_in_z(d)} for d in (1, -1)]
            + spot.sum_peers()
            + [{"pix": p} for p in (spot.before, spot.after)],
            expected,
            prepare,
        )
        rows.send_rows()
        row_sums = jnp.sum(trunk[...].astype(F32), axis=1)
        sums = jnp.zeros((8, 512), F32)
        for r in range(OWN_ROWS):
            sums = add_at(sums, row_sums[r : r + 1], tile_at(tiles, OWN_ROWS * i + r))
        near[spot.k] = sums
        for d in range(1, GROUP):
            marks["near", d] = posts.post(
                lambda d=d: (near.at[spot.k], near.at[spot.k], {"pix": spot.pix_in_group(d)})
            )
        rows.pass_own()
        post_x(0)
        rows.await_halo(j)

    @pl.when(step == 1)
    def _():
        for d in range(1, GROUP):
            posts.arrive(marks["near", d], near.at[spot.in_group(-d)])
        total = near[0]
        for k in range(1, GROUP):
            total = total + near[k]
        across[spot.group] = total
        for d in range(1, 4):
            marks["across", d] = posts.post(
                lambda d=d: (
                    across.at[spot.group], across.at[spot.group], {"pix": spot.pix_in_x(d)}
                )
            )

    @pl.when(step == 3)
    def _():
        rows.pass_sides()
        post_x(1)
        post_x(2)
        pass_x(0)
        for d in range(1, 4):
            posts.arrive(marks["across", d], across.at[spot.x_of(-d)])
        sums = across[0] + across[1] + across[2] + across[3]
        mean = sums / tile_sizes(tile_grid[...])[:, 0:1]
        mean_all[j] = jnp.concatenate([mean, jnp.zeros((8, 512), F32)], axis=0).astype(BF16)
        for d in (2, 1, 3):
            marks["mean", d] = posts.post(
                lambda d=d: (mean_all.at[j], mean_all.at[j], {"chan": spot.chan(d)})
            )
        rows.await_halo(blocks[1])

    @pl.when(step == 6)
    def _():
        rows.await_halo(blocks[2])
        for d in (1, 2, 3):
            posts.arrive(marks["mean", d], mean_all.at[spot.chan(-d)])
        mean_kept[...] = mean_all[...]
        act = None
        for c in range(CHAN):
            term = dot_nt(mean_all[c], pooled_weight[:, 512 * c : 512 * (c + 1)])
            act = term if act is None else act + term
        pre_pooled[...] = act
        act = silu(act).astype(BF16).astype(F32)
        for r in range(OWN_ROWS):
            row = rows_at(act, tiles[row_of(OWN_ROWS * i + r)])
            pooled[TILE_W * r : TILE_W * (r + 1)] = jnp.broadcast_to(row, (TILE_W, BRANCH)).astype(
                BF16
            )
        rows.pass_far()
        post_x(3)
        own_copy().start()
        pass_x(1)
        pass_x(2)

    @pl.when(step == 9)
    def _():
        rows.await_halo(blocks[3])
        pass_x(3)

    @pl.when(turn < 4)
    def _():
        chan = order_at(turn, j)
        for a in range(3):
            for r in range(OWN_ROWS):
                slot = REACH + r + (a - 1) * (rate + 1)
                row = x[chan, slot]
                if a != 1:
                    row = jnp.where(keys[REACH + r] == keys[slot], row, jnp.zeros_like(row))
                lhs[TILE_W * r : TILE_W * (r + 1), 512 * a : 512 * (a + 1)] = row
        taps = jnp.concatenate([kernel[:, 0, a].reshape(3 * BRANCH, 512) for a in range(3)], axis=1)
        product = dot_nt(lhs[...], taps)

        @pl.when(turn == 0)
        def _():
            acc[rate] = product

        @pl.when(turn > 0)
        def _():
            acc[rate] += product

        @pl.when(rate == 0)
        def _():
            lanes = pl.ds(pl.multiple_of(512 * chan, 512), 512)
            own = x[chan, REACH : REACH + OWN_ROWS].reshape(OWN_ROWS * TILE_W, 512)
            term = dot_nt(own, point[:, :, lanes].reshape(BRANCH, 512))
            pre[3] = jnp.where(turn > 0, pre[3], 0.0) + term

    @pl.when(step == 11)
    def _():
        col = lax.broadcasted_iota(jnp.int32, (OWN_ROWS * TILE_W, HEAD), 0) % TILE_W
        for which, dilation in enumerate(head_rates):
            for t in range(TASKS):
                behind, total, ahead = (
                    acc[which, :, BRANCH * t + HEAD * b : BRANCH * t + HEAD * (b + 1)]
                    for b in range(3)
                )
                behind = pltpu.roll(behind, dilation, 0)
                ahead = pltpu.roll(ahead, OWN_ROWS * TILE_W - dilation, 0)
                total = total + jnp.where(col >= dilation, behind, 0.0)
                total = total + jnp.where(col < TILE_W - dilation, ahead, 0.0)
                pre[which, :, HEAD * t : HEAD * (t + 1)] = total
        cot = jnp.concatenate([maps_in[c].reshape(-1, BRANCH) for c in range(CHAN)], axis=1)
        head = None
        for which in range(5):
            if which < 4:
                before = pre[which]
                logistic = jax.nn.sigmoid(before)
                joined = (before * logistic).astype(BF16)
            else:
                joined = pooled[...]
            weight = spread[which]
            term = dot_nt(joined, weight)
            head = term if head is None else head + term
            grads = dot_tn(joined, cot)
            for t in range(TASKS):
                for c in range(CHAN):
                    lane = BRANCH * c + HEAD * t
                    grad_project[c, which, t] = grads[
                        HEAD * t : HEAD * (t + 1), lane : lane + HEAD
                    ].astype(BF16)
            back = dot_nn(cot, weight)
            if which < 4:
                grad = back * (logistic * (1.0 + before * (1.0 - logistic)))
                grad_pre[:, :, BRANCH * which : BRANCH * (which + 1)] = grad.astype(BF16).reshape(
                    OWN_ROWS, TILE_W, BRANCH
                )
            else:
                sums = jnp.sum(back.reshape(OWN_ROWS, TILE_W, BRANCH), axis=1)
                pool_rows[:, :BRANCH] = sums
                pool_rows[:, BRANCH:] = jnp.zeros((OWN_ROWS, 256 - BRANCH), F32)
        for c in range(CHAN):
            part = head[:, BRANCH * c : BRANCH * (c + 1)].astype(BF16)
            head_part[c] = part.reshape(OWN_ROWS, TILE_W, BRANCH)
        start_grads()

    @pl.when(grad_step == 0)
    def _():
        posts.arrive(marks["low"], low)
        posts.arrive(marks["high"], high)
        widen(0, low)
        widen(REACH + OWN_ROWS, high)

        def one_row(r, carry):
            is_low = lax.broadcasted_iota(jnp.int32, (TILE_W, 2 * HEAD), 1) < HEAD
            out_rows = pl.ds(pl.multiple_of(r * TILE_W, TILE_W), TILE_W)
            for which, dilation in enumerate(head_rates):

                def shifted(tap):
                    t, a, b = tap // 9, tap // 3 % 3 - 1, tap % 3 - 1
                    piece = wide[
                        3 * t + which,
                        r + REACH - a * (which + 1),
                        PAD - b * dilation : PAD - b * dilation + TILE_W,
                    ]
                    same = keys[REACH + r] == keys[REACH + r - a * (which + 1)]
                    return jnp.where(same, piece, 0.0)

                for pair in range(14):
                    first = shifted(2 * pair)
                    second = shifted(2 * pair + 1) if pair < 13 else jnp.zeros_like(first)
                    taps[which, out_rows, 2 * HEAD * pair : 2 * HEAD * (pair + 1)] = jnp.where(
                        is_low, first, second
                    ).astype(BF16)
            return carry

        lax.fori_loop(0, OWN_ROWS, one_row, 0)

    @pl.when(grad_step == 2)
    def _():
        for d in range(1, GROUP):
            posts.arrive(marks["near b", d], near_b.at[spot.in_group(-d)])
        total = near_b[0]
        for k in range(1, GROUP):
            total = total + near_b[k]
        across_b[spot.group] = total
        for d in range(1, 4):
            marks["across b", d] = posts.post(
                lambda d=d: (
                    across_b.at[spot.group], across_b.at[spot.group], {"pix": spot.pix_in_x(d)}
                )
            )

    @pl.when(grad_step == 4)
    def _():
        for d in range(1, 4):
            posts.arrive(marks["across b", d], across_b.at[spot.x_of(-d)])
        sums = across_b[0] + across_b[1] + across_b[2] + across_b[3]
        pooled_pre = sums[:, :BRANCH] * slope(pre_pooled[0:8])
        tall[...] = jnp.concatenate([pooled_pre, jnp.zeros((8, BRANCH), F32)], axis=0).astype(BF16)
        for c in range(CHAN):
            mean_out[c] = dot_nn(tall[...], pooled_weight[:, 512 * c : 512 * (c + 1)]).astype(BF16)
        for d in (2, 1, 3):
            marks["mean b", d] = posts.post(
                lambda d=d: (mean_out.at[spot.chan(d)], mean_in.at[d - 1], {"chan": spot.chan(d)})
            )

    @pl.when(grad_step == 8)
    def _():
        mean = mean_out[j].astype(F32)
        for d in (1, 3, 2):
            posts.arrive(marks["mean b", d], mean_in.at[d - 1])
            mean = mean + mean_in[d - 1].astype(F32)
        mean = mean[0:8] / tile_sizes(tile_grid[...])[:, 0:1]
        for r in range(OWN_ROWS):
            mean_rows[r : r + 1] = rows_at(mean, tiles[OWN_ROWS * i + r])
        for d in (1, 3, 2):
            posts.arrive(marks["head", d], head_in.at[d - 1])
        for s in range(OWN_ROWS):
            held = parts[j, s].astype(F32)
            for d in (1, 2, 3):
                held = held + head_in[d - 1, s].astype(F32)
            for t in range(TASKS):
                maps_sum[s, t] = held[:, HEAD * t : HEAD * (t + 1)].astype(BF16)
            target, (away, here) = row_send(s)
            pl.when(target != i)(lambda: away().start())
            pl.when(target == i)(lambda: here().start())

    @pl.when(grad_step == 5)
    def _():
        for half, d in enumerate((1, -1)):
            posts.arrive(marks["z", d, half], g_rows(-d, spot.core, half))
            marks["far g", half] = posts.post(
                lambda half=half, d=d: (
                    g_rows(-d, spot.core, half),
                    g_rows(-d, spot.core, half),
                    {"pix": spot.pix_in_z(d)},
                )
            )

    @pl.when(grad_step == 10)
    def _():
        for half, d in enumerate((-1, 1)):
            posts.arrive(marks["z", d, half], g_rows(-d, spot.core, half))

    @pl.when(turn >= 4)
    def _():
        product = dot_nn(taps[rate, :, : 27 * HEAD], kernel_b[...].reshape(27 * HEAD, -1))

        @pl.when(rate == 0)
        def _():
            lanes = pl.ds(pl.multiple_of(512 * block_at(n, j), 512), 512)
            grads = mid[...].reshape(OWN_ROWS * TILE_W, -1)[:, 3 * BRANCH :]
            acc_b[...] = product + dot_nn(grads, point[:, :, lanes].reshape(BRANCH, 512))

        @pl.when(rate == 1)
        def _():
            acc_b[...] += product

        @pl.when(rate == 2)
        def _():
            total = acc_b[...] + product
            out[block_at(n, j)] = total.astype(BF16).reshape(OWN_ROWS, TILE_W, 512)

    def side_send(chan, s):
        turn = int_rem(chan + CHAN - j, CHAN) - 1
        return remote(
            out.at[chan, s], out_in.at[turn, s], ss_side.at[turn, s], rs_side.at[turn, s], chan=chan
        )

    @pl.when((turn >= 4) & (rate == 2) & (n < 3))
    def _():
        for s in range(OWN_ROWS):
            side_send(block_at(n, j), s).start()

    def back_send(s):
        row = row_of(OWN_ROWS * i + s)
        target, slot = int_div(row, OWN_ROWS), int_rem(row, OWN_ROWS)
        return target, (
            lambda: remote(
                out_sum.at[s], trunk_grad.at[slot], ss_back.at[s], rs_back.at[slot], pix=target
            ),
            lambda: pltpu.make_async_copy(out_sum.at[s], trunk_grad.at[slot], rs_back.at[slot]),
        )

    def side_arrival(turn, s):
        dst = out_in.at[turn, s]
        return remote(dst, dst, ss_side.at[turn, s], rs_side.at[turn, s], chan=spot.chan(1))

    @pl.when(grad_step == 11)
    def _():
        for s in range(OWN_ROWS):
            held = out[j, s].astype(F32)
            for turn in range(3):
                side_arrival(turn, s).wait_recv()
                held = held + out_in[turn, s].astype(F32)
            out_sum[s] = held.astype(BF16)
            target, (away, here) = back_send(s)
            pl.when(target != i)(lambda: away().start())
            pl.when(target == i)(lambda: here().start())
        for half in range(2):
            posts.arrive(marks["far g", half], g_rows(2, spot.core, half))
        g_copy().wait()
        for s in range(OWN_ROWS):
            pltpu.make_async_copy(out_sum.at[s], trunk_grad.at[s], rs_back.at[s]).wait()
            target, (away, here) = back_send(s)
            pl.when(target != i)(lambda: away().wait_send())
            for d in (1, 2, 3):
                side_send(spot.chan(d), s).wait_send()
            pltpu.make_async_copy(maps_sum.at[s], maps_out.at[:, s], rs_row.at[s]).wait()
            target, (away, here) = row_send(s)
            pl.when(target != i)(lambda: away().wait_send())
        for q in range(4):
            for d in (1, -1):
                posts.arrive(marks["x", d, q], x_rows(-d, spot.core, blocks[q]))
            posts.arrive(marks["far", q], x_rows(2, spot.core, blocks[q]))
        own_copy().wait()
        rows.drain()
        posts.finish()


def heads(*operands):
    pixels = OWN_ROWS * TILE_W
    whole = pl.BlockSpec(memory_space=pltpu.VMEM)
    hbm = pl.BlockSpec(memory_space=pl.ANY)
    dma = pltpu.SemaphoreType.DMA
    shape = jax.ShapeDtypeStruct
    maps, rows = (OWN_ROWS, TILE_W, BRANCH), (OWN_ROWS, TILE_W, 512)

    def forward_block(q, r):
        chan = order_at(jnp.minimum(q, 3), lax.axis_index("chan"))
        return (0, jnp.where(q < 4, r, 2), 0, 0, 0, chan)

    def grad_block(q, r):
        chan = block_at(jnp.maximum(q - 4, 0), lax.axis_index("chan"))
        return (0, jnp.where(q < 4, 0, r), 0, 0, 0, chan)

    return pl.pallas_call(
        heads_kernel,
        grid=(8, 3),
        in_specs=[pl.BlockSpec(memory_space=pltpu.SMEM)]
        + [whole] * 3
        + [pl.BlockSpec((TASKS, 1, 3, 3, HEAD, 512), forward_block)]
        + [whole] * 3
        + [pl.BlockSpec((TASKS, 1, 3, 3, HEAD, 512), grad_block)],
        out_specs=[whole, hbm, whole, hbm, hbm, hbm, whole, whole],
        out_shape=[
            shape((CHAN, 5, TASKS, HEAD, HEAD), BF16),
            shape((CHAN, GROUP_ROWS, TILE_W, 128), BF16),
            shape((CHAN, 16, 512), BF16),
            shape(rows, BF16),
            shape((GROUP_ROWS, TILE_W, 4 * BRANCH), BF16),
            shape((TASKS, OWN_ROWS, TILE_W, HEAD), BF16),
            shape((OWN_ROWS, 512), F32),
            shape((16, BRANCH), BF16),
        ],
        scratch_shapes=[
            pltpu.SMEM((EXT_ROWS,), jnp.int32),
            pltpu.VMEM((CHAN, 16, 512), BF16),
            pltpu.VMEM((pixels, BRANCH), BF16),
            pltpu.VMEM((CHAN, EXT_ROWS, TILE_W, 512), BF16),
            pltpu.VMEM((pixels, 3 * 512), BF16),
            pltpu.VMEM((3, pixels, 3 * BRANCH), F32),
            pltpu.VMEM((4, pixels, BRANCH), F32),
            pltpu.VMEM((4, OWN_ROWS, TILE_W, 128), BF16),
            pltpu.VMEM((5, 256 * TASKS, BRANCH), BF16),
            pltpu.VMEM((GROUP, 8, 512), F32),
            pltpu.VMEM((4, 8, 512), F32),
            pltpu.VMEM((OWN_ROWS, TILE_W, 4 * BRANCH), BF16),
            pltpu.VMEM((CHAN, *maps), BF16),
            pltpu.VMEM((OWN_ROWS, 256), F32),
            pltpu.VMEM((16, BRANCH), F32),
            pltpu.VMEM((9, EXT_ROWS, PADDED, 2 * HEAD), F32),
            pltpu.VMEM((3, pixels, 28 * HEAD), BF16),
            pltpu.VMEM((pixels, 512), F32),
            pltpu.VMEM((2, REACH, TILE_W, 4 * BRANCH), BF16),
            pltpu.VMEM((CHAN - 1, *maps), BF16),
            pltpu.VMEM((OWN_ROWS, TASKS, TILE_W, HEAD), BF16),
            pltpu.VMEM((CHAN, *rows), BF16),
            pltpu.VMEM((CHAN - 1, *rows), BF16),
            pltpu.VMEM(rows, BF16),
            pltpu.VMEM((GROUP, 8, 256), F32),
            pltpu.VMEM((4, 8, 256), F32),
            pltpu.VMEM((CHAN, 16, 512), BF16),
            pltpu.VMEM((CHAN - 1, 16, 512), BF16),
            dma((64,)),
            dma((64,)),
            dma((2,)),
            dma((OWN_ROWS,)),
            dma((OWN_ROWS,)),
            dma((CHAN - 1, OWN_ROWS)),
            dma((CHAN - 1, OWN_ROWS)),
            dma((OWN_ROWS,)),
            dma((OWN_ROWS,)),
            *gather_sems(REACH),
        ],
        compiler_params=pltpu.CompilerParams(
            collective_id=2, has_side_effects=True, vmem_limit_bytes=VMEM_LIMIT
        ),
        cost_estimate=pl.CostEstimate(
            flops=24_000_000_000, bytes_accessed=56_000_000, transcendentals=0
        ),
        name="heads",
    )(*operands)


class GroupSum:
    def __init__(self, out, relay_in, side_in, spot, links):
        self.out, self.relay_in, self.side_in, self.spot, self.links = out, relay_in, side_in, spot, links
        self.ready, self.open, self.arrivals = [], [], []

    def flush(self):
        self.relay()
        for n, way in self.ready:
            self.send(n, way)
        self.ready = []

    def send(self, n, way):
        spot, links, out = self.spot, self.links, self.out
        relay = links.send(out.at[n, spot.x_of(2)], self.relay_in.at[n], pix=spot.pix_in_x(way))
        side = links.send(
            out.at[n, spot.x_of(-way)], self.side_in.at[n, 0], pix=spot.pix_in_x(-way)
        )
        self.arrivals.append((side, n, 0))
        self.open.append((n, way, relay))

    def relay(self):
        for n, way, relay in self.open:
            self.links.arrive(relay, self.relay_in.at[n])
            target = self.spot.x_of(way)
            both = self.out[n, target].astype(F32) + self.relay_in[n].astype(F32)
            self.out[n, target] = both.astype(BF16)
            side = self.links.send(
                self.out.at[n, target], self.side_in.at[n, 1], pix=self.spot.pix_in_x(way)
            )
            self.arrivals.append((side, n, 1))
        self.open = []

    def finish(self, place):
        for side, n, which in self.arrivals:
            self.links.arrive(side, self.side_in.at[n, which])
        for n in range(self.out.shape[0]):
            total = self.out[n, self.spot.group].astype(F32)
            place(n, total + self.side_in[n, 0].astype(F32) + self.side_in[n, 1].astype(F32))


class Links:
    def __init__(self, send_sems, recv_sems):
        self.send_sems, self.recv_sems, self.count, self.sent = send_sems, recv_sems, 0, []

    def send(self, src, dst, **where):
        n = self.count
        self.count += 1
        copy = remote(src, dst, self.send_sems.at[n], self.recv_sems.at[n], **where)
        copy.start()
        self.sent.append(copy)
        return n

    def arrive(self, n, dst):
        beside = {"chan": int_rem(lax.axis_index("chan") + 1, CHAN)}
        remote(dst, dst, self.send_sems.at[n], self.recv_sems.at[n], **beside).wait_recv()

    def finish(self):
        for copy in self.sent:
            copy.wait_send()


def sum_over_pix(value, near, across, spot, links, meanwhile=lambda: None):
    near[spot.k] = value
    sent = [
        links.send(near.at[spot.k], near.at[spot.k], pix=spot.pix_in_group(d))
        for d in range(1, GROUP)
    ]
    meanwhile()
    for d, n in zip(range(1, GROUP), sent):
        links.arrive(n, near.at[spot.in_group(-d)])
    total = near[0]
    for k in range(1, GROUP):
        total = total + near[k]
    across[spot.group] = total
    sent = [
        links.send(across.at[spot.group], across.at[spot.group], pix=spot.pix_in_x(d))
        for d in range(1, 4)
    ]
    meanwhile()
    for d, n in zip(range(1, 4), sent):
        links.arrive(n, across.at[spot.x_of(-d)])
    return across[0] + across[1] + across[2] + across[3]


def two_sums(first, second):
    width = first.shape[1]
    rows = [jnp.sum(first, axis=0, keepdims=True), jnp.sum(second, axis=0, keepdims=True)]
    return jnp.concatenate(rows + [jnp.zeros((6, width), F32)], axis=0)


PIXELS = NROWS * TILE_W
OWN = OWN_ROWS * TILE_W
MID_OWN = 128
FEAT_OWN = 512


def col_shift(value, distance):
    col = lax.broadcasted_iota(jnp.int32, value.shape, 0) % TILE_W
    rows = value.shape[0]
    moved = pltpu.roll(value, (rows - distance) % rows, 0)
    inside = (col < TILE_W - distance) if distance > 0 else (col >= -distance)
    return jnp.where(inside, moved, 0.0)


def section_forward_kernel(
    tiles, draws, pixels, wr, wd, we, gain_r, bias_r, gain_d, bias_d, gain_e, bias_e, project, cotangent,
    trunk, unit_r, unit_d, unit_e, act_r, act_d, wr_all, inv_mid, inv_feat, project_all, maps_in,
    keep, project_out, part_out, part_in, near_m, across_m, near_f, across_f, maps_own,
    send_sems, recv_sems, ss_map, rs_map,
):
    spot = Spot()
    links = Links(send_sems, recv_sems)
    i, j = spot.i, spot.j
    expected = greet_origins(i)

    def map_send(s):
        place = place_of(OWN_ROWS * i + s)
        target, slot = int_div(place, OWN_ROWS), int_rem(place, OWN_ROWS)
        return target, (
            lambda: remote(
                maps_own.at[s], maps_in.at[j, slot], ss_map.at[s], rs_map.at[slot], pix=target
            ),
            lambda: pltpu.make_async_copy(maps_own.at[s], maps_in.at[j, slot], rs_map.at[slot]),
        )

    def prepare():
        fill_keep(tiles, keep, spot.i)
        lane = lax.broadcasted_iota(jnp.int32, (8, 128), 1)
        drawn = jnp.full((8, 128), -1e30, F32)
        for t in range(TASKS):
            drawn = jnp.where(lane == t, draws[t].astype(F32) / 3.0, drawn)
        grown = jnp.where(lane < TASKS, jnp.exp(drawn - jnp.max(drawn, axis=1, keepdims=True)), 0.0)
        grown = grown / jnp.sum(grown, axis=1, keepdims=True)
        for t in range(TASKS):
            weight = jnp.sum(jnp.where(lane == t, grown, 0.0), axis=1, keepdims=True)[0:1]
            scaled = (cotangent[t].astype(F32).T * weight).astype(BF16)
            maps_own[:, :, HEAD * t : HEAD * (t + 1)] = scaled.reshape(OWN_ROWS, TILE_W, HEAD)
        for c in range(CHAN):
            for b in range(5):
                lane = HEAD * (b % 2)
                project_out[c, b // 2, :, :, lane : lane + HEAD] = project[
                    :, :, 256 * b + HEAD * c : 256 * b + HEAD * (c + 1)
                ]
            project_out[c, 2, :, :, HEAD:] = jnp.zeros((TASKS, HEAD, HEAD), BF16)

    greet(
        [{"chan": spot.chan(d)} for d in (1, 2, 3)]
        + spot.sum_peers()
        + [{"pix": p} for p in (spot.before, spot.after, spot.mate)],
        expected,
        prepare,
    )
    half = FEAT_OWN // 2

    def half_of(chan, core):
        return pl.ds(pl.multiple_of(FEAT_OWN * chan + half * core, half), half)

    own_half = half_of(0, spot.core)
    other_half = half_of(0, 1 - spot.core)
    sent = {
        d: links.send(
            wr.at[half_of(spot.chan(d), spot.core)], wr_all.at[j, own_half], chan=spot.chan(d)
        )
        for d in (2, 1, 3)
    }
    for s in range(OWN_ROWS):
        target, (away, here) = map_send(s)
        pl.when(target != i)(lambda: away().start())
        pl.when(target == i)(lambda: here().start())
    wr_all[j] = wr[pl.ds(pl.multiple_of(FEAT_OWN * j, FEAT_OWN), FEAT_OWN)]
    pre = dot_nn(pixels[...], wr_all[j])
    mates = {}
    for d in (1, 3, 2):
        source = spot.chan(-d)
        links.arrive(sent[d], wr_all.at[source, own_half])
        mates[d] = links.send(
            wr_all.at[source, own_half], wr_all.at[source, own_half], pix=spot.mate
        )
    back = {}
    for d in (1, 3, 2):
        source = spot.chan(-d)
        links.arrive(mates[d], wr_all.at[source, other_half])
        part_out[d - 1] = dot_nn(pixels[...], wr_all[source]).astype(BF16)
        back[d] = links.send(part_out.at[d - 1], part_in.at[d - 1], chan=source)
    for d in (1, 3, 2):
        links.arrive(back[d], part_in.at[d - 1])
        pre = pre + part_in[d - 1].astype(F32)

    project_sent = {}

    def send_project():
        for d in (2, 1, 3):
            for last, part in ((False, spot.core), (True, 2)):
                project_sent[d, last] = links.send(
                    project_out.at[spot.chan(d), part], project_all.at[j, part], chan=spot.chan(d)
                )

    def swap_project():
        for d in (1, 3, 2):
            source = spot.chan(-d)
            links.arrive(project_sent[d, False], project_all.at[source, spot.core])
            links.arrive(project_sent[d, True], project_all.at[source, 2])
            project_sent[d] = links.send(
                project_all.at[source, spot.core], project_all.at[source, spot.core], pix=spot.mate
            )

    halves = (slice(0, OWN_ROWS // 2), slice(OWN_ROWS // 2, OWN_ROWS))
    maps_sent = {}

    def send_maps():
        for s in range(OWN_ROWS):
            pltpu.make_async_copy(maps_own.at[s], maps_in.at[j, s], rs_map.at[s]).wait()
        for part in halves:
            for d in (1, -1):
                block = maps_in.at[j, part]
                maps_sent[d, part.start] = links.send(block, block, chan=spot.chan(d))

    def pass_maps():
        for d in (1, -1):
            for part in halves:
                links.arrive(maps_sent[d, part.start], maps_in.at[spot.chan(-d), part])
        for d, part in zip((1, -1), halves):
            block = maps_in.at[spot.chan(-d), part]
            maps_sent[part.start] = links.send(block, block, chan=spot.chan(d))

    todo = [send_project, send_maps, swap_project, pass_maps]

    def meanwhile():
        if todo:
            todo.pop(0)()

    def norm(value, near, across, gain, bias):
        sums = sum_over_pix(two_sums(value, value * value), near, across, spot, links, meanwhile)
        center = sums[0:1] / PIXELS
        inv = lax.rsqrt(sums[1:2] / PIXELS - center * center + eps)
        unit = (value - center) * inv
        return unit, unit * gain + bias, inv

    unit, normed, inv_r = norm(pre, near_m.at[0], across_m.at[0], gain_r[...], bias_r[...])
    unit_r[...] = unit
    own = slice(section_rate, section_rate + OWN_ROWS)
    act_r[j, own] = silu(normed).astype(BF16).reshape(OWN_ROWS, TILE_W, MID_OWN)
    low, high = slice(0, section_rate), slice(section_rate + OWN_ROWS, 2 * section_rate + OWN_ROWS)
    first, last = slice(section_rate, 2 * section_rate), slice(OWN_ROWS, section_rate + OWN_ROWS)
    sent = {
        d: links.send(act_r.at[j, own], act_r.at[j, own], chan=spot.chan(d)) for d in (2, 1, 3)
    }
    arrivals = []
    for d in (0, 1, 3, 2):
        source = spot.chan(-d)
        if d:
            links.arrive(sent[d], act_r.at[source, own])
        n = links.send(act_r.at[source, first], act_r.at[source, high], pix=spot.before)
        arrivals.append((n, act_r.at[source, high]))
        n = links.send(act_r.at[source, last], act_r.at[source, low], pix=spot.after)
        arrivals.append((n, act_r.at[source, low]))
    for n, dst in arrivals:
        links.arrive(n, dst)
    pre = jnp.zeros((OWN, MID_OWN), F32)
    for a in range(3):
        rows = slice(section_rate * a, section_rate * a + OWN_ROWS)
        window = jnp.concatenate(
            [act_r[c, rows].reshape(OWN, MID_OWN) for c in range(CHAN)], axis=1
        )
        terms = [dot_nn(window, wd[3 * a + b]) for b in range(3)]
        term = terms[1] + col_shift(terms[0], -section_rate) + col_shift(terms[2], section_rate)
        pre = pre + (term if a == 1 else term * keep[a // 2])

    unit, normed, inv_d = norm(pre, near_m.at[1], across_m.at[1], gain_d[...], bias_d[...])
    unit_d[...] = unit
    inv_mid[...] = jnp.concatenate([inv_r, inv_d, jnp.zeros((6, MID_OWN), F32)], axis=0)
    act_d[j] = silu(normed).astype(BF16)
    sent = {d: links.send(act_d.at[j], act_d.at[j], chan=spot.chan(d)) for d in (2, 1, 3)}
    for d in (1, 3, 2):
        links.arrive(sent[d], act_d.at[spot.chan(-d)])
    full = jnp.concatenate([act_d[c] for c in range(CHAN)], axis=1)
    unit, normed, inv_e = norm(
        dot_nn(full, we[...]), near_f, across_f, gain_e[...], bias_e[...]
    )
    unit_e[...] = unit
    inv_feat[...] = jnp.concatenate([inv_e, jnp.zeros((7, FEAT_OWN), F32)], axis=0)
    out = silu(normed + pixels[...].astype(F32)).astype(BF16)
    trunk[...] = out.reshape(OWN_ROWS, TILE_W, FEAT_OWN)
    for d in (1, 3, 2):
        links.arrive(project_sent[d], project_all.at[spot.chan(-d), 1 - spot.core])
    project_all[j] = project_out[j]
    for part in halves:
        links.arrive(maps_sent[part.start], maps_in.at[spot.chan(2), part])
    for s in range(OWN_ROWS):
        target, (away, here) = map_send(s)
        pl.when(target != i)(lambda: away().wait_send())
    links.finish()


def section_forward(*operands):
    whole = pl.BlockSpec(memory_space=pltpu.VMEM)
    shape = jax.ShapeDtypeStruct
    mid, feat = (OWN, MID_OWN), (OWN, FEAT_OWN)
    dma = pltpu.SemaphoreType.DMA
    return pl.pallas_call(
        section_forward_kernel,
        in_specs=[pl.BlockSpec(memory_space=pltpu.SMEM)] * 2 + [whole] * 12,
        out_specs=[whole] * 11,
        out_shape=[
            shape((OWN_ROWS, TILE_W, FEAT_OWN), BF16),
            shape(mid, F32),
            shape(mid, F32),
            shape(feat, F32),
            shape((CHAN, OWN_ROWS + 2 * section_rate, TILE_W, MID_OWN), BF16),
            shape((CHAN, *mid), BF16),
            shape((CHAN, FEAT_OWN, MID_OWN), BF16),
            shape((8, MID_OWN), F32),
            shape((8, FEAT_OWN), F32),
            shape((CHAN, 3, TASKS, HEAD, 2 * HEAD), BF16),
            shape((CHAN, OWN_ROWS, TILE_W, BRANCH), BF16),
        ],
        scratch_shapes=[
            pltpu.VMEM((2, OWN, MID_OWN), F32),
            pltpu.VMEM((CHAN, 3, TASKS, HEAD, 2 * HEAD), BF16),
            pltpu.VMEM((3, *mid), BF16),
            pltpu.VMEM((3, *mid), BF16),
            pltpu.VMEM((2, GROUP, 8, MID_OWN), F32),
            pltpu.VMEM((2, 4, 8, MID_OWN), F32),
            pltpu.VMEM((GROUP, 8, FEAT_OWN), F32),
            pltpu.VMEM((4, 8, FEAT_OWN), F32),
            pltpu.VMEM((OWN_ROWS, TILE_W, BRANCH), BF16),
            dma((72,)),
            dma((72,)),
            dma((OWN_ROWS,)),
            dma((OWN_ROWS,)),
        ],
        compiler_params=pltpu.CompilerParams(
            collective_id=5, has_side_effects=True, vmem_limit_bytes=VMEM_LIMIT
        ),
        cost_estimate=pl.CostEstimate(
            flops=2_000_000_000, bytes_accessed=120_000_000, transcendentals=0
        ),
        name="section_forward",
    )(*operands)


class Scatter:
    def __init__(self, parts, mate_in, near, near_in, far, far_in, spot, links):
        self.parts, self.mate_in, self.near, self.near_in = parts, mate_in, near, near_in
        self.far, self.far_in, self.spot, self.links = far, far_in, spot, links

    def start(self):
        spot = self.spot
        self.sent = self.links.send(self.parts.at[1 - spot.core], self.mate_in, pix=spot.mate)

    def along_z(self):
        spot, links = self.spot, self.links
        links.arrive(self.sent, self.mate_in)
        for z in range(4):
            self.near[z] = (
                self.parts[spot.core, z].astype(F32) + self.mate_in[z].astype(F32)
            ).astype(BF16)
        self.sent = {
            d: links.send(
                self.near.at[spot.z_of(d)], self.near_in.at[d - 1], pix=spot.pix_in_z(d)
            )
            for d in (2, 1, 3)
        }

    def along_x(self):
        spot, links = self.spot, self.links
        total = self.near[spot.z].astype(F32)
        for d in (1, 3, 2):
            links.arrive(self.sent[d], self.near_in.at[d - 1])
            total = total + self.near_in[d - 1].astype(F32)
        self.far[...] = total.astype(BF16)
        self.sent = {
            d: links.send(self.far.at[spot.x_of(d)], self.far_in.at[d - 1], pix=spot.pix_in_x(d))
            for d in (2, 1, 3)
        }

    def finish(self):
        spot, links = self.spot, self.links
        total = self.far[spot.group].astype(F32)
        for d in (1, 3, 2):
            links.arrive(self.sent[d], self.far_in.at[d - 1])
            total = total + self.far_in[d - 1].astype(F32)
        return total


def scatter_scratch(*shape):
    return [
        pltpu.VMEM((2, 4, 4, *shape), BF16),
        pltpu.VMEM((4, 4, *shape), BF16),
        pltpu.VMEM((4, 4, *shape), BF16),
        pltpu.VMEM((3, 4, *shape), BF16),
        pltpu.VMEM((4, *shape), BF16),
        pltpu.VMEM((3, *shape), BF16),
    ]


def spot_of(device):
    return device % 2, device % GROUP // 2, device // GROUP


def section_backward_kernel(
    tiles, trunk_grad, pixels, unit_r, unit_d, unit_e, act_r, act_d, wr_all, wd, we,
    gain_r, bias_r, gain_d, bias_d, gain_e, bias_e, inv_mid, inv_feat, mean_rows, projects, x_group,
    g_group, *refs,
):
    (
        grad_pixels, grad_reduce, grad_gain_r, grad_bias_r, grad_dilate, grad_gain_d, grad_bias_d,
        grad_expand, grad_gain_e, grad_bias_e, grad_point, grad_atrous, grad_project,
    ) = refs[:13]
    scratch = refs[13:]
    (
        keys, keep, wd_cat, side_out, side_in, halo, taps, full, project_in, project_wide, reduce_out,
        near_m, across_m, near_f, across_f, x_all, x_base, x_now, g_all, g_now,
    ) = scratch[:20]
    send_sems, recv_sems, ss_reduce, rs_reduce, load_sems, edge_sems = scratch[-6:]
    buffers = scratch[20:-6]
    spot = Spot()
    links = Links(send_sems, recv_sems)
    i, j = spot.i, spot.j
    by_expand, by_dilate, by_project, by_reduce = [
        Scatter(*buffers[6 * n : 6 * n + 6], spot, links) for n in range(4)
    ]
    owner_i, owner_j = GROUP * j + int_div(i, 4), int_rem(i, 4)
    maker_i, maker_j = 4 * int_rem(i, GROUP) + j, spot.group
    stays = (owner_i == i) & (owner_j == j)
    barrier = pltpu.get_barrier_semaphore()

    @pl.when(jnp.logical_not(stays))
    def _():
        signal(barrier, pix=maker_i, chan=maker_j)

    peers = [{"chan": spot.chan(d)} for d in (1, 2, 3)] + spot.sum_peers()
    peers += [{"pix": spot.before}, {"pix": spot.after}]

    def core_rows(z, core, first=0):
        return pl.ds(first + OWN_ROWS * (2 * z + core), OWN_ROWS)

    def shares(core):
        pairs = []
        for z in range(4):
            rows, moved = core_rows(z, core), core_rows(z, core, REACH)
            pairs.append((x_group.at[:, rows], x_all.at[:, rows]))
            pairs.append((g_group.at[rows], g_all.at[moved]))
        return pairs

    loads = [
        pltpu.make_async_copy(src, dst, load_sems.at[n])
        for n, (src, dst) in enumerate(shares(spot.core))
    ]

    def prepare():
        for load in loads:
            load.start()
        fill_keep(tiles, keep, i)
        fill_keys(tiles, keys, GROUP_ROWS * spot.group - REACH, GROUP_ROWS + 2 * REACH)
        for tap in range(9):
            wd_cat[:, MID_OWN * tap : MID_OWN * (tap + 1)] = wd[tap]

    for step in (1, -1):
        x_maker = int_rem(spot.group + 4 - step, 4)
        maker_core = (1 + step) // 2
        peers.append({"pix": GROUP * x_maker + 2 * spot.z + maker_core})
    peers.append({"pix": spot.mate})
    greet(peers, 1 - stays.astype(jnp.int32), prepare)

    atrous_sum = GroupSum(*buffers[24:27], spot, links)
    point_sum = GroupSum(*buffers[27:30], spot, links)
    x_target = int_rem(spot.group + 3 + 2 * spot.core, 4)

    def edge_copy(core):
        return remote(
            g_group.at[pl.ds(spot.core * (GROUP_ROWS - REACH), REACH)],
            g_all.at[pl.ds((1 - spot.core) * (GROUP_ROWS + REACH), REACH)],
            edge_sems.at[core],
            edge_sems.at[2 + 1 - spot.core],
            pix=GROUP * x_target + 2 * spot.z + core,
        )

    def edge_arrival(high):
        dst = g_all.at[pl.ds(high * (GROUP_ROWS + REACH), REACH)]
        return remote(dst, dst, edge_sems.at[0], edge_sems.at[2 + high], chan=spot.chan(1))

    for core in range(2):
        edge_copy(core).start()
    mates = [links.send(src, dst, pix=spot.mate) for src, dst in shares(spot.core)]

    def row_block(r):
        return pl.ds(pl.multiple_of(r * TILE_W, TILE_W), TILE_W)

    def take():
        for load in loads:
            load.wait()
        for n, (_, dst) in zip(mates, shares(1 - spot.core)):
            links.arrive(n, dst)
        for high in range(2):
            edge_arrival(high).wait_recv()

        def one_row(r, carry):
            is_low = lax.broadcasted_iota(jnp.int32, (TILE_W, 2 * HEAD), 1) < HEAD
            for pair in range(2):
                first = x_all[2 * pair, r].astype(F32)
                second = x_all[2 * pair + 1, r].astype(F32)
                lower = jnp.where(is_low, first, pltpu.roll(second, HEAD, 1))
                upper = jnp.where(is_low, pltpu.roll(first, HEAD, 1), second)
                x_base[row_block(r), 2 * HEAD * pair : 2 * HEAD * (pair + 1)] = jnp.where(
                    spot.core == 0, lower, upper
                ).astype(BF16)
            return carry

        lax.fori_loop(0, GROUP_ROWS, one_row, 0, unroll=4)

    def pick(which):
        def one_row(r, carry):
            pieces = []
            for a in range(3):
                piece = g_all[
                    r + REACH - (a - 1) * (which + 1), :, BRANCH * which : BRANCH * (which + 1)
                ]
                same = keys[r + REACH] == keys[r + REACH - (a - 1) * (which + 1)]
                pieces.append(jnp.where(same, piece, jnp.zeros_like(piece)))
            g_now[row_block(r)] = jnp.concatenate(pieces, axis=1)
            return carry

        lax.fori_loop(0, GROUP_ROWS, one_row, 0, unroll=4)

    def multiply(which, b):
        held = x_base
        if b != 1:
            held = x_now

            def one_row(r, carry):
                row = x_base[row_block(r)].astype(F32)
                x_now[row_block(r)] = col_shift(row, (b - 1) * head_rates[which]).astype(BF16)
                return carry

            lax.fori_loop(0, GROUP_ROWS, one_row, 0, unroll=4)
        product = dot_tn(g_now[...], held[...]).T.astype(BF16)
        n = 3 * which + b
        for c in range(CHAN):
            atrous_sum.out[n, c] = product[HEAD * c : HEAD * (c + 1)]
        atrous_sum.ready.append((n, 1 if n % 2 else -1))

    def multiply_point():
        grads = g_all[REACH : REACH + GROUP_ROWS, :, 3 * BRANCH :].reshape(-1, BRANCH)
        product = dot_tn(grads, x_base[...]).T.astype(BF16)
        for c in range(CHAN):
            point_sum.out[0, c] = product[HEAD * c : HEAD * (c + 1)]
        point_sum.ready.append((0, 1))

    tasks = [lambda: None, lambda: None, take]
    for which in range(3):
        tasks.append(functools.partial(pick, which))
        tasks += [functools.partial(multiply, which, b) for b in range(3)]
    tasks += [multiply_point]
    queue = iter(tasks)

    def flush():
        atrous_sum.flush()
        point_sum.flush()

    def meanwhile(count=1):
        for _ in range(count):
            task = next(queue, None)
            if task is not None:
                task()

    project_sent = {
        d: links.send(projects.at[spot.chan(d)], project_in.at[d - 1], chan=spot.chan(d))
        for d in (2, 1, 3)
    }

    def norm_back(grad, unit, near, across, scale):
        sums = sum_over_pix(two_sums(grad, grad * unit), near, across, spot, links, meanwhile)
        pre = scale * (grad - sums[0:1] / PIXELS - unit * (sums[1:2] / PIXELS))
        return pre.astype(BF16), sums

    grad_trunk = trunk_grad[...].astype(F32) + mean_rows[...][:, None, :]
    grad_trunk = grad_trunk.reshape(OWN, FEAT_OWN)
    unit = unit_e[...]
    summed = unit * gain_e[...] + bias_e[...] + pixels[...].astype(F32)
    grad_summed = grad_trunk * slope(summed)
    g_expand, sums = norm_back(grad_summed, unit, near_f, across_f, gain_e[...] * inv_feat[0:1])
    grad_bias_e[...] = sums[0:1]
    grad_gain_e[...] = sums[1:2]

    def sides(turn, make):
        sent = {}
        for d in (2, 1, 3):
            side_out[turn, d - 1] = make(spot.chan(d)).astype(BF16)
            sent[d] = links.send(
                side_out.at[turn, d - 1], side_in.at[turn, d - 1], chan=spot.chan(d)
            )
        return sent

    def side_sum(turn, own, sent):
        for d in (1, 3, 2):
            links.arrive(sent[d], side_in.at[turn, d - 1])
            own = own + side_in[turn, d - 1].astype(F32)
        return own

    def mid_rows(chan):
        return pl.ds(pl.multiple_of(MID_OWN * chan, MID_OWN), MID_OWN)

    sent = sides(0, lambda c: dot_nt(g_expand, we[mid_rows(c)]))
    own = dot_nt(g_expand, we[mid_rows(j)])
    part = 16
    for c in range(CHAN):
        grads = dot_tn(act_d[c], g_expand).astype(BF16)
        for n in range(8):
            by_expand.parts[spot_of(8 * c + n)] = grads[part * n : part * (n + 1)]
    by_expand.start()
    flush()
    meanwhile(3)
    grad_act = side_sum(0, own, sent)

    unit = unit_d[...]
    grad = grad_act * slope(unit * gain_d[...] + bias_d[...])
    g_dilate, sums = norm_back(
        grad, unit, near_m.at[0], across_m.at[0], gain_d[...] * inv_mid[1:2]
    )
    grad_bias_d[...] = sums[0:1]
    grad_gain_d[...] = sums[1:2]
    own_rows = slice(section_rate, section_rate + OWN_ROWS)
    halo[own_rows] = g_dilate.reshape(OWN_ROWS, TILE_W, MID_OWN)
    low, high = slice(0, section_rate), slice(section_rate + OWN_ROWS, 2 * section_rate + OWN_ROWS)
    first, last = slice(section_rate, 2 * section_rate), slice(OWN_ROWS, section_rate + OWN_ROWS)
    to_before = links.send(halo.at[first], halo.at[high], pix=spot.before)
    to_after = links.send(halo.at[last], halo.at[low], pix=spot.after)
    by_expand.along_z()
    flush()
    meanwhile()
    for d in (1, 3, 2):
        links.arrive(project_sent[d], project_in.at[d - 1])
        project_wide[spot.chan(-d)] = project_in[d - 1].astype(F32)
    project_wide[j] = projects[j].astype(F32)
    links.arrive(to_before, halo.at[high])
    links.arrive(to_after, halo.at[low])
    for a in range(3):
        rows = halo[section_rate * (2 - a) : section_rate * (2 - a) + OWN_ROWS]
        rows = rows.reshape(OWN, MID_OWN).astype(F32)
        if a != 1:
            rows = rows * keep[1 - a // 2]
        for b in range(3):
            moved = rows if b == 1 else col_shift(rows, -section_rate * (b - 1))
            tap = 3 * a + b
            taps[:, MID_OWN * tap : MID_OWN * (tap + 1)] = moved.astype(BF16)
    sent = sides(1, lambda c: dot_nt(taps[...], wd_cat[mid_rows(c)]))
    own = dot_nt(taps[...], wd_cat[mid_rows(j)])
    for c in range(CHAN):
        act = act_r[c, own_rows].reshape(OWN, MID_OWN)
        grads = dot_tn(act, taps[...]).astype(BF16)
        for n in range(8):
            for tap in range(9):
                by_dilate.parts[(*spot_of(8 * c + n), tap)] = grads[
                    part * n : part * (n + 1), MID_OWN * tap : MID_OWN * (tap + 1)
                ]
    by_dilate.start()
    flush()
    meanwhile(2)
    grad_act = side_sum(1, own, sent)
    by_expand.along_x()

    unit = unit_r[...]
    grad = grad_act * slope(unit * gain_r[...] + bias_r[...])
    g_reduce, sums = norm_back(
        grad, unit, near_m.at[1], across_m.at[1], gain_r[...] * inv_mid[0:1]
    )
    grad_bias_r[...] = sums[0:1]
    grad_gain_r[...] = sums[1:2]
    full[j] = g_reduce
    sent = {d: links.send(full.at[j], full.at[j], chan=spot.chan(d)) for d in (2, 1, 3)}
    by_dilate.along_z()
    flush()
    for t in range(TASKS):
        for device in range(PIX):
            rows = []
            for start in range(40 * device, 40 * device + 40, 8):
                b, src, d = start // 256, start // HEAD % CHAN, start % HEAD
                rows.append(project_wide[src, BRANCH_PLACE[b], t, d : d + 8])
            rows.append(jnp.zeros((8, HEAD), F32))
            by_project.parts[(*spot_of(device), t)] = jnp.concatenate(rows, axis=0).astype(BF16)
    by_project.start()
    grad_expand[...] = by_expand.finish()
    meanwhile(2)
    for d in (1, 3, 2):
        links.arrive(sent[d], full.at[spot.chan(-d)])
    g_reduce = jnp.concatenate([full[c] for c in range(CHAN)], axis=1)
    weight = jnp.concatenate([wr_all[c] for c in range(CHAN)], axis=1)
    grads = dot_tn(pixels[...], g_reduce).astype(BF16)
    for c in range(CHAN):
        for n in range(8):
            by_reduce.parts[spot_of(4 * n + c)] = grads[
                HEAD * n : HEAD * (n + 1), MID_OWN * c : MID_OWN * (c + 1)
            ]
    by_reduce.start()
    grad_pixels[...] = (grad_summed + dot_nt(g_reduce, weight)).astype(BF16)
    by_reduce.along_z()
    by_project.along_z()
    meanwhile(2)
    by_reduce.along_x()
    flush()
    by_dilate.along_x()
    meanwhile(len(tasks))
    by_project.along_x()
    flush()
    reduce_out[...] = by_reduce.finish()

    def reduce_copies():
        return (
            lambda: remote(
                reduce_out, grad_reduce, ss_reduce.at[0], rs_reduce.at[0], pix=owner_i, chan=owner_j
            ),
            lambda: pltpu.make_async_copy(reduce_out, grad_reduce, rs_reduce.at[0]),
        )

    away, here = reduce_copies()
    pl.when(jnp.logical_not(stays))(lambda: away().start())
    pl.when(stays)(lambda: here().start())
    flush()
    grad_dilate[...] = by_dilate.finish()
    grad_project[...] = by_project.finish()[:, :40]

    def place(n, total):
        which, b = n // 3, n % 3
        for a in range(3):
            for t in range(TASKS):
                lane = BRANCH * a + HEAD * t
                grad_atrous[t, which, 3 * a + b] = total[:, lane : lane + HEAD]

    def place_point(n, total):
        for t in range(TASKS):
            grad_point[t] = total[:, HEAD * t : HEAD * (t + 1)]

    atrous_sum.finish(place)
    point_sum.finish(place_point)
    for core in range(2):
        edge_copy(core).wait_send()

    pltpu.make_async_copy(reduce_out, grad_reduce, rs_reduce.at[0]).wait()
    pl.when(jnp.logical_not(stays))(lambda: away().wait_send())
    links.finish()


def group_scratch(count, *shape):
    return [
        pltpu.VMEM((count, 4, *shape), BF16),
        pltpu.VMEM((count, *shape), BF16),
        pltpu.VMEM((count, 2, *shape), BF16),
    ]


def section_backward(*operands):
    whole = pl.BlockSpec(memory_space=pltpu.VMEM)
    shape = jax.ShapeDtypeStruct
    dma = pltpu.SemaphoreType.DMA
    mid, feat = (OWN, MID_OWN), (OWN, FEAT_OWN)
    return pl.pallas_call(
        section_backward_kernel,
        in_specs=[pl.BlockSpec(memory_space=pltpu.SMEM)]
        + [whole] * 20
        + [pl.BlockSpec(memory_space=pl.ANY)] * 2,
        out_specs=[whole] * 13,
        out_shape=[
            shape(feat, BF16),
            shape((HEAD, MID_OWN), F32),
            shape((1, MID_OWN), F32),
            shape((1, MID_OWN), F32),
            shape((9, 16, MID_OWN), F32),
            shape((1, MID_OWN), F32),
            shape((1, MID_OWN), F32),
            shape((16, FEAT_OWN), F32),
            shape((1, FEAT_OWN), F32),
            shape((1, FEAT_OWN), F32),
            shape((TASKS, HEAD, HEAD), F32),
            shape((TASKS, 3, 9, HEAD, HEAD), F32),
            shape((TASKS, 40, HEAD), F32),
        ],
        scratch_shapes=[
            pltpu.SMEM((GROUP_ROWS + 2 * REACH,), jnp.int32),
            pltpu.VMEM((2, OWN, MID_OWN), F32),
            pltpu.VMEM((FEAT_OWN, 9 * MID_OWN), BF16),
            pltpu.VMEM((2, 3, *mid), BF16),
            pltpu.VMEM((2, 3, *mid), BF16),
            pltpu.VMEM((OWN_ROWS + 2 * section_rate, TILE_W, MID_OWN), BF16),
            pltpu.VMEM((OWN, 9 * MID_OWN), BF16),
            pltpu.VMEM((CHAN, *mid), BF16),
            pltpu.VMEM((3, 5, TASKS, HEAD, HEAD), BF16),
            pltpu.VMEM((CHAN, 5, TASKS, HEAD, HEAD), F32),
            pltpu.VMEM((HEAD, MID_OWN), F32),
            pltpu.VMEM((2, GROUP, 8, MID_OWN), F32),
            pltpu.VMEM((2, 4, 8, MID_OWN), F32),
            pltpu.VMEM((GROUP, 8, FEAT_OWN), F32),
            pltpu.VMEM((4, 8, FEAT_OWN), F32),
            pltpu.VMEM((CHAN, GROUP_ROWS, TILE_W, 128), BF16),
            pltpu.VMEM((GROUP_ROWS * TILE_W, 256), BF16),
            pltpu.VMEM((GROUP_ROWS * TILE_W, 256), BF16),
            pltpu.VMEM((GROUP_ROWS + 2 * REACH, TILE_W, 4 * BRANCH), BF16),
            pltpu.VMEM((GROUP_ROWS * TILE_W, 3 * BRANCH), BF16),
            *scatter_scratch(16, FEAT_OWN),
            *scatter_scratch(9, 16, MID_OWN),
            *scatter_scratch(TASKS, 48, HEAD),
            *scatter_scratch(HEAD, MID_OWN),
            *group_scratch(9, HEAD, 3 * BRANCH),
            *group_scratch(1, HEAD, BRANCH),
            dma((112,)),
            dma((112,)),
            dma((1,)),
            dma((1,)),
            dma((8,)),
            dma((4,)),
        ],
        compiler_params=pltpu.CompilerParams(
            collective_id=6, has_side_effects=True, vmem_limit_bytes=VMEM_LIMIT
        ),
        cost_estimate=pl.CostEstimate(
            flops=16_000_000_000, bytes_accessed=250_000_000, transcendentals=0
        ),
        name="section_backward",
    )(*operands)


def hand_out_kernel(maps, tall, mean_all, *refs):
    count = (len(refs) - 3) // 2
    grads, (task_maps, grad_pooled), outs, sems = (
        refs[:count], refs[count : count + 2], refs[count + 2 : -1], refs[-1],
    )
    copies = [pltpu.make_async_copy(src, dst, sems.at[n]) for n, (src, dst) in enumerate(zip(grads, outs))]
    for copy in copies:
        copy.start()
    for c in range(CHAN):
        part = dot_tn(tall[...], mean_all[c])
        for t in range(TASKS):
            grad_pooled[t, :, 512 * c : 512 * (c + 1)] = part[HEAD * t : HEAD * (t + 1)]
    for t in range(TASKS):
        task_maps[t] = maps[t].reshape(OWN, HEAD).astype(F32).T.astype(BF16)
    for copy in copies:
        copy.wait()


def hand_out(maps, pooled_grad, mean_all, *grads):
    whole = pl.BlockSpec(memory_space=pltpu.VMEM)
    shape = jax.ShapeDtypeStruct
    return pl.pallas_call(
        hand_out_kernel,
        in_specs=[whole] * 3 + [pl.BlockSpec(memory_space=pl.ANY)] * len(grads),
        out_specs=[whole] * 2 + [pl.BlockSpec(memory_space=pl.ANY)] * len(grads),
        out_shape=[shape((TASKS, HEAD, OWN), BF16), shape((TASKS, HEAD, CHAN * 512), F32)]
        + [shape(grad.shape, grad.dtype) for grad in grads],
        scratch_shapes=[pltpu.SemaphoreType.DMA((len(grads),))],
        compiler_params=pltpu.CompilerParams(vmem_limit_bytes=VMEM_LIMIT),
        cost_estimate=pl.CostEstimate(flops=0, bytes_accessed=10_000_000, transcendentals=0),
        name="hand_out",
    )(maps, pooled_grad, mean_all, *grads)


def shards(
    pixels,
    tile_number,
    task_draws,
    reduce_weight,
    reduce_gain,
    reduce_bias,
    dilate_weight,
    dilate_gain,
    dilate_bias,
    expand_weight,
    expand_gain,
    expand_bias,
    point_weight,
    atrous_weight,
    pooled_weight,
    project_weight,
    cotangent,
):
    tile_grid = tile_number.reshape(2, 128)
    norms = [
        v.reshape(1, -1)
        for v in (reduce_gain, reduce_bias, dilate_gain, dilate_bias, expand_gain, expand_bias)
    ]
    pooled_rows = pooled_weight.reshape(BRANCH, -1)
    (
        trunk, unit_reduce, unit_dilate, unit_expand, act_reduce, act_dilate, reduce_all, inv_mid,
        inv_feat, project_all, maps_all,
    ) = section_forward(
        tile_number, task_draws, pixels, reduce_weight, dilate_weight, expand_weight, *norms,
        project_weight, jnp.swapaxes(cotangent, 1, 2),
    )
    kernels = atrous_weight.reshape(TASKS, 3, 3, 3, HEAD, -1)
    grad_project, x_group, mean_all, trunk_grad, g_group, maps, mean_rows, pooled_grad = heads(
        tile_number, tile_grid, trunk, maps_all, kernels, point_weight, project_all, pooled_rows, kernels
    )
    grads = section_backward(
        tile_number, trunk_grad, pixels, unit_reduce, unit_dilate, unit_expand, act_reduce, act_dilate,
        reduce_all, dilate_weight, expand_weight, *norms, inv_mid, inv_feat, mean_rows, grad_project,
        x_group, g_group,
    )
    (
        task_maps, grad_pooled, grad_pixels, grad_reduce, grad_gain_r, grad_bias_r, grad_dilate,
        grad_gain_d, grad_bias_d, grad_expand, grad_gain_e, grad_bias_e, grad_point, grad_atrous,
        grad_project,
    ) = hand_out(maps, pooled_grad, mean_all, *grads)
    return (
        jnp.swapaxes(task_maps, 1, 2),
        grad_pixels,
        grad_reduce,
        grad_gain_r[0],
        grad_bias_r[0],
        grad_dilate,
        grad_gain_d[0],
        grad_bias_d[0],
        grad_expand,
        grad_gain_e[0],
        grad_bias_e[0],
        grad_point,
        grad_atrous,
        jnp.swapaxes(grad_pooled, 1, 2),
        grad_project,
    )


def solution(mesh):
    placed = (
        P("pix", "chan"),
        P(),
        P(),
        P(None, "chan"),
        P("chan"),
        P("chan"),
        P(None, None, "chan"),
        P("chan"),
        P("chan"),
        P(None, "chan"),
        P("chan"),
        P("chan"),
        P(None, "chan", None),
        P(None, None, None, "chan", None),
        P(None, "chan", None),
        P(None, "chan", None),
        P(None, "pix", "chan"),
    )
    return jax.shard_map(
        shards,
        mesh=mesh,
        in_specs=placed,
        out_specs=(
            P(None, "pix", "chan"),
            P("pix", "chan"),
            P("pix", "chan"),
            P("chan"),
            P("chan"),
            P(None, "pix", "chan"),
            P("chan"),
            P("chan"),
            P("pix", "chan"),
            P("chan"),
            P("chan"),
            P(None, "pix", "chan"),
            P(None, None, None, "pix", "chan"),
            P(None, None, "chan"),
            P(None, "pix", "chan"),
        ),
        check_vma=False,
    )
```

```python
import functools

import jax
import jax.numpy as jnp
from jax import lax
from jax.experimental import pallas as pl
from jax.experimental.pallas import tpu as pltpu
from jax.sharding import PartitionSpec as P

TASKS = 3
TILE_W = 64
NROWS = 256
PIX = 32
CHAN = 4
OWN_ROWS = NROWS // PIX
REACH = 3
EXT_ROWS = OWN_ROWS + 2 * REACH
HEAD = 64
BRANCH = TASKS * HEAD
BRANCH_ORDER = (1, 2, 3, 0, 4)
BRANCH_PLACE = (3, 0, 1, 2, 4)

F32 = jnp.float32
BF16 = jnp.bfloat16
MESH = pl.DeviceIdType.MESH
eps = 1e-05
section_rate = 4
head_rates = (6, 12, 18)
VMEM_LIMIT = 60 * 2**20


def int_div(a, b):
    if b & (b - 1) == 0:
        return lax.shift_right_logical(a, jnp.int32(b.bit_length() - 1))
    return lax.shift_right_logical(a * (2**16 // b + 1), jnp.int32(16))


def int_rem(a, b):
    return a - b * int_div(a, b)


def place_of(row):
    kind = int_rem(row, 6)
    return 43 * kind - int_div(kind, 5) + int_div(row, 6)


def row_of(place):
    kind = int_div(place + int_div(place, 214), 43)
    return 6 * (place - 43 * kind + int_div(kind, 5)) + kind


def tile_at(tiles, row):
    return jnp.where((row >= 0) & (row < NROWS), tiles[jnp.clip(row, 0, NROWS - 1)], -1)


def fill_keys(tiles, keys, first, count):
    start = row_of(jnp.maximum(first, 0))

    def one(n, carry):
        row, kind = carry
        inside = (first + n >= 0) & (first + n < NROWS)
        keys[n] = jnp.where(inside, tiles[row] + 8 * kind, -1)
        end = row + 6 >= NROWS
        next_kind = jnp.where(end, jnp.minimum(kind + 1, 5), kind)
        next_row = jnp.where(end, next_kind, row + 6)
        return jnp.where(inside, next_row, row), jnp.where(inside, next_kind, kind)

    lax.fori_loop(0, count, one, (start, int_rem(start, 6)))


def fill_keep(tiles, keep, i):
    for r in range(OWN_ROWS):
        here = tile_at(tiles, OWN_ROWS * i + r)
        for side, step in enumerate((-section_rate, section_rate)):
            same = jnp.where(tile_at(tiles, OWN_ROWS * i + r + step) == here, 1.0, 0.0)
            keep[side, TILE_W * r : TILE_W * (r + 1)] = jnp.full((TILE_W, 128), same, F32)


def rows_at(value, tile):
    row = lax.broadcasted_iota(jnp.int32, value.shape, 0)
    return jnp.sum(jnp.where(row == tile, value, 0.0), axis=0, keepdims=True)


def add_at(sums, row, tile):
    return sums + jnp.where(lax.broadcasted_iota(jnp.int32, sums.shape, 0) == tile, row, 0.0)


def tile_sizes(grid):
    sizes = jnp.zeros((8, 128), F32)
    for tile in range(8):
        here = jnp.sum(jnp.where(grid == tile, 1.0, 0.0), axis=1, keepdims=True)
        sizes = add_at(sizes, TILE_W * jnp.sum(here, axis=0, keepdims=True), tile)
    return jnp.maximum(sizes, 1.0)


def signal(sem, **where):
    pl.semaphore_signal(sem, inc=1, device_id=where, device_id_type=MESH)


def remote(src, dst, send_sem, recv_sem, **where):
    return pltpu.make_async_remote_copy(
        src_ref=src,
        dst_ref=dst,
        send_sem=send_sem,
        recv_sem=recv_sem,
        device_id=where,
        device_id_type=MESH,
    )


def greet_origins(i):
    barrier, expected = pltpu.get_barrier_semaphore(), 0
    for s in range(OWN_ROWS):
        origin = int_div(row_of(OWN_ROWS * i + s), OWN_ROWS)

        @pl.when(origin != i)
        def _():
            signal(barrier, pix=origin)

        target = int_div(place_of(OWN_ROWS * i + s), OWN_ROWS)
        expected = expected + (target != i).astype(jnp.int32)
    return expected


class RowGather:
    def __init__(self, reach, src, out, spot, sems):
        self.reach, self.src, self.out, self.spot = reach, src, out, spot
        (
            self.ss_row, self.rs_row, self.ss_side, self.rs_side, self.ss_far, self.rs_far, self.ss_halo,
            self.rs_halo,
        ) = sems
        self.order = (0, 7, 1, 6, 2, 5, 3, 4)
        self.edge = [s for s in self.order if s < reach or s >= OWN_ROWS - reach]

    def row_send(self, s):
        place = place_of(OWN_ROWS * self.spot.i + s)
        target, slot = int_div(place, OWN_ROWS), int_rem(place, OWN_ROWS)
        src, landing = self.src.at[s], self.out.at[self.spot.j, self.reach + slot]
        return target, (
            lambda: remote(src, landing, self.ss_row.at[s], self.rs_row.at[slot], pix=target),
            lambda: pltpu.make_async_copy(src, landing, self.rs_row.at[slot]),
        )

    def block(self, chan, s):
        return self.out.at[chan, self.reach + s]

    def side(self, way):
        return self.spot.chan((1, -1)[way])

    def side_copy(self, way, s, chan):
        block = self.block(chan, s)
        return remote(
            block, block, self.ss_side.at[way, s], self.rs_side.at[way, s], chan=self.side(way)
        )

    def far_way(self, s):
        return 0 if s < OWN_ROWS // 2 else 1

    def far_copy(self, s, chan):
        block = self.block(chan, s)
        return remote(
            block, block, self.ss_far.at[s], self.rs_far.at[s], chan=self.side(self.far_way(s))
        )

    def halo_copy(self, turn, chan, s):
        reach = self.reach
        if s < reach:
            lane, slot, target = s, reach + OWN_ROWS + s, self.spot.before
        else:
            lane, slot, target = s - OWN_ROWS + 2 * reach, s - OWN_ROWS + reach, self.spot.after
        return remote(
            self.block(chan, s),
            self.out.at[chan, slot],
            self.ss_halo.at[turn, lane],
            self.rs_halo.at[chan, lane],
            pix=target,
        )

    def halo_arrival(self, chan, lane):
        slot = self.reach + OWN_ROWS + lane if lane < self.reach else lane - self.reach
        dst = self.out.at[chan, slot]
        return remote(
            dst, dst, self.ss_halo.at[0, lane], self.rs_halo.at[chan, lane], pix=self.spot.after
        )

    def send_rows(self):
        for s in range(OWN_ROWS):
            target, (away, here) = self.row_send(s)
            pl.when(target != self.spot.i)(lambda: away().start())
            pl.when(target == self.spot.i)(lambda: here().start())

    def pass_own(self):
        j = self.spot.j
        for s in self.order:
            pltpu.make_async_copy(self.src.at[s], self.block(j, s), self.rs_row.at[s]).wait()
            self.side_copy(0, s, j).start()
            self.side_copy(1, s, j).start()
            if s in self.edge:
                self.halo_copy(0, j, s).start()

    def pass_sides(self):
        for s in self.order:
            for way in range(2):
                chan = self.side(1 - way)
                self.side_copy(way, s, chan).wait_recv()
                if way == self.far_way(s):
                    self.far_copy(s, chan).start()
                if s in self.edge:
                    self.halo_copy(1 + way, chan, s).start()

    def pass_far(self):
        far = self.spot.chan(2)
        for s in self.order:
            self.far_copy(s, far).wait_recv()
            if s in self.edge:
                self.halo_copy(3, far, s).start()

    def await_halo(self, chan):
        for lane in range(2 * self.reach):
            self.halo_arrival(chan, lane).wait_recv()

    def drain(self):
        spot, far = self.spot, self.spot.chan(2)
        for s in range(OWN_ROWS):
            target, (away, here) = self.row_send(s)
            pl.when(target != spot.i)(lambda: away().wait_send())
            self.side_copy(0, s, spot.j).wait_send()
            self.side_copy(1, s, spot.j).wait_send()
            self.far_copy(s, self.side(1 - self.far_way(s))).wait_send()
        for turn, chan in enumerate((spot.j, self.side(1), self.side(0), far)):
            for s in self.edge:
                self.halo_copy(turn, chan, s).wait_send()


def gather_sems(reach):
    dma = pltpu.SemaphoreType.DMA
    return [
        dma((OWN_ROWS,)),
        dma((OWN_ROWS,)),
        dma((2, OWN_ROWS)),
        dma((2, OWN_ROWS)),
        dma((OWN_ROWS,)),
        dma((OWN_ROWS,)),
        dma((CHAN, 2 * reach)),
        dma((CHAN, 2 * reach)),
    ]


GROUP = 8
GROUP_ROWS = GROUP * OWN_ROWS


class Posts:
    def __init__(self, send_sems, recv_sems):
        self.send_sems, self.recv_sems, self.made = send_sems, recv_sems, []

    def copy(self, n, make):
        src, dst, where = make()
        return remote(src, dst, self.send_sems.at[n], self.recv_sems.at[n], **where)

    def post(self, make):
        n = len(self.made)
        self.made.append(make)
        self.copy(n, make).start()
        return n

    def arrive(self, n, dst):
        beside = {"chan": int_rem(lax.axis_index("chan") + 1, CHAN)}
        remote(dst, dst, self.send_sems.at[n], self.recv_sems.at[n], **beside).wait_recv()

    def finish(self):
        for n, make in enumerate(self.made):
            self.copy(n, make).wait_send()


def greet(peers, more=0, meanwhile=lambda: None):
    barrier = pltpu.get_barrier_semaphore()
    for where in peers:
        signal(barrier, **where)
    meanwhile()
    pl.semaphore_wait(barrier, len(peers) + more)


class Spot:
    def __init__(self):
        self.i, self.j = lax.axis_index("pix"), lax.axis_index("chan")
        self.group, self.k = int_div(self.i, GROUP), int_rem(self.i, GROUP)
        self.z, self.core = int_div(self.k, 2), int_rem(self.k, 2)
        self.before, self.after = int_rem(self.i + PIX - 1, PIX), int_rem(self.i + 1, PIX)
        self.mate = self.i + 1 - 2 * self.core

    def chan(self, distance):
        return int_rem(self.j + CHAN + distance, CHAN)

    def in_group(self, distance):
        return int_rem(self.k + GROUP + distance, GROUP)

    def pix_in_group(self, distance):
        return GROUP * self.group + self.in_group(distance)

    def x_of(self, distance):
        return int_rem(self.group + 4 + distance, 4)

    def pix_in_x(self, distance):
        return GROUP * self.x_of(distance) + self.k

    def z_of(self, distance):
        return int_rem(self.z + 4 + distance, 4)

    def pix_in_z(self, distance):
        return GROUP * self.group + 2 * self.z_of(distance) + self.core

    def sum_peers(self):
        return [{"pix": self.pix_in_group(d)} for d in range(1, GROUP)] + [
            {"pix": self.pix_in_x(d)} for d in range(1, 4)
        ]


def dot_nt(a, b):
    return lax.dot_general(a, b, (((1,), (1,)), ((), ())), preferred_element_type=F32)


def dot_tn(a, b):
    return lax.dot_general(a, b, (((0,), (0,)), ((), ())), preferred_element_type=F32)


def dot_nn(a, b):
    return jnp.dot(a, b, preferred_element_type=F32)


def slope(v):
    s = jax.nn.sigmoid(v)
    return s * (1.0 + v * (1.0 - s))


def silu(v):
    return v * jax.nn.sigmoid(v)


def order_at(turn, chan):
    ahead = jnp.where(turn == 0, 0, jnp.where(turn == 1, 3, jnp.where(turn == 2, 1, 2)))
    return int_rem(chan + ahead, CHAN)


def greet_returns(i):
    barrier, expected = pltpu.get_barrier_semaphore(), 0
    for s in range(OWN_ROWS):
        origin = int_div(place_of(OWN_ROWS * i + s), OWN_ROWS)

        @pl.when(origin != i)
        def _():
            signal(barrier, pix=origin)

        target = int_div(row_of(OWN_ROWS * i + s), OWN_ROWS)
        expected = expected + (target != i).astype(jnp.int32)
    return expected


PAD = 24
PADDED = PAD + TILE_W + PAD


def block_at(n, chan):
    ahead = jnp.where(n == 0, 2, jnp.where(n == 1, 1, jnp.where(n == 2, 3, 0)))
    return int_rem(chan + ahead, CHAN)


def heads_kernel(
    tiles, tile_grid, trunk, maps_in, kernel, point, project, pooled_weight, kernel_b,
    grad_project, x_group, mean_kept, trunk_grad, g_group, maps_out, mean_rows, tall,
    keys, mean_all, pooled, x, lhs, acc, pre, relay, spread, near, across, mid, parts, pool_rows, pre_pooled,
    wide, taps, acc_b, edges, head_in, maps_sum, out, out_in, out_sum, near_b, across_b, mean_out, mean_in,
    send_sems, recv_sems, own_sem, ss_row, rs_row, ss_side, rs_side, ss_back, rs_back, *gather,
):
    turn, rate = pl.program_id(0), pl.program_id(1)
    step = 3 * turn + rate
    n, grad_step = turn - 4, step - 12
    spot = Spot()
    posts = Posts(send_sems, recv_sems)
    rows = RowGather(REACH, trunk, x, spot, gather)
    i, j = spot.i, spot.j
    grad_pre, head_part = mid, parts
    blocks = (j, spot.chan(-1), spot.chan(1), spot.chan(2))
    relay_way = (1, 1, -1, -1)
    half_rows = OWN_ROWS // 2
    marks = {}

    low, high = edges.at[0], edges.at[1]

    def g_rows(distance, core, half=None):
        start = OWN_ROWS * (2 * spot.z_of(distance) + core)
        if half is None:
            return g_group.at[pl.ds(start, OWN_ROWS)]
        return g_group.at[pl.ds(start + half_rows * half, half_rows)]

    def g_copy():
        return pltpu.make_async_copy(mid, g_rows(0, spot.core), own_sem.at[1])

    def row_send(s):
        row = row_of(OWN_ROWS * i + s)
        target, slot = int_div(row, OWN_ROWS), int_rem(row, OWN_ROWS)
        return target, (
            lambda: remote(
                maps_sum.at[s], maps_out.at[:, slot], ss_row.at[s], rs_row.at[slot], pix=target
            ),
            lambda: pltpu.make_async_copy(
                maps_sum.at[s], maps_out.at[:, slot], rs_row.at[slot]
            ),
        )

    def widen(start, part):
        held = part[...].astype(F32)
        for which in range(3):
            for t in range(TASKS):
                lane = BRANCH * which + HEAD * t
                one = held[:, :, lane : lane + HEAD]
                wide[3 * t + which, start : start + held.shape[0], PAD : PAD + TILE_W] = (
                    jnp.concatenate([one, one], axis=2)
                )

    def start_grads():
        g_copy().start()
        marks["low"] = posts.post(
            lambda: (mid.at[OWN_ROWS - REACH :], low, {"pix": spot.after})
        )
        marks["high"] = posts.post(lambda: (mid.at[:REACH], high, {"pix": spot.before}))
        for d in (2, 1, 3):
            marks["head", d] = posts.post(
                lambda d=d: (parts.at[spot.chan(d)], head_in.at[d - 1], {"chan": spot.chan(d)})
            )
        for turn in range(2):
            for d in (1, -1):
                half = turn if d == 1 else 1 - turn
                marks["z", d, half] = posts.post(
                    lambda half=half, d=d: (
                        mid.at[half_rows * half : half_rows * (half + 1)],
                        g_rows(0, spot.core, half),
                        {"pix": spot.pix_in_z(d)},
                    )
                )
        sums = jnp.zeros((8, 256), F32)
        for r in range(OWN_ROWS):
            sums = add_at(sums, pool_rows[r : r + 1], tiles[row_of(OWN_ROWS * i + r)])
        near_b[spot.k] = sums
        for d in range(1, GROUP):
            marks["near b", d] = posts.post(
                lambda d=d: (near_b.at[spot.k], near_b.at[spot.k], {"pix": spot.pix_in_group(d)})
            )
        wide[...] = jnp.zeros_like(wide)
        widen(REACH, mid)

    def x_slice(distance, chan=slice(0, CHAN)):
        lanes = pl.ds(pl.multiple_of(128 * spot.z_of(distance), 128), 128)
        return x.at[chan, REACH : REACH + OWN_ROWS, :, lanes]

    def x_rows(distance, core, chan=slice(0, CHAN)):
        return x_group.at[chan, pl.ds(OWN_ROWS * (2 * spot.z_of(distance) + core), OWN_ROWS)]

    def own_copy():
        return pltpu.make_async_copy(x_slice(0), x_rows(0, spot.core), own_sem.at[0])

    def post_x(q):
        way = relay_way[q]
        marks["relay", q] = posts.post(
            lambda: (x_slice(2, blocks[q]), relay.at[q], {"pix": spot.pix_in_z(way)})
        )
        for d in (1, -1):
            marks["x", d, q] = posts.post(
                lambda d=d: (
                    x_slice(d, blocks[q]), x_rows(0, spot.core, blocks[q]), {"pix": spot.pix_in_z(d)}
                )
            )

    def pass_x(q):
        way = relay_way[q]
        posts.arrive(marks["relay", q], relay.at[q])
        marks["far", q] = posts.post(
            lambda: (relay.at[q], x_rows(-way, spot.core, blocks[q]), {"pix": spot.pix_in_z(way)})
        )

    @pl.when(step == 0)
    def _():
        expected = greet_origins(i) + greet_returns(i)

        def prepare():
            fill_keys(tiles, keys, OWN_ROWS * i - REACH, EXT_ROWS)
            spread[...] = jnp.zeros_like(spread)
            for which, b in enumerate(BRANCH_ORDER):
                for c in range(CHAN):
                    for t in range(TASKS):
                        start = BRANCH * c + HEAD * t
                        spread[which, start : start + HEAD, HEAD * t : HEAD * (t + 1)] = project[
                            c, b // 2, t, :, HEAD * (b % 2) : HEAD * (b % 2 + 1)
                        ]

        greet(
            [{"chan": spot.chan(d)} for d in (1, 2, 3)]
            + [{"pix": spot.pix_in_z(d)} for d in (1, -1)]
            + spot.sum_peers()
            + [{"pix": p} for p in (spot.before, spot.after)],
            expected,
            prepare,
        )
        rows.send_rows()
        row_sums = jnp.sum(trunk[...].astype(F32), axis=1)
        sums = jnp.zeros((8, 512), F32)
        for r in range(OWN_ROWS):
            sums = add_at(sums, row_sums[r : r + 1], tile_at(tiles, OWN_ROWS * i + r))
        near[spot.k] = sums
        for d in range(1, GROUP):
            marks["near", d] = posts.post(
                lambda d=d: (near.at[spot.k], near.at[spot.k], {"pix": spot.pix_in_group(d)})
            )
        rows.pass_own()
        post_x(0)
        rows.await_halo(j)

    @pl.when(step == 1)
    def _():
        for d in range(1, GROUP):
            posts.arrive(marks["near", d], near.at[spot.in_group(-d)])
        total = near[0]
        for k in range(1, GROUP):
            total = total + near[k]
        across[spot.group] = total
        for d in range(1, 4):
            marks["across", d] = posts.post(
                lambda d=d: (
                    across.at[spot.group], across.at[spot.group], {"pix": spot.pix_in_x(d)}
                )
            )

    @pl.when(step == 3)
    def _():
        rows.pass_sides()
        post_x(1)
        post_x(2)
        pass_x(0)
        for d in range(1, 4):
            posts.arrive(marks["across", d], across.at[spot.x_of(-d)])
        sums = across[0] + across[1] + across[2] + across[3]
        mean = sums / tile_sizes(tile_grid[...])[:, 0:1]
        mean_all[j] = jnp.concatenate([mean, jnp.zeros((8, 512), F32)], axis=0).astype(BF16)
        for d in (2, 1, 3):
            marks["mean", d] = posts.post(
                lambda d=d: (mean_all.at[j], mean_all.at[j], {"chan": spot.chan(d)})
            )
        rows.await_halo(blocks[1])

    @pl.when(step == 6)
    def _():
        rows.await_halo(blocks[2])
        for d in (1, 2, 3):
            posts.arrive(marks["mean", d], mean_all.at[spot.chan(-d)])
        mean_kept[...] = mean_all[...]
        act = None
        for c in range(CHAN):
            term = dot_nt(mean_all[c], pooled_weight[:, 512 * c : 512 * (c + 1)])
            act = term if act is None else act + term
        pre_pooled[...] = act
        act = silu(act).astype(BF16).astype(F32)
        for r in range(OWN_ROWS):
            row = rows_at(act, tiles[row_of(OWN_ROWS * i + r)])
            pooled[TILE_W * r : TILE_W * (r + 1)] = jnp.broadcast_to(row, (TILE_W, BRANCH)).astype(
                BF16
            )
        rows.pass_far()
        post_x(3)
        own_copy().start()
        pass_x(1)
        pass_x(2)

    @pl.when(step == 9)
    def _():
        rows.await_halo(blocks[3])
        pass_x(3)

    @pl.when(turn < 4)
    def _():
        chan = order_at(turn, j)
        for a in range(3):
            for r in range(OWN_ROWS):
                slot = REACH + r + (a - 1) * (rate + 1)
                row = x[chan, slot]
                if a != 1:
                    row = jnp.where(keys[REACH + r] == keys[slot], row, jnp.zeros_like(row))
                lhs[TILE_W * r : TILE_W * (r + 1), 512 * a : 512 * (a + 1)] = row
        taps = jnp.concatenate([kernel[:, 0, a].reshape(3 * BRANCH, 512) for a in range(3)], axis=1)
        product = dot_nt(lhs[...], taps)

        @pl.when(turn == 0)
        def _():
            acc[rate] = product

        @pl.when(turn > 0)
        def _():
            acc[rate] += product

        @pl.when(rate == 0)
        def _():
            lanes = pl.ds(pl.multiple_of(512 * chan, 512), 512)
            own = x[chan, REACH : REACH + OWN_ROWS].reshape(OWN_ROWS * TILE_W, 512)
            term = dot_nt(own, point[:, :, lanes].reshape(BRANCH, 512))
            pre[3] = jnp.where(turn > 0, pre[3], 0.0) + term

    @pl.when(step == 11)
    def _():
        col = lax.broadcasted_iota(jnp.int32, (OWN_ROWS * TILE_W, HEAD), 0) % TILE_W
        for which, dilation in enumerate(head_rates):
            for t in range(TASKS):
                behind, total, ahead = (
                    acc[which, :, BRANCH * t + HEAD * b : BRANCH * t + HEAD * (b + 1)]
                    for b in range(3)
                )
                behind = pltpu.roll(behind, dilation, 0)
                ahead = pltpu.roll(ahead, OWN_ROWS * TILE_W - dilation, 0)
                total = total + jnp.where(col >= dilation, behind, 0.0)
                total = total + jnp.where(col < TILE_W - dilation, ahead, 0.0)
                pre[which, :, HEAD * t : HEAD * (t + 1)] = total
        cot = jnp.concatenate([maps_in[c].reshape(-1, BRANCH) for c in range(CHAN)], axis=1)
        head = None
        for which in range(5):
            if which < 4:
                before = pre[which]
                logistic = jax.nn.sigmoid(before)
                joined = (before * logistic).astype(BF16)
            else:
                joined = pooled[...]
            weight = spread[which]
            term = dot_nt(joined, weight)
            head = term if head is None else head + term
            grads = dot_tn(joined, cot)
            for t in range(TASKS):
                for c in range(CHAN):
                    lane = BRANCH * c + HEAD * t
                    grad_project[c, which, t] = grads[
                        HEAD * t : HEAD * (t + 1), lane : lane + HEAD
                    ].astype(BF16)
            back = dot_nn(cot, weight)
            if which < 4:
                grad = back * (logistic * (1.0 + before * (1.0 - logistic)))
                grad_pre[:, :, BRANCH * which : BRANCH * (which + 1)] = grad.astype(BF16).reshape(
                    OWN_ROWS, TILE_W, BRANCH
                )
            else:
                sums = jnp.sum(back.reshape(OWN_ROWS, TILE_W, BRANCH), axis=1)
                pool_rows[:, :BRANCH] = sums
                pool_rows[:, BRANCH:] = jnp.zeros((OWN_ROWS, 256 - BRANCH), F32)
        for c in range(CHAN):
            part = head[:, BRANCH * c : BRANCH * (c + 1)].astype(BF16)
            head_part[c] = part.reshape(OWN_ROWS, TILE_W, BRANCH)
        start_grads()

    @pl.when(grad_step == 0)
    def _():
        posts.arrive(marks["low"], low)
        posts.arrive(marks["high"], high)
        widen(0, low)
        widen(REACH + OWN_ROWS, high)

        def one_row(r, carry):
            is_low = lax.broadcasted_iota(jnp.int32, (TILE_W, 2 * HEAD), 1) < HEAD
            out_rows = pl.ds(pl.multiple_of(r * TILE_W, TILE_W), TILE_W)
            for which, dilation in enumerate(head_rates):

                def shifted(tap):
                    t, a, b = tap // 9, tap // 3 % 3 - 1, tap % 3 - 1
                    piece = wide[
                        3 * t + which,
                        r + REACH - a * (which + 1),
                        PAD - b * dilation : PAD - b * dilation + TILE_W,
                    ]
                    same = keys[REACH + r] == keys[REACH + r - a * (which + 1)]
                    return jnp.where(same, piece, 0.0)

                for pair in range(14):
                    first = shifted(2 * pair)
                    second = shifted(2 * pair + 1) if pair < 13 else jnp.zeros_like(first)
                    taps[which, out_rows, 2 * HEAD * pair : 2 * HEAD * (pair + 1)] = jnp.where(
                        is_low, first, second
                    ).astype(BF16)
            return carry

        lax.fori_loop(0, OWN_ROWS, one_row, 0)

    @pl.when(grad_step == 2)
    def _():
        for d in range(1, GROUP):
            posts.arrive(marks["near b", d], near_b.at[spot.in_group(-d)])
        total = near_b[0]
        for k in range(1, GROUP):
            total = total + near_b[k]
        across_b[spot.group] = total
        for d in range(1, 4):
            marks["across b", d] = posts.post(
                lambda d=d: (
                    across_b.at[spot.group], across_b.at[spot.group], {"pix": spot.pix_in_x(d)}
                )
            )

    @pl.when(grad_step == 4)
    def _():
        for d in range(1, 4):
            posts.arrive(marks["across b", d], across_b.at[spot.x_of(-d)])
        sums = across_b[0] + across_b[1] + across_b[2] + across_b[3]
        pooled_pre = sums[:, :BRANCH] * slope(pre_pooled[0:8])
        tall[...] = jnp.concatenate([pooled_pre, jnp.zeros((8, BRANCH), F32)], axis=0).astype(BF16)
        for c in range(CHAN):
            mean_out[c] = dot_nn(tall[...], pooled_weight[:, 512 * c : 512 * (c + 1)]).astype(BF16)
        for d in (2, 1, 3):
            marks["mean b", d] = posts.post(
                lambda d=d: (mean_out.at[spot.chan(d)], mean_in.at[d - 1], {"chan": spot.chan(d)})
            )

    @pl.when(grad_step == 8)
    def _():
        mean = mean_out[j].astype(F32)
        for d in (1, 3, 2):
            posts.arrive(marks["mean b", d], mean_in.at[d - 1])
            mean = mean + mean_in[d - 1].astype(F32)
        mean = mean[0:8] / tile_sizes(tile_grid[...])[:, 0:1]
        for r in range(OWN_ROWS):
            mean_rows[r : r + 1] = rows_at(mean, tiles[OWN_ROWS * i + r])
        for d in (1, 3, 2):
            posts.arrive(marks["head", d], head_in.at[d - 1])
        for s in range(OWN_ROWS):
            held = parts[j, s].astype(F32)
            for d in (1, 2, 3):
                held = held + head_in[d - 1, s].astype(F32)
            for t in range(TASKS):
                maps_sum[s, t] = held[:, HEAD * t : HEAD * (t + 1)].astype(BF16)
            target, (away, here) = row_send(s)
            pl.when(target != i)(lambda: away().start())
            pl.when(target == i)(lambda: here().start())

    @pl.when(grad_step == 5)
    def _():
        for half, d in enumerate((1, -1)):
            posts.arrive(marks["z", d, half], g_rows(-d, spot.core, half))
            marks["far g", half] = posts.post(
                lambda half=half, d=d: (
                    g_rows(-d, spot.core, half),
                    g_rows(-d, spot.core, half),
                    {"pix": spot.pix_in_z(d)},
                )
            )

    @pl.when(grad_step == 10)
    def _():
        for half, d in enumerate((-1, 1)):
            posts.arrive(marks["z", d, half], g_rows(-d, spot.core, half))

    @pl.when(turn >= 4)
    def _():
        product = dot_nn(taps[rate, :, : 27 * HEAD], kernel_b[...].reshape(27 * HEAD, -1))

        @pl.when(rate == 0)
        def _():
            lanes = pl.ds(pl.multiple_of(512 * block_at(n, j), 512), 512)
            grads = mid[...].reshape(OWN_ROWS * TILE_W, -1)[:, 3 * BRANCH :]
            acc_b[...] = product + dot_nn(grads, point[:, :, lanes].reshape(BRANCH, 512))

        @pl.when(rate == 1)
        def _():
            acc_b[...] += product

        @pl.when(rate == 2)
        def _():
            total = acc_b[...] + product
            out[block_at(n, j)] = total.astype(BF16).reshape(OWN_ROWS, TILE_W, 512)

    def side_send(chan, s):
        turn = int_rem(chan + CHAN - j, CHAN) - 1
        return remote(
            out.at[chan, s], out_in.at[turn, s], ss_side.at[turn, s], rs_side.at[turn, s], chan=chan
        )

    @pl.when((turn >= 4) & (rate == 2) & (n < 3))
    def _():
        for s in range(OWN_ROWS):
            side_send(block_at(n, j), s).start()

    def back_send(s):
        row = row_of(OWN_ROWS * i + s)
        target, slot = int_div(row, OWN_ROWS), int_rem(row, OWN_ROWS)
        return target, (
            lambda: remote(
                out_sum.at[s], trunk_grad.at[slot], ss_back.at[s], rs_back.at[slot], pix=target
            ),
            lambda: pltpu.make_async_copy(out_sum.at[s], trunk_grad.at[slot], rs_back.at[slot]),
        )

    def side_arrival(turn, s):
        dst = out_in.at[turn, s]
        return remote(dst, dst, ss_side.at[turn, s], rs_side.at[turn, s], chan=spot.chan(1))

    @pl.when(grad_step == 11)
    def _():
        for s in range(OWN_ROWS):
            held = out[j, s].astype(F32)
            for turn in range(3):
                side_arrival(turn, s).wait_recv()
                held = held + out_in[turn, s].astype(F32)
            out_sum[s] = held.astype(BF16)
            target, (away, here) = back_send(s)
            pl.when(target != i)(lambda: away().start())
            pl.when(target == i)(lambda: here().start())
        for half in range(2):
            posts.arrive(marks["far g", half], g_rows(2, spot.core, half))
        g_copy().wait()
        for s in range(OWN_ROWS):
            pltpu.make_async_copy(out_sum.at[s], trunk_grad.at[s], rs_back.at[s]).wait()
            target, (away, here) = back_send(s)
            pl.when(target != i)(lambda: away().wait_send())
            for d in (1, 2, 3):
                side_send(spot.chan(d), s).wait_send()
            pltpu.make_async_copy(maps_sum.at[s], maps_out.at[:, s], rs_row.at[s]).wait()
            target, (away, here) = row_send(s)
            pl.when(target != i)(lambda: away().wait_send())
        for q in range(4):
            for d in (1, -1):
                posts.arrive(marks["x", d, q], x_rows(-d, spot.core, blocks[q]))
            posts.arrive(marks["far", q], x_rows(2, spot.core, blocks[q]))
        own_copy().wait()
        rows.drain()
        posts.finish()


def heads(*operands):
    pixels = OWN_ROWS * TILE_W
    whole = pl.BlockSpec(memory_space=pltpu.VMEM)
    hbm = pl.BlockSpec(memory_space=pl.ANY)
    dma = pltpu.SemaphoreType.DMA
    shape = jax.ShapeDtypeStruct
    maps, rows = (OWN_ROWS, TILE_W, BRANCH), (OWN_ROWS, TILE_W, 512)

    def forward_block(q, r):
        chan = order_at(jnp.minimum(q, 3), lax.axis_index("chan"))
        return (0, jnp.where(q < 4, r, 2), 0, 0, 0, chan)

    def grad_block(q, r):
        chan = block_at(jnp.maximum(q - 4, 0), lax.axis_index("chan"))
        return (0, jnp.where(q < 4, 0, r), 0, 0, 0, chan)

    return pl.pallas_call(
        heads_kernel,
        grid=(8, 3),
        in_specs=[pl.BlockSpec(memory_space=pltpu.SMEM)]
        + [whole] * 3
        + [pl.BlockSpec((TASKS, 1, 3, 3, HEAD, 512), forward_block)]
        + [whole] * 3
        + [pl.BlockSpec((TASKS, 1, 3, 3, HEAD, 512), grad_block)],
        out_specs=[whole, hbm, whole, hbm, hbm, hbm, whole, whole],
        out_shape=[
            shape((CHAN, 5, TASKS, HEAD, HEAD), BF16),
            shape((CHAN, GROUP_ROWS, TILE_W, 128), BF16),
            shape((CHAN, 16, 512), BF16),
            shape(rows, BF16),
            shape((GROUP_ROWS, TILE_W, 4 * BRANCH), BF16),
            shape((TASKS, OWN_ROWS, TILE_W, HEAD), BF16),
            shape((OWN_ROWS, 512), F32),
            shape((16, BRANCH), BF16),
        ],
        scratch_shapes=[
            pltpu.SMEM((EXT_ROWS,), jnp.int32),
            pltpu.VMEM((CHAN, 16, 512), BF16),
            pltpu.VMEM((pixels, BRANCH), BF16),
            pltpu.VMEM((CHAN, EXT_ROWS, TILE_W, 512), BF16),
            pltpu.VMEM((pixels, 3 * 512), BF16),
            pltpu.VMEM((3, pixels, 3 * BRANCH), F32),
            pltpu.VMEM((4, pixels, BRANCH), F32),
            pltpu.VMEM((4, OWN_ROWS, TILE_W, 128), BF16),
            pltpu.VMEM((5, 256 * TASKS, BRANCH), BF16),
            pltpu.VMEM((GROUP, 8, 512), F32),
            pltpu.VMEM((4, 8, 512), F32),
            pltpu.VMEM((OWN_ROWS, TILE_W, 4 * BRANCH), BF16),
            pltpu.VMEM((CHAN, *maps), BF16),
            pltpu.VMEM((OWN_ROWS, 256), F32),
            pltpu.VMEM((16, BRANCH), F32),
            pltpu.VMEM((9, EXT_ROWS, PADDED, 2 * HEAD), F32),
            pltpu.VMEM((3, pixels, 28 * HEAD), BF16),
            pltpu.VMEM((pixels, 512), F32),
            pltpu.VMEM((2, REACH, TILE_W, 4 * BRANCH), BF16),
            pltpu.VMEM((CHAN - 1, *maps), BF16),
            pltpu.VMEM((OWN_ROWS, TASKS, TILE_W, HEAD), BF16),
            pltpu.VMEM((CHAN, *rows), BF16),
            pltpu.VMEM((CHAN - 1, *rows), BF16),
            pltpu.VMEM(rows, BF16),
            pltpu.VMEM((GROUP, 8, 256), F32),
            pltpu.VMEM((4, 8, 256), F32),
            pltpu.VMEM((CHAN, 16, 512), BF16),
            pltpu.VMEM((CHAN - 1, 16, 512), BF16),
            dma((64,)),
            dma((64,)),
            dma((2,)),
            dma((OWN_ROWS,)),
            dma((OWN_ROWS,)),
            dma((CHAN - 1, OWN_ROWS)),
            dma((CHAN - 1, OWN_ROWS)),
            dma((OWN_ROWS,)),
            dma((OWN_ROWS,)),
            *gather_sems(REACH),
        ],
        compiler_params=pltpu.CompilerParams(
            collective_id=2, has_side_effects=True, vmem_limit_bytes=VMEM_LIMIT
        ),
        cost_estimate=pl.CostEstimate(
            flops=24_000_000_000, bytes_accessed=56_000_000, transcendentals=0
        ),
        name="heads",
    )(*operands)


class GroupSum:
    def __init__(self, out, relay_in, side_in, spot, links):
        self.out, self.relay_in, self.side_in, self.spot, self.links = out, relay_in, side_in, spot, links
        self.ready, self.open, self.arrivals = [], [], []

    def flush(self):
        self.relay()
        for n, way in self.ready:
            self.send(n, way)
        self.ready = []

    def send(self, n, way):
        spot, links, out = self.spot, self.links, self.out
        relay = links.send(out.at[n, spot.x_of(2)], self.relay_in.at[n], pix=spot.pix_in_x(way))
        side = links.send(
            out.at[n, spot.x_of(-way)], self.side_in.at[n, 0], pix=spot.pix_in_x(-way)
        )
        self.arrivals.append((side, n, 0))
        self.open.append((n, way, relay))

    def relay(self):
        for n, way, relay in self.open:
            self.links.arrive(relay, self.relay_in.at[n])
            target = self.spot.x_of(way)
            both = self.out[n, target].astype(F32) + self.relay_in[n].astype(F32)
            self.out[n, target] = both.astype(BF16)
            side = self.links.send(
                self.out.at[n, target], self.side_in.at[n, 1], pix=self.spot.pix_in_x(way)
            )
            self.arrivals.append((side, n, 1))
        self.open = []

    def finish(self, place):
        for side, n, which in self.arrivals:
            self.links.arrive(side, self.side_in.at[n, which])
        for n in range(self.out.shape[0]):
            total = self.out[n, self.spot.group].astype(F32)
            place(n, total + self.side_in[n, 0].astype(F32) + self.side_in[n, 1].astype(F32))


class Links:
    def __init__(self, send_sems, recv_sems):
        self.send_sems, self.recv_sems, self.count, self.sent = send_sems, recv_sems, 0, []

    def send(self, src, dst, **where):
        n = self.count
        self.count += 1
        copy = remote(src, dst, self.send_sems.at[n], self.recv_sems.at[n], **where)
        copy.start()
        self.sent.append(copy)
        return n

    def arrive(self, n, dst):
        beside = {"chan": int_rem(lax.axis_index("chan") + 1, CHAN)}
        remote(dst, dst, self.send_sems.at[n], self.recv_sems.at[n], **beside).wait_recv()

    def finish(self):
        for copy in self.sent:
            copy.wait_send()


def sum_over_pix(value, near, across, spot, links, meanwhile=lambda: None):
    near[spot.k] = value
    sent = [
        links.send(near.at[spot.k], near.at[spot.k], pix=spot.pix_in_group(d))
        for d in range(1, GROUP)
    ]
    meanwhile()
    for d, n in zip(range(1, GROUP), sent):
        links.arrive(n, near.at[spot.in_group(-d)])
    total = near[0]
    for k in range(1, GROUP):
        total = total + near[k]
    across[spot.group] = total
    sent = [
        links.send(across.at[spot.group], across.at[spot.group], pix=spot.pix_in_x(d))
        for d in range(1, 4)
    ]
    meanwhile()
    for d, n in zip(range(1, 4), sent):
        links.arrive(n, across.at[spot.x_of(-d)])
    return across[0] + across[1] + across[2] + across[3]


def two_sums(first, second):
    width = first.shape[1]
    rows = [jnp.sum(first, axis=0, keepdims=True), jnp.sum(second, axis=0, keepdims=True)]
    return jnp.concatenate(rows + [jnp.zeros((6, width), F32)], axis=0)


PIXELS = NROWS * TILE_W
OWN = OWN_ROWS * TILE_W
MID_OWN = 128
FEAT_OWN = 512


def col_shift(value, distance):
    col = lax.broadcasted_iota(jnp.int32, value.shape, 0) % TILE_W
    rows = value.shape[0]
    moved = pltpu.roll(value, (rows - distance) % rows, 0)
    inside = (col < TILE_W - distance) if distance > 0 else (col >= -distance)
    return jnp.where(inside, moved, 0.0)


def section_forward_kernel(
    tiles, draws, pixels, wr, wd, we, gain_r, bias_r, gain_d, bias_d, gain_e, bias_e, project, cotangent,
    trunk, unit_r, unit_d, unit_e, act_r, act_d, wr_all, inv_mid, inv_feat, project_all, maps_in,
    keep, project_out, part_out, part_in, near_m, across_m, near_f, across_f, maps_own,
    send_sems, recv_sems, ss_map, rs_map,
):
    spot = Spot()
    links = Links(send_sems, recv_sems)
    i, j = spot.i, spot.j
    expected = greet_origins(i)

    def map_send(s):
        place = place_of(OWN_ROWS * i + s)
        target, slot = int_div(place, OWN_ROWS), int_rem(place, OWN_ROWS)
        return target, (
            lambda: remote(
                maps_own.at[s], maps_in.at[j, slot], ss_map.at[s], rs_map.at[slot], pix=target
            ),
            lambda: pltpu.make_async_copy(maps_own.at[s], maps_in.at[j, slot], rs_map.at[slot]),
        )

    def prepare():
        fill_keep(tiles, keep, spot.i)
        lane = lax.broadcasted_iota(jnp.int32, (8, 128), 1)
        drawn = jnp.full((8, 128), -1e30, F32)
        for t in range(TASKS):
            drawn = jnp.where(lane == t, draws[t].astype(F32) / 3.0, drawn)
        grown = jnp.where(lane < TASKS, jnp.exp(drawn - jnp.max(drawn, axis=1, keepdims=True)), 0.0)
        grown = grown / jnp.sum(grown, axis=1, keepdims=True)
        for t in range(TASKS):
            weight = jnp.sum(jnp.where(lane == t, grown, 0.0), axis=1, keepdims=True)[0:1]
            scaled = (cotangent[t].astype(F32).T * weight).astype(BF16)
            maps_own[:, :, HEAD * t : HEAD * (t + 1)] = scaled.reshape(OWN_ROWS, TILE_W, HEAD)
        for c in range(CHAN):
            for b in range(5):
                lane = HEAD * (b % 2)
                project_out[c, b // 2, :, :, lane : lane + HEAD] = project[
                    :, :, 256 * b + HEAD * c : 256 * b + HEAD * (c + 1)
                ]
            project_out[c, 2, :, :, HEAD:] = jnp.zeros((TASKS, HEAD, HEAD), BF16)

    greet(
        [{"chan": spot.chan(d)} for d in (1, 2, 3)]
        + spot.sum_peers()
        + [{"pix": p} for p in (spot.before, spot.after, spot.mate)],
        expected,
        prepare,
    )
    half = FEAT_OWN // 2

    def half_of(chan, core):
        return pl.ds(pl.multiple_of(FEAT_OWN * chan + half * core, half), half)

    own_half = half_of(0, spot.core)
    other_half = half_of(0, 1 - spot.core)
    sent = {
        d: links.send(
            wr.at[half_of(spot.chan(d), spot.core)], wr_all.at[j, own_half], chan=spot.chan(d)
        )
        for d in (2, 1, 3)
    }
    for s in range(OWN_ROWS):
        target, (away, here) = map_send(s)
        pl.when(target != i)(lambda: away().start())
        pl.when(target == i)(lambda: here().start())
    wr_all[j] = wr[pl.ds(pl.multiple_of(FEAT_OWN * j, FEAT_OWN), FEAT_OWN)]
    pre = dot_nn(pixels[...], wr_all[j])
    mates = {}
    for d in (1, 3, 2):
        source = spot.chan(-d)
        links.arrive(sent[d], wr_all.at[source, own_half])
        mates[d] = links.send(
            wr_all.at[source, own_half], wr_all.at[source, own_half], pix=spot.mate
        )
    back = {}
    for d in (1, 3, 2):
        source = spot.chan(-d)
        links.arrive(mates[d], wr_all.at[source, other_half])
        part_out[d - 1] = dot_nn(pixels[...], wr_all[source]).astype(BF16)
        back[d] = links.send(part_out.at[d - 1], part_in.at[d - 1], chan=source)
    for d in (1, 3, 2):
        links.arrive(back[d], part_in.at[d - 1])
        pre = pre + part_in[d - 1].astype(F32)

    project_sent = {}

    def send_project():
        for d in (2, 1, 3):
            for last, part in ((False, spot.core), (True, 2)):
                project_sent[d, last] = links.send(
                    project_out.at[spot.chan(d), part], project_all.at[j, part], chan=spot.chan(d)
                )

    def swap_project():
        for d in (1, 3, 2):
            source = spot.chan(-d)
            links.arrive(project_sent[d, False], project_all.at[source, spot.core])
            links.arrive(project_sent[d, True], project_all.at[source, 2])
            project_sent[d] = links.send(
                project_all.at[source, spot.core], project_all.at[source, spot.core], pix=spot.mate
            )

    halves = (slice(0, OWN_ROWS // 2), slice(OWN_ROWS // 2, OWN_ROWS))
    maps_sent = {}

    def send_maps():
        for s in range(OWN_ROWS):
            pltpu.make_async_copy(maps_own.at[s], maps_in.at[j, s], rs_map.at[s]).wait()
        for part in halves:
            for d in (1, -1):
                block = maps_in.at[j, part]
                maps_sent[d, part.start] = links.send(block, block, chan=spot.chan(d))

    def pass_maps():
        for d in (1, -1):
            for part in halves:
                links.arrive(maps_sent[d, part.start], maps_in.at[spot.chan(-d), part])
        for d, part in zip((1, -1), halves):
            block = maps_in.at[spot.chan(-d), part]
            maps_sent[part.start] = links.send(block, block, chan=spot.chan(d))

    todo = [send_project, send_maps, swap_project, pass_maps]

    def meanwhile():
        if todo:
            todo.pop(0)()

    def norm(value, near, across, gain, bias):
        sums = sum_over_pix(two_sums(value, value * value), near, across, spot, links, meanwhile)
        center = sums[0:1] / PIXELS
        inv = lax.rsqrt(sums[1:2] / PIXELS - center * center + eps)
        unit = (value - center) * inv
        return unit, unit * gain + bias, inv

    unit, normed, inv_r = norm(pre, near_m.at[0], across_m.at[0], gain_r[...], bias_r[...])
    unit_r[...] = unit
    own = slice(section_rate, section_rate + OWN_ROWS)
    act_r[j, own] = silu(normed).astype(BF16).reshape(OWN_ROWS, TILE_W, MID_OWN)
    low, high = slice(0, section_rate), slice(section_rate + OWN_ROWS, 2 * section_rate + OWN_ROWS)
    first, last = slice(section_rate, 2 * section_rate), slice(OWN_ROWS, section_rate + OWN_ROWS)
    sent = {
        d: links.send(act_r.at[j, own], act_r.at[j, own], chan=spot.chan(d)) for d in (2, 1, 3)
    }
    arrivals = []
    for d in (0, 1, 3, 2):
        source = spot.chan(-d)
        if d:
            links.arrive(sent[d], act_r.at[source, own])
        n = links.send(act_r.at[source, first], act_r.at[source, high], pix=spot.before)
        arrivals.append((n, act_r.at[source, high]))
        n = links.send(act_r.at[source, last], act_r.at[source, low], pix=spot.after)
        arrivals.append((n, act_r.at[source, low]))
    for n, dst in arrivals:
        links.arrive(n, dst)
    pre = jnp.zeros((OWN, MID_OWN), F32)
    for a in range(3):
        rows = slice(section_rate * a, section_rate * a + OWN_ROWS)
        window = jnp.concatenate(
            [act_r[c, rows].reshape(OWN, MID_OWN) for c in range(CHAN)], axis=1
        )
        terms = [dot_nn(window, wd[3 * a + b]) for b in range(3)]
        term = terms[1] + col_shift(terms[0], -section_rate) + col_shift(terms[2], section_rate)
        pre = pre + (term if a == 1 else term * keep[a // 2])

    unit, normed, inv_d = norm(pre, near_m.at[1], across_m.at[1], gain_d[...], bias_d[...])
    unit_d[...] = unit
    inv_mid[...] = jnp.concatenate([inv_r, inv_d, jnp.zeros((6, MID_OWN), F32)], axis=0)
    act_d[j] = silu(normed).astype(BF16)
    sent = {d: links.send(act_d.at[j], act_d.at[j], chan=spot.chan(d)) for d in (2, 1, 3)}
    for d in (1, 3, 2):
        links.arrive(sent[d], act_d.at[spot.chan(-d)])
    full = jnp.concatenate([act_d[c] for c in range(CHAN)], axis=1)
    unit, normed, inv_e = norm(
        dot_nn(full, we[...]), near_f, across_f, gain_e[...], bias_e[...]
    )
    unit_e[...] = unit
    inv_feat[...] = jnp.concatenate([inv_e, jnp.zeros((7, FEAT_OWN), F32)], axis=0)
    out = silu(normed + pixels[...].astype(F32)).astype(BF16)
    trunk[...] = out.reshape(OWN_ROWS, TILE_W, FEAT_OWN)
    for d in (1, 3, 2):
        links.arrive(project_sent[d], project_all.at[spot.chan(-d), 1 - spot.core])
    project_all[j] = project_out[j]
    for part in halves:
        links.arrive(maps_sent[part.start], maps_in.at[spot.chan(2), part])
    for s in range(OWN_ROWS):
        target, (away, here) = map_send(s)
        pl.when(target != i)(lambda: away().wait_send())
    links.finish()


def section_forward(*operands):
    whole = pl.BlockSpec(memory_space=pltpu.VMEM)
    shape = jax.ShapeDtypeStruct
    mid, feat = (OWN, MID_OWN), (OWN, FEAT_OWN)
    dma = pltpu.SemaphoreType.DMA
    return pl.pallas_call(
        section_forward_kernel,
        in_specs=[pl.BlockSpec(memory_space=pltpu.SMEM)] * 2 + [whole] * 12,
        out_specs=[whole] * 11,
        out_shape=[
            shape((OWN_ROWS, TILE_W, FEAT_OWN), BF16),
            shape(mid, F32),
            shape(mid, F32),
            shape(feat, F32),
            shape((CHAN, OWN_ROWS + 2 * section_rate, TILE_W, MID_OWN), BF16),
            shape((CHAN, *mid), BF16),
            shape((CHAN, FEAT_OWN, MID_OWN), BF16),
            shape((8, MID_OWN), F32),
            shape((8, FEAT_OWN), F32),
            shape((CHAN, 3, TASKS, HEAD, 2 * HEAD), BF16),
            shape((CHAN, OWN_ROWS, TILE_W, BRANCH), BF16),
        ],
        scratch_shapes=[
            pltpu.VMEM((2, OWN, MID_OWN), F32),
            pltpu.VMEM((CHAN, 3, TASKS, HEAD, 2 * HEAD), BF16),
            pltpu.VMEM((3, *mid), BF16),
            pltpu.VMEM((3, *mid), BF16),
            pltpu.VMEM((2, GROUP, 8, MID_OWN), F32),
            pltpu.VMEM((2, 4, 8, MID_OWN), F32),
            pltpu.VMEM((GROUP, 8, FEAT_OWN), F32),
            pltpu.VMEM((4, 8, FEAT_OWN), F32),
            pltpu.VMEM((OWN_ROWS, TILE_W, BRANCH), BF16),
            dma((72,)),
            dma((72,)),
            dma((OWN_ROWS,)),
            dma((OWN_ROWS,)),
        ],
        compiler_params=pltpu.CompilerParams(
            collective_id=5, has_side_effects=True, vmem_limit_bytes=VMEM_LIMIT
        ),
        cost_estimate=pl.CostEstimate(
            flops=2_000_000_000, bytes_accessed=120_000_000, transcendentals=0
        ),
        name="section_forward",
    )(*operands)


class Scatter:
    def __init__(self, parts, mate_in, near, near_in, far, far_in, spot, links):
        self.parts, self.mate_in, self.near, self.near_in = parts, mate_in, near, near_in
        self.far, self.far_in, self.spot, self.links = far, far_in, spot, links

    def start(self):
        spot = self.spot
        self.sent = self.links.send(self.parts.at[1 - spot.core], self.mate_in, pix=spot.mate)

    def along_z(self):
        spot, links = self.spot, self.links
        links.arrive(self.sent, self.mate_in)
        for z in range(4):
            self.near[z] = (
                self.parts[spot.core, z].astype(F32) + self.mate_in[z].astype(F32)
            ).astype(BF16)
        self.sent = {
            d: links.send(
                self.near.at[spot.z_of(d)], self.near_in.at[d - 1], pix=spot.pix_in_z(d)
            )
            for d in (2, 1, 3)
        }

    def along_x(self):
        spot, links = self.spot, self.links
        total = self.near[spot.z].astype(F32)
        for d in (1, 3, 2):
            links.arrive(self.sent[d], self.near_in.at[d - 1])
            total = total + self.near_in[d - 1].astype(F32)
        self.far[...] = total.astype(BF16)
        self.sent = {
            d: links.send(self.far.at[spot.x_of(d)], self.far_in.at[d - 1], pix=spot.pix_in_x(d))
            for d in (2, 1, 3)
        }

    def finish(self):
        spot, links = self.spot, self.links
        total = self.far[spot.group].astype(F32)
        for d in (1, 3, 2):
            links.arrive(self.sent[d], self.far_in.at[d - 1])
            total = total + self.far_in[d - 1].astype(F32)
        return total


def scatter_scratch(*shape):
    return [
        pltpu.VMEM((2, 4, 4, *shape), BF16),
        pltpu.VMEM((4, 4, *shape), BF16),
        pltpu.VMEM((4, 4, *shape), BF16),
        pltpu.VMEM((3, 4, *shape), BF16),
        pltpu.VMEM((4, *shape), BF16),
        pltpu.VMEM((3, *shape), BF16),
    ]


def spot_of(device):
    return device % 2, device % GROUP // 2, device // GROUP


def section_backward_kernel(
    tiles, trunk_grad, pixels, unit_r, unit_d, unit_e, act_r, act_d, wr_all, wd, we,
    gain_r, bias_r, gain_d, bias_d, gain_e, bias_e, inv_mid, inv_feat, mean_rows, projects, x_group,
    g_group, *refs,
):
    (
        grad_pixels, grad_reduce, grad_gain_r, grad_bias_r, grad_dilate, grad_gain_d, grad_bias_d,
        grad_expand, grad_gain_e, grad_bias_e, grad_point, grad_atrous, grad_project,
    ) = refs[:13]
    scratch = refs[13:]
    (
        keys, keep, wd_cat, side_out, side_in, halo, taps, full, project_in, project_wide, reduce_out,
        near_m, across_m, near_f, across_f, x_all, x_base, x_now, g_all, g_now,
    ) = scratch[:20]
    send_sems, recv_sems, ss_reduce, rs_reduce, load_sems, edge_sems = scratch[-6:]
    buffers = scratch[20:-6]
    spot = Spot()
    links = Links(send_sems, recv_sems)
    i, j = spot.i, spot.j
    by_expand, by_dilate, by_project, by_reduce = [
        Scatter(*buffers[6 * n : 6 * n + 6], spot, links) for n in range(4)
    ]
    owner_i, owner_j = GROUP * j + int_div(i, 4), int_rem(i, 4)
    maker_i, maker_j = 4 * int_rem(i, GROUP) + j, spot.group
    stays = (owner_i == i) & (owner_j == j)
    barrier = pltpu.get_barrier_semaphore()

    @pl.when(jnp.logical_not(stays))
    def _():
        signal(barrier, pix=maker_i, chan=maker_j)

    peers = [{"chan": spot.chan(d)} for d in (1, 2, 3)] + spot.sum_peers()
    peers += [{"pix": spot.before}, {"pix": spot.after}]

    def core_rows(z, core, first=0):
        return pl.ds(first + OWN_ROWS * (2 * z + core), OWN_ROWS)

    def shares(core):
        pairs = []
        for z in range(4):
            rows, moved = core_rows(z, core), core_rows(z, core, REACH)
            pairs.append((x_group.at[:, rows], x_all.at[:, rows]))
            pairs.append((g_group.at[rows], g_all.at[moved]))
        return pairs

    loads = [
        pltpu.make_async_copy(src, dst, load_sems.at[n])
        for n, (src, dst) in enumerate(shares(spot.core))
    ]

    def prepare():
        for load in loads:
            load.start()
        fill_keep(tiles, keep, i)
        fill_keys(tiles, keys, GROUP_ROWS * spot.group - REACH, GROUP_ROWS + 2 * REACH)
        for tap in range(9):
            wd_cat[:, MID_OWN * tap : MID_OWN * (tap + 1)] = wd[tap]

    for step in (1, -1):
        x_maker = int_rem(spot.group + 4 - step, 4)
        maker_core = (1 + step) // 2
        peers.append({"pix": GROUP * x_maker + 2 * spot.z + maker_core})
    peers.append({"pix": spot.mate})
    greet(peers, 1 - stays.astype(jnp.int32), prepare)

    atrous_sum = GroupSum(*buffers[24:27], spot, links)
    point_sum = GroupSum(*buffers[27:30], spot, links)
    x_target = int_rem(spot.group + 3 + 2 * spot.core, 4)

    def edge_copy(core):
        return remote(
            g_group.at[pl.ds(spot.core * (GROUP_ROWS - REACH), REACH)],
            g_all.at[pl.ds((1 - spot.core) * (GROUP_ROWS + REACH), REACH)],
            edge_sems.at[core],
            edge_sems.at[2 + 1 - spot.core],
            pix=GROUP * x_target + 2 * spot.z + core,
        )

    def edge_arrival(high):
        dst = g_all.at[pl.ds(high * (GROUP_ROWS + REACH), REACH)]
        return remote(dst, dst, edge_sems.at[0], edge_sems.at[2 + high], chan=spot.chan(1))

    for core in range(2):
        edge_copy(core).start()
    mates = [links.send(src, dst, pix=spot.mate) for src, dst in shares(spot.core)]

    def row_block(r):
        return pl.ds(pl.multiple_of(r * TILE_W, TILE_W), TILE_W)

    def take():
        for load in loads:
            load.wait()
        for n, (_, dst) in zip(mates, shares(1 - spot.core)):
            links.arrive(n, dst)
        for high in range(2):
            edge_arrival(high).wait_recv()

        def one_row(r, carry):
            is_low = lax.broadcasted_iota(jnp.int32, (TILE_W, 2 * HEAD), 1) < HEAD
            for pair in range(2):
                first = x_all[2 * pair, r].astype(F32)
                second = x_all[2 * pair + 1, r].astype(F32)
                lower = jnp.where(is_low, first, pltpu.roll(second, HEAD, 1))
                upper = jnp.where(is_low, pltpu.roll(first, HEAD, 1), second)
                x_base[row_block(r), 2 * HEAD * pair : 2 * HEAD * (pair + 1)] = jnp.where(
                    spot.core == 0, lower, upper
                ).astype(BF16)
            return carry

        lax.fori_loop(0, GROUP_ROWS, one_row, 0, unroll=4)

    def pick(which):
        def one_row(r, carry):
            pieces = []
            for a in range(3):
                piece = g_all[
                    r + REACH - (a - 1) * (which + 1), :, BRANCH * which : BRANCH * (which + 1)
                ]
                same = keys[r + REACH] == keys[r + REACH - (a - 1) * (which + 1)]
                pieces.append(jnp.where(same, piece, jnp.zeros_like(piece)))
            g_now[row_block(r)] = jnp.concatenate(pieces, axis=1)
            return carry

        lax.fori_loop(0, GROUP_ROWS, one_row, 0, unroll=4)

    def multiply(which, b):
        held = x_base
        if b != 1:
            held = x_now

            def one_row(r, carry):
                row = x_base[row_block(r)].astype(F32)
                x_now[row_block(r)] = col_shift(row, (b - 1) * head_rates[which]).astype(BF16)
                return carry

            lax.fori_loop(0, GROUP_ROWS, one_row, 0, unroll=4)
        product = dot_tn(g_now[...], held[...]).T.astype(BF16)
        n = 3 * which + b
        for c in range(CHAN):
            atrous_sum.out[n, c] = product[HEAD * c : HEAD * (c + 1)]
        atrous_sum.ready.append((n, 1 if n % 2 else -1))

    def multiply_point():
        grads = g_all[REACH : REACH + GROUP_ROWS, :, 3 * BRANCH :].reshape(-1, BRANCH)
        product = dot_tn(grads, x_base[...]).T.astype(BF16)
        for c in range(CHAN):
            point_sum.out[0, c] = product[HEAD * c : HEAD * (c + 1)]
        point_sum.ready.append((0, 1))

    tasks = [lambda: None, lambda: None, take]
    for which in range(3):
        tasks.append(functools.partial(pick, which))
        tasks += [functools.partial(multiply, which, b) for b in range(3)]
    tasks += [multiply_point]
    queue = iter(tasks)

    def flush():
        atrous_sum.flush()
        point_sum.flush()

    def meanwhile(count=1):
        for _ in range(count):
            task = next(queue, None)
            if task is not None:
                task()

    project_sent = {
        d: links.send(projects.at[spot.chan(d)], project_in.at[d - 1], chan=spot.chan(d))
        for d in (2, 1, 3)
    }

    def norm_back(grad, unit, near, across, scale):
        sums = sum_over_pix(two_sums(grad, grad * unit), near, across, spot, links, meanwhile)
        pre = scale * (grad - sums[0:1] / PIXELS - unit * (sums[1:2] / PIXELS))
        return pre.astype(BF16), sums

    grad_trunk = trunk_grad[...].astype(F32) + mean_rows[...][:, None, :]
    grad_trunk = grad_trunk.reshape(OWN, FEAT_OWN)
    unit = unit_e[...]
    summed = unit * gain_e[...] + bias_e[...] + pixels[...].astype(F32)
    grad_summed = grad_trunk * slope(summed)
    g_expand, sums = norm_back(grad_summed, unit, near_f, across_f, gain_e[...] * inv_feat[0:1])
    grad_bias_e[...] = sums[0:1]
    grad_gain_e[...] = sums[1:2]

    def sides(turn, make):
        sent = {}
        for d in (2, 1, 3):
            side_out[turn, d - 1] = make(spot.chan(d)).astype(BF16)
            sent[d] = links.send(
                side_out.at[turn, d - 1], side_in.at[turn, d - 1], chan=spot.chan(d)
            )
        return sent

    def side_sum(turn, own, sent):
        for d in (1, 3, 2):
            links.arrive(sent[d], side_in.at[turn, d - 1])
            own = own + side_in[turn, d - 1].astype(F32)
        return own

    def mid_rows(chan):
        return pl.ds(pl.multiple_of(MID_OWN * chan, MID_OWN), MID_OWN)

    sent = sides(0, lambda c: dot_nt(g_expand, we[mid_rows(c)]))
    own = dot_nt(g_expand, we[mid_rows(j)])
    part = 16
    for c in range(CHAN):
        grads = dot_tn(act_d[c], g_expand).astype(BF16)
        for n in range(8):
            by_expand.parts[spot_of(8 * c + n)] = grads[part * n : part * (n + 1)]
    by_expand.start()
    flush()
    meanwhile(3)
    grad_act = side_sum(0, own, sent)

    unit = unit_d[...]
    grad = grad_act * slope(unit * gain_d[...] + bias_d[...])
    g_dilate, sums = norm_back(
        grad, unit, near_m.at[0], across_m.at[0], gain_d[...] * inv_mid[1:2]
    )
    grad_bias_d[...] = sums[0:1]
    grad_gain_d[...] = sums[1:2]
    own_rows = slice(section_rate, section_rate + OWN_ROWS)
    halo[own_rows] = g_dilate.reshape(OWN_ROWS, TILE_W, MID_OWN)
    low, high = slice(0, section_rate), slice(section_rate + OWN_ROWS, 2 * section_rate + OWN_ROWS)
    first, last = slice(section_rate, 2 * section_rate), slice(OWN_ROWS, section_rate + OWN_ROWS)
    to_before = links.send(halo.at[first], halo.at[high], pix=spot.before)
    to_after = links.send(halo.at[last], halo.at[low], pix=spot.after)
    by_expand.along_z()
    flush()
    meanwhile()
    for d in (1, 3, 2):
        links.arrive(project_sent[d], project_in.at[d - 1])
        project_wide[spot.chan(-d)] = project_in[d - 1].astype(F32)
    project_wide[j] = projects[j].astype(F32)
    links.arrive(to_before, halo.at[high])
    links.arrive(to_after, halo.at[low])
    for a in range(3):
        rows = halo[section_rate * (2 - a) : section_rate * (2 - a) + OWN_ROWS]
        rows = rows.reshape(OWN, MID_OWN).astype(F32)
        if a != 1:
            rows = rows * keep[1 - a // 2]
        for b in range(3):
            moved = rows if b == 1 else col_shift(rows, -section_rate * (b - 1))
            tap = 3 * a + b
            taps[:, MID_OWN * tap : MID_OWN * (tap + 1)] = moved.astype(BF16)
    sent = sides(1, lambda c: dot_nt(taps[...], wd_cat[mid_rows(c)]))
    own = dot_nt(taps[...], wd_cat[mid_rows(j)])
    for c in range(CHAN):
        act = act_r[c, own_rows].reshape(OWN, MID_OWN)
        grads = dot_tn(act, taps[...]).astype(BF16)
        for n in range(8):
            for tap in range(9):
                by_dilate.parts[(*spot_of(8 * c + n), tap)] = grads[
                    part * n : part * (n + 1), MID_OWN * tap : MID_OWN * (tap + 1)
                ]
    by_dilate.start()
    flush()
    meanwhile(2)
    grad_act = side_sum(1, own, sent)
    by_expand.along_x()

    unit = unit_r[...]
    grad = grad_act * slope(unit * gain_r[...] + bias_r[...])
    g_reduce, sums = norm_back(
        grad, unit, near_m.at[1], across_m.at[1], gain_r[...] * inv_mid[0:1]
    )
    grad_bias_r[...] = sums[0:1]
    grad_gain_r[...] = sums[1:2]
    full[j] = g_reduce
    sent = {d: links.send(full.at[j], full.at[j], chan=spot.chan(d)) for d in (2, 1, 3)}
    by_dilate.along_z()
    flush()
    for t in range(TASKS):
        for device in range(PIX):
            rows = []
            for start in range(40 * device, 40 * device + 40, 8):
                b, src, d = start // 256, start // HEAD % CHAN, start % HEAD
                rows.append(project_wide[src, BRANCH_PLACE[b], t, d : d + 8])
            rows.append(jnp.zeros((8, HEAD), F32))
            by_project.parts[(*spot_of(device), t)] = jnp.concatenate(rows, axis=0).astype(BF16)
    by_project.start()
    grad_expand[...] = by_expand.finish()
    meanwhile(2)
    for d in (1, 3, 2):
        links.arrive(sent[d], full.at[spot.chan(-d)])
    g_reduce = jnp.concatenate([full[c] for c in range(CHAN)], axis=1)
    weight = jnp.concatenate([wr_all[c] for c in range(CHAN)], axis=1)
    grads = dot_tn(pixels[...], g_reduce).astype(BF16)
    for c in range(CHAN):
        for n in range(8):
            by_reduce.parts[spot_of(4 * n + c)] = grads[
                HEAD * n : HEAD * (n + 1), MID_OWN * c : MID_OWN * (c + 1)
            ]
    by_reduce.start()
    grad_pixels[...] = (grad_summed + dot_nt(g_reduce, weight)).astype(BF16)
    by_reduce.along_z()
    by_project.along_z()
    meanwhile(2)
    by_reduce.along_x()
    flush()
    by_dilate.along_x()
    meanwhile(len(tasks))
    by_project.along_x()
    flush()
    reduce_out[...] = by_reduce.finish()

    def reduce_copies():
        return (
            lambda: remote(
                reduce_out, grad_reduce, ss_reduce.at[0], rs_reduce.at[0], pix=owner_i, chan=owner_j
            ),
            lambda: pltpu.make_async_copy(reduce_out, grad_reduce, rs_reduce.at[0]),
        )

    away, here = reduce_copies()
    pl.when(jnp.logical_not(stays))(lambda: away().start())
    pl.when(stays)(lambda: here().start())
    flush()
    grad_dilate[...] = by_dilate.finish()
    grad_project[...] = by_project.finish()[:, :40]

    def place(n, total):
        which, b = n // 3, n % 3
        for a in range(3):
            for t in range(TASKS):
                lane = BRANCH * a + HEAD * t
                grad_atrous[t, which, 3 * a + b] = total[:, lane : lane + HEAD]

    def place_point(n, total):
        for t in range(TASKS):
            grad_point[t] = total[:, HEAD * t : HEAD * (t + 1)]

    atrous_sum.finish(place)
    point_sum.finish(place_point)
    for core in range(2):
        edge_copy(core).wait_send()

    pltpu.make_async_copy(reduce_out, grad_reduce, rs_reduce.at[0]).wait()
    pl.when(jnp.logical_not(stays))(lambda: away().wait_send())
    links.finish()


def group_scratch(count, *shape):
    return [
        pltpu.VMEM((count, 4, *shape), BF16),
        pltpu.VMEM((count, *shape), BF16),
        pltpu.VMEM((count, 2, *shape), BF16),
    ]


def section_backward(*operands):
    whole = pl.BlockSpec(memory_space=pltpu.VMEM)
    shape = jax.ShapeDtypeStruct
    dma = pltpu.SemaphoreType.DMA
    mid, feat = (OWN, MID_OWN), (OWN, FEAT_OWN)
    return pl.pallas_call(
        section_backward_kernel,
        in_specs=[pl.BlockSpec(memory_space=pltpu.SMEM)]
        + [whole] * 20
        + [pl.BlockSpec(memory_space=pl.ANY)] * 2,
        out_specs=[whole] * 13,
        out_shape=[
            shape(feat, BF16),
            shape((HEAD, MID_OWN), F32),
            shape((1, MID_OWN), F32),
            shape((1, MID_OWN), F32),
            shape((9, 16, MID_OWN), F32),
            shape((1, MID_OWN), F32),
            shape((1, MID_OWN), F32),
            shape((16, FEAT_OWN), F32),
            shape((1, FEAT_OWN), F32),
            shape((1, FEAT_OWN), F32),
            shape((TASKS, HEAD, HEAD), F32),
            shape((TASKS, 3, 9, HEAD, HEAD), F32),
            shape((TASKS, 40, HEAD), F32),
        ],
        scratch_shapes=[
            pltpu.SMEM((GROUP_ROWS + 2 * REACH,), jnp.int32),
            pltpu.VMEM((2, OWN, MID_OWN), F32),
            pltpu.VMEM((FEAT_OWN, 9 * MID_OWN), BF16),
            pltpu.VMEM((2, 3, *mid), BF16),
            pltpu.VMEM((2, 3, *mid), BF16),
            pltpu.VMEM((OWN_ROWS + 2 * section_rate, TILE_W, MID_OWN), BF16),
            pltpu.VMEM((OWN, 9 * MID_OWN), BF16),
            pltpu.VMEM((CHAN, *mid), BF16),
            pltpu.VMEM((3, 5, TASKS, HEAD, HEAD), BF16),
            pltpu.VMEM((CHAN, 5, TASKS, HEAD, HEAD), F32),
            pltpu.VMEM((HEAD, MID_OWN), F32),
            pltpu.VMEM((2, GROUP, 8, MID_OWN), F32),
            pltpu.VMEM((2, 4, 8, MID_OWN), F32),
            pltpu.VMEM((GROUP, 8, FEAT_OWN), F32),
            pltpu.VMEM((4, 8, FEAT_OWN), F32),
            pltpu.VMEM((CHAN, GROUP_ROWS, TILE_W, 128), BF16),
            pltpu.VMEM((GROUP_ROWS * TILE_W, 256), BF16),
            pltpu.VMEM((GROUP_ROWS * TILE_W, 256), BF16),
            pltpu.VMEM((GROUP_ROWS + 2 * REACH, TILE_W, 4 * BRANCH), BF16),
            pltpu.VMEM((GROUP_ROWS * TILE_W, 3 * BRANCH), BF16),
            *scatter_scratch(16, FEAT_OWN),
            *scatter_scratch(9, 16, MID_OWN),
            *scatter_scratch(TASKS, 48, HEAD),
            *scatter_scratch(HEAD, MID_OWN),
            *group_scratch(9, HEAD, 3 * BRANCH),
            *group_scratch(1, HEAD, BRANCH),
            dma((112,)),
            dma((112,)),
            dma((1,)),
            dma((1,)),
            dma((8,)),
            dma((4,)),
        ],
        compiler_params=pltpu.CompilerParams(
            collective_id=6, has_side_effects=True, vmem_limit_bytes=VMEM_LIMIT
        ),
        cost_estimate=pl.CostEstimate(
            flops=16_000_000_000, bytes_accessed=250_000_000, transcendentals=0
        ),
        name="section_backward",
    )(*operands)


def hand_out_kernel(maps, tall, mean_all, *refs):
    count = (len(refs) - 3) // 2
    grads, (task_maps, grad_pooled), outs, sems = (
        refs[:count], refs[count : count + 2], refs[count + 2 : -1], refs[-1],
    )
    copies = [pltpu.make_async_copy(src, dst, sems.at[n]) for n, (src, dst) in enumerate(zip(grads, outs))]
    for copy in copies:
        copy.start()
    for c in range(CHAN):
        part = dot_tn(tall[...], mean_all[c])
        for t in range(TASKS):
            grad_pooled[t, :, 512 * c : 512 * (c + 1)] = part[HEAD * t : HEAD * (t + 1)]
    for t in range(TASKS):
        task_maps[t] = maps[t].reshape(OWN, HEAD).astype(F32).T.astype(BF16)
    for copy in copies:
        copy.wait()


def hand_out(maps, pooled_grad, mean_all, *grads):
    whole = pl.BlockSpec(memory_space=pltpu.VMEM)
    shape = jax.ShapeDtypeStruct
    return pl.pallas_call(
        hand_out_kernel,
        in_specs=[whole] * (3 + len(grads)),
        out_specs=[whole] * 2 + [pl.BlockSpec(memory_space=pl.ANY)] * len(grads),
        out_shape=[shape((TASKS, HEAD, OWN), BF16), shape((TASKS, HEAD, CHAN * 512), F32)]
        + [shape(grad.shape, grad.dtype) for grad in grads],
        scratch_shapes=[pltpu.SemaphoreType.DMA((len(grads),))],
        compiler_params=pltpu.CompilerParams(vmem_limit_bytes=VMEM_LIMIT),
        cost_estimate=pl.CostEstimate(flops=0, bytes_accessed=10_000_000, transcendentals=0),
        name="hand_out",
    )(maps, pooled_grad, mean_all, *grads)


def shards(
    pixels,
    tile_number,
    task_draws,
    reduce_weight,
    reduce_gain,
    reduce_bias,
    dilate_weight,
    dilate_gain,
    dilate_bias,
    expand_weight,
    expand_gain,
    expand_bias,
    point_weight,
    atrous_weight,
    pooled_weight,
    project_weight,
    cotangent,
):
    tile_grid = tile_number.reshape(2, 128)
    norms = [
        v.reshape(1, -1)
        for v in (reduce_gain, reduce_bias, dilate_gain, dilate_bias, expand_gain, expand_bias)
    ]
    pooled_rows = pooled_weight.reshape(BRANCH, -1)
    (
        trunk, unit_reduce, unit_dilate, unit_expand, act_reduce, act_dilate, reduce_all, inv_mid,
        inv_feat, project_all, maps_all,
    ) = section_forward(
        tile_number, task_draws, pixels, reduce_weight, dilate_weight, expand_weight, *norms,
        project_weight, jnp.swapaxes(cotangent, 1, 2),
    )
    kernels = atrous_weight.reshape(TASKS, 3, 3, 3, HEAD, -1)
    grad_project, x_group, mean_all, trunk_grad, g_group, maps, mean_rows, pooled_grad = heads(
        tile_number, tile_grid, trunk, maps_all, kernels, point_weight, project_all, pooled_rows, kernels
    )
    grads = section_backward(
        tile_number, trunk_grad, pixels, unit_reduce, unit_dilate, unit_expand, act_reduce, act_dilate,
        reduce_all, dilate_weight, expand_weight, *norms, inv_mid, inv_feat, mean_rows, grad_project,
        x_group, g_group,
    )
    (
        task_maps, grad_pooled, grad_pixels, grad_reduce, grad_gain_r, grad_bias_r, grad_dilate,
        grad_gain_d, grad_bias_d, grad_expand, grad_gain_e, grad_bias_e, grad_point, grad_atrous,
        grad_project,
    ) = hand_out(maps, pooled_grad, mean_all, *grads)
    return (
        jnp.swapaxes(task_maps, 1, 2),
        grad_pixels,
        grad_reduce,
        grad_gain_r[0],
        grad_bias_r[0],
        grad_dilate,
        grad_gain_d[0],
        grad_bias_d[0],
        grad_expand,
        grad_gain_e[0],
        grad_bias_e[0],
        grad_point,
        grad_atrous,
        jnp.swapaxes(grad_pooled, 1, 2),
        grad_project,
    )


def solution(mesh):
    placed = (
        P("pix", "chan"),
        P(),
        P(),
        P(None, "chan"),
        P("chan"),
        P("chan"),
        P(None, None, "chan"),
        P("chan"),
        P("chan"),
        P(None, "chan"),
        P("chan"),
        P("chan"),
        P(None, "chan", None),
        P(None, None, None, "chan", None),
        P(None, "chan", None),
        P(None, "chan", None),
        P(None, "pix", "chan"),
    )
    return jax.shard_map(
        shards,
        mesh=mesh,
        in_specs=placed,
        out_specs=(
            P(None, "pix", "chan"),
            P("pix", "chan"),
            P("pix", "chan"),
            P("chan"),
            P("chan"),
            P(None, "pix", "chan"),
            P("chan"),
            P("chan"),
            P("pix", "chan"),
            P("chan"),
            P("chan"),
            P(None, "pix", "chan"),
            P(None, None, None, "pix", "chan"),
            P(None, None, "chan"),
            P(None, "pix", "chan"),
        ),
        check_vma=False,
    )
```

```python
import functools

import jax
import jax.numpy as jnp
from jax import lax
from jax.experimental import pallas as pl
from jax.experimental.pallas import tpu as pltpu
from jax.sharding import PartitionSpec as P

TASKS = 3
TILE_W = 64
NROWS = 256
PIX = 32
CHAN = 4
OWN_ROWS = NROWS // PIX
REACH = 3
EXT_ROWS = OWN_ROWS + 2 * REACH
HEAD = 64
BRANCH = TASKS * HEAD
BRANCH_ORDER = (1, 2, 3, 0, 4)
BRANCH_PLACE = (3, 0, 1, 2, 4)

F32 = jnp.float32
BF16 = jnp.bfloat16
MESH = pl.DeviceIdType.MESH
eps = 1e-05
section_rate = 4
head_rates = (6, 12, 18)
VMEM_LIMIT = 60 * 2**20


def int_div(a, b):
    if b & (b - 1) == 0:
        return lax.shift_right_logical(a, jnp.int32(b.bit_length() - 1))
    return lax.shift_right_logical(a * (2**16 // b + 1), jnp.int32(16))


def int_rem(a, b):
    return a - b * int_div(a, b)


def place_of(row):
    kind = int_rem(row, 6)
    return 43 * kind - int_div(kind, 5) + int_div(row, 6)


def row_of(place):
    kind = int_div(place + int_div(place, 214), 43)
    return 6 * (place - 43 * kind + int_div(kind, 5)) + kind


def tile_at(tiles, row):
    return jnp.where((row >= 0) & (row < NROWS), tiles[jnp.clip(row, 0, NROWS - 1)], -1)


def fill_keys(tiles, keys, first, count):
    start = row_of(jnp.maximum(first, 0))

    def one(n, carry):
        row, kind = carry
        inside = (first + n >= 0) & (first + n < NROWS)
        keys[n] = jnp.where(inside, tiles[row] + 8 * kind, -1)
        end = row + 6 >= NROWS
        next_kind = jnp.where(end, jnp.minimum(kind + 1, 5), kind)
        next_row = jnp.where(end, next_kind, row + 6)
        return jnp.where(inside, next_row, row), jnp.where(inside, next_kind, kind)

    lax.fori_loop(0, count, one, (start, int_rem(start, 6)))


def fill_keep(tiles, keep, i):
    for r in range(OWN_ROWS):
        here = tile_at(tiles, OWN_ROWS * i + r)
        for side, step in enumerate((-section_rate, section_rate)):
            same = jnp.where(tile_at(tiles, OWN_ROWS * i + r + step) == here, 1.0, 0.0)
            keep[side, TILE_W * r : TILE_W * (r + 1)] = jnp.full((TILE_W, 128), same, F32)


def rows_at(value, tile):
    row = lax.broadcasted_iota(jnp.int32, value.shape, 0)
    return jnp.sum(jnp.where(row == tile, value, 0.0), axis=0, keepdims=True)


def add_at(sums, row, tile):
    return sums + jnp.where(lax.broadcasted_iota(jnp.int32, sums.shape, 0) == tile, row, 0.0)


def tile_sizes(grid):
    sizes = jnp.zeros((8, 128), F32)
    for tile in range(8):
        here = jnp.sum(jnp.where(grid == tile, 1.0, 0.0), axis=1, keepdims=True)
        sizes = add_at(sizes, TILE_W * jnp.sum(here, axis=0, keepdims=True), tile)
    return jnp.maximum(sizes, 1.0)


def signal(sem, **where):
    pl.semaphore_signal(sem, inc=1, device_id=where, device_id_type=MESH)


def remote(src, dst, send_sem, recv_sem, **where):
    return pltpu.make_async_remote_copy(
        src_ref=src,
        dst_ref=dst,
        send_sem=send_sem,
        recv_sem=recv_sem,
        device_id=where,
        device_id_type=MESH,
    )


def greet_origins(i):
    barrier, expected = pltpu.get_barrier_semaphore(), 0
    for s in range(OWN_ROWS):
        origin = int_div(row_of(OWN_ROWS * i + s), OWN_ROWS)

        @pl.when(origin != i)
        def _():
            signal(barrier, pix=origin)

        target = int_div(place_of(OWN_ROWS * i + s), OWN_ROWS)
        expected = expected + (target != i).astype(jnp.int32)
    return expected


class RowGather:
    def __init__(self, reach, src, out, spot, sems):
        self.reach, self.src, self.out, self.spot = reach, src, out, spot
        (
            self.ss_row, self.rs_row, self.ss_side, self.rs_side, self.ss_far, self.rs_far, self.ss_halo,
            self.rs_halo,
        ) = sems
        self.order = (0, 7, 1, 6, 2, 5, 3, 4)
        self.edge = [s for s in self.order if s < reach or s >= OWN_ROWS - reach]

    def row_send(self, s):
        place = place_of(OWN_ROWS * self.spot.i + s)
        target, slot = int_div(place, OWN_ROWS), int_rem(place, OWN_ROWS)
        src, landing = self.src.at[s], self.out.at[self.spot.j, self.reach + slot]
        return target, (
            lambda: remote(src, landing, self.ss_row.at[s], self.rs_row.at[slot], pix=target),
            lambda: pltpu.make_async_copy(src, landing, self.rs_row.at[slot]),
        )

    def block(self, chan, s):
        return self.out.at[chan, self.reach + s]

    def side(self, way):
        return self.spot.chan((1, -1)[way])

    def side_copy(self, way, s, chan):
        block = self.block(chan, s)
        return remote(
            block, block, self.ss_side.at[way, s], self.rs_side.at[way, s], chan=self.side(way)
        )

    def far_way(self, s):
        return 0 if s < OWN_ROWS // 2 else 1

    def far_copy(self, s, chan):
        block = self.block(chan, s)
        return remote(
            block, block, self.ss_far.at[s], self.rs_far.at[s], chan=self.side(self.far_way(s))
        )

    def halo_copy(self, turn, chan, s):
        reach = self.reach
        if s < reach:
            lane, slot, target = s, reach + OWN_ROWS + s, self.spot.before
        else:
            lane, slot, target = s - OWN_ROWS + 2 * reach, s - OWN_ROWS + reach, self.spot.after
        return remote(
            self.block(chan, s),
            self.out.at[chan, slot],
            self.ss_halo.at[turn, lane],
            self.rs_halo.at[chan, lane],
            pix=target,
        )

    def halo_arrival(self, chan, lane):
        slot = self.reach + OWN_ROWS + lane if lane < self.reach else lane - self.reach
        dst = self.out.at[chan, slot]
        return remote(
            dst, dst, self.ss_halo.at[0, lane], self.rs_halo.at[chan, lane], pix=self.spot.after
        )

    def send_rows(self):
        for s in range(OWN_ROWS):
            target, (away, here) = self.row_send(s)
            pl.when(target != self.spot.i)(lambda: away().start())
            pl.when(target == self.spot.i)(lambda: here().start())

    def pass_own(self):
        j = self.spot.j
        for s in self.order:
            pltpu.make_async_copy(self.src.at[s], self.block(j, s), self.rs_row.at[s]).wait()
            self.side_copy(0, s, j).start()
            self.side_copy(1, s, j).start()
            if s in self.edge:
                self.halo_copy(0, j, s).start()

    def pass_sides(self):
        for s in self.order:
            for way in range(2):
                chan = self.side(1 - way)
                self.side_copy(way, s, chan).wait_recv()
                if way == self.far_way(s):
                    self.far_copy(s, chan).start()
                if s in self.edge:
                    self.halo_copy(1 + way, chan, s).start()

    def pass_far(self):
        far = self.spot.chan(2)
        for s in self.order:
            self.far_copy(s, far).wait_recv()
            if s in self.edge:
                self.halo_copy(3, far, s).start()

    def await_halo(self, chan):
        for lane in range(2 * self.reach):
            self.halo_arrival(chan, lane).wait_recv()

    def drain(self):
        spot, far = self.spot, self.spot.chan(2)
        for s in range(OWN_ROWS):
            target, (away, here) = self.row_send(s)
            pl.when(target != spot.i)(lambda: away().wait_send())
            self.side_copy(0, s, spot.j).wait_send()
            self.side_copy(1, s, spot.j).wait_send()
            self.far_copy(s, self.side(1 - self.far_way(s))).wait_send()
        for turn, chan in enumerate((spot.j, self.side(1), self.side(0), far)):
            for s in self.edge:
                self.halo_copy(turn, chan, s).wait_send()


def gather_sems(reach):
    dma = pltpu.SemaphoreType.DMA
    return [
        dma((OWN_ROWS,)),
        dma((OWN_ROWS,)),
        dma((2, OWN_ROWS)),
        dma((2, OWN_ROWS)),
        dma((OWN_ROWS,)),
        dma((OWN_ROWS,)),
        dma((CHAN, 2 * reach)),
        dma((CHAN, 2 * reach)),
    ]


GROUP = 8
GROUP_ROWS = GROUP * OWN_ROWS


class Posts:
    def __init__(self, send_sems, recv_sems):
        self.send_sems, self.recv_sems, self.made = send_sems, recv_sems, []

    def copy(self, n, make):
        src, dst, where = make()
        return remote(src, dst, self.send_sems.at[n], self.recv_sems.at[n], **where)

    def post(self, make):
        n = len(self.made)
        self.made.append(make)
        self.copy(n, make).start()
        return n

    def arrive(self, n, dst):
        beside = {"chan": int_rem(lax.axis_index("chan") + 1, CHAN)}
        remote(dst, dst, self.send_sems.at[n], self.recv_sems.at[n], **beside).wait_recv()

    def finish(self):
        for n, make in enumerate(self.made):
            self.copy(n, make).wait_send()


def greet(peers, more=0, meanwhile=lambda: None):
    barrier = pltpu.get_barrier_semaphore()
    for where in peers:
        signal(barrier, **where)
    meanwhile()
    pl.semaphore_wait(barrier, len(peers) + more)


class Spot:
    def __init__(self):
        self.i, self.j = lax.axis_index("pix"), lax.axis_index("chan")
        self.group, self.k = int_div(self.i, GROUP), int_rem(self.i, GROUP)
        self.z, self.core = int_div(self.k, 2), int_rem(self.k, 2)
        self.before, self.after = int_rem(self.i + PIX - 1, PIX), int_rem(self.i + 1, PIX)
        self.mate = self.i + 1 - 2 * self.core

    def chan(self, distance):
        return int_rem(self.j + CHAN + distance, CHAN)

    def in_group(self, distance):
        return int_rem(self.k + GROUP + distance, GROUP)

    def pix_in_group(self, distance):
        return GROUP * self.group + self.in_group(distance)

    def x_of(self, distance):
        return int_rem(self.group + 4 + distance, 4)

    def pix_in_x(self, distance):
        return GROUP * self.x_of(distance) + self.k

    def z_of(self, distance):
        return int_rem(self.z + 4 + distance, 4)

    def pix_in_z(self, distance):
        return GROUP * self.group + 2 * self.z_of(distance) + self.core

    def sum_peers(self):
        return [{"pix": self.pix_in_group(d)} for d in range(1, GROUP)] + [
            {"pix": self.pix_in_x(d)} for d in range(1, 4)
        ]


def dot_nt(a, b):
    return lax.dot_general(a, b, (((1,), (1,)), ((), ())), preferred_element_type=F32)


def dot_tn(a, b):
    return lax.dot_general(a, b, (((0,), (0,)), ((), ())), preferred_element_type=F32)


def dot_nn(a, b):
    return jnp.dot(a, b, preferred_element_type=F32)


def slope(v):
    s = jax.nn.sigmoid(v)
    return s * (1.0 + v * (1.0 - s))


def silu(v):
    return v * jax.nn.sigmoid(v)


def order_at(turn, chan):
    ahead = jnp.where(turn == 0, 0, jnp.where(turn == 1, 3, jnp.where(turn == 2, 1, 2)))
    return int_rem(chan + ahead, CHAN)


def greet_returns(i):
    barrier, expected = pltpu.get_barrier_semaphore(), 0
    for s in range(OWN_ROWS):
        origin = int_div(place_of(OWN_ROWS * i + s), OWN_ROWS)

        @pl.when(origin != i)
        def _():
            signal(barrier, pix=origin)

        target = int_div(row_of(OWN_ROWS * i + s), OWN_ROWS)
        expected = expected + (target != i).astype(jnp.int32)
    return expected


PAD = 24
PADDED = PAD + TILE_W + PAD


def block_at(n, chan):
    ahead = jnp.where(n == 0, 2, jnp.where(n == 1, 1, jnp.where(n == 2, 3, 0)))
    return int_rem(chan + ahead, CHAN)


def heads_kernel(
    tiles, tile_grid, trunk, maps_in, kernel, point, project, pooled_weight, kernel_b,
    grad_project, x_group, mean_kept, trunk_grad, g_group, maps_out, mean_rows, tall,
    keys, mean_all, pooled, x, lhs, acc, pre, relay, spread, near, across, mid, parts, pool_rows, pre_pooled,
    wide, taps, acc_b, edges, head_in, maps_sum, out, out_in, out_sum, near_b, across_b, mean_out, mean_in,
    send_sems, recv_sems, own_sem, ss_row, rs_row, ss_side, rs_side, ss_back, rs_back, *gather,
):
    turn, rate = pl.program_id(0), pl.program_id(1)
    step = 3 * turn + rate
    n, grad_step = turn - 4, step - 12
    spot = Spot()
    posts = Posts(send_sems, recv_sems)
    rows = RowGather(REACH, trunk, x, spot, gather)
    i, j = spot.i, spot.j
    grad_pre, head_part = mid, parts
    blocks = (j, spot.chan(-1), spot.chan(1), spot.chan(2))
    relay_way = (1, 1, -1, -1)
    half_rows = OWN_ROWS // 2
    marks = {}

    low, high = edges.at[0], edges.at[1]

    def g_rows(distance, core, half=None):
        start = OWN_ROWS * (2 * spot.z_of(distance) + core)
        if half is None:
            return g_group.at[pl.ds(start, OWN_ROWS)]
        return g_group.at[pl.ds(start + half_rows * half, half_rows)]

    def g_copy():
        return pltpu.make_async_copy(mid, g_rows(0, spot.core), own_sem.at[1])

    def row_send(s):
        row = row_of(OWN_ROWS * i + s)
        target, slot = int_div(row, OWN_ROWS), int_rem(row, OWN_ROWS)
        return target, (
            lambda: remote(
                maps_sum.at[s], maps_out.at[:, slot], ss_row.at[s], rs_row.at[slot], pix=target
            ),
            lambda: pltpu.make_async_copy(
                maps_sum.at[s], maps_out.at[:, slot], rs_row.at[slot]
            ),
        )

    def widen(start, part):
        held = part[...].astype(F32)
        for which in range(3):
            for t in range(TASKS):
                lane = BRANCH * which + HEAD * t
                one = held[:, :, lane : lane + HEAD]
                wide[3 * t + which, start : start + held.shape[0], PAD : PAD + TILE_W] = (
                    jnp.concatenate([one, one], axis=2)
                )

    def start_grads():
        g_copy().start()
        marks["low"] = posts.post(
            lambda: (mid.at[OWN_ROWS - REACH :], low, {"pix": spot.after})
        )
        marks["high"] = posts.post(lambda: (mid.at[:REACH], high, {"pix": spot.before}))
        for d in (2, 1, 3):
            marks["head", d] = posts.post(
                lambda d=d: (parts.at[spot.chan(d)], head_in.at[d - 1], {"chan": spot.chan(d)})
            )
        for turn in range(2):
            for d in (1, -1):
                half = turn if d == 1 else 1 - turn
                marks["z", d, half] = posts.post(
                    lambda half=half, d=d: (
                        mid.at[half_rows * half : half_rows * (half + 1)],
                        g_rows(0, spot.core, half),
                        {"pix": spot.pix_in_z(d)},
                    )
                )
        sums = jnp.zeros((8, 256), F32)
        for r in range(OWN_ROWS):
            sums = add_at(sums, pool_rows[r : r + 1], tiles[row_of(OWN_ROWS * i + r)])
        near_b[spot.k] = sums
        for d in range(1, GROUP):
            marks["near b", d] = posts.post(
                lambda d=d: (near_b.at[spot.k], near_b.at[spot.k], {"pix": spot.pix_in_group(d)})
            )
        wide[...] = jnp.zeros_like(wide)
        widen(REACH, mid)

    def x_slice(distance, chan=slice(0, CHAN)):
        lanes = pl.ds(pl.multiple_of(128 * spot.z_of(distance), 128), 128)
        return x.at[chan, REACH : REACH + OWN_ROWS, :, lanes]

    def x_rows(distance, core, chan=slice(0, CHAN)):
        return x_group.at[chan, pl.ds(OWN_ROWS * (2 * spot.z_of(distance) + core), OWN_ROWS)]

    def own_copy():
        return pltpu.make_async_copy(x_slice(0), x_rows(0, spot.core), own_sem.at[0])

    def post_x(q):
        way = relay_way[q]
        marks["relay", q] = posts.post(
            lambda: (x_slice(2, blocks[q]), relay.at[q], {"pix": spot.pix_in_z(way)})
        )
        for d in (1, -1):
            marks["x", d, q] = posts.post(
                lambda d=d: (
                    x_slice(d, blocks[q]), x_rows(0, spot.core, blocks[q]), {"pix": spot.pix_in_z(d)}
                )
            )

    def pass_x(q):
        way = relay_way[q]
        posts.arrive(marks["relay", q], relay.at[q])
        marks["far", q] = posts.post(
            lambda: (relay.at[q], x_rows(-way, spot.core, blocks[q]), {"pix": spot.pix_in_z(way)})
        )

    @pl.when(step == 0)
    def _():
        expected = greet_origins(i) + greet_returns(i)

        def prepare():
            fill_keys(tiles, keys, OWN_ROWS * i - REACH, EXT_ROWS)
            spread[...] = jnp.zeros_like(spread)
            for which, b in enumerate(BRANCH_ORDER):
                for c in range(CHAN):
                    for t in range(TASKS):
                        start = BRANCH * c + HEAD * t
                        spread[which, start : start + HEAD, HEAD * t : HEAD * (t + 1)] = project[
                            c, b // 2, t, :, HEAD * (b % 2) : HEAD * (b % 2 + 1)
                        ]

        greet(
            [{"chan": spot.chan(d)} for d in (1, 2, 3)]
            + [{"pix": spot.pix_in_z(d)} for d in (1, -1)]
            + spot.sum_peers()
            + [{"pix": p} for p in (spot.before, spot.after)],
            expected,
            prepare,
        )
        rows.send_rows()
        row_sums = jnp.sum(trunk[...].astype(F32), axis=1)
        sums = jnp.zeros((8, 512), F32)
        for r in range(OWN_ROWS):
            sums = add_at(sums, row_sums[r : r + 1], tile_at(tiles, OWN_ROWS * i + r))
        near[spot.k] = sums
        for d in range(1, GROUP):
            marks["near", d] = posts.post(
                lambda d=d: (near.at[spot.k], near.at[spot.k], {"pix": spot.pix_in_group(d)})
            )
        rows.pass_own()
        post_x(0)
        rows.await_halo(j)

    @pl.when(step == 1)
    def _():
        for d in range(1, GROUP):
            posts.arrive(marks["near", d], near.at[spot.in_group(-d)])
        total = near[0]
        for k in range(1, GROUP):
            total = total + near[k]
        across[spot.group] = total
        for d in range(1, 4):
            marks["across", d] = posts.post(
                lambda d=d: (
                    across.at[spot.group], across.at[spot.group], {"pix": spot.pix_in_x(d)}
                )
            )

    @pl.when(step == 3)
    def _():
        rows.pass_sides()
        post_x(1)
        post_x(2)
        pass_x(0)
        for d in range(1, 4):
            posts.arrive(marks["across", d], across.at[spot.x_of(-d)])
        sums = across[0] + across[1] + across[2] + across[3]
        mean = sums / tile_sizes(tile_grid[...])[:, 0:1]
        mean_all[j] = jnp.concatenate([mean, jnp.zeros((8, 512), F32)], axis=0).astype(BF16)
        for d in (2, 1, 3):
            marks["mean", d] = posts.post(
                lambda d=d: (mean_all.at[j], mean_all.at[j], {"chan": spot.chan(d)})
            )
        rows.await_halo(blocks[1])

    @pl.when(step == 6)
    def _():
        rows.await_halo(blocks[2])
        for d in (1, 2, 3):
            posts.arrive(marks["mean", d], mean_all.at[spot.chan(-d)])
        mean_kept[...] = mean_all[...]
        act = None
        for c in range(CHAN):
            term = dot_nt(mean_all[c], pooled_weight[:, 512 * c : 512 * (c + 1)])
            act = term if act is None else act + term
        pre_pooled[...] = act
        act = silu(act).astype(BF16).astype(F32)
        for r in range(OWN_ROWS):
            row = rows_at(act, tiles[row_of(OWN_ROWS * i + r)])
            pooled[TILE_W * r : TILE_W * (r + 1)] = jnp.broadcast_to(row, (TILE_W, BRANCH)).astype(
                BF16
            )
        rows.pass_far()
        post_x(3)
        own_copy().start()
        pass_x(1)
        pass_x(2)

    @pl.when(step == 9)
    def _():
        rows.await_halo(blocks[3])
        pass_x(3)

    @pl.when(turn < 4)
    def _():
        chan = order_at(turn, j)
        for a in range(3):
            for r in range(OWN_ROWS):
                slot = REACH + r + (a - 1) * (rate + 1)
                row = x[chan, slot]
                if a != 1:
                    row = jnp.where(keys[REACH + r] == keys[slot], row, jnp.zeros_like(row))
                lhs[TILE_W * r : TILE_W * (r + 1), 512 * a : 512 * (a + 1)] = row
        taps = jnp.concatenate([kernel[:, 0, a].reshape(3 * BRANCH, 512) for a in range(3)], axis=1)
        product = dot_nt(lhs[...], taps)

        @pl.when(turn == 0)
        def _():
            acc[rate] = product

        @pl.when(turn > 0)
        def _():
            acc[rate] += product

        @pl.when(rate == 0)
        def _():
            lanes = pl.ds(pl.multiple_of(512 * chan, 512), 512)
            own = x[chan, REACH : REACH + OWN_ROWS].reshape(OWN_ROWS * TILE_W, 512)
            term = dot_nt(own, point[:, :, lanes].reshape(BRANCH, 512))
            pre[3] = jnp.where(turn > 0, pre[3], 0.0) + term

    @pl.when(step == 11)
    def _():
        col = lax.broadcasted_iota(jnp.int32, (OWN_ROWS * TILE_W, HEAD), 0) % TILE_W
        for which, dilation in enumerate(head_rates):
            for t in range(TASKS):
                behind, total, ahead = (
                    acc[which, :, BRANCH * t + HEAD * b : BRANCH * t + HEAD * (b + 1)]
                    for b in range(3)
                )
                behind = pltpu.roll(behind, dilation, 0)
                ahead = pltpu.roll(ahead, OWN_ROWS * TILE_W - dilation, 0)
                total = total + jnp.where(col >= dilation, behind, 0.0)
                total = total + jnp.where(col < TILE_W - dilation, ahead, 0.0)
                pre[which, :, HEAD * t : HEAD * (t + 1)] = total
        cot = jnp.concatenate([maps_in[c].reshape(-1, BRANCH) for c in range(CHAN)], axis=1)
        head = None
        for which in range(5):
            if which < 4:
                before = pre[which]
                logistic = jax.nn.sigmoid(before)
                joined = (before * logistic).astype(BF16)
            else:
                joined = pooled[...]
            weight = spread[which]
            term = dot_nt(joined, weight)
            head = term if head is None else head + term
            grads = dot_tn(joined, cot)
            for t in range(TASKS):
                for c in range(CHAN):
                    lane = BRANCH * c + HEAD * t
                    grad_project[c, which, t] = grads[
                        HEAD * t : HEAD * (t + 1), lane : lane + HEAD
                    ].astype(BF16)
            back = dot_nn(cot, weight)
            if which < 4:
                grad = back * (logistic * (1.0 + before * (1.0 - logistic)))
                grad_pre[:, :, BRANCH * which : BRANCH * (which + 1)] = grad.astype(BF16).reshape(
                    OWN_ROWS, TILE_W, BRANCH
                )
            else:
                sums = jnp.sum(back.reshape(OWN_ROWS, TILE_W, BRANCH), axis=1)
                pool_rows[:, :BRANCH] = sums
                pool_rows[:, BRANCH:] = jnp.zeros((OWN_ROWS, 256 - BRANCH), F32)
        for c in range(CHAN):
            part = head[:, BRANCH * c : BRANCH * (c + 1)].astype(BF16)
            head_part[c] = part.reshape(OWN_ROWS, TILE_W, BRANCH)
        start_grads()

    @pl.when(grad_step == 0)
    def _():
        posts.arrive(marks["low"], low)
        posts.arrive(marks["high"], high)
        widen(0, low)
        widen(REACH + OWN_ROWS, high)

        def one_row(r, carry):
            is_low = lax.broadcasted_iota(jnp.int32, (TILE_W, 2 * HEAD), 1) < HEAD
            out_rows = pl.ds(pl.multiple_of(r * TILE_W, TILE_W), TILE_W)
            for which, dilation in enumerate(head_rates):

                def shifted(tap):
                    t, a, b = tap // 9, tap // 3 % 3 - 1, tap % 3 - 1
                    piece = wide[
                        3 * t + which,
                        r + REACH - a * (which + 1),
                        PAD - b * dilation : PAD - b * dilation + TILE_W,
                    ]
                    same = keys[REACH + r] == keys[REACH + r - a * (which + 1)]
                    return jnp.where(same, piece, 0.0)

                for pair in range(14):
                    first = shifted(2 * pair)
                    second = shifted(2 * pair + 1) if pair < 13 else jnp.zeros_like(first)
                    taps[which, out_rows, 2 * HEAD * pair : 2 * HEAD * (pair + 1)] = jnp.where(
                        is_low, first, second
                    ).astype(BF16)
            return carry

        lax.fori_loop(0, OWN_ROWS, one_row, 0)

    @pl.when(grad_step == 2)
    def _():
        for d in range(1, GROUP):
            posts.arrive(marks["near b", d], near_b.at[spot.in_group(-d)])
        total = near_b[0]
        for k in range(1, GROUP):
            total = total + near_b[k]
        across_b[spot.group] = total
        for d in range(1, 4):
            marks["across b", d] = posts.post(
                lambda d=d: (
                    across_b.at[spot.group], across_b.at[spot.group], {"pix": spot.pix_in_x(d)}
                )
            )

    @pl.when(grad_step == 4)
    def _():
        for d in range(1, 4):
            posts.arrive(marks["across b", d], across_b.at[spot.x_of(-d)])
        sums = across_b[0] + across_b[1] + across_b[2] + across_b[3]
        pooled_pre = sums[:, :BRANCH] * slope(pre_pooled[0:8])
        tall[...] = jnp.concatenate([pooled_pre, jnp.zeros((8, BRANCH), F32)], axis=0).astype(BF16)
        for c in range(CHAN):
            mean_out[c] = dot_nn(tall[...], pooled_weight[:, 512 * c : 512 * (c + 1)]).astype(BF16)
        for d in (2, 1, 3):
            marks["mean b", d] = posts.post(
                lambda d=d: (mean_out.at[spot.chan(d)], mean_in.at[d - 1], {"chan": spot.chan(d)})
            )

    @pl.when(grad_step == 8)
    def _():
        mean = mean_out[j].astype(F32)
        for d in (1, 3, 2):
            posts.arrive(marks["mean b", d], mean_in.at[d - 1])
            mean = mean + mean_in[d - 1].astype(F32)
        mean = mean[0:8] / tile_sizes(tile_grid[...])[:, 0:1]
        for r in range(OWN_ROWS):
            mean_rows[r : r + 1] = rows_at(mean, tiles[OWN_ROWS * i + r])
        for d in (1, 3, 2):
            posts.arrive(marks["head", d], head_in.at[d - 1])
        for s in range(OWN_ROWS):
            held = parts[j, s].astype(F32)
            for d in (1, 2, 3):
                held = held + head_in[d - 1, s].astype(F32)
            for t in range(TASKS):
                maps_sum[s, t] = held[:, HEAD * t : HEAD * (t + 1)].astype(BF16)
            target, (away, here) = row_send(s)
            pl.when(target != i)(lambda: away().start())
            pl.when(target == i)(lambda: here().start())

    @pl.when(grad_step == 5)
    def _():
        for half, d in enumerate((1, -1)):
            posts.arrive(marks["z", d, half], g_rows(-d, spot.core, half))
            marks["far g", half] = posts.post(
                lambda half=half, d=d: (
                    g_rows(-d, spot.core, half),
                    g_rows(-d, spot.core, half),
                    {"pix": spot.pix_in_z(d)},
                )
            )

    @pl.when(grad_step == 10)
    def _():
        for half, d in enumerate((-1, 1)):
            posts.arrive(marks["z", d, half], g_rows(-d, spot.core, half))

    @pl.when(turn >= 4)
    def _():
        product = dot_nn(taps[rate, :, : 27 * HEAD], kernel_b[...].reshape(27 * HEAD, -1))

        @pl.when(rate == 0)
        def _():
            lanes = pl.ds(pl.multiple_of(512 * block_at(n, j), 512), 512)
            grads = mid[...].reshape(OWN_ROWS * TILE_W, -1)[:, 3 * BRANCH :]
            acc_b[...] = product + dot_nn(grads, point[:, :, lanes].reshape(BRANCH, 512))

        @pl.when(rate == 1)
        def _():
            acc_b[...] += product

        @pl.when(rate == 2)
        def _():
            total = acc_b[...] + product
            out[block_at(n, j)] = total.astype(BF16).reshape(OWN_ROWS, TILE_W, 512)

    def side_send(chan, s):
        turn = int_rem(chan + CHAN - j, CHAN) - 1
        return remote(
            out.at[chan, s], out_in.at[turn, s], ss_side.at[turn, s], rs_side.at[turn, s], chan=chan
        )

    @pl.when((turn >= 4) & (rate == 2) & (n < 3))
    def _():
        for s in range(OWN_ROWS):
            side_send(block_at(n, j), s).start()

    def back_send(s):
        row = row_of(OWN_ROWS * i + s)
        target, slot = int_div(row, OWN_ROWS), int_rem(row, OWN_ROWS)
        return target, (
            lambda: remote(
                out_sum.at[s], trunk_grad.at[slot], ss_back.at[s], rs_back.at[slot], pix=target
            ),
            lambda: pltpu.make_async_copy(out_sum.at[s], trunk_grad.at[slot], rs_back.at[slot]),
        )

    def side_arrival(turn, s):
        dst = out_in.at[turn, s]
        return remote(dst, dst, ss_side.at[turn, s], rs_side.at[turn, s], chan=spot.chan(1))

    @pl.when(grad_step == 11)
    def _():
        for s in range(OWN_ROWS):
            held = out[j, s].astype(F32)
            for turn in range(3):
                side_arrival(turn, s).wait_recv()
                held = held + out_in[turn, s].astype(F32)
            out_sum[s] = held.astype(BF16)
            target, (away, here) = back_send(s)
            pl.when(target != i)(lambda: away().start())
            pl.when(target == i)(lambda: here().start())
        for half in range(2):
            posts.arrive(marks["far g", half], g_rows(2, spot.core, half))
        g_copy().wait()
        for s in range(OWN_ROWS):
            pltpu.make_async_copy(out_sum.at[s], trunk_grad.at[s], rs_back.at[s]).wait()
            target, (away, here) = back_send(s)
            pl.when(target != i)(lambda: away().wait_send())
            for d in (1, 2, 3):
                side_send(spot.chan(d), s).wait_send()
            pltpu.make_async_copy(maps_sum.at[s], maps_out.at[:, s], rs_row.at[s]).wait()
            target, (away, here) = row_send(s)
            pl.when(target != i)(lambda: away().wait_send())
        for q in range(4):
            for d in (1, -1):
                posts.arrive(marks["x", d, q], x_rows(-d, spot.core, blocks[q]))
            posts.arrive(marks["far", q], x_rows(2, spot.core, blocks[q]))
        own_copy().wait()
        rows.drain()
        posts.finish()


def heads(*operands):
    pixels = OWN_ROWS * TILE_W
    whole = pl.BlockSpec(memory_space=pltpu.VMEM)
    hbm = pl.BlockSpec(memory_space=pl.ANY)
    dma = pltpu.SemaphoreType.DMA
    shape = jax.ShapeDtypeStruct
    maps, rows = (OWN_ROWS, TILE_W, BRANCH), (OWN_ROWS, TILE_W, 512)

    def forward_block(q, r):
        chan = order_at(jnp.minimum(q, 3), lax.axis_index("chan"))
        return (0, jnp.where(q < 4, r, 2), 0, 0, 0, chan)

    def grad_block(q, r):
        chan = block_at(jnp.maximum(q - 4, 0), lax.axis_index("chan"))
        return (0, jnp.where(q < 4, 0, r), 0, 0, 0, chan)

    return pl.pallas_call(
        heads_kernel,
        grid=(8, 3),
        in_specs=[pl.BlockSpec(memory_space=pltpu.SMEM)]
        + [whole] * 3
        + [pl.BlockSpec((TASKS, 1, 3, 3, HEAD, 512), forward_block)]
        + [whole] * 3
        + [pl.BlockSpec((TASKS, 1, 3, 3, HEAD, 512), grad_block)],
        out_specs=[whole, hbm, whole, hbm, hbm, hbm, whole, whole],
        out_shape=[
            shape((CHAN, 5, TASKS, HEAD, HEAD), BF16),
            shape((CHAN, GROUP_ROWS, TILE_W, 128), BF16),
            shape((CHAN, 16, 512), BF16),
            shape(rows, BF16),
            shape((GROUP_ROWS, TILE_W, 4 * BRANCH), BF16),
            shape((TASKS, OWN_ROWS, TILE_W, HEAD), BF16),
            shape((OWN_ROWS, 512), F32),
            shape((16, BRANCH), BF16),
        ],
        scratch_shapes=[
            pltpu.SMEM((EXT_ROWS,), jnp.int32),
            pltpu.VMEM((CHAN, 16, 512), BF16),
            pltpu.VMEM((pixels, BRANCH), BF16),
            pltpu.VMEM((CHAN, EXT_ROWS, TILE_W, 512), BF16),
            pltpu.VMEM((pixels, 3 * 512), BF16),
            pltpu.VMEM((3, pixels, 3 * BRANCH), F32),
            pltpu.VMEM((4, pixels, BRANCH), F32),
            pltpu.VMEM((4, OWN_ROWS, TILE_W, 128), BF16),
            pltpu.VMEM((5, 256 * TASKS, BRANCH), BF16),
            pltpu.VMEM((GROUP, 8, 512), F32),
            pltpu.VMEM((4, 8, 512), F32),
            pltpu.VMEM((OWN_ROWS, TILE_W, 4 * BRANCH), BF16),
            pltpu.VMEM((CHAN, *maps), BF16),
            pltpu.VMEM((OWN_ROWS, 256), F32),
            pltpu.VMEM((16, BRANCH), F32),
            pltpu.VMEM((9, EXT_ROWS, PADDED, 2 * HEAD), F32),
            pltpu.VMEM((3, pixels, 28 * HEAD), BF16),
            pltpu.VMEM((pixels, 512), F32),
            pltpu.VMEM((2, REACH, TILE_W, 4 * BRANCH), BF16),
            pltpu.VMEM((CHAN - 1, *maps), BF16),
            pltpu.VMEM((OWN_ROWS, TASKS, TILE_W, HEAD), BF16),
            pltpu.VMEM((CHAN, *rows), BF16),
            pltpu.VMEM((CHAN - 1, *rows), BF16),
            pltpu.VMEM(rows, BF16),
            pltpu.VMEM((GROUP, 8, 256), F32),
            pltpu.VMEM((4, 8, 256), F32),
            pltpu.VMEM((CHAN, 16, 512), BF16),
            pltpu.VMEM((CHAN - 1, 16, 512), BF16),
            dma((64,)),
            dma((64,)),
            dma((2,)),
            dma((OWN_ROWS,)),
            dma((OWN_ROWS,)),
            dma((CHAN - 1, OWN_ROWS)),
            dma((CHAN - 1, OWN_ROWS)),
            dma((OWN_ROWS,)),
            dma((OWN_ROWS,)),
            *gather_sems(REACH),
        ],
        compiler_params=pltpu.CompilerParams(
            collective_id=2, has_side_effects=True, vmem_limit_bytes=VMEM_LIMIT
        ),
        cost_estimate=pl.CostEstimate(
            flops=24_000_000_000, bytes_accessed=56_000_000, transcendentals=0
        ),
        name="heads",
    )(*operands)


class GroupSum:
    def __init__(self, out, relay_in, side_in, spot, links):
        self.out, self.relay_in, self.side_in, self.spot, self.links = out, relay_in, side_in, spot, links
        self.ready, self.open, self.arrivals = [], [], []

    def flush(self):
        self.relay()
        for n, way in self.ready:
            self.send(n, way)
        self.ready = []

    def send(self, n, way):
        spot, links, out = self.spot, self.links, self.out
        relay = links.send(out.at[n, spot.x_of(2)], self.relay_in.at[n], pix=spot.pix_in_x(way))
        side = links.send(
            out.at[n, spot.x_of(-way)], self.side_in.at[n, 0], pix=spot.pix_in_x(-way)
        )
        self.arrivals.append((side, n, 0))
        self.open.append((n, way, relay))

    def relay(self):
        for n, way, relay in self.open:
            self.links.arrive(relay, self.relay_in.at[n])
            target = self.spot.x_of(way)
            both = self.out[n, target].astype(F32) + self.relay_in[n].astype(F32)
            self.out[n, target] = both.astype(BF16)
            side = self.links.send(
                self.out.at[n, target], self.side_in.at[n, 1], pix=self.spot.pix_in_x(way)
            )
            self.arrivals.append((side, n, 1))
        self.open = []

    def finish(self, place):
        for side, n, which in self.arrivals:
            self.links.arrive(side, self.side_in.at[n, which])
        for n in range(self.out.shape[0]):
            total = self.out[n, self.spot.group].astype(F32)
            place(n, total + self.side_in[n, 0].astype(F32) + self.side_in[n, 1].astype(F32))


class Links:
    def __init__(self, send_sems, recv_sems):
        self.send_sems, self.recv_sems, self.count, self.sent = send_sems, recv_sems, 0, []

    def send(self, src, dst, **where):
        n = self.count
        self.count += 1
        copy = remote(src, dst, self.send_sems.at[n], self.recv_sems.at[n], **where)
        copy.start()
        self.sent.append(copy)
        return n

    def arrive(self, n, dst):
        beside = {"chan": int_rem(lax.axis_index("chan") + 1, CHAN)}
        remote(dst, dst, self.send_sems.at[n], self.recv_sems.at[n], **beside).wait_recv()

    def finish(self):
        for copy in self.sent:
            copy.wait_send()


def sum_over_pix(value, near, across, spot, links, meanwhile=lambda: None):
    near[spot.k] = value
    sent = [
        links.send(near.at[spot.k], near.at[spot.k], pix=spot.pix_in_group(d))
        for d in range(1, GROUP)
    ]
    meanwhile()
    for d, n in zip(range(1, GROUP), sent):
        links.arrive(n, near.at[spot.in_group(-d)])
    total = near[0]
    for k in range(1, GROUP):
        total = total + near[k]
    across[spot.group] = total
    sent = [
        links.send(across.at[spot.group], across.at[spot.group], pix=spot.pix_in_x(d))
        for d in range(1, 4)
    ]
    meanwhile()
    for d, n in zip(range(1, 4), sent):
        links.arrive(n, across.at[spot.x_of(-d)])
    return across[0] + across[1] + across[2] + across[3]


def two_sums(first, second):
    width = first.shape[1]
    rows = [jnp.sum(first, axis=0, keepdims=True), jnp.sum(second, axis=0, keepdims=True)]
    return jnp.concatenate(rows + [jnp.zeros((6, width), F32)], axis=0)


PIXELS = NROWS * TILE_W
OWN = OWN_ROWS * TILE_W
MID_OWN = 128
FEAT_OWN = 512


def col_shift(value, distance):
    col = lax.broadcasted_iota(jnp.int32, value.shape, 0) % TILE_W
    rows = value.shape[0]
    moved = pltpu.roll(value, (rows - distance) % rows, 0)
    inside = (col < TILE_W - distance) if distance > 0 else (col >= -distance)
    return jnp.where(inside, moved, 0.0)


def section_forward_kernel(
    tiles, draws, pixels, wr, wd, we, gain_r, bias_r, gain_d, bias_d, gain_e, bias_e, project, cotangent,
    trunk, unit_r, unit_d, unit_e, act_r, act_d, wr_all, inv_mid, inv_feat, project_all, maps_in,
    keep, project_out, part_out, part_in, near_m, across_m, near_f, across_f, maps_own,
    send_sems, recv_sems, ss_map, rs_map,
):
    spot = Spot()
    links = Links(send_sems, recv_sems)
    i, j = spot.i, spot.j
    expected = greet_origins(i)

    def map_send(s):
        place = place_of(OWN_ROWS * i + s)
        target, slot = int_div(place, OWN_ROWS), int_rem(place, OWN_ROWS)
        return target, (
            lambda: remote(
                maps_own.at[s], maps_in.at[j, slot], ss_map.at[s], rs_map.at[slot], pix=target
            ),
            lambda: pltpu.make_async_copy(maps_own.at[s], maps_in.at[j, slot], rs_map.at[slot]),
        )

    def prepare():
        fill_keep(tiles, keep, spot.i)
        lane = lax.broadcasted_iota(jnp.int32, (8, 128), 1)
        drawn = jnp.full((8, 128), -1e30, F32)
        for t in range(TASKS):
            drawn = jnp.where(lane == t, draws[t].astype(F32) / 3.0, drawn)
        grown = jnp.where(lane < TASKS, jnp.exp(drawn - jnp.max(drawn, axis=1, keepdims=True)), 0.0)
        grown = grown / jnp.sum(grown, axis=1, keepdims=True)
        for t in range(TASKS):
            weight = jnp.sum(jnp.where(lane == t, grown, 0.0), axis=1, keepdims=True)[0:1]
            scaled = (cotangent[t].astype(F32).T * weight).astype(BF16)
            maps_own[:, :, HEAD * t : HEAD * (t + 1)] = scaled.reshape(OWN_ROWS, TILE_W, HEAD)
        for c in range(CHAN):
            for b in range(5):
                lane = HEAD * (b % 2)
                project_out[c, b // 2, :, :, lane : lane + HEAD] = project[
                    :, :, 256 * b + HEAD * c : 256 * b + HEAD * (c + 1)
                ]
            project_out[c, 2, :, :, HEAD:] = jnp.zeros((TASKS, HEAD, HEAD), BF16)

    greet(
        [{"chan": spot.chan(d)} for d in (1, 2, 3)]
        + spot.sum_peers()
        + [{"pix": p} for p in (spot.before, spot.after, spot.mate)],
        expected,
        prepare,
    )
    half = FEAT_OWN // 2

    def half_of(chan, core):
        return pl.ds(pl.multiple_of(FEAT_OWN * chan + half * core, half), half)

    own_half = half_of(0, spot.core)
    other_half = half_of(0, 1 - spot.core)
    sent = {
        d: links.send(
            wr.at[half_of(spot.chan(d), spot.core)], wr_all.at[j, own_half], chan=spot.chan(d)
        )
        for d in (2, 1, 3)
    }
    for s in range(OWN_ROWS):
        target, (away, here) = map_send(s)
        pl.when(target != i)(lambda: away().start())
        pl.when(target == i)(lambda: here().start())
    wr_all[j] = wr[pl.ds(pl.multiple_of(FEAT_OWN * j, FEAT_OWN), FEAT_OWN)]
    pre = dot_nn(pixels[...], wr_all[j])
    mates = {}
    for d in (1, 3, 2):
        source = spot.chan(-d)
        links.arrive(sent[d], wr_all.at[source, own_half])
        mates[d] = links.send(
            wr_all.at[source, own_half], wr_all.at[source, own_half], pix=spot.mate
        )
    back = {}
    for d in (1, 3, 2):
        source = spot.chan(-d)
        links.arrive(mates[d], wr_all.at[source, other_half])
        part_out[d - 1] = dot_nn(pixels[...], wr_all[source]).astype(BF16)
        back[d] = links.send(part_out.at[d - 1], part_in.at[d - 1], chan=source)
    for d in (1, 3, 2):
        links.arrive(back[d], part_in.at[d - 1])
        pre = pre + part_in[d - 1].astype(F32)

    project_sent = {}

    def send_project():
        for d in (2, 1, 3):
            for last, part in ((False, spot.core), (True, 2)):
                project_sent[d, last] = links.send(
                    project_out.at[spot.chan(d), part], project_all.at[j, part], chan=spot.chan(d)
                )

    def swap_project():
        for d in (1, 3, 2):
            source = spot.chan(-d)
            links.arrive(project_sent[d, False], project_all.at[source, spot.core])
            links.arrive(project_sent[d, True], project_all.at[source, 2])
            project_sent[d] = links.send(
                project_all.at[source, spot.core], project_all.at[source, spot.core], pix=spot.mate
            )

    halves = (slice(0, OWN_ROWS // 2), slice(OWN_ROWS // 2, OWN_ROWS))
    maps_sent = {}

    def send_maps():
        for s in range(OWN_ROWS):
            pltpu.make_async_copy(maps_own.at[s], maps_in.at[j, s], rs_map.at[s]).wait()
        for part in halves:
            for d in (1, -1):
                block = maps_in.at[j, part]
                maps_sent[d, part.start] = links.send(block, block, chan=spot.chan(d))

    def pass_maps():
        for d in (1, -1):
            for part in halves:
                links.arrive(maps_sent[d, part.start], maps_in.at[spot.chan(-d), part])
        for d, part in zip((1, -1), halves):
            block = maps_in.at[spot.chan(-d), part]
            maps_sent[part.start] = links.send(block, block, chan=spot.chan(d))

    todo = [send_project, lambda: None, swap_project]

    def meanwhile():
        if todo:
            todo.pop(0)()

    def norm(value, near, across, gain, bias):
        sums = sum_over_pix(two_sums(value, value * value), near, across, spot, links, meanwhile)
        center = sums[0:1] / PIXELS
        inv = lax.rsqrt(sums[1:2] / PIXELS - center * center + eps)
        unit = (value - center) * inv
        return unit, unit * gain + bias, inv

    unit, normed, inv_r = norm(pre, near_m.at[0], across_m.at[0], gain_r[...], bias_r[...])
    unit_r[...] = unit
    own = slice(section_rate, section_rate + OWN_ROWS)
    act_r[j, own] = silu(normed).astype(BF16).reshape(OWN_ROWS, TILE_W, MID_OWN)
    low, high = slice(0, section_rate), slice(section_rate + OWN_ROWS, 2 * section_rate + OWN_ROWS)
    first, last = slice(section_rate, 2 * section_rate), slice(OWN_ROWS, section_rate + OWN_ROWS)
    sent = {
        d: links.send(act_r.at[j, own], act_r.at[j, own], chan=spot.chan(d)) for d in (2, 1, 3)
    }
    send_maps()
    arrivals = []
    for d in (0, 1, 3, 2):
        source = spot.chan(-d)
        if d:
            links.arrive(sent[d], act_r.at[source, own])
        n = links.send(act_r.at[source, first], act_r.at[source, high], pix=spot.before)
        arrivals.append((n, act_r.at[source, high]))
        n = links.send(act_r.at[source, last], act_r.at[source, low], pix=spot.after)
        arrivals.append((n, act_r.at[source, low]))
    for n, dst in arrivals:
        links.arrive(n, dst)
    pre = jnp.zeros((OWN, MID_OWN), F32)
    for a in range(3):
        rows = slice(section_rate * a, section_rate * a + OWN_ROWS)
        window = jnp.concatenate(
            [act_r[c, rows].reshape(OWN, MID_OWN) for c in range(CHAN)], axis=1
        )
        terms = [dot_nn(window, wd[3 * a + b]) for b in range(3)]
        term = terms[1] + col_shift(terms[0], -section_rate) + col_shift(terms[2], section_rate)
        pre = pre + (term if a == 1 else term * keep[a // 2])

    unit, normed, inv_d = norm(pre, near_m.at[1], across_m.at[1], gain_d[...], bias_d[...])
    unit_d[...] = unit
    inv_mid[...] = jnp.concatenate([inv_r, inv_d, jnp.zeros((6, MID_OWN), F32)], axis=0)
    act_d[j] = silu(normed).astype(BF16)
    sent = {d: links.send(act_d.at[j], act_d.at[j], chan=spot.chan(d)) for d in (2, 1, 3)}
    pass_maps()
    for d in (1, 3, 2):
        links.arrive(sent[d], act_d.at[spot.chan(-d)])
    full = jnp.concatenate([act_d[c] for c in range(CHAN)], axis=1)
    unit, normed, inv_e = norm(
        dot_nn(full, we[...]), near_f, across_f, gain_e[...], bias_e[...]
    )
    unit_e[...] = unit
    inv_feat[...] = jnp.concatenate([inv_e, jnp.zeros((7, FEAT_OWN), F32)], axis=0)
    out = silu(normed + pixels[...].astype(F32)).astype(BF16)
    trunk[...] = out.reshape(OWN_ROWS, TILE_W, FEAT_OWN)
    for d in (1, 3, 2):
        links.arrive(project_sent[d], project_all.at[spot.chan(-d), 1 - spot.core])
    project_all[j] = project_out[j]
    for part in halves:
        links.arrive(maps_sent[part.start], maps_in.at[spot.chan(2), part])
    for s in range(OWN_ROWS):
        target, (away, here) = map_send(s)
        pl.when(target != i)(lambda: away().wait_send())
    links.finish()


def section_forward(*operands):
    whole = pl.BlockSpec(memory_space=pltpu.VMEM)
    shape = jax.ShapeDtypeStruct
    mid, feat = (OWN, MID_OWN), (OWN, FEAT_OWN)
    dma = pltpu.SemaphoreType.DMA
    return pl.pallas_call(
        section_forward_kernel,
        in_specs=[pl.BlockSpec(memory_space=pltpu.SMEM)] * 2 + [whole] * 12,
        out_specs=[whole] * 11,
        out_shape=[
            shape((OWN_ROWS, TILE_W, FEAT_OWN), BF16),
            shape(mid, F32),
            shape(mid, F32),
            shape(feat, F32),
            shape((CHAN, OWN_ROWS + 2 * section_rate, TILE_W, MID_OWN), BF16),
            shape((CHAN, *mid), BF16),
            shape((CHAN, FEAT_OWN, MID_OWN), BF16),
            shape((8, MID_OWN), F32),
            shape((8, FEAT_OWN), F32),
            shape((CHAN, 3, TASKS, HEAD, 2 * HEAD), BF16),
            shape((CHAN, OWN_ROWS, TILE_W, BRANCH), BF16),
        ],
        scratch_shapes=[
            pltpu.VMEM((2, OWN, MID_OWN), F32),
            pltpu.VMEM((CHAN, 3, TASKS, HEAD, 2 * HEAD), BF16),
            pltpu.VMEM((3, *mid), BF16),
            pltpu.VMEM((3, *mid), BF16),
            pltpu.VMEM((2, GROUP, 8, MID_OWN), F32),
            pltpu.VMEM((2, 4, 8, MID_OWN), F32),
            pltpu.VMEM((GROUP, 8, FEAT_OWN), F32),
            pltpu.VMEM((4, 8, FEAT_OWN), F32),
            pltpu.VMEM((OWN_ROWS, TILE_W, BRANCH), BF16),
            dma((72,)),
            dma((72,)),
            dma((OWN_ROWS,)),
            dma((OWN_ROWS,)),
        ],
        compiler_params=pltpu.CompilerParams(
            collective_id=5, has_side_effects=True, vmem_limit_bytes=VMEM_LIMIT
        ),
        cost_estimate=pl.CostEstimate(
            flops=2_000_000_000, bytes_accessed=120_000_000, transcendentals=0
        ),
        name="section_forward",
    )(*operands)


class Scatter:
    def __init__(self, parts, mate_in, near, near_in, far, far_in, spot, links):
        self.parts, self.mate_in, self.near, self.near_in = parts, mate_in, near, near_in
        self.far, self.far_in, self.spot, self.links = far, far_in, spot, links

    def start(self):
        spot = self.spot
        self.sent = self.links.send(self.parts.at[1 - spot.core], self.mate_in, pix=spot.mate)

    def along_z(self):
        spot, links = self.spot, self.links
        links.arrive(self.sent, self.mate_in)
        for z in range(4):
            self.near[z] = (
                self.parts[spot.core, z].astype(F32) + self.mate_in[z].astype(F32)
            ).astype(BF16)
        self.sent = {
            d: links.send(
                self.near.at[spot.z_of(d)], self.near_in.at[d - 1], pix=spot.pix_in_z(d)
            )
            for d in (2, 1, 3)
        }

    def along_x(self):
        spot, links = self.spot, self.links
        total = self.near[spot.z].astype(F32)
        for d in (1, 3, 2):
            links.arrive(self.sent[d], self.near_in.at[d - 1])
            total = total + self.near_in[d - 1].astype(F32)
        self.far[...] = total.astype(BF16)
        self.sent = {
            d: links.send(self.far.at[spot.x_of(d)], self.far_in.at[d - 1], pix=spot.pix_in_x(d))
            for d in (2, 1, 3)
        }

    def finish(self):
        spot, links = self.spot, self.links
        total = self.far[spot.group].astype(F32)
        for d in (1, 3, 2):
            links.arrive(self.sent[d], self.far_in.at[d - 1])
            total = total + self.far_in[d - 1].astype(F32)
        return total


def scatter_scratch(*shape):
    return [
        pltpu.VMEM((2, 4, 4, *shape), BF16),
        pltpu.VMEM((4, 4, *shape), BF16),
        pltpu.VMEM((4, 4, *shape), BF16),
        pltpu.VMEM((3, 4, *shape), BF16),
        pltpu.VMEM((4, *shape), BF16),
        pltpu.VMEM((3, *shape), BF16),
    ]


def spot_of(device):
    return device % 2, device % GROUP // 2, device // GROUP


def section_backward_kernel(
    tiles, trunk_grad, pixels, unit_r, unit_d, unit_e, act_r, act_d, wr_all, wd, we,
    gain_r, bias_r, gain_d, bias_d, gain_e, bias_e, inv_mid, inv_feat, mean_rows, projects, x_group,
    g_group, *refs,
):
    (
        grad_pixels, grad_reduce, grad_gain_r, grad_bias_r, grad_dilate, grad_gain_d, grad_bias_d,
        grad_expand, grad_gain_e, grad_bias_e, grad_point, grad_atrous, grad_project,
    ) = refs[:13]
    scratch = refs[13:]
    (
        keys, keep, wd_cat, side_out, side_in, halo, taps, full, project_in, project_wide, reduce_out,
        near_m, across_m, near_f, across_f, x_all, x_base, x_now, g_all, g_now,
    ) = scratch[:20]
    send_sems, recv_sems, ss_reduce, rs_reduce, load_sems, edge_sems = scratch[-6:]
    buffers = scratch[20:-6]
    spot = Spot()
    links = Links(send_sems, recv_sems)
    i, j = spot.i, spot.j
    by_expand, by_dilate, by_project, by_reduce = [
        Scatter(*buffers[6 * n : 6 * n + 6], spot, links) for n in range(4)
    ]
    owner_i, owner_j = GROUP * j + int_div(i, 4), int_rem(i, 4)
    maker_i, maker_j = 4 * int_rem(i, GROUP) + j, spot.group
    stays = (owner_i == i) & (owner_j == j)
    barrier = pltpu.get_barrier_semaphore()

    @pl.when(jnp.logical_not(stays))
    def _():
        signal(barrier, pix=maker_i, chan=maker_j)

    peers = [{"chan": spot.chan(d)} for d in (1, 2, 3)] + spot.sum_peers()
    peers += [{"pix": spot.before}, {"pix": spot.after}]

    def core_rows(z, core, first=0):
        return pl.ds(first + OWN_ROWS * (2 * z + core), OWN_ROWS)

    def shares(core):
        pairs = []
        for z in range(4):
            rows, moved = core_rows(z, core), core_rows(z, core, REACH)
            pairs.append((x_group.at[:, rows], x_all.at[:, rows]))
            pairs.append((g_group.at[rows], g_all.at[moved]))
        return pairs

    loads = [
        pltpu.make_async_copy(src, dst, load_sems.at[n])
        for n, (src, dst) in enumerate(shares(spot.core))
    ]

    def prepare():
        for load in loads:
            load.start()
        fill_keep(tiles, keep, i)
        fill_keys(tiles, keys, GROUP_ROWS * spot.group - REACH, GROUP_ROWS + 2 * REACH)
        for tap in range(9):
            wd_cat[:, MID_OWN * tap : MID_OWN * (tap + 1)] = wd[tap]

    for step in (1, -1):
        x_maker = int_rem(spot.group + 4 - step, 4)
        maker_core = (1 + step) // 2
        peers.append({"pix": GROUP * x_maker + 2 * spot.z + maker_core})
    peers.append({"pix": spot.mate})
    greet(peers, 1 - stays.astype(jnp.int32), prepare)

    atrous_sum = GroupSum(*buffers[24:27], spot, links)
    point_sum = GroupSum(*buffers[27:30], spot, links)
    x_target = int_rem(spot.group + 3 + 2 * spot.core, 4)

    def edge_copy(core):
        return remote(
            g_group.at[pl.ds(spot.core * (GROUP_ROWS - REACH), REACH)],
            g_all.at[pl.ds((1 - spot.core) * (GROUP_ROWS + REACH), REACH)],
            edge_sems.at[core],
            edge_sems.at[2 + 1 - spot.core],
            pix=GROUP * x_target + 2 * spot.z + core,
        )

    def edge_arrival(high):
        dst = g_all.at[pl.ds(high * (GROUP_ROWS + REACH), REACH)]
        return remote(dst, dst, edge_sems.at[0], edge_sems.at[2 + high], chan=spot.chan(1))

    for core in range(2):
        edge_copy(core).start()
    mates = [links.send(src, dst, pix=spot.mate) for src, dst in shares(spot.core)]

    def row_block(r):
        return pl.ds(pl.multiple_of(r * TILE_W, TILE_W), TILE_W)

    def take():
        for load in loads:
            load.wait()
        for n, (_, dst) in zip(mates, shares(1 - spot.core)):
            links.arrive(n, dst)
        for high in range(2):
            edge_arrival(high).wait_recv()

        def one_row(r, carry):
            is_low = lax.broadcasted_iota(jnp.int32, (TILE_W, 2 * HEAD), 1) < HEAD
            for pair in range(2):
                first = x_all[2 * pair, r].astype(F32)
                second = x_all[2 * pair + 1, r].astype(F32)
                lower = jnp.where(is_low, first, pltpu.roll(second, HEAD, 1))
                upper = jnp.where(is_low, pltpu.roll(first, HEAD, 1), second)
                x_base[row_block(r), 2 * HEAD * pair : 2 * HEAD * (pair + 1)] = jnp.where(
                    spot.core == 0, lower, upper
                ).astype(BF16)
            return carry

        lax.fori_loop(0, GROUP_ROWS, one_row, 0, unroll=4)

    def pick(which):
        def one_row(r, carry):
            pieces = []
            for a in range(3):
                piece = g_all[
                    r + REACH - (a - 1) * (which + 1), :, BRANCH * which : BRANCH * (which + 1)
                ]
                same = keys[r + REACH] == keys[r + REACH - (a - 1) * (which + 1)]
                pieces.append(jnp.where(same, piece, jnp.zeros_like(piece)))
            g_now[row_block(r)] = jnp.concatenate(pieces, axis=1)
            return carry

        lax.fori_loop(0, GROUP_ROWS, one_row, 0, unroll=4)

    def multiply(which, b):
        held = x_base
        if b != 1:
            held = x_now

            def one_row(r, carry):
                row = x_base[row_block(r)].astype(F32)
                x_now[row_block(r)] = col_shift(row, (b - 1) * head_rates[which]).astype(BF16)
                return carry

            lax.fori_loop(0, GROUP_ROWS, one_row, 0, unroll=4)
        product = dot_tn(g_now[...], held[...]).T.astype(BF16)
        n = 3 * which + b
        for c in range(CHAN):
            atrous_sum.out[n, c] = product[HEAD * c : HEAD * (c + 1)]
        atrous_sum.ready.append((n, 1 if n % 2 else -1))

    def multiply_point():
        grads = g_all[REACH : REACH + GROUP_ROWS, :, 3 * BRANCH :].reshape(-1, BRANCH)
        product = dot_tn(grads, x_base[...]).T.astype(BF16)
        for c in range(CHAN):
            point_sum.out[0, c] = product[HEAD * c : HEAD * (c + 1)]
        point_sum.ready.append((0, 1))

    tasks = [lambda: None, lambda: None, take]
    for which in range(3):
        tasks.append(functools.partial(pick, which))
        tasks += [functools.partial(multiply, which, b) for b in range(3)]
    tasks += [multiply_point]
    queue = iter(tasks)

    def flush():
        atrous_sum.flush()
        point_sum.flush()

    def meanwhile(count=1):
        for _ in range(count):
            task = next(queue, None)
            if task is not None:
                task()

    project_sent = {
        d: links.send(projects.at[spot.chan(d)], project_in.at[d - 1], chan=spot.chan(d))
        for d in (2, 1, 3)
    }

    def norm_back(grad, unit, near, across, scale):
        sums = sum_over_pix(two_sums(grad, grad * unit), near, across, spot, links, meanwhile)
        pre = scale * (grad - sums[0:1] / PIXELS - unit * (sums[1:2] / PIXELS))
        return pre.astype(BF16), sums

    grad_trunk = trunk_grad[...].astype(F32) + mean_rows[...][:, None, :]
    grad_trunk = grad_trunk.reshape(OWN, FEAT_OWN)
    unit = unit_e[...]
    summed = unit * gain_e[...] + bias_e[...] + pixels[...].astype(F32)
    grad_summed = grad_trunk * slope(summed)
    g_expand, sums = norm_back(grad_summed, unit, near_f, across_f, gain_e[...] * inv_feat[0:1])
    grad_bias_e[...] = sums[0:1]
    grad_gain_e[...] = sums[1:2]

    def sides(turn, make):
        sent = {}
        for d in (2, 1, 3):
            side_out[turn, d - 1] = make(spot.chan(d)).astype(BF16)
            sent[d] = links.send(
                side_out.at[turn, d - 1], side_in.at[turn, d - 1], chan=spot.chan(d)
            )
        return sent

    def side_sum(turn, own, sent):
        for d in (1, 3, 2):
            links.arrive(sent[d], side_in.at[turn, d - 1])
            own = own + side_in[turn, d - 1].astype(F32)
        return own

    def mid_rows(chan):
        return pl.ds(pl.multiple_of(MID_OWN * chan, MID_OWN), MID_OWN)

    sent = sides(0, lambda c: dot_nt(g_expand, we[mid_rows(c)]))
    own = dot_nt(g_expand, we[mid_rows(j)])
    part = 16
    for c in range(CHAN):
        grads = dot_tn(act_d[c], g_expand).astype(BF16)
        for n in range(8):
            by_expand.parts[spot_of(8 * c + n)] = grads[part * n : part * (n + 1)]
    by_expand.start()
    flush()
    meanwhile(3)
    grad_act = side_sum(0, own, sent)

    unit = unit_d[...]
    grad = grad_act * slope(unit * gain_d[...] + bias_d[...])
    g_dilate, sums = norm_back(
        grad, unit, near_m.at[0], across_m.at[0], gain_d[...] * inv_mid[1:2]
    )
    grad_bias_d[...] = sums[0:1]
    grad_gain_d[...] = sums[1:2]
    own_rows = slice(section_rate, section_rate + OWN_ROWS)
    halo[own_rows] = g_dilate.reshape(OWN_ROWS, TILE_W, MID_OWN)
    low, high = slice(0, section_rate), slice(section_rate + OWN_ROWS, 2 * section_rate + OWN_ROWS)
    first, last = slice(section_rate, 2 * section_rate), slice(OWN_ROWS, section_rate + OWN_ROWS)
    to_before = links.send(halo.at[first], halo.at[high], pix=spot.before)
    to_after = links.send(halo.at[last], halo.at[low], pix=spot.after)
    by_expand.along_z()
    flush()
    meanwhile()
    for d in (1, 3, 2):
        links.arrive(project_sent[d], project_in.at[d - 1])
        project_wide[spot.chan(-d)] = project_in[d - 1].astype(F32)
    project_wide[j] = projects[j].astype(F32)
    links.arrive(to_before, halo.at[high])
    links.arrive(to_after, halo.at[low])
    for a in range(3):
        rows = halo[section_rate * (2 - a) : section_rate * (2 - a) + OWN_ROWS]
        rows = rows.reshape(OWN, MID_OWN).astype(F32)
        if a != 1:
            rows = rows * keep[1 - a // 2]
        for b in range(3):
            moved = rows if b == 1 else col_shift(rows, -section_rate * (b - 1))
            tap = 3 * a + b
            taps[:, MID_OWN * tap : MID_OWN * (tap + 1)] = moved.astype(BF16)
    sent = sides(1, lambda c: dot_nt(taps[...], wd_cat[mid_rows(c)]))
    own = dot_nt(taps[...], wd_cat[mid_rows(j)])
    for c in range(CHAN):
        act = act_r[c, own_rows].reshape(OWN, MID_OWN)
        grads = dot_tn(act, taps[...]).astype(BF16)
        for n in range(8):
            for tap in range(9):
                by_dilate.parts[(*spot_of(8 * c + n), tap)] = grads[
                    part * n : part * (n + 1), MID_OWN * tap : MID_OWN * (tap + 1)
                ]
    by_dilate.start()
    flush()
    meanwhile(2)
    grad_act = side_sum(1, own, sent)
    by_expand.along_x()

    unit = unit_r[...]
    grad = grad_act * slope(unit * gain_r[...] + bias_r[...])
    g_reduce, sums = norm_back(
        grad, unit, near_m.at[1], across_m.at[1], gain_r[...] * inv_mid[0:1]
    )
    grad_bias_r[...] = sums[0:1]
    grad_gain_r[...] = sums[1:2]
    full[j] = g_reduce
    sent = {d: links.send(full.at[j], full.at[j], chan=spot.chan(d)) for d in (2, 1, 3)}
    by_dilate.along_z()
    flush()
    for t in range(TASKS):
        for device in range(PIX):
            rows = []
            for start in range(40 * device, 40 * device + 40, 8):
                b, src, d = start // 256, start // HEAD % CHAN, start % HEAD
                rows.append(project_wide[src, BRANCH_PLACE[b], t, d : d + 8])
            rows.append(jnp.zeros((8, HEAD), F32))
            by_project.parts[(*spot_of(device), t)] = jnp.concatenate(rows, axis=0).astype(BF16)
    by_project.start()
    grad_expand[...] = by_expand.finish()
    meanwhile(2)
    for d in (1, 3, 2):
        links.arrive(sent[d], full.at[spot.chan(-d)])
    g_reduce = jnp.concatenate([full[c] for c in range(CHAN)], axis=1)
    weight = jnp.concatenate([wr_all[c] for c in range(CHAN)], axis=1)
    grads = dot_tn(pixels[...], g_reduce).astype(BF16)
    for c in range(CHAN):
        for n in range(8):
            by_reduce.parts[spot_of(4 * n + c)] = grads[
                HEAD * n : HEAD * (n + 1), MID_OWN * c : MID_OWN * (c + 1)
            ]
    by_reduce.start()
    grad_pixels[...] = (grad_summed + dot_nt(g_reduce, weight)).astype(BF16)
    by_reduce.along_z()
    by_project.along_z()
    meanwhile(2)
    by_reduce.along_x()
    flush()
    by_dilate.along_x()
    meanwhile(len(tasks))
    by_project.along_x()
    flush()
    reduce_out[...] = by_reduce.finish()

    def reduce_copies():
        return (
            lambda: remote(
                reduce_out, grad_reduce, ss_reduce.at[0], rs_reduce.at[0], pix=owner_i, chan=owner_j
            ),
            lambda: pltpu.make_async_copy(reduce_out, grad_reduce, rs_reduce.at[0]),
        )

    away, here = reduce_copies()
    pl.when(jnp.logical_not(stays))(lambda: away().start())
    pl.when(stays)(lambda: here().start())
    flush()
    grad_dilate[...] = by_dilate.finish()
    grad_project[...] = by_project.finish()[:, :40]

    def place(n, total):
        which, b = n // 3, n % 3
        for a in range(3):
            for t in range(TASKS):
                lane = BRANCH * a + HEAD * t
                grad_atrous[t, which, 3 * a + b] = total[:, lane : lane + HEAD]

    def place_point(n, total):
        for t in range(TASKS):
            grad_point[t] = total[:, HEAD * t : HEAD * (t + 1)]

    atrous_sum.finish(place)
    point_sum.finish(place_point)
    for core in range(2):
        edge_copy(core).wait_send()

    pltpu.make_async_copy(reduce_out, grad_reduce, rs_reduce.at[0]).wait()
    pl.when(jnp.logical_not(stays))(lambda: away().wait_send())
    links.finish()


def group_scratch(count, *shape):
    return [
        pltpu.VMEM((count, 4, *shape), BF16),
        pltpu.VMEM((count, *shape), BF16),
        pltpu.VMEM((count, 2, *shape), BF16),
    ]


def section_backward(*operands):
    whole = pl.BlockSpec(memory_space=pltpu.VMEM)
    shape = jax.ShapeDtypeStruct
    dma = pltpu.SemaphoreType.DMA
    mid, feat = (OWN, MID_OWN), (OWN, FEAT_OWN)
    return pl.pallas_call(
        section_backward_kernel,
        in_specs=[pl.BlockSpec(memory_space=pltpu.SMEM)]
        + [whole] * 20
        + [pl.BlockSpec(memory_space=pl.ANY)] * 2,
        out_specs=[whole] * 13,
        out_shape=[
            shape(feat, BF16),
            shape((HEAD, MID_OWN), F32),
            shape((1, MID_OWN), F32),
            shape((1, MID_OWN), F32),
            shape((9, 16, MID_OWN), F32),
            shape((1, MID_OWN), F32),
            shape((1, MID_OWN), F32),
            shape((16, FEAT_OWN), F32),
            shape((1, FEAT_OWN), F32),
            shape((1, FEAT_OWN), F32),
            shape((TASKS, HEAD, HEAD), F32),
            shape((TASKS, 3, 9, HEAD, HEAD), F32),
            shape((TASKS, 40, HEAD), F32),
        ],
        scratch_shapes=[
            pltpu.SMEM((GROUP_ROWS + 2 * REACH,), jnp.int32),
            pltpu.VMEM((2, OWN, MID_OWN), F32),
            pltpu.VMEM((FEAT_OWN, 9 * MID_OWN), BF16),
            pltpu.VMEM((2, 3, *mid), BF16),
            pltpu.VMEM((2, 3, *mid), BF16),
            pltpu.VMEM((OWN_ROWS + 2 * section_rate, TILE_W, MID_OWN), BF16),
            pltpu.VMEM((OWN, 9 * MID_OWN), BF16),
            pltpu.VMEM((CHAN, *mid), BF16),
            pltpu.VMEM((3, 5, TASKS, HEAD, HEAD), BF16),
            pltpu.VMEM((CHAN, 5, TASKS, HEAD, HEAD), F32),
            pltpu.VMEM((HEAD, MID_OWN), F32),
            pltpu.VMEM((2, GROUP, 8, MID_OWN), F32),
            pltpu.VMEM((2, 4, 8, MID_OWN), F32),
            pltpu.VMEM((GROUP, 8, FEAT_OWN), F32),
            pltpu.VMEM((4, 8, FEAT_OWN), F32),
            pltpu.VMEM((CHAN, GROUP_ROWS, TILE_W, 128), BF16),
            pltpu.VMEM((GROUP_ROWS * TILE_W, 256), BF16),
            pltpu.VMEM((GROUP_ROWS * TILE_W, 256), BF16),
            pltpu.VMEM((GROUP_ROWS + 2 * REACH, TILE_W, 4 * BRANCH), BF16),
            pltpu.VMEM((GROUP_ROWS * TILE_W, 3 * BRANCH), BF16),
            *scatter_scratch(16, FEAT_OWN),
            *scatter_scratch(9, 16, MID_OWN),
            *scatter_scratch(TASKS, 48, HEAD),
            *scatter_scratch(HEAD, MID_OWN),
            *group_scratch(9, HEAD, 3 * BRANCH),
            *group_scratch(1, HEAD, BRANCH),
            dma((112,)),
            dma((112,)),
            dma((1,)),
            dma((1,)),
            dma((8,)),
            dma((4,)),
        ],
        compiler_params=pltpu.CompilerParams(
            collective_id=6, has_side_effects=True, vmem_limit_bytes=VMEM_LIMIT
        ),
        cost_estimate=pl.CostEstimate(
            flops=16_000_000_000, bytes_accessed=250_000_000, transcendentals=0
        ),
        name="section_backward",
    )(*operands)


def hand_out_kernel(maps, tall, mean_all, *refs):
    count = (len(refs) - 3) // 2
    grads, (task_maps, grad_pooled), outs, sems = (
        refs[:count], refs[count : count + 2], refs[count + 2 : -1], refs[-1],
    )
    copies = [pltpu.make_async_copy(src, dst, sems.at[n]) for n, (src, dst) in enumerate(zip(grads, outs))]
    for copy in copies:
        copy.start()
    for c in range(CHAN):
        part = dot_tn(tall[...], mean_all[c])
        for t in range(TASKS):
            grad_pooled[t, :, 512 * c : 512 * (c + 1)] = part[HEAD * t : HEAD * (t + 1)]
    for t in range(TASKS):
        task_maps[t] = maps[t].reshape(OWN, HEAD).astype(F32).T.astype(BF16)
    for copy in copies:
        copy.wait()


def hand_out(maps, pooled_grad, mean_all, *grads):
    whole = pl.BlockSpec(memory_space=pltpu.VMEM)
    shape = jax.ShapeDtypeStruct
    return pl.pallas_call(
        hand_out_kernel,
        in_specs=[whole] * (3 + len(grads)),
        out_specs=[whole] * 2 + [pl.BlockSpec(memory_space=pl.ANY)] * len(grads),
        out_shape=[shape((TASKS, HEAD, OWN), BF16), shape((TASKS, HEAD, CHAN * 512), F32)]
        + [shape(grad.shape, grad.dtype) for grad in grads],
        scratch_shapes=[pltpu.SemaphoreType.DMA((len(grads),))],
        compiler_params=pltpu.CompilerParams(vmem_limit_bytes=VMEM_LIMIT),
        cost_estimate=pl.CostEstimate(flops=0, bytes_accessed=10_000_000, transcendentals=0),
        name="hand_out",
    )(maps, pooled_grad, mean_all, *grads)


def shards(
    pixels,
    tile_number,
    task_draws,
    reduce_weight,
    reduce_gain,
    reduce_bias,
    dilate_weight,
    dilate_gain,
    dilate_bias,
    expand_weight,
    expand_gain,
    expand_bias,
    point_weight,
    atrous_weight,
    pooled_weight,
    project_weight,
    cotangent,
):
    tile_grid = tile_number.reshape(2, 128)
    norms = [
        v.reshape(1, -1)
        for v in (reduce_gain, reduce_bias, dilate_gain, dilate_bias, expand_gain, expand_bias)
    ]
    pooled_rows = pooled_weight.reshape(BRANCH, -1)
    (
        trunk, unit_reduce, unit_dilate, unit_expand, act_reduce, act_dilate, reduce_all, inv_mid,
        inv_feat, project_all, maps_all,
    ) = section_forward(
        tile_number, task_draws, pixels, reduce_weight, dilate_weight, expand_weight, *norms,
        project_weight, jnp.swapaxes(cotangent, 1, 2),
    )
    kernels = atrous_weight.reshape(TASKS, 3, 3, 3, HEAD, -1)
    grad_project, x_group, mean_all, trunk_grad, g_group, maps, mean_rows, pooled_grad = heads(
        tile_number, tile_grid, trunk, maps_all, kernels, point_weight, project_all, pooled_rows, kernels
    )
    grads = section_backward(
        tile_number, trunk_grad, pixels, unit_reduce, unit_dilate, unit_expand, act_reduce, act_dilate,
        reduce_all, dilate_weight, expand_weight, *norms, inv_mid, inv_feat, mean_rows, grad_project,
        x_group, g_group,
    )
    (
        task_maps, grad_pooled, grad_pixels, grad_reduce, grad_gain_r, grad_bias_r, grad_dilate,
        grad_gain_d, grad_bias_d, grad_expand, grad_gain_e, grad_bias_e, grad_point, grad_atrous,
        grad_project,
    ) = hand_out(maps, pooled_grad, mean_all, *grads)
    return (
        jnp.swapaxes(task_maps, 1, 2),
        grad_pixels,
        grad_reduce,
        grad_gain_r[0],
        grad_bias_r[0],
        grad_dilate,
        grad_gain_d[0],
        grad_bias_d[0],
        grad_expand,
        grad_gain_e[0],
        grad_bias_e[0],
        grad_point,
        grad_atrous,
        jnp.swapaxes(grad_pooled, 1, 2),
        grad_project,
    )


def solution(mesh):
    placed = (
        P("pix", "chan"),
        P(),
        P(),
        P(None, "chan"),
        P("chan"),
        P("chan"),
        P(None, None, "chan"),
        P("chan"),
        P("chan"),
        P(None, "chan"),
        P("chan"),
        P("chan"),
        P(None, "chan", None),
        P(None, None, None, "chan", None),
        P(None, "chan", None),
        P(None, "chan", None),
        P(None, "pix", "chan"),
    )
    return jax.shard_map(
        shards,
        mesh=mesh,
        in_specs=placed,
        out_specs=(
            P(None, "pix", "chan"),
            P("pix", "chan"),
            P("pix", "chan"),
            P("chan"),
            P("chan"),
            P(None, "pix", "chan"),
            P("chan"),
            P("chan"),
            P("pix", "chan"),
            P("chan"),
            P("chan"),
            P(None, "pix", "chan"),
            P(None, None, None, "pix", "chan"),
            P(None, None, "chan"),
            P(None, "pix", "chan"),
        ),
        check_vma=False,
    )
```
